32 devices in a mesh: dp: 4 (over z), wide: 4 (over x, core), narrow: 2 (over y).
Axes of the slice: x: 2, y: 2, z: 4, core: 2. Of those that a mesh axis runs over, the one named last changes fastest.
Arguments:
- tokens: bfloat16 [16384, 768], P(('dp', 'wide')), may hold values from -6 to 6
- memory: bfloat16 [32, 2048, 768], P(('dp', 'wide')), may hold values from -6 to 6
- cotangent: bfloat16 [16384, 768], P(('dp', 'wide')), may hold values from -6 to 6
- norm1_gain: bfloat16 [768], P('wide'), may hold values from 0.5 to 1.5
- norm2_gain: bfloat16 [768], P('wide'), may hold values from 0.5 to 1.5
- norm3_gain: bfloat16 [768], P('wide'), may hold values from 0.5 to 1.5
- q_weight: bfloat16 [768, 768], P('wide', 'narrow'), may hold values from -0.3125 to 0.3125
- k_weight: bfloat16 [768, 768], P('wide', 'narrow'), may hold values from -0.3125 to 0.3125
- v_weight: bfloat16 [768, 768], P('wide', 'narrow'), may hold values from -0.21875 to 0.21875
- o_weight: bfloat16 [768, 768], P('wide', 'narrow'), may hold values from -0.4375 to 0.4375
- cross_q: bfloat16 [768, 768], P('wide', 'narrow'), may hold values from -0.3125 to 0.3125
- cross_k: bfloat16 [768, 768], P('wide', 'narrow'), may hold values from -0.3125 to 0.3125
- cross_v: bfloat16 [768, 768], P('wide', 'narrow'), may hold values from -0.21875 to 0.21875
- cross_o: bfloat16 [768, 768], P('wide', 'narrow'), may hold values from -1.25 to 1.25
- gate_weight: bfloat16 [768, 2048], P('wide', 'narrow'), may hold values from -0.21875 to 0.21875
- up_weight: bfloat16 [768, 2048], P('wide', 'narrow'), may hold values from -0.21875 to 0.21875
- down_weight: bfloat16 [768, 2048], P('wide', 'narrow'), may hold values from -0.1875 to 0.1875
- segment_ids: int32 [16, 1024], P(('dp', 'wide')), may hold values from 0 to 7, never falling along the last dimension, each value on 1 to 256 neighbouring positions
- block_ids: int32 [16, 1024], P(('dp', 'wide')), may hold values from 0 to 63, never falling along the last dimension, each value on 1 to 32 neighbouring positions
- image_table: int32 [16, 8], P(('dp', 'wide')), may hold values from 0 to 1
Outputs:
- output: bfloat16 [16384, 768], P(('dp', 'wide'))
- tokens_grad: bfloat16 [16384, 768], P(('dp', 'wide'))
- memory_grad: bfloat16 [32, 2048, 768], P(('dp', 'wide'), None, 'narrow')
- norm1_gain_grad: float32 [768], P('wide')
- norm2_gain_grad: float32 [768], P('wide')
- norm3_gain_grad: float32 [768], P('wide')
- q_weight_grad: float32 [768, 768], P('wide', 'narrow')
- k_weight_grad: float32 [768, 768], P('wide', 'narrow')
- v_weight_grad: float32 [768, 768], P('wide', 'narrow')
- o_weight_grad: float32 [768, 768], P('wide', 'narrow')
- cross_q_grad: float32 [768, 768], P('wide', 'narrow')
- cross_k_grad: float32 [768, 768], P('wide', 'narrow')
- cross_v_grad: float32 [768, 768], P('wide', 'narrow')
- cross_o_grad: float32 [768, 768], P('wide', 'narrow')
- gate_weight_grad: float32 [768, 2048], P('wide', 'narrow')
- up_weight_grad: float32 [768, 2048], P('wide', 'narrow')
- down_weight_grad: float32 [768, 2048], P('wide', 'narrow')
The draws below stay inside these ranges and needn't reach their ends.
Inputs may be any that keep to these rules, and one draw needn't show every extreme that they name: `segment_ids`: in each decoder row the ids never fall and every id occurs, each on 1 to 256 positions, some id on exactly that many. `block_ids`: in each decoder row the ids never fall and every id occurs, each on 1 to 32 positions, some id on exactly that many. `image_table`: entry r, s names one of the 2 images stored with decoder row r, the images r * 2 to r * 2 + 1.
All inputs are finite; a program needn't handle non-finite values.
Results may differ from the reference program's by a relative error of at most 0.038.
Values may be sent and summed in bfloat16 or wider, within the bound.
No kernel may reach another device: no remote copies, remote signals or barrier semaphores. Data moves between devices by JAX's collectives and lax.ppermute only.
A program may use at most 384 MiB of HBM per device.

```python
import functools
import math
import jax
import jax.numpy as jnp
import numpy as np
from jax import lax

D = 768
HEADS = 12
HEAD_DIM = 64
INNER = 768
FF = 2048
MEM = 2048
SEQ = 1024
SEGS = 8
BLOCKS = 64
IMG_DEV = 2
ROWS = 16
TOKENS = 16384
IMAGES = 32
N_NARROW = 2


def set_ends(values, key, low, top_value):
    shape = values.shape
    place = [jax.random.randint(jax.random.fold_in(key, axis), (), 0, shape[axis]) for axis in range(len(shape))]
    values = values.at[tuple(place)].set(low)
    longest = shape.index(max(shape))
    place[longest] = (place[longest] + 1) % shape[longest]
    return values.at[tuple(place)].set(top_value)


def level_of(own_key, dims, shards, least, largest):
    loudness = 1.0
    for position, shards_of in shards:
        heights = jax.random.uniform(jax.random.fold_in(jax.random.fold_in(own_key, 6), position), (shards_of,), jnp.float32, least / len(shards), largest / len(shards))
        loudness = loudness * jnp.repeat(jnp.exp(heights), dims[position] // shards_of).reshape((-1,) + (1,) * (len(dims) - 1 - position))
    return loudness


def profile(number_of, total, most, skew):
    portions = [(1 << 20) // math.isqrt(standing ** skew) + 1 for standing in range(2, number_of + 1)]
    spare, holding = total - most - (number_of - 1), [1] * (number_of - 1)
    while spare > 0:
        candidates = [i for i in range(number_of - 1) if holding[i] < most]
        mass, budget = sum([portions[i] for i in candidates]), spare
        for i in candidates:
            extra = min(most - holding[i], max(1, budget * portions[i] // mass), spare)
            holding[i] = holding[i] + extra
            spare = spare - extra
    return np.array([most] + holding)


def ragged_sizes(stream_key, count, total, reach, slope):
    if count == 2:
        one = jax.random.randint(stream_key, (), max(1, total - reach), min(reach, total - 1) + 1)
        return jnp.stack([one, total - one])
    sizes = jnp.asarray(profile(count, total, reach, slope), jnp.int32)
    couples = (count - 1) // 2
    donor, receiver = sizes[1:1 + 2 * couples:2], sizes[2:2 + 2 * couples:2]
    room = jnp.minimum(donor - 1, reach - receiver)
    shifted = jax.random.randint(jax.random.fold_in(stream_key, 1), (couples,), 0, 1 << 20) % (room + 1)
    sizes = sizes.at[1:1 + 2 * couples:2].set(donor - shifted).at[2:2 + 2 * couples:2].set(receiver + shifted)
    return sizes[jax.random.permutation(jax.random.fold_in(stream_key, 2), count)]


def bell_draw(own_key, shape, deviation, bound, shards=(), kind=jnp.bfloat16):
    gain = level_of(own_key, shape, shards, -0.22, 0.18) if shards else 1.0
    array = jax.random.normal(own_key, shape, jnp.float32) * deviation * gain
    return jnp.minimum(jnp.maximum(array, -bound), bound).astype(kind)


def setup_inputs(seed: int = 0) -> dict:
    arg_keys = jax.random.split(jax.random.key(seed), 21)
    tokens = bell_draw(arg_keys[0], (TOKENS, D), 1.0, 6.0, ((0, 16),))
    memory = bell_draw(arg_keys[1], (IMAGES, MEM, D), 1.0, 6.0, ((0, 16),))
    cotangent = bell_draw(arg_keys[2], (TOKENS, D), 1.0, 6.0, ((0, 16),))
    norm1_gain = jnp.clip(1.0 + 0.1 * jax.random.normal(arg_keys[3], (D,), jnp.float32), 0.5, 1.5).astype(jnp.bfloat16)
    norm2_gain = jnp.clip(1.0 + 0.1 * jax.random.normal(arg_keys[4], (D,), jnp.float32), 0.5, 1.5).astype(jnp.bfloat16)
    norm3_gain = jnp.clip(1.0 + 0.1 * jax.random.normal(arg_keys[5], (D,), jnp.float32), 0.5, 1.5).astype(jnp.bfloat16)
    q_weight = bell_draw(arg_keys[6], (D, INNER), (D // 2) ** -0.5, 0.3125, ((0, 4), (1, 2)))
    k_weight = bell_draw(arg_keys[7], (D, INNER), (D // 2) ** -0.5, 0.3125, ((0, 4), (1, 2)))
    v_weight = bell_draw(arg_keys[8], (D, INNER), D ** -0.5, 0.21875, ((0, 4), (1, 2)))
    o_weight = bell_draw(arg_keys[9], (D, INNER), (INNER // 4) ** -0.5, 0.4375, ((0, 4), (1, 2)))
    cross_q = bell_draw(arg_keys[10], (D, INNER), (D // 2) ** -0.5, 0.3125, ((0, 4), (1, 2)))
    cross_k = bell_draw(arg_keys[11], (D, INNER), (D // 2) ** -0.5, 0.3125, ((0, 4), (1, 2)))
    cross_v = bell_draw(arg_keys[12], (D, INNER), D ** -0.5, 0.21875, ((0, 4), (1, 2)))
    cross_o = bell_draw(arg_keys[13], (D, INNER), (INNER // 32) ** -0.5, 1.25, ((0, 4), (1, 2)))
    gate_weight = bell_draw(arg_keys[14], (D, FF), D ** -0.5, 0.21875, ((0, 4), (1, 2)))
    up_weight = bell_draw(arg_keys[15], (D, FF), D ** -0.5, 0.21875, ((0, 4), (1, 2)))
    down_weight = bell_draw(arg_keys[16], (D, FF), (FF // 2) ** -0.5, 0.1875, ((0, 4), (1, 2)))
    segment_ids = jax.vmap(lambda own: jnp.searchsorted(jnp.cumsum(ragged_sizes(own, SEGS, SEQ, 2 * SEQ // SEGS, 1)), jnp.arange(SEQ), side="right"))(jax.random.split(arg_keys[17], ROWS)).reshape((ROWS, SEQ)).astype(jnp.int32)
    block_ids = jax.vmap(lambda own: jnp.searchsorted(jnp.cumsum(ragged_sizes(own, BLOCKS, SEQ, 2 * SEQ // BLOCKS, 1)), jnp.arange(SEQ), side="right"))(jax.random.split(arg_keys[18], ROWS)).reshape((ROWS, SEQ)).astype(jnp.int32)
    image_table = set_ends(jax.random.randint(arg_keys[19], (ROWS, SEGS), 0, IMG_DEV), jax.random.fold_in(arg_keys[19], 1), 0, IMG_DEV - 1).astype(jnp.int32)
    return dict(tokens=tokens, memory=memory, cotangent=cotangent, norm1_gain=norm1_gain, norm2_gain=norm2_gain, norm3_gain=norm3_gain, q_weight=q_weight, k_weight=k_weight, v_weight=v_weight, o_weight=o_weight, cross_q=cross_q, cross_k=cross_k, cross_v=cross_v, cross_o=cross_o, gate_weight=gate_weight, up_weight=up_weight, down_weight=down_weight, segment_ids=segment_ids, block_ids=block_ids, image_table=image_table)


EPSILON = 1e-06
ROOT_TWO_OVER_PI = 0.7978845608028654
HIGHEST_PRECISION = lax.Precision.HIGHEST

@jax.custom_vjp
def low(v):
    return lax.optimization_barrier(v.astype(jnp.bfloat16)).astype(jnp.float32)

@jax.custom_vjp
def low_back(v):
    return v

def low_keep(v):
    return (low(v), None)

def low_pass(kept, grad):
    return (grad,)

def back_keep(v):
    return (v, None)

def back_low(kept, grad):
    return (low(grad),)
low.defvjp(low_keep, low_pass)
low_back.defvjp(back_keep, back_low)

def rounded_both(values):
    return low(low_back(values))

def matrix_product(left, right):
    return jnp.dot(left, right, precision=HIGHEST_PRECISION, preferred_element_type=jnp.float32)

def rms_norm(values, gain_vector):
    factor = lax.rsqrt(lax.optimization_barrier(jnp.mean(values * values, axis=1, keepdims=True)) + EPSILON)
    return values * factor * gain_vector[None, :]

def gelu_tanh(values):
    return 0.5 * values * (1.0 + jnp.tanh(ROOT_TWO_OVER_PI * (values + 0.044715 * values * values * values)))

def attend(queries, keys_all, values_all, visible):
    scores = low_back(jnp.einsum('qhd,khd->hqk', queries, keys_all, precision=HIGHEST_PRECISION) * HEAD_DIM ** (-0.5))
    scores = jnp.where(visible[None, :, :], scores, -jnp.inf)
    highest = lax.optimization_barrier(jnp.max(scores, axis=2, keepdims=True))
    exponent = jnp.exp(scores - highest)
    probabilities = low(exponent / lax.optimization_barrier(jnp.sum(exponent, axis=2, keepdims=True)))
    return jnp.einsum('hqk,khd->qhd', probabilities, values_all, precision=HIGHEST_PRECISION)

def self_group(inputs):
    queries, keys_all, values_all, segments, blocks = inputs
    block_rows = min(512, SEQ)
    num_blocks = SEQ // block_rows

    def one_block(portion):
        query_part, segment_part, block_part = portion
        visible = (segment_part[:, None] == segments[None, :]) & (blocks[None, :] <= block_part[:, None])
        return attend(query_part, keys_all, values_all, visible)
    result = lax.map(jax.checkpoint(one_block), (queries.reshape(num_blocks, block_rows, HEADS, HEAD_DIM), segments.reshape(num_blocks, block_rows), blocks.reshape(num_blocks, block_rows)))
    return result.reshape(SEQ, INNER)

def cross_group(inputs):
    queries, keys_all, values_all, images = inputs
    block_rows = min(512, SEQ)
    num_blocks = SEQ // block_rows
    key_images = jnp.arange(IMG_DEV * MEM, dtype=jnp.int32) // MEM

    def one_block(portion):
        query_part, image_part = portion
        visible = image_part[:, None] == key_images[None, :]
        return attend(query_part, keys_all, values_all, visible)
    result = lax.map(jax.checkpoint(one_block), (queries.reshape(num_blocks, block_rows, HEADS, HEAD_DIM), images.reshape(num_blocks, block_rows)))
    return result.reshape(SEQ, INNER)

def branch(values, weight):
    partials = jnp.einsum('tgc,dgc->gtd', values.reshape(TOKENS, N_NARROW, -1), weight.reshape(D, N_NARROW, -1), precision=HIGHEST_PRECISION)
    return low_back(lax.optimization_barrier(jnp.sum(low(partials), axis=0)))

def layer(segment_ids, block_ids, image_table, tokens, memory, norm1_gain, norm2_gain, norm3_gain, q_weight, k_weight, v_weight, o_weight, cross_q, cross_k, cross_v, cross_o, gate_weight, up_weight, down_weight):
    row_shape = (ROWS, SEQ, HEADS, HEAD_DIM)
    normed_one = low(rms_norm(tokens, norm1_gain))
    queries = rounded_both(matrix_product(normed_one, q_weight))
    keys_self = rounded_both(matrix_product(normed_one, k_weight))
    values_self = rounded_both(matrix_product(normed_one, v_weight))
    attended = lax.map(self_group, (queries.reshape(row_shape), keys_self.reshape(row_shape), values_self.reshape(row_shape), segment_ids, block_ids))
    attended = rounded_both(attended.reshape(TOKENS, INNER))
    middle = tokens + branch(attended, o_weight)
    normed_two = low(rms_norm(middle, norm2_gain))
    cross_queries = rounded_both(matrix_product(normed_two, cross_q))
    flat_memory = memory.reshape(IMAGES * MEM, D)
    memory_shape = (ROWS, IMG_DEV * MEM, HEADS, HEAD_DIM)
    cross_keys = rounded_both(matrix_product(flat_memory, cross_k)).reshape(memory_shape)
    cross_values = rounded_both(matrix_product(flat_memory, cross_v)).reshape(memory_shape)
    token_images = jnp.take_along_axis(image_table, segment_ids, axis=1)
    crossed = lax.map(cross_group, (cross_queries.reshape(row_shape), cross_keys, cross_values, token_images))
    crossed = rounded_both(crossed.reshape(TOKENS, INNER))
    after_cross = middle + branch(crossed, cross_o)
    normed_three = low(rms_norm(after_cross, norm3_gain))
    gate_value = low_back(matrix_product(normed_three, gate_weight))
    up_value = low_back(matrix_product(normed_three, up_weight))
    hidden = low(gelu_tanh(gate_value) * up_value)
    return after_cross + branch(hidden, down_weight)

def reference(tokens, memory, cotangent, norm1_gain, norm2_gain, norm3_gain, q_weight, k_weight, v_weight, o_weight, cross_q, cross_k, cross_v, cross_o, gate_weight, up_weight, down_weight, segment_ids, block_ids, image_table):
    layer_of_floats = functools.partial(layer, segment_ids, block_ids, image_table)
    result, pullback = jax.vjp(layer_of_floats, tokens.astype(jnp.float32), memory.astype(jnp.float32), norm1_gain.astype(jnp.float32), norm2_gain.astype(jnp.float32), norm3_gain.astype(jnp.float32), q_weight.astype(jnp.float32), k_weight.astype(jnp.float32), v_weight.astype(jnp.float32), o_weight.astype(jnp.float32), cross_q.astype(jnp.float32), cross_k.astype(jnp.float32), cross_v.astype(jnp.float32), cross_o.astype(jnp.float32), gate_weight.astype(jnp.float32), up_weight.astype(jnp.float32), down_weight.astype(jnp.float32))
    gradients = pullback(cotangent.astype(jnp.float32))
    return (result.astype(jnp.bfloat16), gradients[0].astype(jnp.bfloat16), gradients[1].astype(jnp.bfloat16), gradients[2], gradients[3], gradients[4], gradients[5], gradients[6], gradients[7], gradients[8], gradients[9], gradients[10], gradients[11], gradients[12], gradients[13], gradients[14], gradients[15])
```

```python
import functools
import math

import jax
import jax.numpy as jnp
from jax import lax
from jax.experimental import pallas as pl
from jax.experimental.pallas import tpu as pltpu
from jax.sharding import PartitionSpec as P

F32 = jnp.float32
BF16 = jnp.bfloat16
EPSILON = 1e-06
ROOT_TWO_OVER_PI = 0.7978845608028654
CUBIC = 0.044715
HEAD_DIM = 64
PAIR = 2 * HEAD_DIM
SCALE = HEAD_DIM ** (-0.5)
EXP2_SCALE = SCALE * math.log2(math.e)
HIDE = 1e30
TILE = 256

NN = (((1,), (0,)), ((), ()))
NT = (((1,), (1,)), ((), ()))
TN = (((0,), (0,)), ((), ()))


def dot(left, right, dims):
    return lax.dot_general(left, right, dims, preferred_element_type=F32)


def params():
    return pltpu.CompilerParams(vmem_limit_bytes=60 * 1024 * 1024)


def cost(flops, nbytes):
    return pl.CostEstimate(flops=int(flops), bytes_accessed=int(nbytes), transcendentals=0)


def shape_of(shape, dtype):
    return jax.ShapeDtypeStruct(shape, dtype)


def whole(shape):
    zeros = (0,) * len(shape)
    return pl.BlockSpec(shape, lambda *_: zeros)


def rows(width, height=TILE):
    return pl.BlockSpec((height, width), lambda t, *_: (t, 0))


def inverse_rms(values):
    return lax.rsqrt(jnp.mean(values * values, axis=1, keepdims=True) + EPSILON)


def norm_back(values, gain, upstream):
    factor = inverse_rms(values)
    scaled = upstream * gain
    mean = jnp.mean(values * scaled, axis=1, keepdims=True)
    grad = factor * scaled - values * (factor * factor * factor * mean)
    return grad, jnp.sum(upstream * values * factor, axis=0, keepdims=True)


def in_half(shape, half):
    return (lax.broadcasted_iota(jnp.int32, shape, 1) // HEAD_DIM) == half


def only_half(values, half):
    return jnp.where(in_half(values.shape, half), values, jnp.zeros_like(values))


def order_kernel(seg, blk, table, x, gy, xp, gyp, row_ids, col_ids, pos_out, scalars, pos):
    step = pl.program_id(0)
    count = seg.shape[1]

    @pl.when(step == 0)
    def _():
        segments = seg[...]
        image = jnp.zeros_like(segments)
        for s in range(table.shape[1]):
            image = jnp.where(segments == s, table[0, s], image)
        first = (image == 0).astype(F32)
        before = lax.broadcasted_iota(jnp.int32, (count, count), 0) < lax.broadcasted_iota(
            jnp.int32, (count, count), 1
        )
        rank = dot(
            jnp.broadcast_to(first, (8, count)).astype(BF16),
            before.astype(F32).astype(BF16),
            NN,
        )[0:1]
        total = jnp.sum(first)
        index = lax.broadcasted_iota(jnp.int32, (1, count), 1).astype(F32)
        place = jnp.where(image == 0, rank, total + index - rank)
        pos[...] = place.astype(jnp.int32)
        pos_out[...] = jnp.broadcast_to(pos[...], (8, count))
        n0 = total.astype(jnp.int32)
        tiles = count // TILE
        visits0 = jnp.maximum(1, (n0 + TILE - 1) // TILE)
        start1 = jnp.minimum(tiles - 1, n0 // TILE)
        visits = visits0 + tiles - start1
        for v in range(tiles + 1):
            real = jnp.minimum(v, visits - 1)
            in_first = real < visits0
            scalars[v] = jnp.where(in_first, real, real - visits0 + start1)
            scalars[8 + v] = jnp.where(in_first, 0, 1)
        scalars[16] = visits
        scalars[17] = n0

    onehot = (
        lax.broadcasted_iota(jnp.int32, (TILE, count), 0) + step * TILE == pos[...]
    ).astype(F32).astype(BF16)
    xp[...] = dot(onehot, x[...], NN).astype(BF16)
    gyp[...] = dot(onehot, gy[...], NN).astype(BF16)
    ids = jnp.concatenate(
        [
            seg[...].astype(F32),
            blk[...].astype(F32),
            jnp.zeros((126, count), F32),
        ],
        axis=0,
    ).astype(BF16)
    row_ids[...] = dot(ids[0:8], onehot, NT)
    col_ids[...] = dot(onehot, ids, NT)


def order_rows(seg, blk, table, x, gy):
    count, width = x.shape
    return pl.pallas_call(
        order_kernel,
        grid=(count // TILE,),
        in_specs=[
            whole((1, count)),
            whole((1, count)),
            pl.BlockSpec(memory_space=pltpu.SMEM),
            whole((count, width)),
            whole((count, width)),
        ],
        out_specs=[
            rows(width),
            rows(width),
            pl.BlockSpec((8, TILE), lambda t: (0, t)),
            rows(128),
            whole((8, count)),
            pl.BlockSpec(memory_space=pltpu.SMEM),
        ],
        out_shape=[
            shape_of((count, width), BF16),
            shape_of((count, width), BF16),
            shape_of((8, count), F32),
            shape_of((count, 128), F32),
            shape_of((8, count), jnp.int32),
            shape_of((32,), jnp.int32),
        ],
        scratch_shapes=[pltpu.VMEM((1, count), jnp.int32)],
        compiler_params=params(),
        cost_estimate=cost(4 * count * count * width, 8 * count * width),
    )(seg, blk, table, x, gy)


def restore_kernel(pos, values, out):
    count = values.shape[0]
    onehot = (
        lax.broadcasted_iota(jnp.int32, (count, TILE), 0) == pos[0:1, :]
    ).astype(F32).astype(BF16)
    out[...] = dot(onehot, values[...], TN).astype(BF16)


def restore_rows(pos, values):
    count, width = values.shape
    return pl.pallas_call(
        restore_kernel,
        grid=(count // TILE,),
        in_specs=[pl.BlockSpec((8, TILE), lambda t: (0, t)), whole((count, width))],
        out_specs=rows(width),
        out_shape=shape_of((count, width), BF16),
        compiler_params=params(),
        cost_estimate=cost(2 * count * count * width, 4 * count * width),
    )(pos, values)


def project_kernel(x, gain, weight, normed, out):
    values = x[...].astype(F32)
    n1 = (values * inverse_rms(values) * gain[...]).astype(BF16)
    normed[...] = n1
    out[...] = dot(n1, weight[...], NN).astype(BF16)


def norm_project(x, gain, weight):
    count, width = x.shape
    outs = weight.shape[1]
    return pl.pallas_call(
        project_kernel,
        grid=(count // TILE,),
        in_specs=[rows(width), whole((1, width)), whole(weight.shape)],
        out_specs=[rows(width), rows(outs)],
        out_shape=[shape_of((count, width), BF16), shape_of((count, outs), BF16)],
        compiler_params=params(),
        cost_estimate=cost(2 * count * width * outs, 4 * count * width + 2 * count * outs),
    )(x, gain, weight)


SELF_TILE = 128
SELF_WINDOW = 512
BACK_WINDOW = 640


def store_logs(ref, columns, logs, extra=None):
    spread = jnp.where(in_half((logs[0].shape[0], PAIR), 0), logs[0], logs[1]).T
    for half in range(2):
        line = spread[half * HEAD_DIM : half * HEAD_DIM + 1, :]
        if extra is not None:
            line = jnp.where(extra, line, ref[half : half + 1, columns])
        ref[half : half + 1, columns] = line


def self_forward_kernel(q, k, v, row_ids, col_ids, out, logs):
    count = q.shape[0]
    for tile in range(count // SELF_TILE):
        base = tile * SELF_TILE
        start = min(max(base - 256, 0), count - SELF_WINDOW)
        spot = slice(base, base + SELF_TILE)
        window = slice(start, start + SELF_WINDOW)
        seen = (col_ids[spot, 0:1] == row_ids[0:1, window]) & (
            row_ids[1:2, window] <= col_ids[spot, 1:2]
        )
        bias = jnp.where(seen, 0.0, -HIDE)
        keys = k[window, :]
        values = v[window, :]
        queries = q[spot, :]
        parts, totals = [], []
        for half in range(2):
            scores = dot(only_half(queries, half), keys, NT) * EXP2_SCALE + bias
            highest = jnp.max(scores, axis=1, keepdims=True)
            weights = jnp.exp2(scores - highest)
            total = jnp.sum(weights, axis=1, keepdims=True)
            parts.append(dot(weights.astype(BF16), values, NN) / total)
            totals.append(highest + jnp.log2(total))
        out[spot, :] = jnp.where(in_half(parts[0].shape, 0), parts[0], parts[1]).astype(BF16)
        store_logs(logs, spot, totals)


def self_forward(qkv, row_ids, col_ids):
    count = qkv.shape[0]
    inner = qkv.shape[1] // 3
    pairs = inner // PAIR

    def part(which):
        return pl.BlockSpec((count, PAIR), lambda p: (0, which * pairs + p))

    return pl.pallas_call(
        self_forward_kernel,
        grid=(pairs,),
        in_specs=[part(0), part(1), part(2), whole((8, count)), whole((count, 128))],
        out_specs=[
            pl.BlockSpec((count, PAIR), lambda p: (0, p)),
            pl.BlockSpec((8, count), lambda p: (p, 0)),
        ],
        out_shape=[shape_of((count, inner), BF16), shape_of((8 * pairs, count), F32)],
        compiler_params=params(),
        cost_estimate=cost(16 * count * SELF_WINDOW * inner, 8 * count * inner),
    )(qkv, qkv, qkv, row_ids, col_ids)


def self_backward_kernel(q, k, v, grad, logs, deltas, row_ids, col_ids, dq, dk, dv, key_sum, value_sum):
    count = q.shape[0]
    key_sum[...] = jnp.zeros_like(key_sum)
    value_sum[...] = jnp.zeros_like(value_sum)
    for tile in range(count // TILE):
        base = tile * TILE
        start = min(max(base - 256, 0), count - BACK_WINDOW)
        spot = slice(base, base + TILE)
        window = slice(start, start + BACK_WINDOW)
        seen = (col_ids[window, 0:1] == row_ids[0:1, spot]) & (
            col_ids[window, 1:2] <= row_ids[1:2, spot]
        )
        bias = jnp.where(seen, 0.0, -HIDE)
        keys = k[window, :]
        values = v[window, :]
        queries = q[spot, :]
        grads = grad[spot, :]
        parts = []
        for half in range(2):
            one_query = only_half(queries, half)
            one_grad = only_half(grads, half)
            scores = dot(keys, one_query, NT) * EXP2_SCALE + bias
            weights = jnp.exp2(scores - logs[half : half + 1, spot])
            slopes = dot(values, one_grad, NT)
            pushed = (weights * (slopes - deltas[half : half + 1, spot])).astype(BF16)
            value_sum[window, :] += dot(weights.astype(BF16), one_grad, NN)
            key_sum[window, :] += dot(pushed, one_query, NN)
            parts.append(dot(pushed, keys, TN))
        dq[spot, :] = (
            jnp.where(in_half(parts[0].shape, 0), parts[0], parts[1]) * SCALE
        ).astype(BF16)
    dk[...] = (key_sum[...] * SCALE).astype(BF16)
    dv[...] = value_sum[...].astype(BF16)


def self_backward(qkv, grad, logs, deltas, row_ids, col_ids):
    count = qkv.shape[0]
    inner = qkv.shape[1] // 3
    pairs = inner // PAIR

    def part(which):
        return pl.BlockSpec((count, PAIR), lambda p: (0, which * pairs + p))

    line = pl.BlockSpec((8, count), lambda p: (p, 0))
    return pl.pallas_call(
        self_backward_kernel,
        grid=(pairs,),
        in_specs=[
            part(0),
            part(1),
            part(2),
            part(0),
            line,
            line,
            whole((8, count)),
            whole((count, 128)),
        ],
        out_specs=[part(0)] * 3,
        out_shape=[shape_of((count, inner), BF16)] * 3,
        scratch_shapes=[pltpu.VMEM((count, PAIR), F32)] * 2,
        compiler_params=params(),
        cost_estimate=cost(40 * count * BACK_WINDOW * inner, 16 * count * inner),
    )(qkv, qkv, qkv, grad, logs, deltas, row_ids, col_ids)


def cross_forward_kernel(scalars, q, k, v, out, logs):
    step = pl.program_id(1)
    tile = scalars[step]
    image = scalars[8 + step]
    again = (step > 0) & (scalars[jnp.maximum(step - 1, 0)] == tile)

    @pl.when(step < scalars[16])
    def _():
        queries = q[...]
        keys = k[...]
        values = v[...]
        parts, totals = [], []
        for half in range(2):
            scores = dot(only_half(queries, half), keys, NT)
            highest = jnp.max(scores, axis=1, keepdims=True) * EXP2_SCALE
            weights = jnp.exp2(scores * EXP2_SCALE - highest)
            total = jnp.sum(weights, axis=1, keepdims=True)
            parts.append(dot(weights.astype(BF16), values, NN) / total)
            totals.append(highest + jnp.log2(total))
        mixed = jnp.where(in_half(parts[0].shape, 0), parts[0], parts[1]).astype(BF16)
        limit = scalars[17] - tile * TILE
        row_mine = (
            lax.broadcasted_iota(jnp.int32, mixed.shape, 0) >= limit
        ) == (image == 1)
        lane_mine = (
            lax.broadcasted_iota(jnp.int32, (1, TILE), 1) >= limit
        ) == (image == 1)
        keep = jnp.logical_not(again)
        out[...] = jnp.where(row_mine | keep, mixed, out[...])
        store_logs(logs, slice(0, TILE), totals, lane_mine | keep)


def cross_forward(scalars, q, keys_values, images):
    count, inner = q.shape
    pairs = inner // PAIR
    memory_rows = keys_values.shape[0] // images
    tile_spec = pl.BlockSpec((TILE, PAIR), lambda p, s, sc: (sc[s], p))

    def part(which):
        return pl.BlockSpec(
            (memory_rows, PAIR), lambda p, s, sc: (sc[8 + s], which * pairs + p)
        )

    return pl.pallas_call(
        cross_forward_kernel,
        grid_spec=pltpu.PrefetchScalarGridSpec(
            num_scalar_prefetch=1,
            grid=(pairs, count // TILE + 1),
            in_specs=[tile_spec, part(0), part(1)],
            out_specs=[
                tile_spec,
                pl.BlockSpec((8, TILE), lambda p, s, sc: (p, sc[s])),
            ],
        ),
        out_shape=[shape_of((count, inner), BF16), shape_of((8 * pairs, count), F32)],
        compiler_params=params(),
        cost_estimate=cost(20 * count * memory_rows * inner, 8 * memory_rows * inner),
    )(scalars, q, keys_values, keys_values)


def cross_backward_kernel(
    scalars, q, k, v, grad, logs, deltas, dq, dk, dv, key_sum, value_sum
):
    step = pl.program_id(1)
    tile = scalars[step]
    image = scalars[8 + step]
    before = jnp.maximum(step - 1, 0)
    visits = scalars[16]
    again = (step > 0) & (scalars[before] == tile)
    first = (step == 0) | (scalars[8 + before] != image)
    after = jnp.minimum(step + 1, visits - 1)
    last = (step == visits - 1) | (scalars[8 + after] != image)

    @pl.when(first)
    def _():
        key_sum[...] = jnp.zeros_like(key_sum)
        value_sum[...] = jnp.zeros_like(value_sum)

    @pl.when(step < visits)
    def _():
        queries = q[...]
        grads = grad[...]
        keys = k[...]
        values = v[...]
        limit = scalars[17] - tile * TILE
        lane_mine = (
            lax.broadcasted_iota(jnp.int32, (1, TILE), 1) >= limit
        ) == (image == 1)
        parts = []
        for half in range(2):
            one_query = only_half(queries, half)
            one_grad = only_half(grads, half)
            log = jnp.where(lane_mine, logs[half : half + 1, :], HIDE)
            scores = dot(keys, one_query, NT)
            weights = jnp.exp2(scores * EXP2_SCALE - log)
            slopes = dot(values, one_grad, NT)
            pushed = (weights * (slopes - deltas[half : half + 1, :])).astype(BF16)
            value_sum[...] += dot(weights.astype(BF16), one_grad, NN)
            key_sum[...] += dot(pushed, one_query, NN)
            parts.append(dot(pushed, keys, TN))
        grad_query = (
            jnp.where(in_half(parts[0].shape, 0), parts[0], parts[1]) * SCALE
        ).astype(BF16)
        dq[...] = jnp.where(again, dq[...] + grad_query, grad_query)

        @pl.when(last)
        def _():
            dk[...] = (key_sum[...] * SCALE).astype(BF16)
            dv[...] = value_sum[...].astype(BF16)


def cross_backward(scalars, q, keys_values, grad, logs, deltas, images):
    count, inner = q.shape
    pairs = inner // PAIR
    memory_rows = keys_values.shape[0] // images
    tile_spec = pl.BlockSpec((TILE, PAIR), lambda p, s, sc: (sc[s], p))
    line = pl.BlockSpec((8, TILE), lambda p, s, sc: (p, sc[s]))

    def part(which):
        return pl.BlockSpec(
            (memory_rows, PAIR), lambda p, s, sc: (sc[8 + s], which * pairs + p)
        )

    return pl.pallas_call(
        cross_backward_kernel,
        grid_spec=pltpu.PrefetchScalarGridSpec(
            num_scalar_prefetch=1,
            grid=(pairs, count // TILE + 1),
            in_specs=[tile_spec, part(0), part(1), tile_spec, line, line],
            out_specs=[tile_spec, part(0), part(0)],
            scratch_shapes=[pltpu.VMEM((memory_rows, PAIR), F32)] * 2,
        ),
        out_shape=[
            shape_of((count, inner), BF16),
            shape_of((images * memory_rows, inner), BF16),
            shape_of((images * memory_rows, inner), BF16),
        ],
        compiler_params=params(),
        cost_estimate=cost(50 * count * memory_rows * inner, 16 * memory_rows * inner),
    )(scalars, q, keys_values, keys_values, grad, logs, deltas)


def middle_kernel(x, mine, theirs, out_mine, out_theirs, gain, query, h1, n2, cq):
    values = (
        x[...].astype(F32)
        + dot(mine[...], out_mine[...], NT)
        + dot(theirs[...], out_theirs[...], NT)
    )
    h1[...] = values
    normed = (values * inverse_rms(values) * gain[...]).astype(BF16)
    n2[...] = normed
    cq[...] = dot(normed, query[...], NN).astype(BF16)


def middle_step(x, mine, theirs, out_mine, out_theirs, gain, query):
    count, width = x.shape
    half = mine.shape[1]
    return pl.pallas_call(
        middle_kernel,
        grid=(count // TILE,),
        in_specs=[
            rows(width),
            rows(half),
            rows(half),
            whole(out_mine.shape),
            whole(out_theirs.shape),
            whole((1, width)),
            whole(query.shape),
        ],
        out_specs=[rows(width), rows(width), rows(half)],
        out_shape=[
            shape_of((count, width), F32),
            shape_of((count, width), BF16),
            shape_of((count, half), BF16),
        ],
        compiler_params=params(),
        cost_estimate=cost(6 * count * width * half, 12 * count * width),
    )(x, mine, theirs, out_mine, out_theirs, gain, query)


def head_sums(left, right):
    product = left.astype(F32) * right.astype(F32)
    width = product.shape[1]
    high = product.astype(BF16)
    low = (product - high.astype(F32)).astype(BF16)
    height = 8 * (width // PAIR)
    line = lax.broadcasted_iota(jnp.int32, (height, width), 0)
    head = lax.broadcasted_iota(jnp.int32, (height, width), 1) // HEAD_DIM
    choose = (
        ((line // 8) * 2 + line % 8 == head) & (line % 8 < 2)
    ).astype(F32).astype(BF16)
    return dot(choose, high, NT) + dot(choose, low, NT)


def units_kernel(
    h1,
    mine,
    theirs,
    out_mine,
    out_theirs,
    gain,
    gy,
    gate_mine,
    up_mine,
    down_mine,
    gate_theirs,
    up_theirs,
    down_theirs,
    output,
    n3,
    hidden,
    grad_gate,
    grad_up,
    dh2,
    e2,
    dc,
    deltas,
    gain_grad,
):
    values = (
        h1[...] + dot(mine[...], out_mine[...], NT) + dot(theirs[...], out_theirs[...], NT)
    )
    normed = (values * inverse_rms(values) * gain[...]).astype(BF16)
    n3[...] = normed
    upstream = gy[...]
    mixed = jnp.zeros_like(values)
    back = jnp.zeros_like(values)
    for own in (True, False):
        gate_weight = gate_mine if own else gate_theirs
        up_weight = up_mine if own else up_theirs
        down_weight = down_mine if own else down_theirs
        gate = dot(normed, gate_weight[...], NN)
        up = dot(normed, up_weight[...], NN)
        square = gate * gate
        bend = jnp.tanh(ROOT_TWO_OVER_PI * gate * (1.0 + CUBIC * square))
        lift = 0.5 * (1.0 + bend)
        gelu = gate * lift
        slope = lift + (0.5 * ROOT_TWO_OVER_PI) * gate * (1.0 - bend * bend) * (
            1.0 + (3.0 * CUBIC) * square
        )
        units = (gelu * up).astype(BF16)
        mixed = mixed + dot(units, down_weight[...], NT)
        pushed = dot(upstream, down_weight[...], NN)
        push_gate = (pushed * up * slope).astype(BF16)
        push_up = (pushed * gelu).astype(BF16)
        back = (
            back + dot(push_gate, gate_weight[...], NT) + dot(push_up, up_weight[...], NT)
        )
        if own:
            hidden[...] = units
            grad_gate[...] = push_gate
            grad_up[...] = push_up
    output[...] = (values + mixed).astype(BF16)
    grad, gain_part = norm_back(values, gain[...], back)
    result = upstream.astype(F32) + grad
    dh2[...] = result
    low = result.astype(BF16)
    e2[...] = low
    crossed = dot(low, out_mine[...], NN).astype(BF16)
    dc[...] = crossed
    deltas[...] = head_sums(crossed, mine[...])

    @pl.when(pl.program_id(0) == 0)
    def _():
        gain_grad[...] = jnp.zeros_like(gain_grad)

    gain_grad[0:1, :] += gain_part


def units_step(h1, mine, theirs, out_mine, out_theirs, gain, gy, own, other):
    count, width = h1.shape
    half = mine.shape[1]
    unit = own[0].shape[1]
    lines = 8 * (half // PAIR)
    return pl.pallas_call(
        units_kernel,
        grid=(count // TILE,),
        in_specs=[
            rows(width),
            rows(half),
            rows(half),
            whole(out_mine.shape),
            whole(out_theirs.shape),
            whole((1, width)),
            rows(width),
        ]
        + [whole((width, unit))] * 6,
        out_specs=[
            rows(width),
            rows(width),
            rows(unit),
            rows(unit),
            rows(unit),
            rows(width),
            rows(width),
            rows(half),
            pl.BlockSpec((lines, TILE), lambda t: (0, t)),
            whole((8, width)),
        ],
        out_shape=[
            shape_of((count, width), BF16),
            shape_of((count, width), BF16),
            shape_of((count, unit), BF16),
            shape_of((count, unit), BF16),
            shape_of((count, unit), BF16),
            shape_of((count, width), F32),
            shape_of((count, width), BF16),
            shape_of((count, half), BF16),
            shape_of((lines, count), F32),
            shape_of((8, width), F32),
        ],
        compiler_params=params(),
        cost_estimate=cost(30 * count * width * unit, 30 * count * width),
    )(h1, mine, theirs, out_mine, out_theirs, gain, gy, *own, *other)


def turn_kernel(
    dh2, h1, mine, theirs, query_mine, query_theirs, gain, out_mine, attended,
    dh1, e1, da, deltas, gain_grad,
):
    back = dot(mine[...], query_mine[...], NT) + dot(theirs[...], query_theirs[...], NT)
    grad, gain_part = norm_back(h1[...], gain[...], back)
    result = dh2[...] + grad
    dh1[...] = result
    low = result.astype(BF16)
    e1[...] = low
    pushed = dot(low, out_mine[...], NN).astype(BF16)
    da[...] = pushed
    deltas[...] = head_sums(pushed, attended[...])

    @pl.when(pl.program_id(0) == 0)
    def _():
        gain_grad[...] = jnp.zeros_like(gain_grad)

    gain_grad[0:1, :] += gain_part


def turn_step(dh2, h1, mine, theirs, query_mine, query_theirs, gain, out_mine, attended):
    count, width = h1.shape
    half = mine.shape[1]
    lines = 8 * (half // PAIR)
    return pl.pallas_call(
        turn_kernel,
        grid=(count // TILE,),
        in_specs=[
            rows(width),
            rows(width),
            rows(half),
            rows(half),
            whole(query_mine.shape),
            whole(query_theirs.shape),
            whole((1, width)),
            whole(out_mine.shape),
            rows(half),
        ],
        out_specs=[
            rows(width),
            rows(width),
            rows(half),
            pl.BlockSpec((lines, TILE), lambda t: (0, t)),
            whole((8, width)),
        ],
        out_shape=[
            shape_of((count, width), F32),
            shape_of((count, width), BF16),
            shape_of((count, half), BF16),
            shape_of((lines, count), F32),
            shape_of((8, width), F32),
        ],
        compiler_params=params(),
        cost_estimate=cost(6 * count * width * half, 16 * count * width),
    )(dh2, h1, mine, theirs, query_mine, query_theirs, gain, out_mine, attended)


def partial_kernel(dq, dk, dv, weight, out):
    inner = dq.shape[1]
    out[...] = (
        dot(dq[...], weight[:, 0:inner], NT)
        + dot(dk[...], weight[:, inner : 2 * inner], NT)
        + dot(dv[...], weight[:, 2 * inner : 3 * inner], NT)
    ).astype(BF16)


def partial_step(dq, dk, dv, weight):
    count, inner = dq.shape
    width = weight.shape[0]
    return pl.pallas_call(
        partial_kernel,
        grid=(count // TILE,),
        in_specs=[rows(inner)] * 3 + [whole(weight.shape)],
        out_specs=rows(width),
        out_shape=shape_of((count, width), BF16),
        compiler_params=params(),
        cost_estimate=cost(6 * count * width * inner, 8 * count * width),
    )(dq, dk, dv, weight)


def first_kernel(dh1, x, mine, theirs, gain, out, gain_grad):
    back = mine[...].astype(F32) + theirs[...].astype(F32)
    grad, gain_part = norm_back(x[...].astype(F32), gain[...], back)
    out[...] = (dh1[...] + grad).astype(BF16)

    @pl.when(pl.program_id(0) == 0)
    def _():
        gain_grad[...] = jnp.zeros_like(gain_grad)

    gain_grad[0:1, :] += gain_part


def first_step(dh1, x, mine, theirs, gain):
    count, width = x.shape
    return pl.pallas_call(
        first_kernel,
        grid=(count // TILE,),
        in_specs=[rows(width)] * 4 + [whole((1, width))],
        out_specs=[rows(width), whole((8, width))],
        out_shape=[shape_of((count, width), BF16), shape_of((8, width), F32)],
        compiler_params=params(),
        cost_estimate=cost(20 * count * width, 12 * count * width),
    )(dh1, x, mine, theirs, gain)


def swap(values, axis, distance):
    size = lax.axis_size(axis)
    return lax.ppermute(values, axis, [(i, i ^ distance) for i in range(size)])


def gather_wide(piece):
    other = swap(piece, "wide", 2)
    pair = jnp.stack([piece, other])
    return pair, swap(pair, "wide", 1)


def in_order(mine, theirs):
    index = lax.axis_index("wide")
    core, chip = index % 2, index // 2
    even = jnp.where(core == 0, mine, theirs)
    odd = jnp.where(core == 0, theirs, mine)
    first = jnp.where(chip == 0, 0, 1)
    parts = []
    for c in range(2):
        for source in (even, odd):
            parts.append(jnp.where(first == c, source[0], source[1]))
    return jnp.concatenate(parts, axis=0)


def sum_line(values):
    size = lax.axis_size("dp")
    if size != 4:
        return lax.psum(values, "dp")
    place = lax.axis_index("dp")
    inner = (place == 1) | (place == 2)
    got = lax.ppermute(values, "dp", [(0, 1), (3, 2)])
    part = jnp.where(inner, values + got, values)
    got = lax.ppermute(part, "dp", [(1, 2), (2, 1)])
    total = part + got
    got = lax.ppermute(total, "dp", [(1, 0), (2, 3)])
    return jnp.where(inner, total, got)


def sum_gradient(gradient):
    height, width = gradient.shape
    index = lax.axis_index("wide")
    core, chip = index % 2, index // 2
    split = gradient.astype(BF16).reshape(2, 2, height // 4, width)
    keep = lax.dynamic_index_in_dim(split, core, 1, False)
    send = lax.dynamic_index_in_dim(split, 1 - core, 1, False)
    part = (keep.astype(F32) + swap(send, "wide", 1).astype(F32)).astype(BF16)
    keep = lax.dynamic_index_in_dim(part, chip, 0, False)
    send = lax.dynamic_index_in_dim(part, 1 - chip, 0, False)
    part = (keep.astype(F32) + swap(send, "wide", 2).astype(F32)).astype(BF16)
    return sum_line(part)


def contract_rows(left, right):
    return dot(left, right, TN)


def local(
    tokens,
    memory,
    cotangent,
    norm1_gain,
    norm2_gain,
    norm3_gain,
    q_weight,
    k_weight,
    v_weight,
    o_weight,
    cross_q,
    cross_k,
    cross_v,
    cross_o,
    gate_weight,
    up_weight,
    down_weight,
    segment_ids,
    block_ids,
    image_table,
):
    width = tokens.shape[1]
    share = q_weight.shape[0]
    inner = q_weight.shape[1]
    unit = gate_weight.shape[1]
    images = memory.shape[0]
    flat_memory = memory.reshape(-1, width)

    gains = jnp.stack([norm1_gain, norm2_gain, norm3_gain])
    gains = jnp.pad(gains, ((0, 13), (0, 3 * inner - share)))
    early = jnp.concatenate(
        [jnp.concatenate([q_weight, k_weight, v_weight], axis=1), gains], axis=0
    )
    early = in_order(*gather_wide(early)).reshape(4, share + 16, 3 * inner)
    qkv_weight = early[:, :share].reshape(4 * share, 3 * inner)
    all_gains = (
        jnp.swapaxes(early[:, share : share + 3, :share], 0, 1)
        .reshape(3, 1, 4 * share)
        .astype(F32)
    )
    mid = jnp.concatenate([o_weight, cross_o, cross_q, cross_k, cross_v], axis=1)
    mid_mine, mid_core = gather_wide(mid)
    mid_full = in_order(mid_mine, mid_core)
    out_mine = mid_full[:, 0:inner]
    cross_out_mine = mid_full[:, inner : 2 * inner]
    cross_query_mine = mid_full[:, 2 * inner : 3 * inner]
    cross_kv = mid_full[:, 3 * inner : 5 * inner]
    mid_y = swap(mid_mine[:, :, : 3 * inner], "narrow", 1)
    mid_other = in_order(mid_y, swap(mid_y, "wide", 1))
    out_theirs = mid_other[:, 0:inner]
    cross_out_theirs = mid_other[:, inner : 2 * inner]
    cross_query_theirs = mid_other[:, 2 * inner : 3 * inner]
    late = jnp.concatenate([gate_weight, up_weight, down_weight], axis=1)
    late_mine, late_core = gather_wide(late)
    late_full = in_order(late_mine, late_core)
    late_y = swap(late_mine, "narrow", 1)
    late_other = in_order(late_y, swap(late_y, "wide", 1))
    units_mine = [late_full[:, i * unit : (i + 1) * unit] for i in range(3)]
    units_theirs = [late_other[:, i * unit : (i + 1) * unit] for i in range(3)]

    x, gy, row_ids, col_ids, pos, scalars = order_rows(
        segment_ids, block_ids, image_table, tokens, cotangent
    )
    n1, qkv = norm_project(x, all_gains[0], qkv_weight)
    attended, self_logs = self_forward(qkv, row_ids, col_ids)
    attended_theirs = swap(attended, "narrow", 1)
    keys_values = dot(flat_memory, cross_kv, NN).astype(BF16)
    h1, n2, cq = middle_step(
        x, attended, attended_theirs, out_mine, out_theirs, all_gains[1], cross_query_mine
    )
    crossed, cross_logs = cross_forward(scalars, cq, keys_values, images)
    crossed_theirs = swap(crossed, "narrow", 1)
    (
        output,
        n3,
        hidden,
        grad_gate,
        grad_up,
        dh2,
        e2,
        dc,
        cross_deltas,
        third_gain,
    ) = units_step(
        h1,
        crossed,
        crossed_theirs,
        cross_out_mine,
        cross_out_theirs,
        all_gains[2],
        gy,
        units_mine,
        units_theirs,
    )

    unit_grads = sum_gradient(
        jnp.concatenate(
            [
                contract_rows(n3, grad_gate).astype(BF16),
                contract_rows(n3, grad_up).astype(BF16),
                contract_rows(gy, hidden).astype(BF16),
            ],
            axis=1,
        )
    )
    dcq, dck, dcv = cross_backward(
        scalars, cq, keys_values, dc, cross_logs, cross_deltas, images
    )
    dcq_theirs = swap(dcq, "narrow", 1)
    memory_part = (
        dot(dck, cross_kv[:, :inner], NT) + dot(dcv, cross_kv[:, inner:], NT)
    ).astype(BF16)
    side = lax.axis_index("narrow")
    memory_keep = lax.dynamic_slice_in_dim(memory_part, side * inner, inner, 1)
    memory_send = lax.dynamic_slice_in_dim(memory_part, (1 - side) * inner, inner, 1)
    memory_grad = (
        memory_keep.astype(F32) + swap(memory_send, "narrow", 1).astype(F32)
    ).astype(BF16)
    memory_grad = memory_grad.reshape(images, -1, inner)
    cross_grads = sum_gradient(
        jnp.concatenate(
            [
                contract_rows(n2, dcq).astype(BF16),
                contract_rows(flat_memory, dck).astype(BF16),
                contract_rows(flat_memory, dcv).astype(BF16),
                contract_rows(e2, crossed).astype(BF16),
            ],
            axis=1,
        )
    )
    dh1, e1, da, self_deltas, second_gain = turn_step(
        dh2,
        h1,
        dcq,
        dcq_theirs,
        cross_query_mine,
        cross_query_theirs,
        all_gains[1],
        out_mine,
        attended,
    )
    dq, dk, dv = self_backward(qkv, da, self_logs, self_deltas, row_ids, col_ids)
    dn1 = partial_step(dq, dk, dv, qkv_weight)
    dn1_theirs = swap(dn1, "narrow", 1)
    tokens_grad, first_gain = first_step(dh1, x, dn1, dn1_theirs, all_gains[0])
    tokens_grad = restore_rows(pos, tokens_grad)
    output = restore_rows(pos, output)
    self_grads = sum_gradient(
        jnp.concatenate(
            [
                contract_rows(n1, dq).astype(BF16),
                contract_rows(n1, dk).astype(BF16),
                contract_rows(n1, dv).astype(BF16),
                contract_rows(e1, attended).astype(BF16),
            ],
            axis=1,
        )
    )
    gain_lines = jnp.concatenate(
        [first_gain[0:1], second_gain[0:1], third_gain[0:1]], axis=0
    )
    gain_sums = lax.psum(gain_lines, ("dp", "wide"))
    gain_sums = lax.dynamic_slice_in_dim(
        gain_sums, lax.axis_index("wide") * share, share, 1
    )

    def grads(array, size, count):
        return [array[:, i * size : (i + 1) * size].astype(F32) for i in range(count)]

    gate_grad, up_grad, down_grad = grads(unit_grads, unit, 3)
    cross_q_grad, cross_k_grad, cross_v_grad, cross_o_grad = grads(cross_grads, inner, 4)
    q_grad, k_grad, v_grad, o_grad = grads(self_grads, inner, 4)
    return (
        output,
        tokens_grad,
        memory_grad,
        gain_sums[0],
        gain_sums[1],
        gain_sums[2],
        q_grad,
        k_grad,
        v_grad,
        o_grad,
        cross_q_grad,
        cross_k_grad,
        cross_v_grad,
        cross_o_grad,
        gate_grad,
        up_grad,
        down_grad,
    )


def solution(mesh):
    both = ("dp", "wide")
    weight = P("wide", "narrow")
    in_specs = (
        (P(both, None), P(both, None, None), P(both, None))
        + (P("wide"),) * 3
        + (weight,) * 11
        + (P(both, None),) * 3
    )
    out_specs = (
        (P(both, None), P(both, None), P(both, None, "narrow"))
        + (P("wide"),) * 3
        + (weight,) * 11
    )
    return jax.shard_map(local, mesh=mesh, in_specs=in_specs, out_specs=out_specs, check_vma=False)
```

```python
import functools
import math

import jax
import jax.numpy as jnp
from jax import lax
from jax.experimental import pallas as pl
from jax.experimental.pallas import tpu as pltpu
from jax.sharding import PartitionSpec as P

F32 = jnp.float32
BF16 = jnp.bfloat16
EPSILON = 1e-06
ROOT_TWO_OVER_PI = 0.7978845608028654
CUBIC = 0.044715
HEAD_DIM = 64
PAIR = 2 * HEAD_DIM
SCALE = HEAD_DIM ** (-0.5)
EXP2_SCALE = SCALE * math.log2(math.e)
HIDE = 1e30
TILE = 256
WEIGH = 4.0

NN = (((1,), (0,)), ((), ()))
NT = (((1,), (1,)), ((), ()))
TN = (((0,), (0,)), ((), ()))


def dot(left, right, dims):
    return lax.dot_general(left, right, dims, preferred_element_type=F32)


def params():
    return pltpu.CompilerParams(vmem_limit_bytes=60 * 1024 * 1024)


def cost(flops, nbytes):
    return pl.CostEstimate(
        flops=int(flops * WEIGH), bytes_accessed=int(nbytes * WEIGH), transcendentals=0
    )


def shape_of(shape, dtype):
    return jax.ShapeDtypeStruct(shape, dtype)


def whole(shape):
    zeros = (0,) * len(shape)
    return pl.BlockSpec(shape, lambda *_: zeros)


def rows(width, height=TILE):
    return pl.BlockSpec((height, width), lambda t, *_: (t, 0))


def inverse_rms(values):
    return lax.rsqrt(jnp.mean(values * values, axis=1, keepdims=True) + EPSILON)


def norm_back(values, gain, upstream):
    factor = inverse_rms(values)
    scaled = upstream * gain
    mean = jnp.mean(values * scaled, axis=1, keepdims=True)
    grad = factor * scaled - values * (factor * factor * factor * mean)
    return grad, jnp.sum(upstream * values * factor, axis=0, keepdims=True)


def in_half(shape, half):
    return (lax.broadcasted_iota(jnp.int32, shape, 1) // HEAD_DIM) == half


def only_half(values, half):
    return jnp.where(in_half(values.shape, half), values, jnp.zeros_like(values))


def order_kernel(seg, blk, table, x, gy, xp, gyp, row_ids, col_ids, pos_out, scalars, pos):
    step = pl.program_id(0)
    count = seg.shape[1]

    @pl.when(step == 0)
    def _():
        segments = seg[...]
        image = jnp.zeros_like(segments)
        for s in range(table.shape[1]):
            image = jnp.where(segments == s, table[0, s], image)
        first = (image == 0).astype(F32)
        before = lax.broadcasted_iota(jnp.int32, (count, count), 0) < lax.broadcasted_iota(
            jnp.int32, (count, count), 1
        )
        rank = dot(
            jnp.broadcast_to(first, (8, count)).astype(BF16),
            before.astype(F32).astype(BF16),
            NN,
        )[0:1]
        total = jnp.sum(first)
        index = lax.broadcasted_iota(jnp.int32, (1, count), 1).astype(F32)
        place = jnp.where(image == 0, rank, total + index - rank)
        pos[...] = place.astype(jnp.int32)
        pos_out[...] = jnp.broadcast_to(pos[...], (8, count))
        n0 = total.astype(jnp.int32)
        tiles = count // TILE
        visits0 = jnp.maximum(1, (n0 + TILE - 1) // TILE)
        start1 = jnp.minimum(tiles - 1, n0 // TILE)
        visits = visits0 + tiles - start1
        for v in range(tiles + 1):
            real = jnp.minimum(v, visits - 1)
            in_first = real < visits0
            scalars[v] = jnp.where(in_first, real, real - visits0 + start1)
            scalars[8 + v] = jnp.where(in_first, 0, 1)
        scalars[16] = visits
        scalars[17] = n0
        scalars[18] = visits0
        scalars[19] = start1
        scalars[20] = tiles - start1

    onehot = (
        lax.broadcasted_iota(jnp.int32, (TILE, count), 0) + step * TILE == pos[...]
    ).astype(F32).astype(BF16)
    xp[...] = dot(onehot, x[...], NN).astype(BF16)
    gyp[...] = dot(onehot, gy[...], NN).astype(BF16)
    ids = jnp.concatenate(
        [
            seg[...].astype(F32),
            blk[...].astype(F32),
            jnp.zeros((126, count), F32),
        ],
        axis=0,
    ).astype(BF16)
    row_ids[...] = dot(ids[0:8], onehot, NT)
    col_ids[...] = dot(onehot, ids, NT)


def order_rows(seg, blk, table, x, gy):
    count, width = x.shape
    return pl.pallas_call(
        order_kernel,
        grid=(count // TILE,),
        in_specs=[
            whole((1, count)),
            whole((1, count)),
            pl.BlockSpec(memory_space=pltpu.SMEM),
            whole((count, width)),
            whole((count, width)),
        ],
        out_specs=[
            rows(width),
            rows(width),
            pl.BlockSpec((8, TILE), lambda t: (0, t)),
            rows(128),
            whole((8, count)),
            pl.BlockSpec(memory_space=pltpu.SMEM),
        ],
        out_shape=[
            shape_of((count, width), BF16),
            shape_of((count, width), BF16),
            shape_of((8, count), F32),
            shape_of((count, 128), F32),
            shape_of((8, count), jnp.int32),
            shape_of((32,), jnp.int32),
        ],
        scratch_shapes=[pltpu.VMEM((1, count), jnp.int32)],
        compiler_params=params(),
        cost_estimate=cost(4 * count * count * width, 8 * count * width),
    )(seg, blk, table, x, gy)


def restore_kernel(pos, values, out):
    count = values.shape[0]
    onehot = (
        lax.broadcasted_iota(jnp.int32, (count, TILE), 0) == pos[0:1, :]
    ).astype(F32).astype(BF16)
    out[...] = dot(onehot, values[...], TN).astype(BF16)


def restore_rows(pos, values):
    count, width = values.shape
    return pl.pallas_call(
        restore_kernel,
        grid=(count // TILE,),
        in_specs=[pl.BlockSpec((8, TILE), lambda t: (0, t)), whole((count, width))],
        out_specs=rows(width),
        out_shape=shape_of((count, width), BF16),
        compiler_params=params(),
        cost_estimate=cost(2 * count * count * width, 4 * count * width),
    )(pos, values)


def fetch(pieces, places, columns, dest, sems, base=0):
    height = dest.shape[0] // 4
    copies = []
    for i, piece in enumerate(pieces):
        start = pl.multiple_of(places[i] * height, 16)
        copies.append(
            pltpu.make_async_copy(
                piece.at[pl.ds(0, height), columns],
                dest.at[pl.ds(start, height), :],
                sems.at[base + i],
            )
        )
    return copies


def fetch_half(gathered, half, columns, dest, sem):
    return pltpu.make_async_copy(gathered.at[half, :, columns], dest, sem)


def start_all(copies):
    for copy in copies:
        copy.start()


def wait_all(copies):
    for copy in copies:
        copy.wait()


ANY = pl.BlockSpec(memory_space=pl.ANY)
SCALARS = pl.BlockSpec(memory_space=pltpu.SMEM)


def project_kernel(places, x, gain, w0, w1, w2, w3, normed, out, weight, sems):
    @pl.when(pl.program_id(0) == 0)
    def _():
        copies = fetch((w0, w1, w2, w3), places, slice(0, weight.shape[1]), weight, sems)
        start_all(copies)
        wait_all(copies)

    values = x[...].astype(F32)
    n1 = (values * inverse_rms(values) * gain[...]).astype(BF16)
    normed[...] = n1
    out[...] = dot(n1, weight[...], NN).astype(BF16)


def norm_project(places, x, gain, pieces):
    count, width = x.shape
    outs = pieces[0].shape[1]
    return pl.pallas_call(
        project_kernel,
        grid=(count // TILE,),
        in_specs=[SCALARS, rows(width), whole((1, width))] + [ANY] * 4,
        out_specs=[rows(width), rows(outs)],
        out_shape=[shape_of((count, width), BF16), shape_of((count, outs), BF16)],
        scratch_shapes=[pltpu.VMEM((width, outs), BF16), pltpu.SemaphoreType.DMA((4,))],
        compiler_params=params(),
        cost_estimate=cost(2 * count * width * outs, 4 * count * width + 2 * count * outs),
    )(places, x, gain, *pieces)


MEMORY_TILE = 512


def memory_kernel(places, columns, memory, w0, w1, w2, w3, out, weight, sems):
    @pl.when(pl.program_id(0) == 0)
    def _():
        copies = fetch((w0, w1, w2, w3), places, columns, weight, sems)
        start_all(copies)
        wait_all(copies)

    out[...] = dot(memory[...], weight[...], NN).astype(BF16)


def project_memory(places, memory, pieces, columns):
    count, width = memory.shape
    outs = columns.stop - columns.start

    def kernel(places, *refs):
        memory_kernel(places, columns, *refs)

    return pl.pallas_call(
        kernel,
        grid=(count // MEMORY_TILE,),
        in_specs=[SCALARS, rows(width, MEMORY_TILE)] + [ANY] * 4,
        out_specs=rows(outs, MEMORY_TILE),
        out_shape=shape_of((count, outs), BF16),
        scratch_shapes=[pltpu.VMEM((width, outs), BF16), pltpu.SemaphoreType.DMA((4,))],
        compiler_params=params(),
        cost_estimate=cost(2 * count * width * outs, 4 * count * width),
    )(places, memory, *pieces)


SELF_TILE = 128
SELF_WINDOW = 512
BACK_WINDOW = 640


def store_logs(ref, columns, logs, extra=None):
    spread = jnp.where(in_half((logs[0].shape[0], PAIR), 0), logs[0], logs[1]).T
    for half in range(2):
        line = spread[half * HEAD_DIM : half * HEAD_DIM + 1, :]
        if extra is not None:
            line = jnp.where(extra, line, ref[half : half + 1, columns])
        ref[half : half + 1, columns] = line


def self_forward_kernel(q, k, v, row_ids, col_ids, out, logs):
    count = q.shape[0]
    for tile in range(count // SELF_TILE):
        base = tile * SELF_TILE
        start = min(max(base - 256, 0), count - SELF_WINDOW)
        spot = slice(base, base + SELF_TILE)
        window = slice(start, start + SELF_WINDOW)
        seen = (col_ids[spot, 0:1] == row_ids[0:1, window]) & (
            row_ids[1:2, window] <= col_ids[spot, 1:2]
        )
        bias = jnp.where(seen, 0.0, -HIDE)
        keys = k[window, :]
        values = v[window, :]
        queries = q[spot, :]
        parts, totals = [], []
        for half in range(2):
            scores = dot(only_half(queries, half), keys, NT) * EXP2_SCALE + bias
            highest = jnp.max(scores, axis=1, keepdims=True)
            weights = jnp.exp2(scores - highest)
            total = jnp.sum(weights, axis=1, keepdims=True)
            parts.append(dot(weights.astype(BF16), values, NN) / total)
            totals.append(highest + jnp.log2(total))
        out[spot, :] = jnp.where(in_half(parts[0].shape, 0), parts[0], parts[1]).astype(BF16)
        store_logs(logs, spot, totals)


def self_forward(pair, qkv, row_ids, col_ids):
    count = qkv.shape[0]
    pairs = qkv.shape[1] // (3 * PAIR)

    def part(which):
        return pl.BlockSpec((count, PAIR), lambda p: (0, which * pairs + pair))

    return pl.pallas_call(
        self_forward_kernel,
        grid=(1,),
        in_specs=[part(0), part(1), part(2), whole((8, count)), whole((count, 128))],
        out_specs=[whole((count, PAIR)), whole((8, count))],
        out_shape=[shape_of((count, PAIR), BF16), shape_of((8, count), F32)],
        compiler_params=params(),
        cost_estimate=cost(16 * count * SELF_WINDOW * PAIR, 8 * count * PAIR),
    )(qkv, qkv, qkv, row_ids, col_ids)


def self_backward_kernel(q, k, v, grad, logs, deltas, row_ids, col_ids, dq, dk, dv, key_sum, value_sum):
    count = q.shape[0]
    key_sum[...] = jnp.zeros_like(key_sum)
    value_sum[...] = jnp.zeros_like(value_sum)
    for tile in range(count // TILE):
        base = tile * TILE
        start = min(max(base - 256, 0), count - BACK_WINDOW)
        spot = slice(base, base + TILE)
        window = slice(start, start + BACK_WINDOW)
        seen = (col_ids[window, 0:1] == row_ids[0:1, spot]) & (
            col_ids[window, 1:2] <= row_ids[1:2, spot]
        )
        bias = jnp.where(seen, 0.0, -HIDE)
        keys = k[window, :]
        values = v[window, :]
        queries = q[spot, :]
        grads = grad[spot, :]
        parts = []
        for half in range(2):
            one_query = only_half(queries, half)
            one_grad = only_half(grads, half)
            scores = dot(keys, one_query, NT) * EXP2_SCALE + bias
            weights = jnp.exp2(scores - logs[half : half + 1, spot])
            slopes = dot(values, one_grad, NT)
            pushed = (weights * (slopes - deltas[half : half + 1, spot])).astype(BF16)
            value_sum[window, :] += dot(weights.astype(BF16), one_grad, NN)
            key_sum[window, :] += dot(pushed, one_query, NN)
            parts.append(dot(pushed, keys, TN))
        dq[spot, :] = (
            jnp.where(in_half(parts[0].shape, 0), parts[0], parts[1]) * SCALE
        ).astype(BF16)
    dk[...] = (key_sum[...] * SCALE).astype(BF16)
    dv[...] = value_sum[...].astype(BF16)


def self_backward(pair, qkv, grad, logs, deltas, row_ids, col_ids):
    count = qkv.shape[0]
    pairs = qkv.shape[1] // (3 * PAIR)

    def part(which):
        return pl.BlockSpec((count, PAIR), lambda p: (0, which * pairs + pair))

    return pl.pallas_call(
        self_backward_kernel,
        grid=(1,),
        in_specs=[
            part(0),
            part(1),
            part(2),
            part(0),
            whole((8, count)),
            pl.BlockSpec((8, count), lambda p: (pair, 0)),
            whole((8, count)),
            whole((count, 128)),
        ],
        out_specs=[whole((count, PAIR))] * 3,
        out_shape=[shape_of((count, PAIR), BF16)] * 3,
        scratch_shapes=[pltpu.VMEM((count, PAIR), F32)] * 2,
        compiler_params=params(),
        cost_estimate=cost(40 * count * BACK_WINDOW * PAIR, 16 * count * PAIR),
    )(qkv, qkv, qkv, grad, logs, deltas, row_ids, col_ids)


def cross_forward_kernel(scalars, q, k, v, out, logs):
    step = pl.program_id(0)
    tile = scalars[step]
    image = scalars[8 + step]
    again = (step > 0) & (scalars[jnp.maximum(step - 1, 0)] == tile)

    @pl.when(step < scalars[16])
    def _():
        queries = q[...]
        keys = k[...]
        values = v[...]
        parts, totals = [], []
        for half in range(2):
            scores = dot(only_half(queries, half), keys, NT)
            highest = jnp.max(scores, axis=1, keepdims=True) * EXP2_SCALE
            weights = jnp.exp2(scores * EXP2_SCALE - highest)
            total = jnp.sum(weights, axis=1, keepdims=True)
            parts.append(dot(weights.astype(BF16), values, NN) / total)
            totals.append(highest + jnp.log2(total))
        mixed = jnp.where(in_half(parts[0].shape, 0), parts[0], parts[1]).astype(BF16)
        limit = scalars[17] - tile * TILE
        row_mine = (
            lax.broadcasted_iota(jnp.int32, mixed.shape, 0) >= limit
        ) == (image == 1)
        lane_mine = (
            lax.broadcasted_iota(jnp.int32, (1, TILE), 1) >= limit
        ) == (image == 1)
        keep = jnp.logical_not(again)
        out[...] = jnp.where(row_mine | keep, mixed, out[...])
        store_logs(logs, slice(0, TILE), totals, lane_mine | keep)


def cross_forward(pair, scalars, q, keys_values, images):
    count, inner = q.shape
    pairs = inner // PAIR
    memory_rows = keys_values.shape[0] // images
    tile_spec = pl.BlockSpec((TILE, PAIR), lambda s, sc: (sc[s], 0))

    def part(which):
        return pl.BlockSpec((memory_rows, PAIR), lambda s, sc: (sc[8 + s], which * pairs + pair))

    return pl.pallas_call(
        cross_forward_kernel,
        grid_spec=pltpu.PrefetchScalarGridSpec(
            num_scalar_prefetch=1,
            grid=(count // TILE + 1,),
            in_specs=[
                pl.BlockSpec((TILE, PAIR), lambda s, sc: (sc[s], pair)),
                part(0),
                part(1),
            ],
            out_specs=[tile_spec, pl.BlockSpec((8, TILE), lambda s, sc: (0, sc[s]))],
        ),
        out_shape=[shape_of((count, PAIR), BF16), shape_of((8, count), F32)],
        compiler_params=params(),
        cost_estimate=cost(20 * count * memory_rows * PAIR, 8 * memory_rows * PAIR),
    )(scalars, q, keys_values, keys_values)


def cross_backward_kernel(
    image, scalars, q, k, v, grad, logs, deltas, old, dq, dk, dv, key_sum, value_sum
):
    step = pl.program_id(1)
    tile = cross_tile(image, scalars, step)

    @pl.when(step == 0)
    def _():
        key_sum[...] = jnp.zeros_like(key_sum)
        value_sum[...] = jnp.zeros_like(value_sum)

    @pl.when(step < scalars[20 if image else 18])
    def _():
        queries = q[...]
        grads = grad[...]
        keys = k[...]
        values = v[...]
        limit = scalars[17] - tile * TILE
        lane_mine = (lax.broadcasted_iota(jnp.int32, (1, TILE), 1) >= limit) == (image == 1)
        parts = []
        for half in range(2):
            one_query = only_half(queries, half)
            one_grad = only_half(grads, half)
            log = jnp.where(lane_mine, logs[half : half + 1, :], HIDE)
            scores = dot(keys, one_query, NT)
            weights = jnp.exp2(scores * EXP2_SCALE - log)
            slopes = dot(values, one_grad, NT)
            pushed = (weights * (slopes - deltas[half : half + 1, :])).astype(BF16)
            value_sum[...] += dot(weights.astype(BF16), one_grad, NN)
            key_sum[...] += dot(pushed, one_query, NN)
            parts.append(dot(pushed, keys, TN))
        grad_query = (
            jnp.where(in_half(parts[0].shape, 0), parts[0], parts[1]) * SCALE
        ).astype(BF16)
        if image:
            row_mine = lax.broadcasted_iota(jnp.int32, grad_query.shape, 0) >= limit
            grad_query = jnp.where(row_mine, grad_query, old[...])
        dq[...] = grad_query

    @pl.when(step == pl.num_programs(1) - 1)
    def _():
        dk[...] = (key_sum[...] * SCALE).astype(BF16)
        dv[...] = value_sum[...].astype(BF16)


def cross_tile(image, scalars, step):
    if image:
        return scalars[19] + jnp.minimum(step, scalars[20] - 1)
    return jnp.minimum(step, scalars[18] - 1)


def cross_backward(image, scalars, q, keys_values, grad, logs, deltas, images, old):
    count, inner = q.shape
    pairs = inner // PAIR
    memory_rows = keys_values.shape[0] // images
    tile_spec = pl.BlockSpec((TILE, PAIR), lambda p, s, sc: (cross_tile(image, sc, s), p))
    line = pl.BlockSpec((8, TILE), lambda p, s, sc: (p, cross_tile(image, sc, s)))
    result = pl.BlockSpec((memory_rows, PAIR), lambda p, s, sc: (0, p))

    def part(which):
        return pl.BlockSpec((memory_rows, PAIR), lambda p, s, sc: (image, which * pairs + p))

    def first_kernel(scalars, q, k, v, grad, logs, deltas, *rest):
        cross_backward_kernel(image, scalars, q, k, v, grad, logs, deltas, None, *rest)

    def second_kernel(*refs):
        cross_backward_kernel(image, *refs)

    extra = [old] if image else []
    return pl.pallas_call(
        second_kernel if image else first_kernel,
        grid_spec=pltpu.PrefetchScalarGridSpec(
            num_scalar_prefetch=1,
            grid=(pairs, count // TILE),
            in_specs=[tile_spec, part(0), part(1), tile_spec, line, line]
            + [tile_spec] * len(extra),
            out_specs=[tile_spec, result, result],
            scratch_shapes=[pltpu.VMEM((memory_rows, PAIR), F32)] * 2,
        ),
        out_shape=[
            shape_of((count, inner), BF16),
            shape_of((memory_rows, inner), BF16),
            shape_of((memory_rows, inner), BF16),
        ],
        input_output_aliases={7: 0} if image else {},
        compiler_params=params(),
        cost_estimate=cost(25 * count * memory_rows * inner, 8 * memory_rows * inner),
    )(scalars, q, keys_values, keys_values, grad, logs, deltas, *extra)


def put_rows(places, product, keep, send):
    height = product.shape[0] // 4
    for i, ref in enumerate((keep, keep, send, send)):
        start = pl.multiple_of(places[i] * height, 16)
        ref[i % 2, 0:height, :] = product[pl.ds(start, height), :].astype(BF16)


def memory_back_kernel(
    columns, last, places, memory, dk, dv, w0, w1, w2, w3, *refs
):
    if last:
        before, keep_part, send_part, keep, send, weight, total, sems = refs
    else:
        keep_part, send_part, total_out, weight, total, sems = refs
    inner = dk.shape[1]

    @pl.when(pl.program_id(0) == 0)
    def _():
        copies = fetch((w0, w1, w2, w3), places, columns, weight, sems)
        start_all(copies)
        if last:
            total[...] = before[...]
        else:
            total[...] = jnp.zeros_like(total)
        wait_all(copies)

    both = jnp.concatenate([dk[...], dv[...]], axis=1)
    side = places[4]
    mine = weight[pl.ds(pl.multiple_of(side * inner, 16), inner), :]
    theirs = weight[pl.ds(pl.multiple_of((1 - side) * inner, 16), inner), :]
    send_part[...] = dot(both, theirs, NT).astype(BF16)
    keep_part[...] = dot(both, mine, NT).astype(BF16)
    total[...] += dot(memory[...], both, TN)

    @pl.when(pl.program_id(0) == pl.num_programs(0) - 1)
    def _():
        if last:
            put_rows(places, total, keep, send)
        else:
            total_out[...] = total[...]


def memory_back(places, memory, dk, dv, pieces, columns, image, before, spare):
    count, inner = dk.shape
    width = memory.shape[1]
    steps = count // MEMORY_TILE
    last = before is not None
    ranks = shape_of((2, width // 4, spare + 2 * inner), BF16)
    rank_spec = pl.BlockSpec((2, width // 4, 2 * inner), lambda t: (0, 0, 0))

    def kernel(*refs):
        memory_back_kernel(columns, last, *refs)

    return pl.pallas_call(
        kernel,
        grid=(steps,),
        in_specs=[
            SCALARS,
            pl.BlockSpec((MEMORY_TILE, width), lambda t: (image * steps + t, 0)),
            rows(inner, MEMORY_TILE),
            rows(inner, MEMORY_TILE),
        ]
        + [ANY] * 4
        + ([whole((width, 2 * inner))] if last else []),
        out_specs=[rows(inner, MEMORY_TILE), rows(inner, MEMORY_TILE)]
        + ([rank_spec, rank_spec] if last else [whole((width, 2 * inner))]),
        out_shape=[shape_of((count, inner), BF16)] * 2
        + ([ranks, ranks] if last else [shape_of((width, 2 * inner), F32)]),
        scratch_shapes=[
            pltpu.VMEM((width, 2 * inner), BF16),
            pltpu.VMEM((width, 2 * inner), F32),
            pltpu.SemaphoreType.DMA((4,)),
        ],
        compiler_params=params(),
        cost_estimate=cost(8 * count * width * inner, 8 * count * width),
    )(places, memory, dk, dv, *pieces, *([before] if last else []))


def weight_grads_kernel(plan, places, left_refs, right_refs, line_refs, keep, send, turned):
    height = turned.shape[0] // 4
    step = pl.program_id(0)
    for at, (left, group) in enumerate(plan):

        @pl.when(step == at)
        def _():
            if at == 0 or plan[at - 1][0] != left:
                turned[...] = left_refs[left][...].T
            right = join([right_refs[g] for g in group])
            for i, ref in enumerate((keep, keep, send, send)):
                start = pl.multiple_of(places[i] * height, 16)
                ref[i % 2, 0:height, :] = dot(turned[pl.ds(start, height), :], right, NN).astype(
                    BF16
                )
                if line_refs:
                    ref[i % 2, height : height + 16, :] = line_refs[0][places[i]].astype(BF16)


def join(refs):
    values = [ref[...] for ref in refs]
    return values[0] if len(values) == 1 else jnp.concatenate(values, axis=1)


def flatten(groups):
    flat, sizes = [], []
    for group in groups:
        group = group if isinstance(group, (list, tuple)) else [group]
        flat += list(group)
        sizes.append(len(group))
    return flat, sizes


def weight_grads(places, lefts, rights, plan, lines=None, into=(), first=0):
    count, width = lefts[0].shape
    flat, sizes = flatten(rights)
    groups, at = [], 0
    for size in sizes:
        groups.append(list(range(at, at + size)))
        at += size
    plan = [(left, [f for g in group for f in groups[g]]) for left, group in plan]
    step_columns = sum(flat[f].shape[1] for f in plan[0][1])
    share = width // 4
    total = (len(plan) + first) * step_columns
    extra = list(into)
    more = []
    height = share
    if lines is not None:
        height = share + 16
        more = [
            jnp.pad(
                jnp.stack(jnp.split(lines, 4, axis=1)), ((0, 0), (0, 0), (0, step_columns - share))
            )
        ]

    def kernel(places, *refs):
        lefts_end = len(lefts)
        rights_end = lefts_end + len(flat)
        more_end = rights_end + len(more)
        weight_grads_kernel(
            plan,
            places,
            refs[:lefts_end],
            refs[lefts_end:rights_end],
            refs[rights_end:more_end],
            *refs[more_end + len(extra) :],
        )

    start = 1 + len(lefts) + len(flat) + len(more)
    return pl.pallas_call(
        kernel,
        grid=(len(plan),),
        in_specs=[SCALARS]
        + [whole(array.shape) for array in list(lefts) + flat + more]
        + [ANY] * len(extra),
        out_specs=[pl.BlockSpec((2, height, step_columns), lambda t: (0, 0, t + first))] * 2,
        out_shape=[shape_of((2, height, total), BF16)] * 2,
        input_output_aliases={start: 0, start + 1: 1} if extra else {},
        scratch_shapes=[pltpu.VMEM((width, count), BF16)],
        compiler_params=params(),
        cost_estimate=cost(
            2 * count * width * step_columns * len(plan), 4 * count * width * len(plan)
        ),
    )(places, *lefts, *flat, *more, *extra)


def middle_kernel(plan, parts, places, x, gain, *refs):
    mine, theirs, refs = refs[:parts], refs[parts : 2 * parts], refs[2 * parts :]
    mid, h1, n2, cq, out_mine, out_theirs, query, sems = refs

    @pl.when(pl.program_id(0) == 0)
    def _():
        side = places[4]
        copies = (
            fetch_half(mid, side, plan[0], out_mine, sems.at[0]),
            fetch_half(mid, 1 - side, plan[0], out_theirs, sems.at[1]),
            fetch_half(mid, side, plan[1], query, sems.at[2]),
        )
        start_all(copies)
        wait_all(copies)

    values = (
        x[...].astype(F32)
        + dot(join(mine), out_mine[...], NT)
        + dot(join(theirs), out_theirs[...], NT)
    )
    h1[...] = values
    normed = (values * inverse_rms(values) * gain[...]).astype(BF16)
    n2[...] = normed
    cq[...] = dot(normed, query[...], NN).astype(BF16)


def middle_step(places, x, mine, theirs, gain, mid, plan):
    count, width = x.shape
    half = sum(part.shape[1] for part in mine)

    def kernel(*refs):
        middle_kernel(plan, len(mine), *refs)

    return pl.pallas_call(
        kernel,
        grid=(count // TILE,),
        in_specs=[SCALARS, rows(width), whole((1, width))]
        + [rows(PAIR)] * (2 * len(mine))
        + [ANY],
        out_specs=[rows(width), rows(width), rows(half)],
        out_shape=[
            shape_of((count, width), F32),
            shape_of((count, width), BF16),
            shape_of((count, half), BF16),
        ],
        scratch_shapes=[pltpu.VMEM((width, half), BF16)] * 3 + [pltpu.SemaphoreType.DMA((3,))],
        compiler_params=params(),
        cost_estimate=cost(6 * count * width * half, 12 * count * width),
    )(places, x, gain, *mine, *theirs, mid)


def head_sums(left, right):
    product = left.astype(F32) * right.astype(F32)
    width = product.shape[1]
    high = product.astype(BF16)
    low = (product - high.astype(F32)).astype(BF16)
    height = 8 * (width // PAIR)
    line = lax.broadcasted_iota(jnp.int32, (height, width), 0)
    head = lax.broadcasted_iota(jnp.int32, (height, width), 1) // HEAD_DIM
    choose = (
        ((line // 8) * 2 + line % 8 == head) & (line % 8 < 2)
    ).astype(F32).astype(BF16)
    return dot(choose, high, NT) + dot(choose, low, NT)


CHUNK = 512


def units_kernel(columns, parts, places, h1, gain, gy, *refs):
    mine, theirs, refs = refs[:parts], refs[parts : 2 * parts], refs[2 * parts :]
    mid, late, refs = refs[0], refs[1], refs[2:]
    (
        output,
        n3,
        hidden,
        grad_gate,
        grad_up,
        dh2,
        e2,
        dc,
        deltas,
        gain_grad,
        out_mine,
        out_theirs,
        units_mine,
        units_theirs,
        sems,
    ) = refs
    step = pl.program_id(0)

    @pl.when(step == 0)
    def _():
        side = places[4]
        every = slice(0, units_mine.shape[1])
        copies = (
            fetch_half(mid, side, columns, out_mine, sems.at[0]),
            fetch_half(mid, 1 - side, columns, out_theirs, sems.at[1]),
            fetch_half(late, side, every, units_mine, sems.at[2]),
            fetch_half(late, 1 - side, every, units_theirs, sems.at[3]),
        )
        start_all(copies)
        gain_grad[...] = jnp.zeros_like(gain_grad)
        wait_all(copies)

    crossed_mine = join(mine)
    values = (
        h1[...] + dot(crossed_mine, out_mine[...], NT) + dot(join(theirs), out_theirs[...], NT)
    )
    normed = (values * inverse_rms(values) * gain[...]).astype(BF16)
    n3[...] = normed
    upstream = gy[...]
    mixed = jnp.zeros_like(values)
    back = jnp.zeros_like(values)
    unit = units_mine.shape[1] // 3
    for own in (True, False):
        weight = units_mine if own else units_theirs
        for start in range(0, unit, CHUNK):
            gate_weight = weight[:, start : start + CHUNK]
            up_weight = weight[:, unit + start : unit + start + CHUNK]
            down_weight = weight[:, 2 * unit + start : 2 * unit + start + CHUNK]
            gate = dot(normed, gate_weight, NN)
            up = dot(normed, up_weight, NN)
            pushed = dot(upstream, down_weight, NN)
            square = gate * gate
            bend = jnp.tanh(ROOT_TWO_OVER_PI * gate * (1.0 + CUBIC * square))
            lift = 0.5 * (1.0 + bend)
            gelu = gate * lift
            slope = lift + (0.5 * ROOT_TWO_OVER_PI) * gate * (1.0 - bend * bend) * (
                1.0 + (3.0 * CUBIC) * square
            )
            units = (gelu * up).astype(BF16)
            push_gate = (pushed * up * slope).astype(BF16)
            push_up = (pushed * gelu).astype(BF16)
            mixed = mixed + dot(units, down_weight, NT)
            back = back + dot(push_gate, gate_weight, NT) + dot(push_up, up_weight, NT)
            if own:
                hidden[:, start : start + CHUNK] = units
                grad_gate[:, start : start + CHUNK] = push_gate
                grad_up[:, start : start + CHUNK] = push_up
    output[...] = (values + mixed).astype(BF16)
    grad, gain_part = norm_back(values, gain[...], back)
    result = upstream.astype(F32) + grad
    dh2[...] = result
    low = result.astype(BF16)
    e2[...] = low
    crossed = dot(low, out_mine[...], NN).astype(BF16)
    dc[...] = crossed
    deltas[...] = head_sums(crossed, crossed_mine)
    gain_grad[0:1, :] += gain_part


def units_step(places, h1, mine, theirs, gain, gy, mid, columns, late):
    count, width = h1.shape
    half = sum(part.shape[1] for part in mine)
    unit = late.shape[2] // 3
    lines = 8 * (half // PAIR)

    def kernel(*refs):
        units_kernel(columns, len(mine), *refs)

    return pl.pallas_call(
        kernel,
        grid=(count // TILE,),
        in_specs=[
            SCALARS,
            rows(width),
            whole((1, width)),
            rows(width),
        ]
        + [rows(PAIR)] * (2 * len(mine))
        + [ANY] * 2,
        out_specs=[
            rows(width),
            rows(width),
            rows(unit),
            rows(unit),
            rows(unit),
            rows(width),
            rows(width),
            rows(half),
            pl.BlockSpec((lines, TILE), lambda t: (0, t)),
            whole((8, width)),
        ],
        out_shape=[
            shape_of((count, width), BF16),
            shape_of((count, width), BF16),
            shape_of((count, unit), BF16),
            shape_of((count, unit), BF16),
            shape_of((count, unit), BF16),
            shape_of((count, width), F32),
            shape_of((count, width), BF16),
            shape_of((count, half), BF16),
            shape_of((lines, count), F32),
            shape_of((8, width), F32),
        ],
        scratch_shapes=[pltpu.VMEM((width, half), BF16)] * 2
        + [pltpu.VMEM((width, 3 * unit), BF16)] * 2
        + [pltpu.SemaphoreType.DMA((4,))],
        compiler_params=params(),
        cost_estimate=cost(30 * count * width * unit, 30 * count * width),
    )(places, h1, gain, gy, *mine, *theirs, mid, late)


def turn_kernel(plan, parts, places, dh2, h1, mine, theirs, gain, *refs):
    attended, refs = refs[:parts], refs[parts:]
    mid, dh1, e1, da, deltas, gain_grad, query_mine, query_theirs, out_mine, sems = refs

    @pl.when(pl.program_id(0) == 0)
    def _():
        side = places[4]
        copies = (
            fetch_half(mid, side, plan[0], out_mine, sems.at[0]),
            fetch_half(mid, side, plan[1], query_mine, sems.at[1]),
            fetch_half(mid, 1 - side, plan[1], query_theirs, sems.at[2]),
        )
        start_all(copies)
        gain_grad[...] = jnp.zeros_like(gain_grad)
        wait_all(copies)

    back = dot(mine[...], query_mine[...], NT) + dot(theirs[...], query_theirs[...], NT)
    grad, gain_part = norm_back(h1[...], gain[...], back)
    result = dh2[...] + grad
    dh1[...] = result
    low = result.astype(BF16)
    e1[...] = low
    pushed = dot(low, out_mine[...], NN).astype(BF16)
    da[...] = pushed
    deltas[...] = head_sums(pushed, join(attended))
    gain_grad[0:1, :] += gain_part


def turn_step(places, dh2, h1, mine, theirs, gain, attended, mid, plan):
    count, width = h1.shape
    half = mine.shape[1]
    lines = 8 * (half // PAIR)

    def kernel(*refs):
        turn_kernel(plan, len(attended), *refs)

    return pl.pallas_call(
        kernel,
        grid=(count // TILE,),
        in_specs=[
            SCALARS,
            rows(width),
            rows(width),
            rows(half),
            rows(half),
            whole((1, width)),
        ]
        + [rows(PAIR)] * len(attended)
        + [ANY],
        out_specs=[
            rows(width),
            rows(width),
            rows(half),
            pl.BlockSpec((lines, TILE), lambda t: (0, t)),
            whole((8, width)),
        ],
        out_shape=[
            shape_of((count, width), F32),
            shape_of((count, width), BF16),
            shape_of((count, half), BF16),
            shape_of((lines, count), F32),
            shape_of((8, width), F32),
        ],
        scratch_shapes=[pltpu.VMEM((width, half), BF16)] * 3 + [pltpu.SemaphoreType.DMA((3,))],
        compiler_params=params(),
        cost_estimate=cost(6 * count * width * half, 16 * count * width),
    )(places, dh2, h1, mine, theirs, gain, *attended, mid)


def partial_kernel(places, x, *refs):
    parts, refs = refs[:-8], refs[-8:]
    w0, w1, w2, w3, out, gain_grad, weight, sems = refs

    @pl.when(pl.program_id(0) == 0)
    def _():
        copies = fetch((w0, w1, w2, w3), places, slice(0, weight.shape[1]), weight, sems)
        start_all(copies)
        gain_grad[...] = jnp.zeros_like(gain_grad)
        wait_all(copies)

    back = dot(join(parts), weight[...], NT)
    out[...] = back.astype(BF16)
    values = x[...].astype(F32)
    gain_grad[0:1, :] += jnp.sum(back * values * inverse_rms(values), axis=0, keepdims=True)


def partial_step(places, parts, x, pieces):
    count, width = x.shape
    inner = sum(part.shape[1] for part in parts)
    return pl.pallas_call(
        partial_kernel,
        grid=(count // TILE,),
        in_specs=[SCALARS, rows(width)] + [rows(PAIR)] * len(parts) + [ANY] * 4,
        out_specs=[rows(width), whole((8, width))],
        out_shape=[shape_of((count, width), BF16), shape_of((8, width), F32)],
        scratch_shapes=[pltpu.VMEM((width, inner), BF16), pltpu.SemaphoreType.DMA((4,))],
        compiler_params=params(),
        cost_estimate=cost(2 * count * width * inner, 8 * count * width),
    )(places, x, *parts, *pieces)


def first_kernel(dh1, x, mine, theirs, gain, out):
    back = mine[...].astype(F32) + theirs[...].astype(F32)
    grad, _ = norm_back(x[...].astype(F32), gain[...], back)
    out[...] = (dh1[...] + grad).astype(BF16)


def first_step(dh1, x, mine, theirs, gain):
    count, width = x.shape
    return pl.pallas_call(
        first_kernel,
        grid=(count // TILE,),
        in_specs=[rows(width)] * 4 + [whole((1, width))],
        out_specs=rows(width),
        out_shape=shape_of((count, width), BF16),
        compiler_params=params(),
        cost_estimate=cost(20 * count * width, 12 * count * width),
    )(dh1, x, mine, theirs, gain)


def swap(values, axis, distance):
    size = lax.axis_size(axis)
    return lax.ppermute(values, axis, [(i, i ^ distance) for i in range(size)])


def after(values, *others):
    return lax.optimization_barrier((values,) + others)[0]


def gather_all(values):
    return lax.all_gather(values, ("narrow", "wide"), axis=0, tiled=True).reshape(
        lax.axis_size("narrow"), -1, values.shape[1]
    )


def sum_wide(values):
    return lax.psum_scatter(values, "wide", scatter_dimension=0, tiled=True)


def add(left, right):
    return (left.astype(F32) + right.astype(F32)).astype(BF16)


def add_pair(keep, got):
    return add(keep[0], got[0]), add(keep[1], got[1])


def line_inner():
    place = lax.axis_index("dp")
    return (place == 1) | (place == 2)


def line_first(values):
    if lax.axis_size("dp") != 4:
        return lax.psum(values, "dp")
    got = lax.ppermute(values, "dp", [(0, 1), (3, 2)])
    return jnp.where(line_inner(), add(values, got), values)


def line_second(values):
    if lax.axis_size("dp") != 4:
        return values
    return add(values, lax.ppermute(values, "dp", [(1, 2), (2, 1)]))


def line_third(values):
    if lax.axis_size("dp") != 4:
        return values
    got = lax.ppermute(values, "dp", [(1, 0), (2, 3)])
    return jnp.where(line_inner(), values, got)


def local(
    tokens,
    memory,
    cotangent,
    norm1_gain,
    norm2_gain,
    norm3_gain,
    q_weight,
    k_weight,
    v_weight,
    o_weight,
    cross_q,
    cross_k,
    cross_v,
    cross_o,
    gate_weight,
    up_weight,
    down_weight,
    segment_ids,
    block_ids,
    image_table,
):
    width = tokens.shape[1]
    share = q_weight.shape[0]
    inner = q_weight.shape[1]
    unit = gate_weight.shape[1]
    images = memory.shape[0]
    flat_memory = memory.reshape(-1, width)
    place = lax.axis_index("wide")
    side = lax.axis_index("narrow")
    places = jnp.stack([place, place ^ 2, place ^ 1, place ^ 3, side]).astype(jnp.int32)

    gains = jnp.stack([norm1_gain, norm2_gain, norm3_gain])
    gains = jnp.pad(gains, ((0, 13), (0, 3 * inner - share)))
    early = jnp.concatenate(
        [jnp.concatenate([q_weight, k_weight, v_weight], axis=1), gains], axis=0
    )
    early_x = swap(early, "wide", 2)
    early_pieces = (early, early_x, swap(early, "wide", 1), swap(early_x, "wide", 1))
    lines = jnp.stack([piece[share : share + 3, :share] for piece in early_pieces])
    lines = lines.astype(F32)
    order = [
        jnp.sum(jnp.where((places[:4] == w)[:, None, None], lines, 0.0), axis=0)
        for w in range(4)
    ]
    all_gains = jnp.concatenate(order, axis=1)[:, None, :]

    kv = jnp.concatenate([cross_k, cross_v], axis=1)
    kv_x = swap(kv, "wide", 2)
    kv_pieces = (kv, kv_x, swap(kv, "wide", 1), swap(kv_x, "wide", 1))
    memory_columns = slice(0, 2 * inner)
    mid = jnp.concatenate([o_weight, cross_o, cross_q], axis=1)
    out_columns = slice(0, inner)
    cross_out_columns = slice(inner, 2 * inner)
    query_columns = slice(2 * inner, 3 * inner)
    late = jnp.concatenate([gate_weight, up_weight, down_weight], axis=1)

    x, gy, row_ids, col_ids, pos, scalars = order_rows(
        segment_ids, block_ids, image_table, tokens, cotangent
    )
    mid = gather_all(after(mid, early_x, x))
    late = gather_all(after(late, early_x, x))
    n1, qkv = norm_project(places, x, all_gains[0], early_pieces)
    pairs = inner // PAIR
    self_parts = [self_forward(0, after(qkv, kv_x), row_ids, col_ids)]
    for pair in range(1, pairs):
        self_parts.append(self_forward(pair, after(qkv, self_parts[-1][0]), row_ids, col_ids))
    attended_theirs = [swap(part[0], "narrow", 1) for part in self_parts]
    attended = [part[0] for part in self_parts]
    keys_values = project_memory(
        places,
        after(flat_memory, self_parts[-1][0], attended_theirs[0]),
        kv_pieces,
        memory_columns,
    )
    h1, n2, cq = middle_step(
        places,
        x,
        attended,
        attended_theirs,
        all_gains[1],
        mid,
        (out_columns, query_columns),
    )
    cross_parts = [cross_forward(0, scalars, cq, keys_values, images)]
    crossed_theirs = []
    for pair in range(1, pairs):
        previous = [cross_parts[-1][0]] + crossed_theirs
        crossed_theirs.append(swap(cross_parts[-1][0], "narrow", 1))
        cross_parts.append(
            cross_forward(pair, scalars, after(cq, *previous), keys_values, images)
        )
    crossed = [part[0] for part in cross_parts]
    crossed_theirs.append(swap(crossed[-1], "narrow", 1))
    cross_logs = jnp.concatenate([part[1] for part in cross_parts], axis=0)
    (
        output,
        n3,
        hidden,
        grad_gate,
        grad_up,
        dh2,
        e2,
        dc,
        cross_deltas,
        third_gain,
    ) = units_step(
        places,
        h1,
        crossed,
        crossed_theirs,
        all_gains[2],
        gy,
        mid,
        cross_out_columns,
        late,
    )

    unit_keep, unit_send = weight_grads(
        places, (n3, gy), (grad_gate, grad_up, hidden), ((0, (0,)), (0, (1,)), (1, (2,)))
    )
    output = restore_rows(pos, after(output, unit_send))
    unit_stay, unit_leave = add_pair(unit_keep, swap(unit_send, "wide", 1))
    dcq, dck, dcv = cross_backward(
        0,
        scalars,
        cq,
        keys_values,
        after(dc, unit_leave, output),
        cross_logs,
        cross_deltas,
        images,
        None,
    )
    unit_part = add(unit_stay, swap(unit_leave, "wide", 2))
    keep0, send0, total = memory_back(
        places,
        flat_memory,
        after(dck, unit_part),
        dcv,
        kv_pieces,
        memory_columns,
        0,
        None,
        0,
    )
    unit_sum = lax.psum(unit_part, "dp")
    dcq, dck, dcv = cross_backward(
        1,
        scalars,
        cq,
        keys_values,
        after(dc, send0),
        cross_logs,
        cross_deltas,
        images,
        dcq,
    )
    dcq_theirs = swap(dcq, "narrow", 1)
    memory0 = add(keep0, swap(send0, "narrow", 1))
    keep1, send1, cross_keep, cross_send = memory_back(
        places,
        flat_memory,
        after(dck, memory0),
        dcv,
        kv_pieces,
        memory_columns,
        1,
        total,
        2 * inner,
    )
    cross_keep, cross_send = weight_grads(
        places,
        (after(n2, send1), e2),
        (dcq, crossed),
        ((0, (0,)), (1, (1,))),
        into=(cross_keep, cross_send),
        first=2,
    )
    dh1, e1, da, self_deltas, second_gain = turn_step(
        places,
        dh2,
        h1,
        after(dcq, cross_send),
        dcq_theirs,
        all_gains[1],
        attended,
        mid,
        (out_columns, query_columns),
    )
    memory1 = add(keep1, swap(after(send1, dcq_theirs), "narrow", 1))
    cross_stay, cross_leave = add_pair(cross_keep, swap(cross_send, "wide", 1))
    da = after(da, cross_leave)
    back = []
    for pair in range(pairs):
        ready = after(da, *[part[0] for part in back])
        back.append(
            self_backward(
                pair, qkv, ready, self_parts[pair][1], self_deltas, row_ids, col_ids
            )
        )
    cross_part = add(cross_stay, swap(cross_leave, "wide", 2))
    early_back = back[: pairs - 1]
    self_keep, self_send = weight_grads(
        places,
        (after(n1, back[-2][0]),),
        [part[i] for part in early_back for i in range(3)],
        ((0, tuple(range(3 * len(early_back)))),),
    )
    dq, dk, dv = [[part[i] for part in back] for i in range(3)]
    dn1, first_gain = partial_step(
        places, dq + dk + dv, after(x, self_send, cross_part), early_pieces
    )
    cross_sum = lax.psum(after(cross_part, unit_sum), "dp")
    first_theirs = swap(first_gain, "narrow", 1)
    dn1_theirs = swap(after(dn1, memory1), "narrow", 1)
    gain_lines = jnp.concatenate(
        [
            first_gain[0:1] + first_theirs[0:1],
            second_gain[0:1],
            third_gain[0:1],
            jnp.zeros((13, width), F32),
        ],
        axis=0,
    )
    last_keep, last_send = weight_grads(
        places,
        (n1, after(e1, dn1)),
        (list(back[-1]), attended),
        ((0, (0,)), (1, (1,))),
        lines=gain_lines,
    )
    self_stay, self_leave = add_pair(self_keep, swap(self_send, "wide", 1))
    self_part = add(self_stay, swap(self_leave, "wide", 2))
    last_stay, last_leave = add_pair(last_keep, swap(last_send, "wide", 1))
    last_part = add(last_stay, swap(last_leave, "wide", 2))
    tokens_grad = first_step(after(dh1, cross_sum), x, dn1, dn1_theirs, all_gains[0])
    tokens_grad = restore_rows(pos, tokens_grad)
    memory_grad = jnp.stack([memory0, memory1])
    self_sum = line_third(line_second(line_first(self_part)))
    last_sum = line_third(line_second(line_first(last_part)))

    def grads(array, size, count):
        return [array[:share, i * size : (i + 1) * size].astype(F32) for i in range(count)]

    gate_grad, up_grad, down_grad = grads(unit_sum, unit, 3)
    cross_k_grad, cross_v_grad, cross_q_grad, cross_o_grad = grads(cross_sum, inner, 4)
    pieces = grads(self_sum, PAIR, 3 * (pairs - 1)) + grads(last_sum, PAIR, 3)
    q_grad, k_grad, v_grad = [jnp.concatenate(pieces[i::3], axis=1) for i in range(3)]
    o_grad = last_sum[:share, inner : 2 * inner].astype(F32)
    gain_sums = last_sum[share : share + 3, :share].astype(F32)
    return (
        output,
        tokens_grad,
        memory_grad,
        gain_sums[0],
        gain_sums[1],
        gain_sums[2],
        q_grad,
        k_grad,
        v_grad,
        o_grad,
        cross_q_grad,
        cross_k_grad,
        cross_v_grad,
        cross_o_grad,
        gate_grad,
        up_grad,
        down_grad,
    )


def solution(mesh):
    both = ("dp", "wide")
    weight = P("wide", "narrow")
    in_specs = (
        (P(both, None), P(both, None, None), P(both, None))
        + (P("wide"),) * 3
        + (weight,) * 11
        + (P(both, None),) * 3
    )
    out_specs = (
        (P(both, None), P(both, None), P(both, None, "narrow"))
        + (P("wide"),) * 3
        + (weight,) * 11
    )
    return jax.shard_map(local, mesh=mesh, in_specs=in_specs, out_specs=out_specs, check_vma=False)
```

```python
import functools
import math

import jax
import jax.numpy as jnp
from jax import lax
from jax.experimental import pallas as pl
from jax.experimental.pallas import tpu as pltpu
from jax.sharding import PartitionSpec as P

F32 = jnp.float32
BF16 = jnp.bfloat16
EPSILON = 1e-06
ROOT_TWO_OVER_PI = 0.7978845608028654
CUBIC = 0.044715
HEAD_DIM = 64
PAIR = 2 * HEAD_DIM
SCALE = HEAD_DIM ** (-0.5)
EXP2_SCALE = SCALE * math.log2(math.e)
HIDE = 1e30
TILE = 256
WEIGH = 4.0

NN = (((1,), (0,)), ((), ()))
NT = (((1,), (1,)), ((), ()))
TN = (((0,), (0,)), ((), ()))


def dot(left, right, dims):
    return lax.dot_general(left, right, dims, preferred_element_type=F32)


def params():
    return pltpu.CompilerParams(vmem_limit_bytes=60 * 1024 * 1024)


def cost(flops, nbytes):
    return pl.CostEstimate(
        flops=int(flops * WEIGH), bytes_accessed=int(nbytes * WEIGH), transcendentals=0
    )


def shape_of(shape, dtype):
    return jax.ShapeDtypeStruct(shape, dtype)


def whole(shape):
    zeros = (0,) * len(shape)
    return pl.BlockSpec(shape, lambda *_: zeros)


def rows(width, height=TILE):
    return pl.BlockSpec((height, width), lambda t, *_: (t, 0))


def inverse_rms(values):
    return lax.rsqrt(jnp.mean(values * values, axis=1, keepdims=True) + EPSILON)


def norm_back(values, gain, upstream):
    factor = inverse_rms(values)
    scaled = upstream * gain
    mean = jnp.mean(values * scaled, axis=1, keepdims=True)
    grad = factor * scaled - values * (factor * factor * factor * mean)
    return grad, jnp.sum(upstream * values * factor, axis=0, keepdims=True)


def in_half(shape, half):
    return (lax.broadcasted_iota(jnp.int32, shape, 1) // HEAD_DIM) == half


def only_half(values, half):
    return jnp.where(in_half(values.shape, half), values, jnp.zeros_like(values))


def order_kernel(seg, blk, table, x, gy, xp, gyp, row_ids, col_ids, pos_out, scalars, pos):
    step = pl.program_id(0)
    count = seg.shape[1]

    @pl.when(step == 0)
    def _():
        segments = seg[...]
        image = jnp.zeros_like(segments)
        for s in range(table.shape[1]):
            image = jnp.where(segments == s, table[0, s], image)
        first = (image == 0).astype(F32)
        before = lax.broadcasted_iota(jnp.int32, (count, count), 0) < lax.broadcasted_iota(
            jnp.int32, (count, count), 1
        )
        rank = dot(
            jnp.broadcast_to(first, (8, count)).astype(BF16),
            before.astype(F32).astype(BF16),
            NN,
        )[0:1]
        total = jnp.sum(first)
        index = lax.broadcasted_iota(jnp.int32, (1, count), 1).astype(F32)
        place = jnp.where(image == 0, rank, total + index - rank)
        pos[...] = place.astype(jnp.int32)
        pos_out[...] = jnp.broadcast_to(pos[...], (8, count))
        n0 = total.astype(jnp.int32)
        tiles = count // TILE
        visits0 = jnp.maximum(1, (n0 + TILE - 1) // TILE)
        start1 = jnp.minimum(tiles - 1, n0 // TILE)
        visits = visits0 + tiles - start1
        for v in range(tiles + 1):
            real = jnp.minimum(v, visits - 1)
            in_first = real < visits0
            scalars[v] = jnp.where(in_first, real, real - visits0 + start1)
            scalars[8 + v] = jnp.where(in_first, 0, 1)
        scalars[16] = visits
        scalars[17] = n0
        scalars[18] = visits0
        scalars[19] = start1
        scalars[20] = tiles - start1

    onehot = (
        lax.broadcasted_iota(jnp.int32, (TILE, count), 0) + step * TILE == pos[...]
    ).astype(F32).astype(BF16)
    xp[...] = dot(onehot, x[...], NN).astype(BF16)
    gyp[...] = dot(onehot, gy[...], NN).astype(BF16)
    ids = jnp.concatenate(
        [
            seg[...].astype(F32),
            blk[...].astype(F32),
            jnp.zeros((126, count), F32),
        ],
        axis=0,
    ).astype(BF16)
    row_ids[...] = dot(ids[0:8], onehot, NT)
    col_ids[...] = dot(onehot, ids, NT)


def order_rows(seg, blk, table, x, gy):
    count, width = x.shape
    return pl.pallas_call(
        order_kernel,
        grid=(count // TILE,),
        in_specs=[
            whole((1, count)),
            whole((1, count)),
            pl.BlockSpec(memory_space=pltpu.SMEM),
            whole((count, width)),
            whole((count, width)),
        ],
        out_specs=[
            rows(width),
            rows(width),
            pl.BlockSpec((8, TILE), lambda t: (0, t)),
            rows(128),
            whole((8, count)),
            pl.BlockSpec(memory_space=pltpu.SMEM),
        ],
        out_shape=[
            shape_of((count, width), BF16),
            shape_of((count, width), BF16),
            shape_of((8, count), F32),
            shape_of((count, 128), F32),
            shape_of((8, count), jnp.int32),
            shape_of((32,), jnp.int32),
        ],
        scratch_shapes=[pltpu.VMEM((1, count), jnp.int32)],
        compiler_params=params(),
        cost_estimate=cost(4 * count * count * width, 8 * count * width),
    )(seg, blk, table, x, gy)


def restore_kernel(pos, values, out):
    count = values.shape[0]
    onehot = (
        lax.broadcasted_iota(jnp.int32, (count, TILE), 0) == pos[0:1, :]
    ).astype(F32).astype(BF16)
    out[...] = dot(onehot, values[...], TN).astype(BF16)


def restore_rows(pos, values):
    count, width = values.shape
    return pl.pallas_call(
        restore_kernel,
        grid=(count // TILE,),
        in_specs=[pl.BlockSpec((8, TILE), lambda t: (0, t)), whole((count, width))],
        out_specs=rows(width),
        out_shape=shape_of((count, width), BF16),
        compiler_params=params(),
        cost_estimate=cost(2 * count * count * width, 4 * count * width),
    )(pos, values)


def fetch(pieces, places, columns, dest, sems, base=0):
    height = dest.shape[0] // 4
    copies = []
    for i, piece in enumerate(pieces):
        start = pl.multiple_of(places[i] * height, 16)
        copies.append(
            pltpu.make_async_copy(
                piece.at[pl.ds(0, height), columns],
                dest.at[pl.ds(start, height), :],
                sems.at[base + i],
            )
        )
    return copies


def fetch_half(gathered, half, columns, dest, sem):
    return pltpu.make_async_copy(gathered.at[half, :, columns], dest, sem)


def start_all(copies):
    for copy in copies:
        copy.start()


def wait_all(copies):
    for copy in copies:
        copy.wait()


ANY = pl.BlockSpec(memory_space=pl.ANY)
SCALARS = pl.BlockSpec(memory_space=pltpu.SMEM)


def project_kernel(places, x, gain, w0, w1, w2, w3, normed, out, weight, sems):
    @pl.when(pl.program_id(0) == 0)
    def _():
        copies = fetch((w0, w1, w2, w3), places, slice(0, weight.shape[1]), weight, sems)
        start_all(copies)
        wait_all(copies)

    values = x[...].astype(F32)
    n1 = (values * inverse_rms(values) * gain[...]).astype(BF16)
    normed[...] = n1
    out[...] = dot(n1, weight[...], NN).astype(BF16)


def norm_project(places, x, gain, pieces):
    count, width = x.shape
    outs = pieces[0].shape[1]
    return pl.pallas_call(
        project_kernel,
        grid=(count // TILE,),
        in_specs=[SCALARS, rows(width), whole((1, width))] + [ANY] * 4,
        out_specs=[rows(width), rows(outs)],
        out_shape=[shape_of((count, width), BF16), shape_of((count, outs), BF16)],
        scratch_shapes=[pltpu.VMEM((width, outs), BF16), pltpu.SemaphoreType.DMA((4,))],
        compiler_params=params(),
        cost_estimate=cost(2 * count * width * outs, 4 * count * width + 2 * count * outs),
    )(places, x, gain, *pieces)


MEMORY_TILE = 512


def memory_kernel(places, columns, memory, w0, w1, w2, w3, out, weight, sems):
    @pl.when(pl.program_id(0) == 0)
    def _():
        copies = fetch((w0, w1, w2, w3), places, columns, weight, sems)
        start_all(copies)
        wait_all(copies)

    out[...] = dot(memory[...], weight[...], NN).astype(BF16)


def project_memory(places, memory, pieces, columns):
    count, width = memory.shape
    outs = columns.stop - columns.start

    def kernel(places, *refs):
        memory_kernel(places, columns, *refs)

    return pl.pallas_call(
        kernel,
        grid=(count // MEMORY_TILE,),
        in_specs=[SCALARS, rows(width, MEMORY_TILE)] + [ANY] * 4,
        out_specs=rows(outs, MEMORY_TILE),
        out_shape=shape_of((count, outs), BF16),
        scratch_shapes=[pltpu.VMEM((width, outs), BF16), pltpu.SemaphoreType.DMA((4,))],
        compiler_params=params(),
        cost_estimate=cost(2 * count * width * outs, 4 * count * width),
    )(places, memory, *pieces)


SELF_TILE = 128
SELF_WINDOW = 512
BACK_WINDOW = 640


def store_logs(ref, columns, logs, extra=None):
    spread = jnp.where(in_half((logs[0].shape[0], PAIR), 0), logs[0], logs[1]).T
    for half in range(2):
        line = spread[half * HEAD_DIM : half * HEAD_DIM + 1, :]
        if extra is not None:
            line = jnp.where(extra, line, ref[half : half + 1, columns])
        ref[half : half + 1, columns] = line


def self_forward_kernel(q, k, v, row_ids, col_ids, out, logs):
    count = q.shape[0]
    for tile in range(count // SELF_TILE):
        base = tile * SELF_TILE
        start = min(max(base - 256, 0), count - SELF_WINDOW)
        spot = slice(base, base + SELF_TILE)
        window = slice(start, start + SELF_WINDOW)
        seen = (col_ids[spot, 0:1] == row_ids[0:1, window]) & (
            row_ids[1:2, window] <= col_ids[spot, 1:2]
        )
        bias = jnp.where(seen, 0.0, -HIDE)
        keys = k[window, :]
        values = v[window, :]
        queries = q[spot, :]
        parts, totals = [], []
        for half in range(2):
            scores = dot(only_half(queries, half), keys, NT) * EXP2_SCALE + bias
            highest = jnp.max(scores, axis=1, keepdims=True)
            weights = jnp.exp2(scores - highest)
            total = jnp.sum(weights, axis=1, keepdims=True)
            parts.append(dot(weights.astype(BF16), values, NN) / total)
            totals.append(highest + jnp.log2(total))
        out[spot, :] = jnp.where(in_half(parts[0].shape, 0), parts[0], parts[1]).astype(BF16)
        store_logs(logs, spot, totals)


def self_forward(pair, qkv, row_ids, col_ids):
    count = qkv.shape[0]
    pairs = qkv.shape[1] // (3 * PAIR)

    def part(which):
        return pl.BlockSpec((count, PAIR), lambda p: (0, which * pairs + pair))

    return pl.pallas_call(
        self_forward_kernel,
        grid=(1,),
        in_specs=[part(0), part(1), part(2), whole((8, count)), whole((count, 128))],
        out_specs=[whole((count, PAIR)), whole((8, count))],
        out_shape=[shape_of((count, PAIR), BF16), shape_of((8, count), F32)],
        compiler_params=params(),
        cost_estimate=cost(16 * count * SELF_WINDOW * PAIR, 8 * count * PAIR),
    )(qkv, qkv, qkv, row_ids, col_ids)


def self_backward_kernel(q, k, v, grad, logs, deltas, row_ids, col_ids, dq, dk, dv, key_sum, value_sum):
    count = q.shape[0]
    key_sum[...] = jnp.zeros_like(key_sum)
    value_sum[...] = jnp.zeros_like(value_sum)
    for tile in range(count // TILE):
        base = tile * TILE
        start = min(max(base - 256, 0), count - BACK_WINDOW)
        spot = slice(base, base + TILE)
        window = slice(start, start + BACK_WINDOW)
        seen = (col_ids[window, 0:1] == row_ids[0:1, spot]) & (
            col_ids[window, 1:2] <= row_ids[1:2, spot]
        )
        bias = jnp.where(seen, 0.0, -HIDE)
        keys = k[window, :]
        values = v[window, :]
        queries = q[spot, :]
        grads = grad[spot, :]
        parts = []
        for half in range(2):
            one_query = only_half(queries, half)
            one_grad = only_half(grads, half)
            scores = dot(keys, one_query, NT) * EXP2_SCALE + bias
            weights = jnp.exp2(scores - logs[half : half + 1, spot])
            slopes = dot(values, one_grad, NT)
            pushed = (weights * (slopes - deltas[half : half + 1, spot])).astype(BF16)
            value_sum[window, :] += dot(weights.astype(BF16), one_grad, NN)
            key_sum[window, :] += dot(pushed, one_query, NN)
            parts.append(dot(pushed, keys, TN))
        dq[spot, :] = (
            jnp.where(in_half(parts[0].shape, 0), parts[0], parts[1]) * SCALE
        ).astype(BF16)
    dk[...] = (key_sum[...] * SCALE).astype(BF16)
    dv[...] = value_sum[...].astype(BF16)


def self_backward(pair, qkv, grad, logs, deltas, row_ids, col_ids):
    count = qkv.shape[0]
    pairs = qkv.shape[1] // (3 * PAIR)

    def part(which):
        return pl.BlockSpec((count, PAIR), lambda p: (0, which * pairs + pair))

    return pl.pallas_call(
        self_backward_kernel,
        grid=(1,),
        in_specs=[
            part(0),
            part(1),
            part(2),
            part(0),
            whole((8, count)),
            pl.BlockSpec((8, count), lambda p: (pair, 0)),
            whole((8, count)),
            whole((count, 128)),
        ],
        out_specs=[whole((count, PAIR))] * 3,
        out_shape=[shape_of((count, PAIR), BF16)] * 3,
        scratch_shapes=[pltpu.VMEM((count, PAIR), F32)] * 2,
        compiler_params=params(),
        cost_estimate=cost(40 * count * BACK_WINDOW * PAIR, 16 * count * PAIR),
    )(qkv, qkv, qkv, grad, logs, deltas, row_ids, col_ids)


def cross_forward_kernel(scalars, q, k, v, out, logs):
    step = pl.program_id(0)
    tile = scalars[step]
    image = scalars[8 + step]
    again = (step > 0) & (scalars[jnp.maximum(step - 1, 0)] == tile)

    @pl.when(step < scalars[16])
    def _():
        queries = q[...]
        keys = k[...]
        values = v[...]
        parts, totals = [], []
        for half in range(2):
            scores = dot(only_half(queries, half), keys, NT)
            highest = jnp.max(scores, axis=1, keepdims=True) * EXP2_SCALE
            weights = jnp.exp2(scores * EXP2_SCALE - highest)
            total = jnp.sum(weights, axis=1, keepdims=True)
            parts.append(dot(weights.astype(BF16), values, NN) / total)
            totals.append(highest + jnp.log2(total))
        mixed = jnp.where(in_half(parts[0].shape, 0), parts[0], parts[1]).astype(BF16)
        limit = scalars[17] - tile * TILE
        row_mine = (
            lax.broadcasted_iota(jnp.int32, mixed.shape, 0) >= limit
        ) == (image == 1)
        lane_mine = (
            lax.broadcasted_iota(jnp.int32, (1, TILE), 1) >= limit
        ) == (image == 1)
        keep = jnp.logical_not(again)
        out[...] = jnp.where(row_mine | keep, mixed, out[...])
        store_logs(logs, slice(0, TILE), totals, lane_mine | keep)


def cross_forward(pair, scalars, q, keys_values, images):
    count, inner = q.shape
    pairs = inner // PAIR
    memory_rows = keys_values.shape[0] // images
    tile_spec = pl.BlockSpec((TILE, PAIR), lambda s, sc: (sc[s], 0))

    def part(which):
        return pl.BlockSpec((memory_rows, PAIR), lambda s, sc: (sc[8 + s], which * pairs + pair))

    return pl.pallas_call(
        cross_forward_kernel,
        grid_spec=pltpu.PrefetchScalarGridSpec(
            num_scalar_prefetch=1,
            grid=(count // TILE + 1,),
            in_specs=[
                pl.BlockSpec((TILE, PAIR), lambda s, sc: (sc[s], pair)),
                part(0),
                part(1),
            ],
            out_specs=[tile_spec, pl.BlockSpec((8, TILE), lambda s, sc: (0, sc[s]))],
        ),
        out_shape=[shape_of((count, PAIR), BF16), shape_of((8, count), F32)],
        compiler_params=params(),
        cost_estimate=cost(20 * count * memory_rows * PAIR, 8 * memory_rows * PAIR),
    )(scalars, q, keys_values, keys_values)


def cross_backward_kernel(
    image, scalars, q, k, v, grad, logs, deltas, old, dq, dk, dv, key_sum, value_sum
):
    step = pl.program_id(1)
    tile = cross_tile(image, scalars, step)

    @pl.when(step == 0)
    def _():
        key_sum[...] = jnp.zeros_like(key_sum)
        value_sum[...] = jnp.zeros_like(value_sum)

    @pl.when(step < scalars[20 if image else 18])
    def _():
        queries = q[...]
        grads = grad[...]
        keys = k[...]
        values = v[...]
        limit = scalars[17] - tile * TILE
        lane_mine = (lax.broadcasted_iota(jnp.int32, (1, TILE), 1) >= limit) == (image == 1)
        parts = []
        for half in range(2):
            one_query = only_half(queries, half)
            one_grad = only_half(grads, half)
            log = jnp.where(lane_mine, logs[half : half + 1, :], HIDE)
            scores = dot(keys, one_query, NT)
            weights = jnp.exp2(scores * EXP2_SCALE - log)
            slopes = dot(values, one_grad, NT)
            pushed = (weights * (slopes - deltas[half : half + 1, :])).astype(BF16)
            value_sum[...] += dot(weights.astype(BF16), one_grad, NN)
            key_sum[...] += dot(pushed, one_query, NN)
            parts.append(dot(pushed, keys, TN))
        grad_query = (
            jnp.where(in_half(parts[0].shape, 0), parts[0], parts[1]) * SCALE
        ).astype(BF16)
        if image:
            row_mine = lax.broadcasted_iota(jnp.int32, grad_query.shape, 0) >= limit
            grad_query = jnp.where(row_mine, grad_query, old[...])
        dq[...] = grad_query

    @pl.when(step == pl.num_programs(1) - 1)
    def _():
        dk[...] = (key_sum[...] * SCALE).astype(BF16)
        dv[...] = value_sum[...].astype(BF16)


def cross_tile(image, scalars, step):
    if image:
        return scalars[19] + jnp.minimum(step, scalars[20] - 1)
    return jnp.minimum(step, scalars[18] - 1)


def cross_backward(image, scalars, q, keys_values, grad, logs, deltas, images, old):
    count, inner = q.shape
    pairs = inner // PAIR
    memory_rows = keys_values.shape[0] // images
    tile_spec = pl.BlockSpec((TILE, PAIR), lambda p, s, sc: (cross_tile(image, sc, s), p))
    line = pl.BlockSpec((8, TILE), lambda p, s, sc: (p, cross_tile(image, sc, s)))
    result = pl.BlockSpec((memory_rows, PAIR), lambda p, s, sc: (0, p))

    def part(which):
        return pl.BlockSpec((memory_rows, PAIR), lambda p, s, sc: (image, which * pairs + p))

    def first_kernel(scalars, q, k, v, grad, logs, deltas, *rest):
        cross_backward_kernel(image, scalars, q, k, v, grad, logs, deltas, None, *rest)

    def second_kernel(*refs):
        cross_backward_kernel(image, *refs)

    extra = [old] if image else []
    return pl.pallas_call(
        second_kernel if image else first_kernel,
        grid_spec=pltpu.PrefetchScalarGridSpec(
            num_scalar_prefetch=1,
            grid=(pairs, count // TILE),
            in_specs=[tile_spec, part(0), part(1), tile_spec, line, line]
            + [tile_spec] * len(extra),
            out_specs=[tile_spec, result, result],
            scratch_shapes=[pltpu.VMEM((memory_rows, PAIR), F32)] * 2,
        ),
        out_shape=[
            shape_of((count, inner), BF16),
            shape_of((memory_rows, inner), BF16),
            shape_of((memory_rows, inner), BF16),
        ],
        input_output_aliases={7: 0} if image else {},
        compiler_params=params(),
        cost_estimate=cost(25 * count * memory_rows * inner, 8 * memory_rows * inner),
    )(scalars, q, keys_values, keys_values, grad, logs, deltas, *extra)


def put_rows(places, product, keep, send):
    height = product.shape[0] // 4
    for i, ref in enumerate((keep, keep, send, send)):
        start = pl.multiple_of(places[i] * height, 16)
        ref[i % 2, 0:height, :] = product[pl.ds(start, height), :].astype(BF16)


def memory_back_kernel(
    columns, last, places, memory, dk, dv, w0, w1, w2, w3, *refs
):
    if last:
        before, keep_part, send_part, keep, send, weight, total, sems = refs
    else:
        keep_part, send_part, total_out, weight, total, sems = refs
    inner = dk.shape[1]

    @pl.when(pl.program_id(0) == 0)
    def _():
        copies = fetch((w0, w1, w2, w3), places, columns, weight, sems)
        start_all(copies)
        if last:
            total[...] = before[...]
        else:
            total[...] = jnp.zeros_like(total)
        wait_all(copies)

    both = jnp.concatenate([dk[...], dv[...]], axis=1)
    side = places[4]
    mine = weight[pl.ds(pl.multiple_of(side * inner, 16), inner), :]
    theirs = weight[pl.ds(pl.multiple_of((1 - side) * inner, 16), inner), :]
    send_part[...] = dot(both, theirs, NT).astype(BF16)
    keep_part[...] = dot(both, mine, NT).astype(BF16)
    total[...] += dot(memory[...], both, TN)

    @pl.when(pl.program_id(0) == pl.num_programs(0) - 1)
    def _():
        if last:
            put_rows(places, total, keep, send)
        else:
            total_out[...] = total[...]


def memory_back(places, memory, dk, dv, pieces, columns, image, before, spare):
    count, inner = dk.shape
    width = memory.shape[1]
    steps = count // MEMORY_TILE
    last = before is not None
    ranks = shape_of((2, width // 4, spare + 2 * inner), BF16)
    rank_spec = pl.BlockSpec((2, width // 4, 2 * inner), lambda t: (0, 0, 0))

    def kernel(*refs):
        memory_back_kernel(columns, last, *refs)

    return pl.pallas_call(
        kernel,
        grid=(steps,),
        in_specs=[
            SCALARS,
            pl.BlockSpec((MEMORY_TILE, width), lambda t: (image * steps + t, 0)),
            rows(inner, MEMORY_TILE),
            rows(inner, MEMORY_TILE),
        ]
        + [ANY] * 4
        + ([whole((width, 2 * inner))] if last else []),
        out_specs=[rows(inner, MEMORY_TILE), rows(inner, MEMORY_TILE)]
        + ([rank_spec, rank_spec] if last else [whole((width, 2 * inner))]),
        out_shape=[shape_of((count, inner), BF16)] * 2
        + ([ranks, ranks] if last else [shape_of((width, 2 * inner), F32)]),
        scratch_shapes=[
            pltpu.VMEM((width, 2 * inner), BF16),
            pltpu.VMEM((width, 2 * inner), F32),
            pltpu.SemaphoreType.DMA((4,)),
        ],
        compiler_params=params(),
        cost_estimate=cost(8 * count * width * inner, 8 * count * width),
    )(places, memory, dk, dv, *pieces, *([before] if last else []))


def weight_grads_kernel(
    plan, spans, places, left_refs, right_refs, keep, send, turned
):
    height = turned.shape[0] // 4
    step = pl.program_id(0)
    for at, (left, group) in enumerate(plan):

        @pl.when(step == at)
        def _():
            if at == 0 or plan[at - 1][0] != left:
                turned[...] = left_refs[left][...].T
            right = join([right_refs[g] for g in group])
            for i, ref in enumerate((keep, keep, send, send)):
                start = pl.multiple_of(places[i] * height, 16)
                ref[i % 2, 0:height, spans[at]] = dot(
                    turned[pl.ds(start, height), :], right, NN
                ).astype(BF16)


def join(refs):
    values = [ref[...] for ref in refs]
    return values[0] if len(values) == 1 else jnp.concatenate(values, axis=1)


def flatten(groups):
    flat, sizes = [], []
    for group in groups:
        group = group if isinstance(group, (list, tuple)) else [group]
        flat += list(group)
        sizes.append(len(group))
    return flat, sizes


def weight_grads(places, lefts, rights, plan, into=(), first=0):
    count, width = lefts[0].shape
    flat, sizes = flatten(rights)
    groups, at = [], 0
    for size in sizes:
        groups.append(list(range(at, at + size)))
        at += size
    plan = [(left, [f for g in group for f in groups[g]]) for left, group in plan]
    columns = [sum(flat[f].shape[1] for f in group) for _, group in plan]
    step_columns = columns[0]
    share = width // 4
    total = sum(columns) + first * step_columns
    even = len(set(columns)) == 1
    spans = [
        slice(0, step_columns) if even else slice(sum(columns[:at]), sum(columns[: at + 1]))
        for at in range(len(plan))
    ]
    extra = list(into)
    def kernel(places, *refs):
        lefts_end = len(lefts)
        rights_end = lefts_end + len(flat)
        weight_grads_kernel(
            plan,
            spans,
            places,
            refs[:lefts_end],
            refs[lefts_end:rights_end],
            *refs[rights_end + len(extra) :],
        )

    start = 1 + len(lefts) + len(flat)
    return pl.pallas_call(
        kernel,
        grid=(len(plan),),
        in_specs=[SCALARS]
        + [whole(array.shape) for array in list(lefts) + flat]
        + [ANY] * len(extra),
        out_specs=[
            pl.BlockSpec((2, share, step_columns), lambda t: (0, 0, t + first))
            if even
            else whole((2, share, total))
        ]
        * 2,
        out_shape=[shape_of((2, share, total), BF16)] * 2,
        input_output_aliases={start: 0, start + 1: 1} if extra else {},
        scratch_shapes=[pltpu.VMEM((width, count), BF16)],
        compiler_params=params(),
        cost_estimate=cost(
            2 * count * width * sum(columns), 4 * count * width * len(plan)
        ),
    )(places, *lefts, *flat, *extra)


def middle_kernel(plan, parts, places, x, gain, *refs):
    mine, theirs, refs = refs[:parts], refs[parts : 2 * parts], refs[2 * parts :]
    mid, h1, n2, cq, out_mine, out_theirs, query, sems = refs

    @pl.when(pl.program_id(0) == 0)
    def _():
        side = places[4]
        copies = (
            fetch_half(mid, side, plan[0], out_mine, sems.at[0]),
            fetch_half(mid, 1 - side, plan[0], out_theirs, sems.at[1]),
            fetch_half(mid, side, plan[1], query, sems.at[2]),
        )
        start_all(copies)
        wait_all(copies)

    values = (
        x[...].astype(F32)
        + dot(join(mine), out_mine[...], NT)
        + dot(join(theirs), out_theirs[...], NT)
    )
    h1[...] = values
    normed = (values * inverse_rms(values) * gain[...]).astype(BF16)
    n2[...] = normed
    cq[...] = dot(normed, query[...], NN).astype(BF16)


def middle_step(places, x, mine, theirs, gain, mid, plan):
    count, width = x.shape
    half = sum(part.shape[1] for part in mine)

    def kernel(*refs):
        middle_kernel(plan, len(mine), *refs)

    return pl.pallas_call(
        kernel,
        grid=(count // TILE,),
        in_specs=[SCALARS, rows(width), whole((1, width))]
        + [rows(PAIR)] * (2 * len(mine))
        + [ANY],
        out_specs=[rows(width), rows(width), rows(half)],
        out_shape=[
            shape_of((count, width), F32),
            shape_of((count, width), BF16),
            shape_of((count, half), BF16),
        ],
        scratch_shapes=[pltpu.VMEM((width, half), BF16)] * 3 + [pltpu.SemaphoreType.DMA((3,))],
        compiler_params=params(),
        cost_estimate=cost(6 * count * width * half, 12 * count * width),
    )(places, x, gain, *mine, *theirs, mid)


def head_sums(left, right):
    product = left.astype(F32) * right.astype(F32)
    width = product.shape[1]
    high = product.astype(BF16)
    low = (product - high.astype(F32)).astype(BF16)
    height = 8 * (width // PAIR)
    line = lax.broadcasted_iota(jnp.int32, (height, width), 0)
    head = lax.broadcasted_iota(jnp.int32, (height, width), 1) // HEAD_DIM
    choose = (
        ((line // 8) * 2 + line % 8 == head) & (line % 8 < 2)
    ).astype(F32).astype(BF16)
    return dot(choose, high, NT) + dot(choose, low, NT)


CHUNK = 512


def units_kernel(columns, parts, places, h1, gain, gy, *refs):
    mine, theirs, refs = refs[:parts], refs[parts : 2 * parts], refs[2 * parts :]
    mid, late, refs = refs[0], refs[1], refs[2:]
    (
        output,
        n3,
        hidden,
        grad_gate,
        grad_up,
        dh2,
        e2,
        dc,
        deltas,
        gain_grad,
        out_mine,
        out_theirs,
        units_mine,
        units_theirs,
        sems,
    ) = refs
    step = pl.program_id(0)

    @pl.when(step == 0)
    def _():
        side = places[4]
        every = slice(0, units_mine.shape[1])
        copies = (
            fetch_half(mid, side, columns, out_mine, sems.at[0]),
            fetch_half(mid, 1 - side, columns, out_theirs, sems.at[1]),
            fetch_half(late, side, every, units_mine, sems.at[2]),
            fetch_half(late, 1 - side, every, units_theirs, sems.at[3]),
        )
        start_all(copies)
        gain_grad[...] = jnp.zeros_like(gain_grad)
        wait_all(copies)

    crossed_mine = join(mine)
    values = (
        h1[...] + dot(crossed_mine, out_mine[...], NT) + dot(join(theirs), out_theirs[...], NT)
    )
    normed = (values * inverse_rms(values) * gain[...]).astype(BF16)
    n3[...] = normed
    upstream = gy[...]
    mixed = jnp.zeros_like(values)
    back = jnp.zeros_like(values)
    unit = units_mine.shape[1] // 3
    for own in (True, False):
        weight = units_mine if own else units_theirs
        for start in range(0, unit, CHUNK):
            gate_weight = weight[:, start : start + CHUNK]
            up_weight = weight[:, unit + start : unit + start + CHUNK]
            down_weight = weight[:, 2 * unit + start : 2 * unit + start + CHUNK]
            gate = dot(normed, gate_weight, NN)
            up = dot(normed, up_weight, NN)
            pushed = dot(upstream, down_weight, NN)
            square = gate * gate
            bend = jnp.tanh(ROOT_TWO_OVER_PI * gate * (1.0 + CUBIC * square))
            lift = 0.5 * (1.0 + bend)
            gelu = gate * lift
            slope = lift + (0.5 * ROOT_TWO_OVER_PI) * gate * (1.0 - bend * bend) * (
                1.0 + (3.0 * CUBIC) * square
            )
            units = (gelu * up).astype(BF16)
            push_gate = (pushed * up * slope).astype(BF16)
            push_up = (pushed * gelu).astype(BF16)
            mixed = mixed + dot(units, down_weight, NT)
            back = back + dot(push_gate, gate_weight, NT) + dot(push_up, up_weight, NT)
            if own:
                hidden[:, start : start + CHUNK] = units
                grad_gate[:, start : start + CHUNK] = push_gate
                grad_up[:, start : start + CHUNK] = push_up
    output[...] = (values + mixed).astype(BF16)
    grad, gain_part = norm_back(values, gain[...], back)
    result = upstream.astype(F32) + grad
    dh2[...] = result
    low = result.astype(BF16)
    e2[...] = low
    crossed = dot(low, out_mine[...], NN).astype(BF16)
    dc[...] = crossed
    deltas[...] = head_sums(crossed, crossed_mine)
    gain_grad[0:1, :] += gain_part


def units_step(places, h1, mine, theirs, gain, gy, mid, columns, late):
    count, width = h1.shape
    half = sum(part.shape[1] for part in mine)
    unit = late.shape[2] // 3
    lines = 8 * (half // PAIR)

    def kernel(*refs):
        units_kernel(columns, len(mine), *refs)

    return pl.pallas_call(
        kernel,
        grid=(count // TILE,),
        in_specs=[
            SCALARS,
            rows(width),
            whole((1, width)),
            rows(width),
        ]
        + [rows(PAIR)] * (2 * len(mine))
        + [ANY] * 2,
        out_specs=[
            rows(width),
            rows(width),
            rows(unit),
            rows(unit),
            rows(unit),
            rows(width),
            rows(width),
            rows(half),
            pl.BlockSpec((lines, TILE), lambda t: (0, t)),
            whole((8, width)),
        ],
        out_shape=[
            shape_of((count, width), BF16),
            shape_of((count, width), BF16),
            shape_of((count, unit), BF16),
            shape_of((count, unit), BF16),
            shape_of((count, unit), BF16),
            shape_of((count, width), F32),
            shape_of((count, width), BF16),
            shape_of((count, half), BF16),
            shape_of((lines, count), F32),
            shape_of((8, width), F32),
        ],
        scratch_shapes=[pltpu.VMEM((width, half), BF16)] * 2
        + [pltpu.VMEM((width, 3 * unit), BF16)] * 2
        + [pltpu.SemaphoreType.DMA((4,))],
        compiler_params=params(),
        cost_estimate=cost(30 * count * width * unit, 30 * count * width),
    )(places, h1, gain, gy, *mine, *theirs, mid, late)


def turn_kernel(plan, parts, places, dh2, h1, mine, theirs, gain, *refs):
    attended, refs = refs[:parts], refs[parts:]
    mid, dh1, e1, da, deltas, gain_grad, query_mine, query_theirs, out_mine, sems = refs

    @pl.when(pl.program_id(0) == 0)
    def _():
        side = places[4]
        copies = (
            fetch_half(mid, side, plan[0], out_mine, sems.at[0]),
            fetch_half(mid, side, plan[1], query_mine, sems.at[1]),
            fetch_half(mid, 1 - side, plan[1], query_theirs, sems.at[2]),
        )
        start_all(copies)
        gain_grad[...] = jnp.zeros_like(gain_grad)
        wait_all(copies)

    back = dot(mine[...], query_mine[...], NT) + dot(theirs[...], query_theirs[...], NT)
    grad, gain_part = norm_back(h1[...], gain[...], back)
    result = dh2[...] + grad
    dh1[...] = result
    low = result.astype(BF16)
    e1[...] = low
    pushed = dot(low, out_mine[...], NN).astype(BF16)
    da[...] = pushed
    deltas[...] = head_sums(pushed, join(attended))
    gain_grad[0:1, :] += gain_part


def turn_step(places, dh2, h1, mine, theirs, gain, attended, mid, plan):
    count, width = h1.shape
    half = mine.shape[1]
    lines = 8 * (half // PAIR)

    def kernel(*refs):
        turn_kernel(plan, len(attended), *refs)

    return pl.pallas_call(
        kernel,
        grid=(count // TILE,),
        in_specs=[
            SCALARS,
            rows(width),
            rows(width),
            rows(half),
            rows(half),
            whole((1, width)),
        ]
        + [rows(PAIR)] * len(attended)
        + [ANY],
        out_specs=[
            rows(width),
            rows(width),
            rows(half),
            pl.BlockSpec((lines, TILE), lambda t: (0, t)),
            whole((8, width)),
        ],
        out_shape=[
            shape_of((count, width), F32),
            shape_of((count, width), BF16),
            shape_of((count, half), BF16),
            shape_of((lines, count), F32),
            shape_of((8, width), F32),
        ],
        scratch_shapes=[pltpu.VMEM((width, half), BF16)] * 3 + [pltpu.SemaphoreType.DMA((3,))],
        compiler_params=params(),
        cost_estimate=cost(6 * count * width * half, 16 * count * width),
    )(places, dh2, h1, mine, theirs, gain, *attended, mid)


def partial_kernel(parts, places, x, n1, second, third, *refs):
    part_refs, refs = refs[:parts], refs[parts:]
    w0, w1, w2, w3, out, keep, send, weight, total, gain_grad, sems = refs
    step = pl.program_id(0)

    @pl.when(step == 0)
    def _():
        copies = fetch((w0, w1, w2, w3), places, slice(0, weight.shape[1]), weight, sems)
        start_all(copies)
        gain_grad[...] = jnp.zeros_like(gain_grad)
        total[...] = jnp.zeros_like(total)
        wait_all(copies)

    back = dot(join(part_refs), weight[...], NT)
    out[...] = back.astype(BF16)
    values = x[...].astype(F32)
    gain_grad[0:1, :] += jnp.sum(back * values * inverse_rms(values), axis=0, keepdims=True)
    last = join([part_refs[i * (parts // 3) + parts // 3 - 1] for i in range(3)])
    total[...] += dot(n1[...], last, TN)

    @pl.when(step == pl.num_programs(0) - 1)
    def _():
        put_rows(places, total, keep, send)
        height = total.shape[0] // 4
        lines = jnp.concatenate(
            [
                gain_grad[0:1, :],
                second[0:1, :],
                third[0:1, :],
                jnp.zeros((13, gain_grad.shape[1]), F32),
            ],
            axis=0,
        )
        shares = [lines[:, w * height : (w + 1) * height] for w in range(4)]
        fill = jnp.zeros((16, total.shape[1] - height), F32)
        for i, ref in enumerate((keep, keep, send, send)):
            share = shares[0]
            for w in range(1, 4):
                share = jnp.where(places[i] == w, shares[w], share)
            ref[i % 2, height : height + 16, :] = jnp.concatenate([share, fill], axis=1).astype(
                BF16
            )


def partial_step(places, parts, x, n1, second, third, pieces):
    count, width = x.shape
    inner = sum(part.shape[1] for part in parts)
    ranks = (2, width // 4 + 16, 3 * PAIR)

    def kernel(*refs):
        partial_kernel(len(parts), *refs)

    return pl.pallas_call(
        kernel,
        grid=(count // TILE,),
        in_specs=[SCALARS, rows(width), rows(width), whole((8, width)), whole((8, width))]
        + [rows(PAIR)] * len(parts)
        + [ANY] * 4,
        out_specs=[rows(width), whole(ranks), whole(ranks)],
        out_shape=[
            shape_of((count, width), BF16),
            shape_of(ranks, BF16),
            shape_of(ranks, BF16),
        ],
        scratch_shapes=[
            pltpu.VMEM((width, inner), BF16),
            pltpu.VMEM((width, 3 * PAIR), F32),
            pltpu.VMEM((8, width), F32),
            pltpu.SemaphoreType.DMA((4,)),
        ],
        compiler_params=params(),
        cost_estimate=cost(2 * count * width * (inner + 3 * PAIR), 8 * count * width),
    )(places, x, n1, second, third, *parts, *pieces)


def first_kernel(dh1, x, mine, theirs, gain, out):
    back = mine[...].astype(F32) + theirs[...].astype(F32)
    grad, _ = norm_back(x[...].astype(F32), gain[...], back)
    out[...] = (dh1[...] + grad).astype(BF16)


def first_step(dh1, x, mine, theirs, gain):
    count, width = x.shape
    return pl.pallas_call(
        first_kernel,
        grid=(count // TILE,),
        in_specs=[rows(width)] * 4 + [whole((1, width))],
        out_specs=rows(width),
        out_shape=shape_of((count, width), BF16),
        compiler_params=params(),
        cost_estimate=cost(20 * count * width, 12 * count * width),
    )(dh1, x, mine, theirs, gain)


def swap(values, axis, distance):
    size = lax.axis_size(axis)
    return lax.ppermute(values, axis, [(i, i ^ distance) for i in range(size)])


def after(values, *others):
    return lax.optimization_barrier((values,) + others)[0]


def gather_all(values):
    return lax.all_gather(values, ("narrow", "wide"), axis=0, tiled=True).reshape(
        lax.axis_size("narrow"), -1, values.shape[1]
    )


def sum_wide(values):
    return lax.psum_scatter(values, "wide", scatter_dimension=0, tiled=True)


def add(left, right):
    return (left.astype(F32) + right.astype(F32)).astype(BF16)


def add_pair(keep, got):
    return add(keep[0], got[0]), add(keep[1], got[1])


def line_inner():
    place = lax.axis_index("dp")
    return (place == 1) | (place == 2)


def line_first(values):
    if lax.axis_size("dp") != 4:
        return lax.psum(values, "dp")
    got = lax.ppermute(values, "dp", [(0, 1), (3, 2)])
    return jnp.where(line_inner(), add(values, got), values)


def line_second(values):
    if lax.axis_size("dp") != 4:
        return values
    return add(values, lax.ppermute(values, "dp", [(1, 2), (2, 1)]))


def line_third(values):
    if lax.axis_size("dp") != 4:
        return values
    got = lax.ppermute(values, "dp", [(1, 0), (2, 3)])
    return jnp.where(line_inner(), values, got)


def local(
    tokens,
    memory,
    cotangent,
    norm1_gain,
    norm2_gain,
    norm3_gain,
    q_weight,
    k_weight,
    v_weight,
    o_weight,
    cross_q,
    cross_k,
    cross_v,
    cross_o,
    gate_weight,
    up_weight,
    down_weight,
    segment_ids,
    block_ids,
    image_table,
):
    width = tokens.shape[1]
    share = q_weight.shape[0]
    inner = q_weight.shape[1]
    unit = gate_weight.shape[1]
    images = memory.shape[0]
    flat_memory = memory.reshape(-1, width)
    place = lax.axis_index("wide")
    side = lax.axis_index("narrow")
    places = jnp.stack([place, place ^ 2, place ^ 1, place ^ 3, side]).astype(jnp.int32)

    gains = jnp.stack([norm1_gain, norm2_gain, norm3_gain])
    gains = jnp.pad(gains, ((0, 13), (0, 3 * inner - share)))
    early = jnp.concatenate(
        [jnp.concatenate([q_weight, k_weight, v_weight], axis=1), gains], axis=0
    )
    early_x = swap(early, "wide", 2)
    early_pieces = (early, early_x, swap(early, "wide", 1), swap(early_x, "wide", 1))
    lines = jnp.stack([piece[share : share + 3, :share] for piece in early_pieces])
    lines = lines.astype(F32)
    order = [
        jnp.sum(jnp.where((places[:4] == w)[:, None, None], lines, 0.0), axis=0)
        for w in range(4)
    ]
    all_gains = jnp.concatenate(order, axis=1)[:, None, :]

    kv = jnp.concatenate([cross_k, cross_v], axis=1)
    kv_x = swap(after(kv, early_x), "wide", 2)
    kv_pieces = (kv, kv_x, swap(kv, "wide", 1), swap(kv_x, "wide", 1))
    memory_columns = slice(0, 2 * inner)
    mid = jnp.concatenate([o_weight, cross_o, cross_q], axis=1)
    out_columns = slice(0, inner)
    cross_out_columns = slice(inner, 2 * inner)
    query_columns = slice(2 * inner, 3 * inner)
    late = jnp.concatenate([gate_weight, up_weight, down_weight], axis=1)

    x, gy, row_ids, col_ids, pos, scalars = order_rows(
        segment_ids, block_ids, image_table, tokens, cotangent
    )
    mid = gather_all(after(mid, early_x, x))
    late = gather_all(after(late, early_x, x))
    n1, qkv = norm_project(places, x, all_gains[0], early_pieces)
    pairs = inner // PAIR
    self_parts = [self_forward(0, qkv, row_ids, col_ids)]
    for pair in range(1, pairs):
        self_parts.append(
            self_forward(pair, after(qkv, kv_x, self_parts[-1][0]), row_ids, col_ids)
        )
    attended_theirs = [swap(part[0], "narrow", 1) for part in self_parts]
    attended = [part[0] for part in self_parts]
    keys_values = project_memory(
        places,
        after(flat_memory, self_parts[-1][0], attended_theirs[0]),
        kv_pieces,
        memory_columns,
    )
    h1, n2, cq = middle_step(
        places,
        x,
        attended,
        attended_theirs,
        all_gains[1],
        mid,
        (out_columns, query_columns),
    )
    cross_parts = [cross_forward(0, scalars, cq, keys_values, images)]
    crossed_theirs = []
    for pair in range(1, pairs):
        previous = [cross_parts[-1][0]] + crossed_theirs
        crossed_theirs.append(swap(cross_parts[-1][0], "narrow", 1))
        cross_parts.append(
            cross_forward(pair, scalars, after(cq, *previous), keys_values, images)
        )
    crossed = [part[0] for part in cross_parts]
    crossed_theirs.append(swap(crossed[-1], "narrow", 1))
    cross_logs = jnp.concatenate([part[1] for part in cross_parts], axis=0)
    (
        output,
        n3,
        hidden,
        grad_gate,
        grad_up,
        dh2,
        e2,
        dc,
        cross_deltas,
        third_gain,
    ) = units_step(
        places,
        h1,
        crossed,
        crossed_theirs,
        all_gains[2],
        gy,
        mid,
        cross_out_columns,
        late,
    )

    unit_keep, unit_send = weight_grads(
        places, (n3, gy), (grad_gate, grad_up, hidden), ((0, (0,)), (0, (1,)), (1, (2,)))
    )
    unit_stay, unit_leave = add_pair(unit_keep, swap(unit_send, "wide", 1))
    dcq, dck, dcv = cross_backward(
        0,
        scalars,
        cq,
        keys_values,
        after(dc, unit_leave),
        cross_logs,
        cross_deltas,
        images,
        None,
    )
    unit_part = add(unit_stay, swap(unit_leave, "wide", 2))
    keep0, send0, total = memory_back(
        places,
        flat_memory,
        after(dck, unit_part),
        dcv,
        kv_pieces,
        memory_columns,
        0,
        None,
        0,
    )
    unit_sum = lax.psum(unit_part, "dp")
    dcq, dck, dcv = cross_backward(
        1,
        scalars,
        cq,
        keys_values,
        after(dc, send0),
        cross_logs,
        cross_deltas,
        images,
        dcq,
    )
    dcq_theirs = swap(dcq, "narrow", 1)
    memory0 = add(keep0, swap(send0, "narrow", 1))
    keep1, send1, cross_keep, cross_send = memory_back(
        places,
        flat_memory,
        after(dck, memory0),
        dcv,
        kv_pieces,
        memory_columns,
        1,
        total,
        2 * inner,
    )
    cross_keep, cross_send = weight_grads(
        places,
        (after(n2, send1), e2),
        (dcq, crossed),
        ((0, (0,)), (1, (1,))),
        into=(cross_keep, cross_send),
        first=2,
    )
    dh1, e1, da, self_deltas, second_gain = turn_step(
        places,
        dh2,
        h1,
        after(dcq, cross_send, unit_sum),
        dcq_theirs,
        all_gains[1],
        attended,
        mid,
        (out_columns, query_columns),
    )
    memory1 = add(keep1, swap(after(send1, dcq_theirs), "narrow", 1))
    cross_stay, cross_leave = add_pair(cross_keep, swap(cross_send, "wide", 1))
    da = after(da, cross_leave)
    back = []
    for pair in range(pairs):
        ready = after(da, *[part[0] for part in back])
        if pair == pairs - 1:
            early_back = list(back)
            self_keep, self_send = weight_grads(
                places,
                (after(n1, back[-1][0]), e1),
                [[part[i] for part in early_back] for i in range(3)] + [attended],
                ((0, (0, 1, 2)), (1, (3,))),
            )
            cross_part = add(cross_stay, swap(cross_leave, "wide", 2))
            ready = after(ready, cross_part, self_send)
            cross_part = line_first(cross_part)
        back.append(
            self_backward(
                pair, qkv, ready, self_parts[pair][1], self_deltas, row_ids, col_ids
            )
        )
    dq, dk, dv = [[part[i] for part in back] for i in range(3)]
    self_stay, self_leave = add_pair(self_keep, swap(self_send, "wide", 1))
    self_part = add(self_stay, swap(self_leave, "wide", 2))
    dn1, last_keep, last_send = partial_step(
        places,
        dq + dk + dv,
        after(x, memory1, self_leave),
        n1,
        second_gain,
        third_gain,
        early_pieces,
    )
    dn1_theirs = swap(dn1, "narrow", 1)
    last_stay, last_leave = add_pair(last_keep, swap(last_send, "wide", 1))
    last_part = add(last_stay, swap(last_leave, "wide", 2))
    output = restore_rows(pos, after(output, last_send, self_part))
    tokens_grad = first_step(dh1, x, dn1, dn1_theirs, all_gains[0])
    tokens_grad = restore_rows(pos, tokens_grad)
    memory_grad = jnp.stack([memory0, memory1])
    cross_sum = line_third(line_second(cross_part))
    self_sum = line_third(line_second(line_first(self_part)))
    last_sum = line_third(line_second(line_first(last_part)))
    gain_sums = last_sum[share:, :share].astype(F32)
    first_gain = gain_sums[0] + swap(gain_sums, "narrow", 1)[0]

    def grads(array, size, count):
        return [array[:share, i * size : (i + 1) * size].astype(F32) for i in range(count)]

    gate_grad, up_grad, down_grad = grads(unit_sum, unit, 3)
    cross_k_grad, cross_v_grad, cross_q_grad, cross_o_grad = grads(cross_sum, inner, 4)
    part = inner - PAIR
    q_grad, k_grad, v_grad = [
        jnp.concatenate([most, rest], axis=1)
        for most, rest in zip(grads(self_sum, part, 3), grads(last_sum, PAIR, 3))
    ]
    o_grad = self_sum[:, 3 * part :].astype(F32)
    return (
        output,
        tokens_grad,
        memory_grad,
        first_gain,
        gain_sums[1],
        gain_sums[2],
        q_grad,
        k_grad,
        v_grad,
        o_grad,
        cross_q_grad,
        cross_k_grad,
        cross_v_grad,
        cross_o_grad,
        gate_grad,
        up_grad,
        down_grad,
    )


def solution(mesh):
    both = ("dp", "wide")
    weight = P("wide", "narrow")
    in_specs = (
        (P(both, None), P(both, None, None), P(both, None))
        + (P("wide"),) * 3
        + (weight,) * 11
        + (P(both, None),) * 3
    )
    out_specs = (
        (P(both, None), P(both, None), P(both, None, "narrow"))
        + (P("wide"),) * 3
        + (weight,) * 11
    )
    return jax.shard_map(local, mesh=mesh, in_specs=in_specs, out_specs=out_specs, check_vma=False)
```

```python
import functools
import math

import jax
import jax.numpy as jnp
from jax import lax
from jax.experimental import pallas as pl
from jax.experimental.pallas import tpu as pltpu
from jax.sharding import PartitionSpec as P

F32 = jnp.float32
BF16 = jnp.bfloat16
EPSILON = 1e-06
ROOT_TWO_OVER_PI = 0.7978845608028654
CUBIC = 0.044715
HEAD_DIM = 64
PAIR = 2 * HEAD_DIM
SCALE = HEAD_DIM ** (-0.5)
EXP2_SCALE = SCALE * math.log2(math.e)
HIDE = 1e30
TILE = 256
WEIGH = 4.0

NN = (((1,), (0,)), ((), ()))
NT = (((1,), (1,)), ((), ()))
TN = (((0,), (0,)), ((), ()))


def dot(left, right, dims):
    return lax.dot_general(left, right, dims, preferred_element_type=F32)


def params(mebibytes=24):
    return pltpu.CompilerParams(vmem_limit_bytes=mebibytes * 1024 * 1024)


def cost(flops, nbytes):
    return pl.CostEstimate(
        flops=int(flops * WEIGH), bytes_accessed=int(nbytes * WEIGH), transcendentals=0
    )


def pin(*arrays):
    return [pltpu.with_memory_space_constraint(array, pltpu.HBM) for array in arrays]


def shape_of(shape, dtype):
    return jax.ShapeDtypeStruct(shape, dtype)


def whole(shape):
    zeros = (0,) * len(shape)
    return pl.BlockSpec(shape, lambda *_: zeros)


def rows(width, height=TILE):
    return pl.BlockSpec((height, width), lambda t, *_: (t, 0))


def inverse_rms(values):
    return lax.rsqrt(jnp.mean(values * values, axis=1, keepdims=True) + EPSILON)


def norm_back(values, gain, upstream):
    factor = inverse_rms(values)
    scaled = upstream * gain
    mean = jnp.mean(values * scaled, axis=1, keepdims=True)
    grad = factor * scaled - values * (factor * factor * factor * mean)
    return grad, jnp.sum(upstream * values * factor, axis=0, keepdims=True)


def in_half(shape, half):
    return (lax.broadcasted_iota(jnp.int32, shape, 1) // HEAD_DIM) == half


def only_half(values, half):
    return jnp.where(in_half(values.shape, half), values, jnp.zeros_like(values))


def order_kernel(seg, blk, table, x, gy, xp, gyp, row_ids, col_ids, pos_out, scalars, pos):
    step = pl.program_id(0)
    count = seg.shape[1]

    @pl.when(step == 0)
    def _():
        segments = seg[...]
        image = jnp.zeros_like(segments)
        for s in range(table.shape[1]):
            image = jnp.where(segments == s, table[0, s], image)
        first = (image == 0).astype(F32)
        before = lax.broadcasted_iota(jnp.int32, (count, count), 0) < lax.broadcasted_iota(
            jnp.int32, (count, count), 1
        )
        rank = dot(
            jnp.broadcast_to(first, (8, count)).astype(BF16),
            before.astype(F32).astype(BF16),
            NN,
        )[0:1]
        total = jnp.sum(first)
        index = lax.broadcasted_iota(jnp.int32, (1, count), 1).astype(F32)
        place = jnp.where(image == 0, rank, total + index - rank)
        pos[...] = place.astype(jnp.int32)
        pos_out[...] = jnp.broadcast_to(pos[...], (8, count))
        n0 = total.astype(jnp.int32)
        tiles = count // TILE
        visits0 = jnp.maximum(1, (n0 + TILE - 1) // TILE)
        start1 = jnp.minimum(tiles - 1, n0 // TILE)
        visits = visits0 + tiles - start1
        for v in range(tiles + 1):
            real = jnp.minimum(v, visits - 1)
            in_first = real < visits0
            scalars[v] = jnp.where(in_first, real, real - visits0 + start1)
            scalars[8 + v] = jnp.where(in_first, 0, 1)
        scalars[16] = visits
        scalars[17] = n0
        scalars[18] = visits0
        scalars[19] = start1
        scalars[20] = tiles - start1

    onehot = (
        lax.broadcasted_iota(jnp.int32, (TILE, count), 0) + step * TILE == pos[...]
    ).astype(F32).astype(BF16)
    xp[...] = dot(onehot, x[...], NN).astype(BF16)
    gyp[...] = dot(onehot, gy[...], NN).astype(BF16)
    ids = jnp.concatenate(
        [
            seg[...].astype(F32),
            blk[...].astype(F32),
            jnp.zeros((126, count), F32),
        ],
        axis=0,
    ).astype(BF16)
    row_ids[...] = dot(ids[0:8], onehot, NT)
    col_ids[...] = dot(onehot, ids, NT)


def order_rows(seg, blk, table, x, gy):
    count, width = x.shape
    return pl.pallas_call(
        order_kernel,
        grid=(count // TILE,),
        in_specs=[
            whole((1, count)),
            whole((1, count)),
            pl.BlockSpec(memory_space=pltpu.SMEM),
            whole((count, width)),
            whole((count, width)),
        ],
        out_specs=[
            rows(width),
            rows(width),
            pl.BlockSpec((8, TILE), lambda t: (0, t)),
            rows(128),
            whole((8, count)),
            pl.BlockSpec(memory_space=pltpu.SMEM),
        ],
        out_shape=[
            pltpu.HBM((count, width), BF16),
            pltpu.HBM((count, width), BF16),
            shape_of((8, count), F32),
            shape_of((count, 128), F32),
            shape_of((8, count), jnp.int32),
            shape_of((32,), jnp.int32),
        ],
        scratch_shapes=[pltpu.VMEM((1, count), jnp.int32)],
        compiler_params=params(),
        cost_estimate=cost(4 * count * count * width, 8 * count * width),
    )(seg, blk, table, *pin(x, gy))


def restore_kernel(pos, values, out):
    count = values.shape[0]
    onehot = (
        lax.broadcasted_iota(jnp.int32, (count, TILE), 0) == pos[0:1, :]
    ).astype(F32).astype(BF16)
    out[...] = dot(onehot, values[...], TN).astype(BF16)


def restore_rows(pos, values):
    count, width = values.shape
    return pl.pallas_call(
        restore_kernel,
        grid=(count // TILE,),
        in_specs=[pl.BlockSpec((8, TILE), lambda t: (0, t)), whole((count, width))],
        out_specs=rows(width),
        out_shape=shape_of((count, width), BF16),
        compiler_params=params(),
        cost_estimate=cost(2 * count * count * width, 4 * count * width),
    )(pos, *pin(values))


def fetch(pieces, places, columns, dest, sems, base=0):
    height = dest.shape[0] // 4
    copies = []
    for i, piece in enumerate(pieces):
        start = pl.multiple_of(places[i] * height, 16)
        copies.append(
            pltpu.make_async_copy(
                piece.at[pl.ds(0, height), columns],
                dest.at[pl.ds(start, height), :],
                sems.at[base + i],
            )
        )
    return copies


def fetch_half(gathered, half, columns, dest, sem):
    return pltpu.make_async_copy(gathered.at[half, :, columns], dest, sem)


def start_all(copies):
    for copy in copies:
        copy.start()


def wait_all(copies):
    for copy in copies:
        copy.wait()


ANY = pl.BlockSpec(memory_space=pl.ANY)
SCALARS = pl.BlockSpec(memory_space=pltpu.SMEM)


def project_kernel(places, x, gain, w0, w1, w2, w3, normed, out, weight, sems):
    @pl.when(pl.program_id(0) == 0)
    def _():
        copies = fetch((w0, w1, w2, w3), places, slice(0, weight.shape[1]), weight, sems)
        start_all(copies)
        wait_all(copies)

    values = x[...].astype(F32)
    n1 = (values * inverse_rms(values) * gain[...]).astype(BF16)
    normed[...] = n1
    out[...] = dot(n1, weight[...], NN).astype(BF16)


def norm_project(places, x, gain, pieces):
    count, width = x.shape
    outs = pieces[0].shape[1]
    return pl.pallas_call(
        project_kernel,
        grid=(count // TILE,),
        in_specs=[SCALARS, rows(width), whole((1, width))] + [ANY] * 4,
        out_specs=[rows(width), rows(outs)],
        out_shape=[pltpu.HBM((count, width), BF16), shape_of((count, outs), BF16)],
        scratch_shapes=[pltpu.VMEM((width, outs), BF16), pltpu.SemaphoreType.DMA((4,))],
        compiler_params=params(),
        cost_estimate=cost(2 * count * width * outs, 4 * count * width + 2 * count * outs),
    )(places, *pin(x), gain, *pieces)


MEMORY_TILE = 512


def memory_kernel(places, columns, memory, w0, w1, w2, w3, out, weight, sems):
    @pl.when(pl.program_id(0) == 0)
    def _():
        copies = fetch((w0, w1, w2, w3), places, columns, weight, sems)
        start_all(copies)
        wait_all(copies)

    out[...] = dot(memory[...], weight[...], NN).astype(BF16)


def project_memory(places, memory, pieces, columns):
    count, width = memory.shape
    outs = columns.stop - columns.start

    def kernel(places, *refs):
        memory_kernel(places, columns, *refs)

    return pl.pallas_call(
        kernel,
        grid=(count // MEMORY_TILE,),
        in_specs=[SCALARS, rows(width, MEMORY_TILE)] + [ANY] * 4,
        out_specs=rows(outs, MEMORY_TILE),
        out_shape=pltpu.HBM((count, outs), BF16),
        scratch_shapes=[pltpu.VMEM((width, outs), BF16), pltpu.SemaphoreType.DMA((4,))],
        compiler_params=params(),
        cost_estimate=cost(2 * count * width * outs, 4 * count * width),
    )(places, *pin(memory), *pieces)


SELF_TILE = 128
SELF_WINDOW = 512
BACK_WINDOW = 640


def store_logs(ref, columns, logs, extra=None):
    spread = jnp.where(in_half((logs[0].shape[0], PAIR), 0), logs[0], logs[1]).T
    for half in range(2):
        line = spread[half * HEAD_DIM : half * HEAD_DIM + 1, :]
        if extra is not None:
            line = jnp.where(extra, line, ref[half : half + 1, columns])
        ref[half : half + 1, columns] = line


def self_forward_kernel(q, k, v, row_ids, col_ids, out, logs):
    count = q.shape[0]
    for tile in range(count // SELF_TILE):
        base = tile * SELF_TILE
        start = min(max(base - 256, 0), count - SELF_WINDOW)
        spot = slice(base, base + SELF_TILE)
        window = slice(start, start + SELF_WINDOW)
        seen = (col_ids[spot, 0:1] == row_ids[0:1, window]) & (
            row_ids[1:2, window] <= col_ids[spot, 1:2]
        )
        bias = jnp.where(seen, 0.0, -HIDE)
        keys = k[window, :]
        values = v[window, :]
        queries = q[spot, :]
        parts, totals = [], []
        for half in range(2):
            scores = dot(only_half(queries, half), keys, NT) * EXP2_SCALE + bias
            highest = jnp.max(scores, axis=1, keepdims=True)
            weights = jnp.exp2(scores - highest)
            total = jnp.sum(weights, axis=1, keepdims=True)
            parts.append(dot(weights.astype(BF16), values, NN) / total)
            totals.append(highest + jnp.log2(total))
        out[spot, :] = jnp.where(in_half(parts[0].shape, 0), parts[0], parts[1]).astype(BF16)
        store_logs(logs, spot, totals)


def self_forward(pair, qkv, row_ids, col_ids):
    count = qkv.shape[0]
    pairs = qkv.shape[1] // (3 * PAIR)

    def part(which):
        return pl.BlockSpec((count, PAIR), lambda p: (0, which * pairs + pair))

    return pl.pallas_call(
        self_forward_kernel,
        grid=(1,),
        in_specs=[part(0), part(1), part(2), whole((8, count)), whole((count, 128))],
        out_specs=[whole((count, PAIR)), whole((8, count))],
        out_shape=[pltpu.HBM((count, PAIR), BF16), pltpu.HBM((8, count), F32)],
        compiler_params=params(),
        cost_estimate=cost(16 * count * SELF_WINDOW * PAIR, 8 * count * PAIR),
    )(qkv, qkv, qkv, row_ids, col_ids)


def self_backward_kernel(q, k, v, grad, logs, deltas, row_ids, col_ids, dq, dk, dv, key_sum, value_sum):
    count = q.shape[0]
    key_sum[...] = jnp.zeros_like(key_sum)
    value_sum[...] = jnp.zeros_like(value_sum)
    for tile in range(count // TILE):
        base = tile * TILE
        start = min(max(base - 256, 0), count - BACK_WINDOW)
        spot = slice(base, base + TILE)
        window = slice(start, start + BACK_WINDOW)
        seen = (col_ids[window, 0:1] == row_ids[0:1, spot]) & (
            col_ids[window, 1:2] <= row_ids[1:2, spot]
        )
        bias = jnp.where(seen, 0.0, -HIDE)
        keys = k[window, :]
        values = v[window, :]
        queries = q[spot, :]
        grads = grad[spot, :]
        parts = []
        for half in range(2):
            one_query = only_half(queries, half)
            one_grad = only_half(grads, half)
            scores = dot(keys, one_query, NT) * EXP2_SCALE + bias
            weights = jnp.exp2(scores - logs[half : half + 1, spot])
            slopes = dot(values, one_grad, NT)
            pushed = (weights * (slopes - deltas[half : half + 1, spot])).astype(BF16)
            value_sum[window, :] += dot(weights.astype(BF16), one_grad, NN)
            key_sum[window, :] += dot(pushed, one_query, NN)
            parts.append(dot(pushed, keys, TN))
        dq[spot, :] = (
            jnp.where(in_half(parts[0].shape, 0), parts[0], parts[1]) * SCALE
        ).astype(BF16)
    dk[...] = (key_sum[...] * SCALE).astype(BF16)
    dv[...] = value_sum[...].astype(BF16)


def self_backward(pair, qkv, grad, logs, deltas, row_ids, col_ids):
    count = qkv.shape[0]
    pairs = qkv.shape[1] // (3 * PAIR)

    def part(which):
        return pl.BlockSpec((count, PAIR), lambda p: (0, which * pairs + pair))

    return pl.pallas_call(
        self_backward_kernel,
        grid=(1,),
        in_specs=[
            part(0),
            part(1),
            part(2),
            part(0),
            whole((8, count)),
            pl.BlockSpec((8, count), lambda p: (pair, 0)),
            whole((8, count)),
            whole((count, 128)),
        ],
        out_specs=[whole((count, PAIR))] * 3,
        out_shape=[pltpu.HBM((count, PAIR), BF16)] * 3,
        scratch_shapes=[pltpu.VMEM((count, PAIR), F32)] * 2,
        compiler_params=params(),
        cost_estimate=cost(40 * count * BACK_WINDOW * PAIR, 16 * count * PAIR),
    )(qkv, qkv, qkv, grad, logs, deltas, row_ids, col_ids)


def cross_forward_kernel(scalars, q, k, v, out, logs):
    step = pl.program_id(0)
    tile = scalars[step]
    image = scalars[8 + step]
    again = (step > 0) & (scalars[jnp.maximum(step - 1, 0)] == tile)

    @pl.when(step < scalars[16])
    def _():
        queries = q[...]
        keys = k[...]
        values = v[...]
        parts, totals = [], []
        for half in range(2):
            scores = dot(only_half(queries, half), keys, NT)
            highest = jnp.max(scores, axis=1, keepdims=True) * EXP2_SCALE
            weights = jnp.exp2(scores * EXP2_SCALE - highest)
            total = jnp.sum(weights, axis=1, keepdims=True)
            parts.append(dot(weights.astype(BF16), values, NN) / total)
            totals.append(highest + jnp.log2(total))
        mixed = jnp.where(in_half(parts[0].shape, 0), parts[0], parts[1]).astype(BF16)
        limit = scalars[17] - tile * TILE
        row_mine = (
            lax.broadcasted_iota(jnp.int32, mixed.shape, 0) >= limit
        ) == (image == 1)
        lane_mine = (
            lax.broadcasted_iota(jnp.int32, (1, TILE), 1) >= limit
        ) == (image == 1)
        keep = jnp.logical_not(again)
        out[...] = jnp.where(row_mine | keep, mixed, out[...])
        store_logs(logs, slice(0, TILE), totals, lane_mine | keep)


def cross_forward(pair, scalars, q, keys_values, images):
    count, inner = q.shape
    pairs = inner // PAIR
    memory_rows = keys_values.shape[0] // images
    tile_spec = pl.BlockSpec((TILE, PAIR), lambda s, sc: (sc[s], 0))

    def part(which):
        return pl.BlockSpec((memory_rows, PAIR), lambda s, sc: (sc[8 + s], which * pairs + pair))

    return pl.pallas_call(
        cross_forward_kernel,
        grid_spec=pltpu.PrefetchScalarGridSpec(
            num_scalar_prefetch=1,
            grid=(count // TILE + 1,),
            in_specs=[
                pl.BlockSpec((TILE, PAIR), lambda s, sc: (sc[s], pair)),
                part(0),
                part(1),
            ],
            out_specs=[tile_spec, pl.BlockSpec((8, TILE), lambda s, sc: (0, sc[s]))],
        ),
        out_shape=[pltpu.HBM((count, PAIR), BF16), pltpu.HBM((8, count), F32)],
        compiler_params=params(),
        cost_estimate=cost(20 * count * memory_rows * PAIR, 8 * memory_rows * PAIR),
    )(scalars, *pin(q, keys_values, keys_values))


def cross_backward_kernel(
    image, scalars, q, k, v, grad, logs, deltas, old, dq, dk, dv, key_sum, value_sum
):
    step = pl.program_id(1)
    tile = cross_tile(image, scalars, step)

    @pl.when(step == 0)
    def _():
        key_sum[...] = jnp.zeros_like(key_sum)
        value_sum[...] = jnp.zeros_like(value_sum)

    @pl.when(step < scalars[20 if image else 18])
    def _():
        queries = q[...]
        grads = grad[...]
        keys = k[...]
        values = v[...]
        limit = scalars[17] - tile * TILE
        lane_mine = (lax.broadcasted_iota(jnp.int32, (1, TILE), 1) >= limit) == (image == 1)
        parts = []
        for half in range(2):
            one_query = only_half(queries, half)
            one_grad = only_half(grads, half)
            log = jnp.where(lane_mine, logs[half : half + 1, :], HIDE)
            scores = dot(keys, one_query, NT)
            weights = jnp.exp2(scores * EXP2_SCALE - log)
            slopes = dot(values, one_grad, NT)
            pushed = (weights * (slopes - deltas[half : half + 1, :])).astype(BF16)
            value_sum[...] += dot(weights.astype(BF16), one_grad, NN)
            key_sum[...] += dot(pushed, one_query, NN)
            parts.append(dot(pushed, keys, TN))
        grad_query = (
            jnp.where(in_half(parts[0].shape, 0), parts[0], parts[1]) * SCALE
        ).astype(BF16)
        if image:
            row_mine = lax.broadcasted_iota(jnp.int32, grad_query.shape, 0) >= limit
            grad_query = jnp.where(row_mine, grad_query, old[...])
        dq[...] = grad_query

    @pl.when(step == pl.num_programs(1) - 1)
    def _():
        dk[...] = (key_sum[...] * SCALE).astype(BF16)
        dv[...] = value_sum[...].astype(BF16)


def cross_tile(image, scalars, step):
    if image:
        return scalars[19] + jnp.minimum(step, scalars[20] - 1)
    return jnp.minimum(step, scalars[18] - 1)


def cross_backward(image, scalars, q, keys_values, grad, logs, deltas, images, old):
    count, inner = q.shape
    pairs = inner // PAIR
    memory_rows = keys_values.shape[0] // images
    tile_spec = pl.BlockSpec((TILE, PAIR), lambda p, s, sc: (cross_tile(image, sc, s), p))
    line = pl.BlockSpec((8, TILE), lambda p, s, sc: (p, cross_tile(image, sc, s)))
    result = pl.BlockSpec((memory_rows, PAIR), lambda p, s, sc: (0, p))

    def part(which):
        return pl.BlockSpec((memory_rows, PAIR), lambda p, s, sc: (image, which * pairs + p))

    def first_kernel(scalars, q, k, v, grad, logs, deltas, *rest):
        cross_backward_kernel(image, scalars, q, k, v, grad, logs, deltas, None, *rest)

    def second_kernel(*refs):
        cross_backward_kernel(image, *refs)

    extra = [old] if image else []
    return pl.pallas_call(
        second_kernel if image else first_kernel,
        grid_spec=pltpu.PrefetchScalarGridSpec(
            num_scalar_prefetch=1,
            grid=(pairs, count // TILE),
            in_specs=[tile_spec, part(0), part(1), tile_spec, line, line]
            + [tile_spec] * len(extra),
            out_specs=[tile_spec, result, result],
            scratch_shapes=[pltpu.VMEM((memory_rows, PAIR), F32)] * 2,
        ),
        out_shape=[
            pltpu.HBM((count, inner), BF16),
            pltpu.HBM((memory_rows, inner), BF16),
            pltpu.HBM((memory_rows, inner), BF16),
        ],
        input_output_aliases={7: 0} if image else {},
        compiler_params=params(),
        cost_estimate=cost(25 * count * memory_rows * inner, 8 * memory_rows * inner),
    )(scalars, *pin(q, keys_values, keys_values, grad), logs, deltas, *pin(*extra))


def put_rows(places, product, keep, send):
    height = product.shape[0] // 4
    for i, ref in enumerate((keep, keep, send, send)):
        start = pl.multiple_of(places[i] * height, 16)
        ref[i % 2, 0:height, :] = product[pl.ds(start, height), :].astype(BF16)


def memory_back_kernel(
    columns, last, places, memory, dk, dv, w0, w1, w2, w3, *refs
):
    if last:
        before, keep_part, send_part, keep, send, weight, total, sems = refs
    else:
        keep_part, send_part, total_out, weight, total, sems = refs
    inner = dk.shape[1]

    @pl.when(pl.program_id(0) == 0)
    def _():
        copies = fetch((w0, w1, w2, w3), places, columns, weight, sems)
        start_all(copies)
        if last:
            total[...] = before[...]
        else:
            total[...] = jnp.zeros_like(total)
        wait_all(copies)

    both = jnp.concatenate([dk[...], dv[...]], axis=1)
    side = places[4]
    mine = weight[pl.ds(pl.multiple_of(side * inner, 16), inner), :]
    theirs = weight[pl.ds(pl.multiple_of((1 - side) * inner, 16), inner), :]
    send_part[...] = dot(both, theirs, NT).astype(BF16)
    keep_part[...] = dot(both, mine, NT).astype(BF16)
    total[...] += dot(memory[...], both, TN)

    @pl.when(pl.program_id(0) == pl.num_programs(0) - 1)
    def _():
        if last:
            put_rows(places, total, keep, send)
        else:
            total_out[...] = total[...]


def memory_back(places, memory, dk, dv, pieces, columns, image, before, spare):
    count, inner = dk.shape
    width = memory.shape[1]
    steps = count // MEMORY_TILE
    last = before is not None
    ranks = pltpu.HBM((2, width // 4, spare + 2 * inner), BF16)
    rank_spec = pl.BlockSpec((2, width // 4, 2 * inner), lambda t: (0, 0, 0))

    def kernel(*refs):
        memory_back_kernel(columns, last, *refs)

    return pl.pallas_call(
        kernel,
        grid=(steps,),
        in_specs=[
            SCALARS,
            pl.BlockSpec((MEMORY_TILE, width), lambda t: (image * steps + t, 0)),
            rows(inner, MEMORY_TILE),
            rows(inner, MEMORY_TILE),
        ]
        + [ANY] * 4
        + ([whole((width, 2 * inner))] if last else []),
        out_specs=[rows(inner, MEMORY_TILE), rows(inner, MEMORY_TILE)]
        + ([rank_spec, rank_spec] if last else [whole((width, 2 * inner))]),
        out_shape=[pltpu.HBM((count, inner), BF16)] * 2
        + ([ranks, ranks] if last else [shape_of((width, 2 * inner), F32)]),
        scratch_shapes=[
            pltpu.VMEM((width, 2 * inner), BF16),
            pltpu.VMEM((width, 2 * inner), F32),
            pltpu.SemaphoreType.DMA((4,)),
        ],
        compiler_params=params(),
        cost_estimate=cost(8 * count * width * inner, 8 * count * width),
    )(places, *pin(memory, dk, dv), *pieces, *([before] if last else []))


def weight_grads_kernel(plan, spans, places, left_refs, right_refs, keep, send, scratch):
    left_holds = scratch[: len(left_refs)]
    right_holds = scratch[len(left_refs) : -2]
    turned, sems = scratch[-2:]
    height = turned.shape[0] // 4
    step = pl.program_id(0)
    lefts = [
        pltpu.make_async_copy(ref, hold, sems.at[i])
        for i, (ref, hold) in enumerate(zip(left_refs, left_holds))
    ]
    rights = [
        pltpu.make_async_copy(ref, hold, sems.at[len(left_refs) + i])
        for i, (ref, hold) in enumerate(zip(right_refs, right_holds))
    ]
    for at, (left, group) in enumerate(plan):
        fresh = at == 0 or plan[at - 1][0] != left

        @pl.when(step == at)
        def _():
            if at == 0:
                seen = set()
                for one, others in plan:
                    if one not in seen:
                        lefts[one].start()
                        seen.add(one)
                    for g in others:
                        rights[g].start()
            if fresh:
                lefts[left].wait()
                turned[...] = left_holds[left][...].T
            for g in group:
                rights[g].wait()
            right = join([right_holds[g] for g in group])
            for i, ref in enumerate((keep, keep, send, send)):
                start = pl.multiple_of(places[i] * height, 16)
                ref[i % 2, 0:height, spans[at]] = dot(
                    turned[pl.ds(start, height), :], right, NN
                ).astype(BF16)


def join(refs):
    values = [ref[...] for ref in refs]
    return values[0] if len(values) == 1 else jnp.concatenate(values, axis=1)


def flatten(groups):
    flat, sizes = [], []
    for group in groups:
        group = group if isinstance(group, (list, tuple)) else [group]
        flat += list(group)
        sizes.append(len(group))
    return flat, sizes


def weight_grads(places, lefts, rights, plan, into=(), first=0):
    count, width = lefts[0].shape
    flat, sizes = flatten(rights)
    groups, at = [], 0
    for size in sizes:
        groups.append(list(range(at, at + size)))
        at += size
    plan = [(left, [f for g in group for f in groups[g]]) for left, group in plan]
    columns = [sum(flat[f].shape[1] for f in group) for _, group in plan]
    step_columns = columns[0]
    share = width // 4
    total = sum(columns) + first * step_columns
    even = len(set(columns)) == 1
    spans = [
        slice(0, step_columns) if even else slice(sum(columns[:at]), sum(columns[: at + 1]))
        for at in range(len(plan))
    ]
    extra = list(into)
    def kernel(places, *refs):
        lefts_end = len(lefts)
        rights_end = lefts_end + len(flat)
        weight_grads_kernel(
            plan,
            spans,
            places,
            refs[:lefts_end],
            refs[lefts_end:rights_end],
            *refs[rights_end + len(extra) : rights_end + len(extra) + 2],
            refs[rights_end + len(extra) + 2 :],
        )

    start = 1 + len(lefts) + len(flat)
    return pl.pallas_call(
        kernel,
        grid=(len(plan),),
        in_specs=[SCALARS]
        + [ANY] * (len(lefts) + len(flat) + len(extra)),
        out_specs=[
            pl.BlockSpec((2, share, step_columns), lambda t: (0, 0, t + first))
            if even
            else whole((2, share, total))
        ]
        * 2,
        out_shape=[pltpu.HBM((2, share, total), BF16)] * 2,
        input_output_aliases={start: 0, start + 1: 1} if extra else {},
        scratch_shapes=[pltpu.VMEM(array.shape, array.dtype) for array in list(lefts) + flat]
        + [
            pltpu.VMEM((width, count), BF16),
            pltpu.SemaphoreType.DMA((len(lefts) + len(flat),)),
        ],
        compiler_params=params(),
        cost_estimate=cost(
            2 * count * width * sum(columns), 4 * count * width * len(plan)
        ),
    )(places, *pin(*lefts, *flat), *extra)


def middle_kernel(plan, parts, places, x, gain, *refs):
    mine, theirs, refs = refs[:parts], refs[parts : 2 * parts], refs[2 * parts :]
    pieces, (h1, n2, cq, out_mine, out_theirs, query, sems) = refs[:8], refs[8:]

    @pl.when(pl.program_id(0) == 0)
    def _():
        copies = (
            fetch(pieces[:4], places, plan[0], out_mine, sems, 0)
            + fetch(pieces[4:], places, plan[1], out_theirs, sems, 4)
            + fetch(pieces[:4], places, plan[2], query, sems, 8)
        )
        start_all(copies)
        wait_all(copies)

    values = (
        x[...].astype(F32)
        + dot(join(mine), out_mine[...], NT)
        + dot(join(theirs), out_theirs[...], NT)
    )
    h1[...] = values
    normed = (values * inverse_rms(values) * gain[...]).astype(BF16)
    n2[...] = normed
    cq[...] = dot(normed, query[...], NN).astype(BF16)


def middle_step(places, x, mine, theirs, gain, pieces, pieces_theirs, plan):
    count, width = x.shape
    half = sum(part.shape[1] for part in mine)

    def kernel(*refs):
        middle_kernel(plan, len(mine), *refs)

    return pl.pallas_call(
        kernel,
        grid=(count // TILE,),
        in_specs=[SCALARS, rows(width), whole((1, width))]
        + [rows(PAIR)] * (2 * len(mine))
        + [ANY] * 8,
        out_specs=[rows(width), rows(width), rows(half)],
        out_shape=[
            pltpu.HBM((count, width), F32),
            pltpu.HBM((count, width), BF16),
            pltpu.HBM((count, half), BF16),
        ],
        scratch_shapes=[pltpu.VMEM((width, half), BF16)] * 3 + [pltpu.SemaphoreType.DMA((12,))],
        compiler_params=params(),
        cost_estimate=cost(6 * count * width * half, 12 * count * width),
    )(places, *pin(x), gain, *pin(*mine), *theirs, *pieces, *pieces_theirs)


def head_sums(left, right):
    product = left.astype(F32) * right.astype(F32)
    width = product.shape[1]
    high = product.astype(BF16)
    low = (product - high.astype(F32)).astype(BF16)
    height = 8 * (width // PAIR)
    line = lax.broadcasted_iota(jnp.int32, (height, width), 0)
    head = lax.broadcasted_iota(jnp.int32, (height, width), 1) // HEAD_DIM
    choose = (
        ((line // 8) * 2 + line % 8 == head) & (line % 8 < 2)
    ).astype(F32).astype(BF16)
    return dot(choose, high, NT) + dot(choose, low, NT)


CHUNK = 512


def units_kernel(plan, parts, places, h1, gain, gy, *refs):
    mine, theirs, refs = refs[:parts], refs[parts : 2 * parts], refs[2 * parts :]
    late, refs = refs[0], refs[1:]
    (
        output,
        n3,
        hidden,
        grad_gate,
        grad_up,
        dh2,
        e2,
        dc,
        deltas,
        gain_grad,
        out_mine,
        out_theirs,
        units_mine,
        units_theirs,
        sems,
    ) = refs
    step = pl.program_id(0)

    side = places[4]
    out_copies = [
        fetch_half(late, side, plan[0], out_mine, sems.at[0]),
        fetch_half(late, 1 - side, plan[0], out_theirs, sems.at[1]),
    ]
    mine_copy = fetch_half(late, side, plan[1], units_mine, sems.at[2])
    theirs_copy = fetch_half(late, 1 - side, plan[1], units_theirs, sems.at[3])

    @pl.when(step == 0)
    def _():
        start_all(out_copies + [mine_copy, theirs_copy])
        gain_grad[...] = jnp.zeros_like(gain_grad)
        wait_all(out_copies)

    crossed_mine = join(mine)
    values = (
        h1[...] + dot(crossed_mine, out_mine[...], NT) + dot(join(theirs), out_theirs[...], NT)
    )
    normed = (values * inverse_rms(values) * gain[...]).astype(BF16)
    n3[...] = normed
    upstream = gy[...]
    mixed = jnp.zeros_like(values)
    back = jnp.zeros_like(values)
    unit = units_mine.shape[1] // 3
    for own in (True, False):
        weight = units_mine if own else units_theirs

        @pl.when(step == 0)
        def _():
            (mine_copy if own else theirs_copy).wait()

        for start in range(0, unit, CHUNK):
            gate_weight = weight[:, start : start + CHUNK]
            up_weight = weight[:, unit + start : unit + start + CHUNK]
            down_weight = weight[:, 2 * unit + start : 2 * unit + start + CHUNK]
            gate = dot(normed, gate_weight, NN)
            up = dot(normed, up_weight, NN)
            pushed = dot(upstream, down_weight, NN)
            square = gate * gate
            bend = jnp.tanh(ROOT_TWO_OVER_PI * gate * (1.0 + CUBIC * square))
            lift = 0.5 * (1.0 + bend)
            gelu = gate * lift
            slope = lift + (0.5 * ROOT_TWO_OVER_PI) * gate * (1.0 - bend * bend) * (
                1.0 + (3.0 * CUBIC) * square
            )
            units = (gelu * up).astype(BF16)
            push_gate = (pushed * up * slope).astype(BF16)
            push_up = (pushed * gelu).astype(BF16)
            mixed = mixed + dot(units, down_weight, NT)
            back = back + dot(push_gate, gate_weight, NT) + dot(push_up, up_weight, NT)
            if own:
                hidden[:, start : start + CHUNK] = units
                grad_gate[:, start : start + CHUNK] = push_gate
                grad_up[:, start : start + CHUNK] = push_up
    output[...] = (values + mixed).astype(BF16)
    grad, gain_part = norm_back(values, gain[...], back)
    result = upstream.astype(F32) + grad
    dh2[...] = result
    low = result.astype(BF16)
    e2[...] = low
    crossed = dot(low, out_mine[...], NN).astype(BF16)
    dc[...] = crossed
    deltas[...] = head_sums(crossed, crossed_mine)
    gain_grad[0:1, :] += gain_part


def units_step(places, h1, mine, theirs, gain, gy, late, plan):
    count, width = h1.shape
    half = sum(part.shape[1] for part in mine)
    unit = (plan[1].stop - plan[1].start) // 3
    lines = 8 * (half // PAIR)

    def kernel(*refs):
        units_kernel(plan, len(mine), *refs)

    return pl.pallas_call(
        kernel,
        grid=(count // TILE,),
        in_specs=[
            SCALARS,
            rows(width),
            whole((1, width)),
            rows(width),
        ]
        + [rows(PAIR)] * (2 * len(mine))
        + [ANY],
        out_specs=[
            rows(width),
            rows(width),
            rows(unit),
            rows(unit),
            rows(unit),
            rows(width),
            rows(width),
            rows(half),
            pl.BlockSpec((lines, TILE), lambda t: (0, t)),
            whole((8, width)),
        ],
        out_shape=[
            pltpu.HBM((count, width), BF16),
            pltpu.HBM((count, width), BF16),
            pltpu.HBM((count, unit), BF16),
            pltpu.HBM((count, unit), BF16),
            pltpu.HBM((count, unit), BF16),
            pltpu.HBM((count, width), F32),
            pltpu.HBM((count, width), BF16),
            pltpu.HBM((count, half), BF16),
            pltpu.HBM((lines, count), F32),
            shape_of((8, width), F32),
        ],
        scratch_shapes=[pltpu.VMEM((width, half), BF16)] * 2
        + [pltpu.VMEM((width, 3 * unit), BF16)] * 2
        + [pltpu.SemaphoreType.DMA((4,))],
        compiler_params=params(40),
        cost_estimate=cost(30 * count * width * unit, 30 * count * width),
    )(places, *pin(h1), gain, *pin(gy, *mine), *theirs, *pin(late))


def turn_kernel(plan, parts, places, dh2, h1, mine, theirs, gain, *refs):
    attended, refs = refs[:parts], refs[parts:]
    pieces, refs = refs[:4], refs[4:]
    late, dh1, e1, da, deltas, gain_grad, query_mine, query_theirs, out_mine, sems = refs

    @pl.when(pl.program_id(0) == 0)
    def _():
        copies = (
            fetch(pieces, places, plan[0], out_mine, sems, 0)
            + fetch(pieces, places, plan[1], query_mine, sems, 4)
            + [fetch_half(late, 1 - places[4], plan[2], query_theirs, sems.at[8])]
        )
        start_all(copies)
        gain_grad[...] = jnp.zeros_like(gain_grad)
        wait_all(copies)

    back = dot(mine[...], query_mine[...], NT) + dot(theirs[...], query_theirs[...], NT)
    grad, gain_part = norm_back(h1[...], gain[...], back)
    result = dh2[...] + grad
    dh1[...] = result
    low = result.astype(BF16)
    e1[...] = low
    pushed = dot(low, out_mine[...], NN).astype(BF16)
    da[...] = pushed
    deltas[...] = head_sums(pushed, join(attended))
    gain_grad[0:1, :] += gain_part


def turn_step(places, dh2, h1, mine, theirs, gain, attended, pieces, late, plan):
    count, width = h1.shape
    half = mine.shape[1]
    lines = 8 * (half // PAIR)

    def kernel(*refs):
        turn_kernel(plan, len(attended), *refs)

    return pl.pallas_call(
        kernel,
        grid=(count // TILE,),
        in_specs=[
            SCALARS,
            rows(width),
            rows(width),
            rows(half),
            rows(half),
            whole((1, width)),
        ]
        + [rows(PAIR)] * len(attended)
        + [ANY] * 5,
        out_specs=[
            rows(width),
            rows(width),
            rows(half),
            pl.BlockSpec((lines, TILE), lambda t: (0, t)),
            whole((8, width)),
        ],
        out_shape=[
            pltpu.HBM((count, width), F32),
            pltpu.HBM((count, width), BF16),
            shape_of((count, half), BF16),
            shape_of((lines, count), F32),
            shape_of((8, width), F32),
        ],
        scratch_shapes=[pltpu.VMEM((width, half), BF16)] * 3 + [pltpu.SemaphoreType.DMA((9,))],
        compiler_params=params(),
        cost_estimate=cost(6 * count * width * half, 16 * count * width),
    )(places, *pin(dh2, h1, mine), theirs, gain, *pin(*attended), *pieces, *pin(late))


def partial_kernel(parts, places, x, n1, second, third, *refs):
    part_refs, refs = refs[:parts], refs[parts:]
    w0, w1, w2, w3, out, keep, send, weight, total, gain_grad, sems = refs
    step = pl.program_id(0)

    @pl.when(step == 0)
    def _():
        copies = fetch((w0, w1, w2, w3), places, slice(0, weight.shape[1]), weight, sems)
        start_all(copies)
        gain_grad[...] = jnp.zeros_like(gain_grad)
        total[...] = jnp.zeros_like(total)
        wait_all(copies)

    back = dot(join(part_refs), weight[...], NT)
    out[...] = back.astype(BF16)
    values = x[...].astype(F32)
    gain_grad[0:1, :] += jnp.sum(back * values * inverse_rms(values), axis=0, keepdims=True)
    last = join([part_refs[i * (parts // 3) + parts // 3 - 1] for i in range(3)])
    total[...] += dot(n1[...], last, TN)

    @pl.when(step == pl.num_programs(0) - 1)
    def _():
        put_rows(places, total, keep, send)
        height = total.shape[0] // 4
        lines = jnp.concatenate(
            [
                gain_grad[0:1, :],
                second[0:1, :],
                third[0:1, :],
                jnp.zeros((13, gain_grad.shape[1]), F32),
            ],
            axis=0,
        )
        shares = [lines[:, w * height : (w + 1) * height] for w in range(4)]
        fill = jnp.zeros((16, total.shape[1] - height), F32)
        for i, ref in enumerate((keep, keep, send, send)):
            share = shares[0]
            for w in range(1, 4):
                share = jnp.where(places[i] == w, shares[w], share)
            ref[i % 2, height : height + 16, :] = jnp.concatenate([share, fill], axis=1).astype(
                BF16
            )


def partial_step(places, parts, x, n1, second, third, pieces):
    count, width = x.shape
    inner = sum(part.shape[1] for part in parts)
    ranks = (2, width // 4 + 16, 3 * PAIR)

    def kernel(*refs):
        partial_kernel(len(parts), *refs)

    return pl.pallas_call(
        kernel,
        grid=(count // TILE,),
        in_specs=[SCALARS, rows(width), rows(width), whole((8, width)), whole((8, width))]
        + [rows(PAIR)] * len(parts)
        + [ANY] * 4,
        out_specs=[rows(width), whole(ranks), whole(ranks)],
        out_shape=[
            pltpu.HBM((count, width), BF16),
            shape_of(ranks, BF16),
            shape_of(ranks, BF16),
        ],
        scratch_shapes=[
            pltpu.VMEM((width, inner), BF16),
            pltpu.VMEM((width, 3 * PAIR), F32),
            pltpu.VMEM((8, width), F32),
            pltpu.SemaphoreType.DMA((4,)),
        ],
        compiler_params=params(),
        cost_estimate=cost(2 * count * width * (inner + 3 * PAIR), 8 * count * width),
    )(places, *pin(x, n1), second, third, *pin(*parts), *pieces)


def first_kernel(dh1, x, mine, theirs, gain, out):
    back = mine[...].astype(F32) + theirs[...].astype(F32)
    grad, _ = norm_back(x[...].astype(F32), gain[...], back)
    out[...] = (dh1[...] + grad).astype(BF16)


def first_step(dh1, x, mine, theirs, gain):
    count, width = x.shape
    return pl.pallas_call(
        first_kernel,
        grid=(count // TILE,),
        in_specs=[rows(width)] * 4 + [whole((1, width))],
        out_specs=rows(width),
        out_shape=pltpu.HBM((count, width), BF16),
        compiler_params=params(),
        cost_estimate=cost(20 * count * width, 12 * count * width),
    )(*pin(dh1, x, mine), theirs, gain)


def swap(values, axis, distance):
    size = lax.axis_size(axis)
    return lax.ppermute(values, axis, [(i, i ^ distance) for i in range(size)])


def after(values, *others):
    return lax.optimization_barrier((values,) + others)[0]


def gather_all(values):
    return lax.all_gather(values, ("narrow", "wide"), axis=0, tiled=True).reshape(
        lax.axis_size("narrow"), -1, values.shape[1]
    )


def sum_wide(values):
    return lax.psum_scatter(values, "wide", scatter_dimension=0, tiled=True)


def add(left, right):
    return (left.astype(F32) + right.astype(F32)).astype(BF16)


def add_pair(keep, got):
    return add(keep[0], got[0]), add(keep[1], got[1])


def line_inner():
    place = lax.axis_index("dp")
    return (place == 1) | (place == 2)


def line_first(values):
    if lax.axis_size("dp") != 4:
        return lax.psum(values, "dp")
    got = lax.ppermute(values, "dp", [(0, 1), (3, 2)])
    return jnp.where(line_inner(), add(values, got), values)


def line_second(values):
    if lax.axis_size("dp") != 4:
        return values
    return add(values, lax.ppermute(values, "dp", [(1, 2), (2, 1)]))


def line_third(values):
    if lax.axis_size("dp") != 4:
        return values
    got = lax.ppermute(values, "dp", [(1, 0), (2, 3)])
    return jnp.where(line_inner(), values, got)


def local(
    tokens,
    memory,
    cotangent,
    norm1_gain,
    norm2_gain,
    norm3_gain,
    q_weight,
    k_weight,
    v_weight,
    o_weight,
    cross_q,
    cross_k,
    cross_v,
    cross_o,
    gate_weight,
    up_weight,
    down_weight,
    segment_ids,
    block_ids,
    image_table,
):
    width = tokens.shape[1]
    share = q_weight.shape[0]
    inner = q_weight.shape[1]
    unit = gate_weight.shape[1]
    images = memory.shape[0]
    flat_memory = memory.reshape(-1, width)
    place = lax.axis_index("wide")
    side = lax.axis_index("narrow")
    places = jnp.stack([place, place ^ 2, place ^ 1, place ^ 3, side]).astype(jnp.int32)

    gains = jnp.stack([norm1_gain, norm2_gain, norm3_gain])
    gains = jnp.pad(gains, ((0, 13), (0, 3 * inner - share)))
    early = jnp.concatenate(
        [jnp.concatenate([q_weight, k_weight, v_weight], axis=1), gains], axis=0
    )
    early_x = swap(early, "wide", 2)
    early_pieces = (early, early_x, swap(early, "wide", 1), swap(early_x, "wide", 1))
    lines = jnp.stack([piece[share : share + 3, :share] for piece in early_pieces])
    lines = lines.astype(F32)
    order = [
        jnp.sum(jnp.where((places[:4] == w)[:, None, None], lines, 0.0), axis=0)
        for w in range(4)
    ]
    all_gains = jnp.concatenate(order, axis=1)[:, None, :]

    mid = jnp.concatenate([cross_k, cross_v, cross_q, o_weight], axis=1)
    memory_columns = slice(0, 2 * inner)
    query_columns = slice(2 * inner, 3 * inner)
    out_columns = slice(3 * inner, 4 * inner)
    mid_x = swap(after(mid, early_x), "wide", 2)
    mid_core = swap(mid, "wide", 1)
    out_y = swap(o_weight, "narrow", 1)
    late = jnp.concatenate([cross_q, cross_o, gate_weight, up_weight, down_weight], axis=1)
    late_query_columns = slice(0, inner)
    late_columns = (slice(inner, 2 * inner), slice(2 * inner, 2 * inner + 3 * unit))

    x, gy, row_ids, col_ids, pos, scalars = order_rows(
        segment_ids, block_ids, image_table, tokens, cotangent
    )
    late = gather_all(after(late, early_x, x))
    n1, qkv = norm_project(places, x, all_gains[0], early_pieces)
    pairs = inner // PAIR
    self_parts = [self_forward(0, after(qkv, out_y, mid_core), row_ids, col_ids)]
    mid_x = after(mid_x, self_parts[0][0])
    mid_pieces = (mid, mid_x, mid_core, swap(mid_x, "wide", 1))
    out_xy = swap(mid_x[:, out_columns], "narrow", 1)
    out_pieces = (out_y, out_xy, swap(out_y, "wide", 1), swap(out_xy, "wide", 1))
    for pair in range(1, pairs):
        self_parts.append(
            self_forward(
                pair, after(qkv, self_parts[-1][0], mid_x), row_ids, col_ids
            )
        )
    attended_theirs = [swap(part[0], "narrow", 1) for part in self_parts]
    attended = [part[0] for part in self_parts]
    keys_values = project_memory(
        places,
        after(flat_memory, self_parts[-1][0], attended_theirs[0], out_xy),
        mid_pieces,
        memory_columns,
    )
    h1, n2, cq = middle_step(
        places,
        after(x, keys_values),
        attended,
        attended_theirs,
        all_gains[1],
        mid_pieces,
        out_pieces,
        (out_columns, slice(0, inner), query_columns),
    )
    cross_parts = [cross_forward(0, scalars, cq, keys_values, images)]
    crossed_theirs = []
    for pair in range(1, pairs):
        previous = [cross_parts[-1][0]] + crossed_theirs
        crossed_theirs.append(swap(cross_parts[-1][0], "narrow", 1))
        cross_parts.append(
            cross_forward(pair, scalars, after(cq, *previous), keys_values, images)
        )
    crossed = [part[0] for part in cross_parts]
    crossed_theirs.append(swap(crossed[-1], "narrow", 1))
    cross_logs = jnp.concatenate([part[1] for part in cross_parts], axis=0)
    (
        output,
        n3,
        hidden,
        grad_gate,
        grad_up,
        dh2,
        e2,
        dc,
        cross_deltas,
        third_gain,
    ) = units_step(
        places,
        h1,
        crossed,
        crossed_theirs,
        all_gains[2],
        gy,
        late,
        late_columns,
    )

    unit_keep, unit_send = weight_grads(
        places, (n3, gy), (grad_gate, grad_up, hidden), ((0, (0,)), (0, (1,)), (1, (2,)))
    )
    unit_stay, unit_leave = add_pair(unit_keep, swap(unit_send, "wide", 1))
    dcq, dck, dcv = cross_backward(
        0,
        scalars,
        cq,
        keys_values,
        after(dc, unit_leave),
        cross_logs,
        cross_deltas,
        images,
        None,
    )
    unit_part = add(unit_stay, swap(unit_leave, "wide", 2))
    keep0, send0, total = memory_back(
        places,
        flat_memory,
        after(dck, unit_part),
        dcv,
        mid_pieces,
        memory_columns,
        0,
        None,
        0,
    )
    unit_sum = lax.psum(unit_part, "dp")
    dcq, dck, dcv = cross_backward(
        1,
        scalars,
        cq,
        keys_values,
        after(dc, send0),
        cross_logs,
        cross_deltas,
        images,
        dcq,
    )
    dcq_theirs = swap(dcq, "narrow", 1)
    memory0 = add(keep0, swap(send0, "narrow", 1))
    keep1, send1, cross_keep, cross_send = memory_back(
        places,
        flat_memory,
        after(dck, memory0),
        dcv,
        mid_pieces,
        memory_columns,
        1,
        total,
        2 * inner,
    )
    cross_keep, cross_send = weight_grads(
        places,
        (after(n2, send1), e2),
        (dcq, crossed),
        ((0, (0,)), (1, (1,))),
        into=(cross_keep, cross_send),
        first=2,
    )
    dh1, e1, da, self_deltas, second_gain = turn_step(
        places,
        dh2,
        h1,
        after(dcq, cross_send, unit_sum),
        dcq_theirs,
        all_gains[1],
        attended,
        mid_pieces,
        late,
        (out_columns, query_columns, late_query_columns),
    )
    memory1 = add(keep1, swap(after(send1, dcq_theirs), "narrow", 1))
    cross_stay, cross_leave = add_pair(cross_keep, swap(cross_send, "wide", 1))
    da = after(da, cross_leave)
    back = []
    for pair in range(pairs):
        ready = after(da, *[part[0] for part in back])
        if pair == pairs - 1:
            early_back = list(back)
            self_keep, self_send = weight_grads(
                places,
                (after(n1, back[-1][0]), e1),
                [[part[i] for part in early_back] for i in range(3)] + [attended],
                ((0, (0, 1, 2)), (1, (3,))),
            )
            cross_part = add(cross_stay, swap(cross_leave, "wide", 2))
            ready = after(ready, cross_part, self_send)
            cross_part = line_first(cross_part)
        back.append(
            self_backward(
                pair, qkv, ready, self_parts[pair][1], self_deltas, row_ids, col_ids
            )
        )
    dq, dk, dv = [[part[i] for part in back] for i in range(3)]
    self_stay, self_leave = add_pair(self_keep, swap(self_send, "wide", 1))
    self_part = add(self_stay, swap(self_leave, "wide", 2))
    dn1, last_keep, last_send = partial_step(
        places,
        dq + dk + dv,
        after(x, memory1, self_leave),
        n1,
        second_gain,
        third_gain,
        early_pieces,
    )
    dn1_theirs = swap(dn1, "narrow", 1)
    last_stay, last_leave = add_pair(last_keep, swap(last_send, "wide", 1))
    last_part = add(last_stay, swap(last_leave, "wide", 2))
    output = restore_rows(pos, after(output, last_send, self_part))
    tokens_grad = first_step(dh1, x, dn1, dn1_theirs, all_gains[0])
    tokens_grad = restore_rows(pos, tokens_grad)
    memory_grad = jnp.stack([after(memory0, self_part), memory1])
    cross_sum = line_third(line_second(cross_part))
    self_sum = line_third(line_second(line_first(self_part)))
    last_sum = line_third(line_second(line_first(last_part)))
    gain_sums = last_sum[share:, :share].astype(F32)
    first_gain = gain_sums[0] + swap(gain_sums, "narrow", 1)[0]

    def grads(array, size, count):
        return [array[:share, i * size : (i + 1) * size].astype(F32) for i in range(count)]

    gate_grad, up_grad, down_grad = grads(after(unit_sum, self_part), unit, 3)
    cross_k_grad, cross_v_grad, cross_q_grad, cross_o_grad = grads(cross_sum, inner, 4)
    part = inner - PAIR
    q_grad, k_grad, v_grad = [
        jnp.concatenate([most, rest], axis=1)
        for most, rest in zip(grads(self_sum, part, 3), grads(last_sum, PAIR, 3))
    ]
    o_grad = self_sum[:, 3 * part :].astype(F32)
    return (
        output,
        tokens_grad,
        memory_grad,
        first_gain,
        gain_sums[1],
        gain_sums[2],
        q_grad,
        k_grad,
        v_grad,
        o_grad,
        cross_q_grad,
        cross_k_grad,
        cross_v_grad,
        cross_o_grad,
        gate_grad,
        up_grad,
        down_grad,
    )


def solution(mesh):
    both = ("dp", "wide")
    weight = P("wide", "narrow")
    in_specs = (
        (P(both, None), P(both, None, None), P(both, None))
        + (P("wide"),) * 3
        + (weight,) * 11
        + (P(both, None),) * 3
    )
    out_specs = (
        (P(both, None), P(both, None), P(both, None, "narrow"))
        + (P("wide"),) * 3
        + (weight,) * 11
    )
    return jax.shard_map(local, mesh=mesh, in_specs=in_specs, out_specs=out_specs, check_vma=False)
```

```python
import functools
import math

import jax
import jax.numpy as jnp
from jax import lax
from jax.experimental import pallas as pl
from jax.experimental.pallas import tpu as pltpu
from jax.sharding import PartitionSpec as P

F32 = jnp.float32
BF16 = jnp.bfloat16
EPSILON = 1e-06
ROOT_TWO_OVER_PI = 0.7978845608028654
CUBIC = 0.044715
HEAD_DIM = 64
PAIR = 2 * HEAD_DIM
SCALE = HEAD_DIM ** (-0.5)
EXP2_SCALE = SCALE * math.log2(math.e)
HIDE = 1e30
TILE = 256
ROWS = 512
WEIGH = 4.0

NN = (((1,), (0,)), ((), ()))
NT = (((1,), (1,)), ((), ()))
TN = (((0,), (0,)), ((), ()))


def dot(left, right, dims):
    return lax.dot_general(left, right, dims, preferred_element_type=F32)


def params(mebibytes=24):
    return pltpu.CompilerParams(vmem_limit_bytes=mebibytes * 1024 * 1024)


def cost(flops, nbytes):
    return pl.CostEstimate(
        flops=int(flops * WEIGH), bytes_accessed=int(nbytes * WEIGH), transcendentals=0
    )


def pin(*arrays):
    return [pltpu.with_memory_space_constraint(array, pltpu.HBM) for array in arrays]


def shape_of(shape, dtype):
    return jax.ShapeDtypeStruct(shape, dtype)


def whole(shape):
    zeros = (0,) * len(shape)
    return pl.BlockSpec(shape, lambda *_: zeros)


def rows(width, height=None):
    height = ROWS if height is None else height
    return pl.BlockSpec((height, width), lambda t, *_: (t, 0))


def inverse_rms(values):
    return lax.rsqrt(jnp.mean(values * values, axis=1, keepdims=True) + EPSILON)


def norm_back(values, gain, upstream):
    factor = inverse_rms(values)
    scaled = upstream * gain
    mean = jnp.mean(values * scaled, axis=1, keepdims=True)
    grad = factor * scaled - values * (factor * factor * factor * mean)
    return grad, jnp.sum(upstream * values * factor, axis=0, keepdims=True)


def in_half(shape, half):
    return (lax.broadcasted_iota(jnp.int32, shape, 1) // HEAD_DIM) == half


def only_half(values, half):
    return jnp.where(in_half(values.shape, half), values, jnp.zeros_like(values))


def order_kernel(seg, blk, table, x, gy, xp, gyp, row_ids, col_ids, pos_out, scalars, pos):
    step = pl.program_id(0)
    count = seg.shape[1]

    @pl.when(step == 0)
    def _():
        segments = seg[...]
        image = jnp.zeros_like(segments)
        for s in range(table.shape[1]):
            image = jnp.where(segments == s, table[0, s], image)
        first = (image == 0).astype(F32)
        before = lax.broadcasted_iota(jnp.int32, (count, count), 0) < lax.broadcasted_iota(
            jnp.int32, (count, count), 1
        )
        rank = dot(
            jnp.broadcast_to(first, (8, count)).astype(BF16),
            before.astype(F32).astype(BF16),
            NN,
        )[0:1]
        total = jnp.sum(first)
        index = lax.broadcasted_iota(jnp.int32, (1, count), 1).astype(F32)
        place = jnp.where(image == 0, rank, total + index - rank)
        pos[...] = place.astype(jnp.int32)
        pos_out[...] = jnp.broadcast_to(pos[...], (8, count))
        n0 = total.astype(jnp.int32)
        tiles = count // TILE
        visits0 = jnp.maximum(1, (n0 + TILE - 1) // TILE)
        start1 = jnp.minimum(tiles - 1, n0 // TILE)
        visits = visits0 + tiles - start1
        for v in range(tiles + 1):
            real = jnp.minimum(v, visits - 1)
            in_first = real < visits0
            scalars[v] = jnp.where(in_first, real, real - visits0 + start1)
            scalars[8 + v] = jnp.where(in_first, 0, 1)
        scalars[16] = visits
        scalars[17] = n0
        scalars[18] = visits0
        scalars[19] = start1
        scalars[20] = tiles - start1

    onehot = (
        lax.broadcasted_iota(jnp.int32, (TILE, count), 0) + step * TILE == pos[...]
    ).astype(F32).astype(BF16)
    xp[...] = dot(onehot, x[...], NN).astype(BF16)
    gyp[...] = dot(onehot, gy[...], NN).astype(BF16)
    ids = jnp.concatenate(
        [
            seg[...].astype(F32),
            blk[...].astype(F32),
            jnp.zeros((126, count), F32),
        ],
        axis=0,
    ).astype(BF16)
    row_ids[...] = dot(ids[0:8], onehot, NT)
    col_ids[...] = dot(onehot, ids, NT)


def order_rows(seg, blk, table, x, gy):
    count, width = x.shape
    return pl.pallas_call(
        order_kernel,
        grid=(count // TILE,),
        in_specs=[
            whole((1, count)),
            whole((1, count)),
            pl.BlockSpec(memory_space=pltpu.SMEM),
            whole((count, width)),
            whole((count, width)),
        ],
        out_specs=[
            rows(width, TILE),
            rows(width, TILE),
            pl.BlockSpec((8, TILE), lambda t: (0, t)),
            rows(128, TILE),
            whole((8, count)),
            pl.BlockSpec(memory_space=pltpu.SMEM),
        ],
        out_shape=[
            pltpu.HBM((count, width), BF16),
            pltpu.HBM((count, width), BF16),
            shape_of((8, count), F32),
            shape_of((count, 128), F32),
            shape_of((8, count), jnp.int32),
            shape_of((32,), jnp.int32),
        ],
        scratch_shapes=[pltpu.VMEM((1, count), jnp.int32)],
        compiler_params=params(),
        cost_estimate=cost(4 * count * count * width, 8 * count * width),
    )(seg, blk, table, *pin(x, gy))


def restore_kernel(pos, values, out):
    count = values.shape[0]
    onehot = (
        lax.broadcasted_iota(jnp.int32, (count, TILE), 0) == pos[0:1, :]
    ).astype(F32).astype(BF16)
    out[...] = dot(onehot, values[...], TN).astype(BF16)


def restore_rows(pos, values):
    count, width = values.shape
    return pl.pallas_call(
        restore_kernel,
        grid=(count // TILE,),
        in_specs=[pl.BlockSpec((8, TILE), lambda t: (0, t)), whole((count, width))],
        out_specs=rows(width, TILE),
        out_shape=shape_of((count, width), BF16),
        compiler_params=params(),
        cost_estimate=cost(2 * count * count * width, 4 * count * width),
    )(pos, *pin(values))


def fetch(pieces, places, columns, dest, sems, base=0):
    height = dest.shape[0] // 4
    copies = []
    for i, piece in enumerate(pieces):
        start = pl.multiple_of(places[i] * height, 16)
        copies.append(
            pltpu.make_async_copy(
                piece.at[pl.ds(0, height), columns],
                dest.at[pl.ds(start, height), :],
                sems.at[base + i],
            )
        )
    return copies


def fetch_half(gathered, half, columns, dest, sem):
    return pltpu.make_async_copy(gathered.at[half, :, columns], dest, sem)


def start_all(copies):
    for copy in copies:
        copy.start()


def wait_all(copies):
    for copy in copies:
        copy.wait()


ANY = pl.BlockSpec(memory_space=pl.ANY)
SCALARS = pl.BlockSpec(memory_space=pltpu.SMEM)


def project_kernel(places, x, gain, w0, w1, w2, w3, normed, out, weight, sems):
    @pl.when(pl.program_id(0) == 0)
    def _():
        copies = fetch((w0, w1, w2, w3), places, slice(0, weight.shape[1]), weight, sems)
        start_all(copies)
        wait_all(copies)

    values = x[...].astype(F32)
    n1 = (values * inverse_rms(values) * gain[...]).astype(BF16)
    normed[...] = n1
    out[...] = dot(n1, weight[...], NN).astype(BF16)


def norm_project(places, x, gain, pieces):
    count, width = x.shape
    outs = pieces[0].shape[1]
    return pl.pallas_call(
        project_kernel,
        grid=(count // ROWS,),
        in_specs=[SCALARS, rows(width), whole((1, width))] + [ANY] * 4,
        out_specs=[rows(width), rows(outs)],
        out_shape=[pltpu.HBM((count, width), BF16), shape_of((count, outs), BF16)],
        scratch_shapes=[pltpu.VMEM((width, outs), BF16), pltpu.SemaphoreType.DMA((4,))],
        compiler_params=params(),
        cost_estimate=cost(2 * count * width * outs, 4 * count * width + 2 * count * outs),
    )(places, *pin(x), gain, *pieces)


MEMORY_TILE = 1024


def memory_kernel(places, columns, memory, w0, w1, w2, w3, out, weight, sems):
    @pl.when(pl.program_id(0) == 0)
    def _():
        copies = fetch((w0, w1, w2, w3), places, columns, weight, sems)
        start_all(copies)
        wait_all(copies)

    out[...] = dot(memory[...], weight[...], NN).astype(BF16)


def project_memory(places, memory, pieces, columns):
    count, width = memory.shape
    outs = columns.stop - columns.start

    def kernel(places, *refs):
        memory_kernel(places, columns, *refs)

    return pl.pallas_call(
        kernel,
        grid=(count // MEMORY_TILE,),
        in_specs=[SCALARS, rows(width, MEMORY_TILE)] + [ANY] * 4,
        out_specs=rows(outs, MEMORY_TILE),
        out_shape=pltpu.HBM((count, outs), BF16),
        scratch_shapes=[pltpu.VMEM((width, outs), BF16), pltpu.SemaphoreType.DMA((4,))],
        compiler_params=params(),
        cost_estimate=cost(2 * count * width * outs, 4 * count * width),
    )(places, *pin(memory), *pieces)


SELF_TILE = 128
SELF_WINDOW = 512
BACK_WINDOW = 640


def store_logs(ref, columns, logs, extra=None):
    spread = jnp.where(in_half((logs[0].shape[0], PAIR), 0), logs[0], logs[1]).T
    for half in range(2):
        line = spread[half * HEAD_DIM : half * HEAD_DIM + 1, :]
        if extra is not None:
            line = jnp.where(extra, line, ref[half : half + 1, columns])
        ref[half : half + 1, columns] = line


def self_forward_kernel(q, k, v, row_ids, col_ids, out, logs):
    count = q.shape[0]
    for tile in range(count // SELF_TILE):
        base = tile * SELF_TILE
        start = min(max(base - 256, 0), count - SELF_WINDOW)
        spot = slice(base, base + SELF_TILE)
        window = slice(start, start + SELF_WINDOW)
        seen = (col_ids[spot, 0:1] == row_ids[0:1, window]) & (
            row_ids[1:2, window] <= col_ids[spot, 1:2]
        )
        bias = jnp.where(seen, 0.0, -HIDE)
        keys = k[window, :]
        values = v[window, :]
        queries = q[spot, :]
        parts, totals = [], []
        for half in range(2):
            scores = dot(only_half(queries, half), keys, NT) * EXP2_SCALE + bias
            highest = jnp.max(scores, axis=1, keepdims=True)
            weights = jnp.exp2(scores - highest)
            total = jnp.sum(weights, axis=1, keepdims=True)
            parts.append(dot(weights.astype(BF16), values, NN) / total)
            totals.append(highest + jnp.log2(total))
        out[spot, :] = jnp.where(in_half(parts[0].shape, 0), parts[0], parts[1]).astype(BF16)
        store_logs(logs, spot, totals)


def self_forward(pair, qkv, row_ids, col_ids):
    count = qkv.shape[0]
    pairs = qkv.shape[1] // (3 * PAIR)

    def part(which):
        return pl.BlockSpec((count, PAIR), lambda p: (0, which * pairs + pair))

    return pl.pallas_call(
        self_forward_kernel,
        grid=(1,),
        in_specs=[part(0), part(1), part(2), whole((8, count)), whole((count, 128))],
        out_specs=[whole((count, PAIR)), whole((8, count))],
        out_shape=[pltpu.HBM((count, PAIR), BF16), pltpu.HBM((8, count), F32)],
        compiler_params=params(),
        cost_estimate=cost(16 * count * SELF_WINDOW * PAIR, 8 * count * PAIR),
    )(qkv, qkv, qkv, row_ids, col_ids)


def self_backward_kernel(q, k, v, grad, logs, deltas, row_ids, col_ids, dq, dk, dv, key_sum, value_sum):
    count = q.shape[0]
    key_sum[...] = jnp.zeros_like(key_sum)
    value_sum[...] = jnp.zeros_like(value_sum)
    for tile in range(count // TILE):
        base = tile * TILE
        start = min(max(base - 256, 0), count - BACK_WINDOW)
        spot = slice(base, base + TILE)
        window = slice(start, start + BACK_WINDOW)
        seen = (col_ids[window, 0:1] == row_ids[0:1, spot]) & (
            col_ids[window, 1:2] <= row_ids[1:2, spot]
        )
        bias = jnp.where(seen, 0.0, -HIDE)
        keys = k[window, :]
        values = v[window, :]
        queries = q[spot, :]
        grads = grad[spot, :]
        parts = []
        for half in range(2):
            one_query = only_half(queries, half)
            one_grad = only_half(grads, half)
            scores = dot(keys, one_query, NT) * EXP2_SCALE + bias
            weights = jnp.exp2(scores - logs[half : half + 1, spot])
            slopes = dot(values, one_grad, NT)
            pushed = (weights * (slopes - deltas[half : half + 1, spot])).astype(BF16)
            value_sum[window, :] += dot(weights.astype(BF16), one_grad, NN)
            key_sum[window, :] += dot(pushed, one_query, NN)
            parts.append(dot(pushed, keys, TN))
        dq[spot, :] = (
            jnp.where(in_half(parts[0].shape, 0), parts[0], parts[1]) * SCALE
        ).astype(BF16)
    dk[...] = (key_sum[...] * SCALE).astype(BF16)
    dv[...] = value_sum[...].astype(BF16)


def self_backward(pair, qkv, grad, logs, deltas, row_ids, col_ids):
    count = qkv.shape[0]
    pairs = qkv.shape[1] // (3 * PAIR)

    def part(which):
        return pl.BlockSpec((count, PAIR), lambda p: (0, which * pairs + pair))

    return pl.pallas_call(
        self_backward_kernel,
        grid=(1,),
        in_specs=[
            part(0),
            part(1),
            part(2),
            part(0),
            whole((8, count)),
            pl.BlockSpec((8, count), lambda p: (pair, 0)),
            whole((8, count)),
            whole((count, 128)),
        ],
        out_specs=[whole((count, PAIR))] * 3,
        out_shape=[pltpu.HBM((count, PAIR), BF16)] * 3,
        scratch_shapes=[pltpu.VMEM((count, PAIR), F32)] * 2,
        compiler_params=params(),
        cost_estimate=cost(40 * count * BACK_WINDOW * PAIR, 16 * count * PAIR),
    )(qkv, qkv, qkv, grad, logs, deltas, row_ids, col_ids)


KEYS = 1024


def cross_forward_kernel(scalars, q, k, v, out, logs):
    step = pl.program_id(0)
    tile = scalars[step]
    image = scalars[8 + step]
    again = (step > 0) & (scalars[jnp.maximum(step - 1, 0)] == tile)

    @pl.when(step < scalars[16])
    def _():
        queries = q[...]
        parts, totals = [], []
        tops, sums = [None, None], [None, None]
        for start in range(0, k.shape[0], KEYS):
            keys = k[start : start + KEYS, :]
            values = v[start : start + KEYS, :]
            both = [dot(only_half(queries, half), keys, NT) for half in range(2)]
            for half, scores in enumerate(both):
                highest = jnp.max(scores, axis=1, keepdims=True) * EXP2_SCALE
                if start:
                    highest = jnp.maximum(highest, tops[half])
                weights = jnp.exp2(scores * EXP2_SCALE - highest).astype(BF16)
                mixed = dot(
                    weights,
                    jnp.where(in_half(values.shape, half), values, jnp.ones_like(values)),
                    NN,
                )
                if start:
                    mixed = mixed + sums[half] * jnp.exp2(tops[half] - highest)
                tops[half], sums[half] = highest, mixed
        for half in range(2):
            total = pltpu.roll(sums[half], HEAD_DIM, 1)
            parts.append(sums[half] / total)
            totals.append(tops[half] + jnp.log2(total))
        mixed = jnp.where(in_half(parts[0].shape, 0), parts[0], parts[1]).astype(BF16)
        limit = scalars[17] - tile * TILE
        row_mine = (
            lax.broadcasted_iota(jnp.int32, mixed.shape, 0) >= limit
        ) == (image == 1)
        lane_mine = (
            lax.broadcasted_iota(jnp.int32, (1, TILE), 1) >= limit
        ) == (image == 1)
        keep = jnp.logical_not(again)
        out[...] = jnp.where(row_mine | keep, mixed, out[...])
        store_logs(logs, slice(0, TILE), totals, lane_mine | keep)


def cross_forward(pair, scalars, q, keys_values, images):
    count, inner = q.shape
    pairs = inner // PAIR
    memory_rows = keys_values.shape[0] // images
    tile_spec = pl.BlockSpec((TILE, PAIR), lambda s, sc: (sc[s], 0))

    def part(which):
        return pl.BlockSpec((memory_rows, PAIR), lambda s, sc: (sc[8 + s], which * pairs + pair))

    return pl.pallas_call(
        cross_forward_kernel,
        grid_spec=pltpu.PrefetchScalarGridSpec(
            num_scalar_prefetch=1,
            grid=(count // TILE + 1,),
            in_specs=[
                pl.BlockSpec((TILE, PAIR), lambda s, sc: (sc[s], pair)),
                part(0),
                part(1),
            ],
            out_specs=[tile_spec, pl.BlockSpec((8, TILE), lambda s, sc: (0, sc[s]))],
        ),
        out_shape=[pltpu.HBM((count, PAIR), BF16), pltpu.HBM((8, count), F32)],
        compiler_params=params(),
        cost_estimate=cost(20 * count * memory_rows * PAIR, 8 * memory_rows * PAIR),
    )(scalars, *pin(q, keys_values, keys_values))


def cross_backward_kernel(
    image, scalars, q, k, v, grad, logs, deltas, old, dq, dk, dv, key_sum, value_sum
):
    step = pl.program_id(1)
    tile = cross_tile(image, scalars, step)

    @pl.when(step == 0)
    def _():
        key_sum[...] = jnp.zeros_like(key_sum)
        value_sum[...] = jnp.zeros_like(value_sum)

    @pl.when(step < scalars[20 if image else 18])
    def _():
        queries = q[...]
        grads = grad[...]
        keys = k[...]
        values = v[...]
        limit = scalars[17] - tile * TILE
        lane_mine = (lax.broadcasted_iota(jnp.int32, (1, TILE), 1) >= limit) == (image == 1)
        parts = []
        for half in range(2):
            one_query = only_half(queries, half)
            one_grad = only_half(grads, half)
            log = jnp.where(lane_mine, logs[half : half + 1, :], HIDE)
            scores = dot(keys, one_query, NT)
            weights = jnp.exp2(scores * EXP2_SCALE - log)
            slopes = dot(values, one_grad, NT)
            pushed = (weights * (slopes - deltas[half : half + 1, :])).astype(BF16)
            value_sum[...] += dot(weights.astype(BF16), one_grad, NN)
            key_sum[...] += dot(pushed, one_query, NN)
            parts.append(dot(pushed, keys, TN))
        grad_query = (
            jnp.where(in_half(parts[0].shape, 0), parts[0], parts[1]) * SCALE
        ).astype(BF16)
        if image:
            row_mine = lax.broadcasted_iota(jnp.int32, grad_query.shape, 0) >= limit
            grad_query = jnp.where(row_mine, grad_query, old[...])
        dq[...] = grad_query

    @pl.when(step == pl.num_programs(1) - 1)
    def _():
        dk[...] = (key_sum[...] * SCALE).astype(BF16)
        dv[...] = value_sum[...].astype(BF16)


def cross_tile(image, scalars, step):
    if image:
        return scalars[19] + jnp.minimum(step, scalars[20] - 1)
    return jnp.minimum(step, scalars[18] - 1)


def cross_backward(image, scalars, q, keys_values, grad, logs, deltas, images, old):
    count, inner = q.shape
    pairs = inner // PAIR
    memory_rows = keys_values.shape[0] // images
    tile_spec = pl.BlockSpec((TILE, PAIR), lambda p, s, sc: (cross_tile(image, sc, s), p))
    line = pl.BlockSpec((8, TILE), lambda p, s, sc: (p, cross_tile(image, sc, s)))
    result = pl.BlockSpec((memory_rows, PAIR), lambda p, s, sc: (0, p))

    def part(which):
        return pl.BlockSpec((memory_rows, PAIR), lambda p, s, sc: (image, which * pairs + p))

    def first_kernel(scalars, q, k, v, grad, logs, deltas, *rest):
        cross_backward_kernel(image, scalars, q, k, v, grad, logs, deltas, None, *rest)

    def second_kernel(*refs):
        cross_backward_kernel(image, *refs)

    extra = [old] if image else []
    return pl.pallas_call(
        second_kernel if image else first_kernel,
        grid_spec=pltpu.PrefetchScalarGridSpec(
            num_scalar_prefetch=1,
            grid=(pairs, count // TILE),
            in_specs=[tile_spec, part(0), part(1), tile_spec, line, line]
            + [tile_spec] * len(extra),
            out_specs=[tile_spec, result, result],
            scratch_shapes=[pltpu.VMEM((memory_rows, PAIR), F32)] * 2,
        ),
        out_shape=[
            pltpu.HBM((count, inner), BF16),
            pltpu.HBM((memory_rows, inner), BF16),
            pltpu.HBM((memory_rows, inner), BF16),
        ],
        input_output_aliases={7: 0} if image else {},
        compiler_params=params(),
        cost_estimate=cost(25 * count * memory_rows * inner, 8 * memory_rows * inner),
    )(scalars, *pin(q, keys_values, keys_values, grad), logs, deltas, *pin(*extra))


def put_rows(places, product, keep, send):
    height = product.shape[0] // 4
    for i, ref in enumerate((keep, keep, send, send)):
        start = pl.multiple_of(places[i] * height, 16)
        ref[i % 2, 0:height, :] = product[pl.ds(start, height), :].astype(BF16)


def memory_back_kernel(
    columns, last, places, memory, dk, dv, w0, w1, w2, w3, *refs
):
    if last:
        before, keep_part, send_part, keep, send, weight, total, sems = refs
    else:
        keep_part, send_part, total_out, weight, total, sems = refs
    inner = dk.shape[1]

    @pl.when(pl.program_id(0) == 0)
    def _():
        copies = fetch((w0, w1, w2, w3), places, columns, weight, sems)
        start_all(copies)
        if last:
            total[...] = before[...]
        else:
            total[...] = jnp.zeros_like(total)
        wait_all(copies)

    both = jnp.concatenate([dk[...], dv[...]], axis=1)
    side = places[4]
    mine = weight[pl.ds(pl.multiple_of(side * inner, 16), inner), :]
    theirs = weight[pl.ds(pl.multiple_of((1 - side) * inner, 16), inner), :]
    send_part[...] = dot(both, theirs, NT).astype(BF16)
    keep_part[...] = dot(both, mine, NT).astype(BF16)
    total[...] += dot(memory[...], both, TN)

    @pl.when(pl.program_id(0) == pl.num_programs(0) - 1)
    def _():
        if last:
            put_rows(places, total, keep, send)
        else:
            total_out[...] = total[...]


def memory_back(places, memory, dk, dv, pieces, columns, image, before, spare):
    count, inner = dk.shape
    width = memory.shape[1]
    steps = count // MEMORY_TILE
    last = before is not None
    ranks = pltpu.HBM((2, width // 4, spare + 2 * inner), BF16)
    rank_spec = pl.BlockSpec((2, width // 4, 2 * inner), lambda t: (0, 0, 0))

    def kernel(*refs):
        memory_back_kernel(columns, last, *refs)

    return pl.pallas_call(
        kernel,
        grid=(steps,),
        in_specs=[
            SCALARS,
            pl.BlockSpec((MEMORY_TILE, width), lambda t: (image * steps + t, 0)),
            rows(inner, MEMORY_TILE),
            rows(inner, MEMORY_TILE),
        ]
        + [ANY] * 4
        + ([whole((width, 2 * inner))] if last else []),
        out_specs=[rows(inner, MEMORY_TILE), rows(inner, MEMORY_TILE)]
        + ([rank_spec, rank_spec] if last else [whole((width, 2 * inner))]),
        out_shape=[pltpu.HBM((count, inner), BF16)] * 2
        + ([ranks, ranks] if last else [shape_of((width, 2 * inner), F32)]),
        scratch_shapes=[
            pltpu.VMEM((width, 2 * inner), BF16),
            pltpu.VMEM((width, 2 * inner), F32),
            pltpu.SemaphoreType.DMA((4,)),
        ],
        compiler_params=params(),
        cost_estimate=cost(8 * count * width * inner, 8 * count * width),
    )(places, *pin(memory, dk, dv), *pieces, *([before] if last else []))


def weight_grads_kernel(plan, spans, places, left_refs, right_refs, keep, send, scratch):
    left_holds = scratch[: len(left_refs)]
    right_holds = scratch[len(left_refs) : -2]
    turned, sems = scratch[-2:]
    height = turned.shape[0] // 4
    step = pl.program_id(0)
    lefts = [
        pltpu.make_async_copy(ref, hold, sems.at[i])
        for i, (ref, hold) in enumerate(zip(left_refs, left_holds))
    ]
    rights = [
        pltpu.make_async_copy(ref, hold, sems.at[len(left_refs) + i])
        for i, (ref, hold) in enumerate(zip(right_refs, right_holds))
    ]
    for at, (left, group) in enumerate(plan):
        fresh = at == 0 or plan[at - 1][0] != left

        @pl.when(step == at)
        def _():
            if at == 0:
                seen = set()
                for one, others in plan:
                    if one not in seen:
                        lefts[one].start()
                        seen.add(one)
                    for g in others:
                        rights[g].start()
            if fresh:
                lefts[left].wait()
                turned[...] = left_holds[left][...].T
            for g in group:
                rights[g].wait()
            right = join([right_holds[g] for g in group])
            for i, ref in enumerate((keep, keep, send, send)):
                start = pl.multiple_of(places[i] * height, 16)
                ref[i % 2, 0:height, spans[at]] = dot(
                    turned[pl.ds(start, height), :], right, NN
                ).astype(BF16)


def join(refs):
    values = [ref[...] for ref in refs]
    return values[0] if len(values) == 1 else jnp.concatenate(values, axis=1)


def flatten(groups):
    flat, sizes = [], []
    for group in groups:
        group = group if isinstance(group, (list, tuple)) else [group]
        flat += list(group)
        sizes.append(len(group))
    return flat, sizes


def weight_grads(places, lefts, rights, plan, into=(), first=0):
    count, width = lefts[0].shape
    flat, sizes = flatten(rights)
    groups, at = [], 0
    for size in sizes:
        groups.append(list(range(at, at + size)))
        at += size
    plan = [(left, [f for g in group for f in groups[g]]) for left, group in plan]
    columns = [sum(flat[f].shape[1] for f in group) for _, group in plan]
    step_columns = columns[0]
    share = width // 4
    total = sum(columns) + first * step_columns
    even = len(set(columns)) == 1
    spans = [
        slice(0, step_columns) if even else slice(sum(columns[:at]), sum(columns[: at + 1]))
        for at in range(len(plan))
    ]
    extra = list(into)
    def kernel(places, *refs):
        lefts_end = len(lefts)
        rights_end = lefts_end + len(flat)
        weight_grads_kernel(
            plan,
            spans,
            places,
            refs[:lefts_end],
            refs[lefts_end:rights_end],
            *refs[rights_end + len(extra) : rights_end + len(extra) + 2],
            refs[rights_end + len(extra) + 2 :],
        )

    start = 1 + len(lefts) + len(flat)
    return pl.pallas_call(
        kernel,
        grid=(len(plan),),
        in_specs=[SCALARS]
        + [ANY] * (len(lefts) + len(flat) + len(extra)),
        out_specs=[
            pl.BlockSpec((2, share, step_columns), lambda t: (0, 0, t + first))
            if even
            else whole((2, share, total))
        ]
        * 2,
        out_shape=[pltpu.HBM((2, share, total), BF16)] * 2,
        input_output_aliases={start: 0, start + 1: 1} if extra else {},
        scratch_shapes=[pltpu.VMEM(array.shape, array.dtype) for array in list(lefts) + flat]
        + [
            pltpu.VMEM((width, count), BF16),
            pltpu.SemaphoreType.DMA((len(lefts) + len(flat),)),
        ],
        compiler_params=params(),
        cost_estimate=cost(
            2 * count * width * sum(columns), 4 * count * width * len(plan)
        ),
    )(places, *pin(*lefts, *flat), *extra)


def middle_kernel(plan, parts, places, x, gain, *refs):
    mine, theirs, refs = refs[:parts], refs[parts : 2 * parts], refs[2 * parts :]
    pieces, (h1, n2, cq, out_mine, out_theirs, query, sems) = refs[:8], refs[8:]

    @pl.when(pl.program_id(0) == 0)
    def _():
        copies = (
            fetch(pieces[:4], places, plan[0], out_mine, sems, 0)
            + fetch(pieces[4:], places, plan[1], out_theirs, sems, 4)
            + fetch(pieces[:4], places, plan[2], query, sems, 8)
        )
        start_all(copies)
        wait_all(copies)

    values = (
        x[...].astype(F32)
        + dot(join(mine), out_mine[...], NT)
        + dot(join(theirs), out_theirs[...], NT)
    )
    h1[...] = values.astype(BF16)
    normed = (values * inverse_rms(values) * gain[...]).astype(BF16)
    n2[...] = normed
    cq[...] = dot(normed, query[...], NN).astype(BF16)


def middle_step(places, x, mine, theirs, gain, pieces, pieces_theirs, plan):
    count, width = x.shape
    half = sum(part.shape[1] for part in mine)

    def kernel(*refs):
        middle_kernel(plan, len(mine), *refs)

    return pl.pallas_call(
        kernel,
        grid=(count // ROWS,),
        in_specs=[SCALARS, rows(width), whole((1, width))]
        + [rows(PAIR)] * (2 * len(mine))
        + [ANY] * 8,
        out_specs=[rows(width), rows(width), rows(half)],
        out_shape=[
            pltpu.HBM((count, width), BF16),
            pltpu.HBM((count, width), BF16),
            pltpu.HBM((count, half), BF16),
        ],
        scratch_shapes=[pltpu.VMEM((width, half), BF16)] * 3 + [pltpu.SemaphoreType.DMA((12,))],
        compiler_params=params(),
        cost_estimate=cost(6 * count * width * half, 12 * count * width),
    )(places, *pin(x), gain, *pin(*mine), *theirs, *pieces, *pieces_theirs)


def head_sums(left, right):
    product = left.astype(F32) * right.astype(F32)
    width = product.shape[1]
    high = product.astype(BF16)
    low = (product - high.astype(F32)).astype(BF16)
    height = 8 * (width // PAIR)
    line = lax.broadcasted_iota(jnp.int32, (height, width), 0)
    head = lax.broadcasted_iota(jnp.int32, (height, width), 1) // HEAD_DIM
    choose = (
        ((line // 8) * 2 + line % 8 == head) & (line % 8 < 2)
    ).astype(F32).astype(BF16)
    return dot(choose, high, NT) + dot(choose, low, NT)


CHUNK = 512


def units_kernel(plan, parts, places, h1, gain, gy, *refs):
    mine, theirs, refs = refs[:parts], refs[parts : 2 * parts], refs[2 * parts :]
    late, refs = refs[0], refs[1:]
    (
        output,
        n3,
        hidden,
        grad_gate,
        grad_up,
        e2,
        dc,
        deltas,
        gain_grad,
        out_mine,
        out_theirs,
        units_mine,
        units_theirs,
        sems,
    ) = refs
    step = pl.program_id(0)

    side = places[4]
    out_copies = [
        fetch_half(late, side, plan[0], out_mine, sems.at[0]),
        fetch_half(late, 1 - side, plan[0], out_theirs, sems.at[1]),
    ]
    mine_copy = fetch_half(late, side, plan[1], units_mine, sems.at[2])
    theirs_copy = fetch_half(late, 1 - side, plan[1], units_theirs, sems.at[3])

    @pl.when(step == 0)
    def _():
        start_all(out_copies + [mine_copy, theirs_copy])
        gain_grad[...] = jnp.zeros_like(gain_grad)
        wait_all(out_copies)

    crossed_mine = join(mine)
    values = (
        h1[...].astype(F32)
        + dot(crossed_mine, out_mine[...], NT)
        + dot(join(theirs), out_theirs[...], NT)
    )
    normed = (values * inverse_rms(values) * gain[...]).astype(BF16)
    n3[...] = normed
    upstream = gy[...]
    mixed = jnp.zeros_like(values)
    back = jnp.zeros_like(values)
    unit = units_mine.shape[1] // 3
    for own in (True, False):
        weight = units_mine if own else units_theirs

        @pl.when(step == 0)
        def _():
            (mine_copy if own else theirs_copy).wait()

        for start in range(0, unit, CHUNK):
            gate_weight = weight[:, start : start + CHUNK]
            up_weight = weight[:, unit + start : unit + start + CHUNK]
            down_weight = weight[:, 2 * unit + start : 2 * unit + start + CHUNK]
            gate = dot(normed, gate_weight, NN)
            up = dot(normed, up_weight, NN)
            pushed = dot(upstream, down_weight, NN)
            square = gate * gate
            bend = jnp.tanh(ROOT_TWO_OVER_PI * gate * (1.0 + CUBIC * square))
            lift = 0.5 * (1.0 + bend)
            gelu = gate * lift
            slope = lift + (0.5 * ROOT_TWO_OVER_PI) * gate * (1.0 - bend * bend) * (
                1.0 + (3.0 * CUBIC) * square
            )
            units = (gelu * up).astype(BF16)
            push_gate = (pushed * up * slope).astype(BF16)
            push_up = (pushed * gelu).astype(BF16)
            mixed = mixed + dot(units, down_weight, NT)
            back = back + dot(push_gate, gate_weight, NT) + dot(push_up, up_weight, NT)
            if own:
                hidden[:, start : start + CHUNK] = units
                grad_gate[:, start : start + CHUNK] = push_gate
                grad_up[:, start : start + CHUNK] = push_up
    output[...] = (values + mixed).astype(BF16)
    grad, gain_part = norm_back(values, gain[...], back)
    low = (upstream.astype(F32) + grad).astype(BF16)
    e2[...] = low
    crossed = dot(low, out_mine[...], NN).astype(BF16)
    dc[...] = crossed
    deltas[...] = head_sums(crossed, crossed_mine)
    gain_grad[0:1, :] += gain_part


def units_step(places, h1, mine, theirs, gain, gy, late, plan):
    count, width = h1.shape
    half = sum(part.shape[1] for part in mine)
    unit = (plan[1].stop - plan[1].start) // 3
    lines = 8 * (half // PAIR)

    def kernel(*refs):
        units_kernel(plan, len(mine), *refs)

    return pl.pallas_call(
        kernel,
        grid=(count // ROWS,),
        in_specs=[
            SCALARS,
            rows(width),
            whole((1, width)),
            rows(width),
        ]
        + [rows(PAIR)] * (2 * len(mine))
        + [ANY],
        out_specs=[
            rows(width),
            rows(width),
            rows(unit),
            rows(unit),
            rows(unit),
            rows(width),
            rows(half),
            pl.BlockSpec((lines, ROWS), lambda t: (0, t)),
            whole((8, width)),
        ],
        out_shape=[
            pltpu.HBM((count, width), BF16),
            pltpu.HBM((count, width), BF16),
            pltpu.HBM((count, unit), BF16),
            pltpu.HBM((count, unit), BF16),
            pltpu.HBM((count, unit), BF16),
            pltpu.HBM((count, width), BF16),
            pltpu.HBM((count, half), BF16),
            pltpu.HBM((lines, count), F32),
            shape_of((8, width), F32),
        ],
        scratch_shapes=[pltpu.VMEM((width, half), BF16)] * 2
        + [pltpu.VMEM((width, 3 * unit), BF16)] * 2
        + [pltpu.SemaphoreType.DMA((4,))],
        compiler_params=params(58),
        cost_estimate=cost(30 * count * width * unit, 30 * count * width),
    )(places, *pin(h1), gain, *pin(gy, *mine), *theirs, *pin(late))


def turn_kernel(plan, parts, places, e2, h1, mine, theirs, gain, *refs):
    attended, refs = refs[:parts], refs[parts:]
    pieces, refs = refs[:4], refs[4:]
    late, e1, da, deltas, gain_grad, query_mine, query_theirs, out_mine, sems = refs

    @pl.when(pl.program_id(0) == 0)
    def _():
        copies = (
            fetch(pieces, places, plan[0], out_mine, sems, 0)
            + fetch(pieces, places, plan[1], query_mine, sems, 4)
            + [fetch_half(late, 1 - places[4], plan[2], query_theirs, sems.at[8])]
        )
        start_all(copies)
        gain_grad[...] = jnp.zeros_like(gain_grad)
        wait_all(copies)

    back = dot(mine[...], query_mine[...], NT) + dot(theirs[...], query_theirs[...], NT)
    grad, gain_part = norm_back(h1[...].astype(F32), gain[...], back)
    low = (e2[...].astype(F32) + grad).astype(BF16)
    e1[...] = low
    pushed = dot(low, out_mine[...], NN).astype(BF16)
    da[...] = pushed
    deltas[...] = head_sums(pushed, join(attended))
    gain_grad[0:1, :] += gain_part


def turn_step(places, e2, h1, mine, theirs, gain, attended, pieces, late, plan):
    count, width = h1.shape
    half = mine.shape[1]
    lines = 8 * (half // PAIR)

    def kernel(*refs):
        turn_kernel(plan, len(attended), *refs)

    return pl.pallas_call(
        kernel,
        grid=(count // ROWS,),
        in_specs=[
            SCALARS,
            rows(width),
            rows(width),
            rows(half),
            rows(half),
            whole((1, width)),
        ]
        + [rows(PAIR)] * len(attended)
        + [ANY] * 5,
        out_specs=[
            rows(width),
            rows(half),
            pl.BlockSpec((lines, ROWS), lambda t: (0, t)),
            whole((8, width)),
        ],
        out_shape=[
            pltpu.HBM((count, width), BF16),
            shape_of((count, half), BF16),
            shape_of((lines, count), F32),
            shape_of((8, width), F32),
        ],
        scratch_shapes=[pltpu.VMEM((width, half), BF16)] * 3 + [pltpu.SemaphoreType.DMA((9,))],
        compiler_params=params(),
        cost_estimate=cost(6 * count * width * half, 16 * count * width),
    )(places, *pin(e2, h1, mine), theirs, gain, *pin(*attended), *pieces, *pin(late))


def partial_kernel(parts, places, x, n1, second, third, *refs):
    part_refs, refs = refs[:parts], refs[parts:]
    w0, w1, w2, w3, out, keep, send, weight, total, gain_grad, sems = refs
    step = pl.program_id(0)

    @pl.when(step == 0)
    def _():
        copies = fetch((w0, w1, w2, w3), places, slice(0, weight.shape[1]), weight, sems)
        start_all(copies)
        gain_grad[...] = jnp.zeros_like(gain_grad)
        total[...] = jnp.zeros_like(total)
        wait_all(copies)

    back = dot(join(part_refs), weight[...], NT)
    out[...] = back.astype(BF16)
    values = x[...].astype(F32)
    gain_grad[0:1, :] += jnp.sum(back * values * inverse_rms(values), axis=0, keepdims=True)
    last = join([part_refs[i * (parts // 3) + parts // 3 - 1] for i in range(3)])
    total[...] += dot(n1[...], last, TN)

    @pl.when(step == pl.num_programs(0) - 1)
    def _():
        put_rows(places, total, keep, send)
        height = total.shape[0] // 4
        lines = jnp.concatenate(
            [
                gain_grad[0:1, :],
                second[0:1, :],
                third[0:1, :],
                jnp.zeros((13, gain_grad.shape[1]), F32),
            ],
            axis=0,
        )
        shares = [lines[:, w * height : (w + 1) * height] for w in range(4)]
        fill = jnp.zeros((16, total.shape[1] - height), F32)
        for i, ref in enumerate((keep, keep, send, send)):
            share = shares[0]
            for w in range(1, 4):
                share = jnp.where(places[i] == w, shares[w], share)
            ref[i % 2, height : height + 16, :] = jnp.concatenate([share, fill], axis=1).astype(
                BF16
            )


def partial_step(places, parts, x, n1, second, third, pieces):
    count, width = x.shape
    inner = sum(part.shape[1] for part in parts)
    ranks = (2, width // 4 + 16, 3 * PAIR)

    def kernel(*refs):
        partial_kernel(len(parts), *refs)

    return pl.pallas_call(
        kernel,
        grid=(count // ROWS,),
        in_specs=[SCALARS, rows(width), rows(width), whole((8, width)), whole((8, width))]
        + [rows(PAIR)] * len(parts)
        + [ANY] * 4,
        out_specs=[rows(width), whole(ranks), whole(ranks)],
        out_shape=[
            pltpu.HBM((count, width), BF16),
            shape_of(ranks, BF16),
            shape_of(ranks, BF16),
        ],
        scratch_shapes=[
            pltpu.VMEM((width, inner), BF16),
            pltpu.VMEM((width, 3 * PAIR), F32),
            pltpu.VMEM((8, width), F32),
            pltpu.SemaphoreType.DMA((4,)),
        ],
        compiler_params=params(),
        cost_estimate=cost(2 * count * width * (inner + 3 * PAIR), 8 * count * width),
    )(places, *pin(x, n1), second, third, *pin(*parts), *pieces)


def first_kernel(e1, x, mine, theirs, gain, out):
    back = mine[...].astype(F32) + theirs[...].astype(F32)
    grad, _ = norm_back(x[...].astype(F32), gain[...], back)
    out[...] = (e1[...].astype(F32) + grad).astype(BF16)


def first_step(e1, x, mine, theirs, gain):
    count, width = x.shape
    return pl.pallas_call(
        first_kernel,
        grid=(count // ROWS,),
        in_specs=[rows(width)] * 4 + [whole((1, width))],
        out_specs=rows(width),
        out_shape=pltpu.HBM((count, width), BF16),
        compiler_params=params(),
        cost_estimate=cost(20 * count * width, 12 * count * width),
    )(*pin(e1, x, mine), theirs, gain)


def swap(values, axis, distance):
    size = lax.axis_size(axis)
    return lax.ppermute(values, axis, [(i, i ^ distance) for i in range(size)])


def after(values, *others):
    return lax.optimization_barrier((values,) + others)[0]


def gather_all(values):
    return lax.all_gather(values, ("narrow", "wide"), axis=0, tiled=True).reshape(
        lax.axis_size("narrow"), -1, values.shape[1]
    )


def sum_wide(values):
    return lax.psum_scatter(values, "wide", scatter_dimension=0, tiled=True)


def add(left, right):
    return (left.astype(F32) + right.astype(F32)).astype(BF16)


def add_pair(keep, got):
    return add(keep[0], got[0]), add(keep[1], got[1])


def line_inner():
    place = lax.axis_index("dp")
    return (place == 1) | (place == 2)


def line_first(values):
    if lax.axis_size("dp") != 4:
        return lax.psum(values, "dp")
    got = lax.ppermute(values, "dp", [(0, 1), (3, 2)])
    return jnp.where(line_inner(), add(values, got), values)


def line_second(values):
    if lax.axis_size("dp") != 4:
        return values
    return add(values, lax.ppermute(values, "dp", [(1, 2), (2, 1)]))


def line_third(values, *others):
    if lax.axis_size("dp") != 4:
        return values
    got = after(lax.ppermute(values, "dp", [(1, 0), (2, 3)]), *others)
    return jnp.where(line_inner(), values, got)


def local(
    tokens,
    memory,
    cotangent,
    norm1_gain,
    norm2_gain,
    norm3_gain,
    q_weight,
    k_weight,
    v_weight,
    o_weight,
    cross_q,
    cross_k,
    cross_v,
    cross_o,
    gate_weight,
    up_weight,
    down_weight,
    segment_ids,
    block_ids,
    image_table,
):
    width = tokens.shape[1]
    share = q_weight.shape[0]
    inner = q_weight.shape[1]
    unit = gate_weight.shape[1]
    images = memory.shape[0]
    flat_memory = memory.reshape(-1, width)
    place = lax.axis_index("wide")
    side = lax.axis_index("narrow")
    places = jnp.stack([place, place ^ 2, place ^ 1, place ^ 3, side]).astype(jnp.int32)

    gains = jnp.stack([norm1_gain, norm2_gain, norm3_gain])
    gains = jnp.pad(gains, ((0, 13), (0, 3 * inner - share)))
    early = jnp.concatenate(
        [jnp.concatenate([q_weight, k_weight, v_weight], axis=1), gains], axis=0
    )
    early_x = swap(early, "wide", 2)
    early_pieces = (early, early_x, swap(early, "wide", 1), swap(early_x, "wide", 1))
    lines = jnp.stack([piece[share : share + 3, :share] for piece in early_pieces])
    lines = lines.astype(F32)
    order = [
        jnp.sum(jnp.where((places[:4] == w)[:, None, None], lines, 0.0), axis=0)
        for w in range(4)
    ]
    all_gains = jnp.concatenate(order, axis=1)[:, None, :]

    mid = jnp.concatenate([cross_k, cross_v, cross_q, o_weight], axis=1)
    memory_columns = slice(0, 2 * inner)
    query_columns = slice(2 * inner, 3 * inner)
    out_columns = slice(3 * inner, 4 * inner)
    mid_x = swap(mid, "wide", 2)
    mid_core = swap(mid, "wide", 1)
    out_y = swap(o_weight, "narrow", 1)
    late = jnp.concatenate([cross_q, cross_o, gate_weight, up_weight, down_weight], axis=1)
    late_query_columns = slice(0, inner)
    late_columns = (slice(inner, 2 * inner), slice(2 * inner, 2 * inner + 3 * unit))

    x, gy, row_ids, col_ids, pos, scalars = order_rows(
        segment_ids, block_ids, image_table, tokens, cotangent
    )
    late = gather_all(after(late, early_x, x))
    n1, qkv = norm_project(places, x, all_gains[0], early_pieces)
    pairs = inner // PAIR
    self_parts = [self_forward(0, after(qkv, out_y, mid_core), row_ids, col_ids)]
    for pair in range(1, pairs):
        self_parts.append(
            self_forward(pair, after(qkv, self_parts[-1][0]), row_ids, col_ids)
        )
    mid_x = after(mid_x, self_parts[-2][0])
    mid_pieces = (mid, mid_x, mid_core, swap(mid_x, "wide", 1))
    out_xy = swap(mid_x[:, out_columns], "narrow", 1)
    out_pieces = (out_y, out_xy, swap(out_y, "wide", 1), swap(out_xy, "wide", 1))
    attended_theirs = [swap(part[0], "narrow", 1) for part in self_parts]
    attended = [part[0] for part in self_parts]
    keys_values = project_memory(
        places,
        after(flat_memory, self_parts[-1][0], attended_theirs[0]),
        mid_pieces,
        memory_columns,
    )
    h1, n2, cq = middle_step(
        places,
        after(x, keys_values),
        attended,
        attended_theirs,
        all_gains[1],
        mid_pieces,
        out_pieces,
        (out_columns, slice(0, inner), query_columns),
    )
    cross_parts = [cross_forward(0, scalars, cq, keys_values, images)]
    crossed_theirs = []
    for pair in range(1, pairs):
        previous = [cross_parts[-1][0]] + crossed_theirs
        crossed_theirs.append(swap(cross_parts[-1][0], "narrow", 1))
        cross_parts.append(
            cross_forward(pair, scalars, after(cq, *previous), keys_values, images)
        )
    crossed = [part[0] for part in cross_parts]
    crossed_theirs.append(swap(crossed[-1], "narrow", 1))
    cross_logs = jnp.concatenate([part[1] for part in cross_parts], axis=0)
    (
        output,
        n3,
        hidden,
        grad_gate,
        grad_up,
        e2,
        dc,
        cross_deltas,
        third_gain,
    ) = units_step(
        places,
        h1,
        crossed,
        crossed_theirs,
        all_gains[2],
        gy,
        late,
        late_columns,
    )

    unit_keep, unit_send = weight_grads(
        places, (n3, gy), (grad_gate, grad_up, hidden), ((0, (0,)), (0, (1,)), (1, (2,)))
    )
    unit_stay, unit_leave = add_pair(unit_keep, swap(unit_send, "wide", 1))
    dcq, dck, dcv = cross_backward(
        0,
        scalars,
        cq,
        keys_values,
        after(dc, unit_leave),
        cross_logs,
        cross_deltas,
        images,
        None,
    )
    unit_part = add(unit_stay, swap(unit_leave, "wide", 2))
    keep0, send0, total = memory_back(
        places,
        flat_memory,
        after(dck, unit_part),
        dcv,
        mid_pieces,
        memory_columns,
        0,
        None,
        0,
    )
    unit_sum = lax.psum(unit_part, "dp")
    dcq, dck, dcv = cross_backward(
        1,
        scalars,
        cq,
        keys_values,
        after(dc, send0),
        cross_logs,
        cross_deltas,
        images,
        dcq,
    )
    dcq_theirs = swap(dcq, "narrow", 1)
    memory0 = add(keep0, swap(send0, "narrow", 1))
    keep1, send1, cross_keep, cross_send = memory_back(
        places,
        flat_memory,
        after(dck, memory0),
        dcv,
        mid_pieces,
        memory_columns,
        1,
        total,
        2 * inner,
    )
    cross_keep, cross_send = weight_grads(
        places,
        (after(n2, send1), e2),
        (dcq, crossed),
        ((0, (0,)), (1, (1,))),
        into=(cross_keep, cross_send),
        first=2,
    )
    e1, da, self_deltas, second_gain = turn_step(
        places,
        e2,
        h1,
        after(dcq, cross_send, unit_sum),
        dcq_theirs,
        all_gains[1],
        attended,
        mid_pieces,
        late,
        (out_columns, query_columns, late_query_columns),
    )
    memory1 = add(keep1, swap(after(send1, dcq_theirs), "narrow", 1))
    cross_stay, cross_leave = add_pair(cross_keep, swap(cross_send, "wide", 1))
    da = after(da, cross_leave)
    back = []
    for pair in range(pairs):
        ready = after(da, *[part[0] for part in back])
        if pair == pairs - 1:
            early_back = list(back)
            self_keep, self_send = weight_grads(
                places,
                (after(n1, back[-1][0]), e1),
                [[part[i] for part in early_back] for i in range(3)] + [attended],
                ((0, (0, 1, 2)), (1, (3,))),
            )
            cross_part = add(cross_stay, swap(cross_leave, "wide", 2))
            ready = after(ready, cross_part, self_send)
            cross_part = line_first(cross_part)
        back.append(
            self_backward(
                pair, qkv, ready, self_parts[pair][1], self_deltas, row_ids, col_ids
            )
        )
    dq, dk, dv = [[part[i] for part in back] for i in range(3)]
    self_stay, self_leave = add_pair(self_keep, swap(self_send, "wide", 1))
    self_part = add(self_stay, swap(self_leave, "wide", 2))
    dn1, last_keep, last_send = partial_step(
        places,
        dq + dk + dv,
        after(x, memory1, self_leave),
        n1,
        second_gain,
        third_gain,
        early_pieces,
    )
    dn1_theirs = swap(dn1, "narrow", 1)
    last_stay, last_leave = add_pair(last_keep, swap(last_send, "wide", 1))
    last_part = add(last_stay, swap(last_leave, "wide", 2))
    output = restore_rows(pos, after(output, last_send, self_part))
    ready = first_step(e1, x, dn1, dn1_theirs, all_gains[0])
    tokens_grad = restore_rows(pos, ready)
    memory_grad = jnp.stack([after(memory0, self_part), memory1])
    cross_sum = line_third(line_second(cross_part), ready)
    self_sum = line_third(line_second(line_first(self_part)), ready)
    last_sum = line_third(line_second(line_first(last_part)))
    gain_sums = last_sum[share:, :share].astype(F32)
    first_gain = gain_sums[0] + swap(gain_sums, "narrow", 1)[0]

    def grads(array, size, count):
        return [array[:share, i * size : (i + 1) * size].astype(F32) for i in range(count)]

    gate_grad, up_grad, down_grad = grads(after(unit_sum, self_part), unit, 3)
    cross_k_grad, cross_v_grad, cross_q_grad, cross_o_grad = grads(cross_sum, inner, 4)
    part = inner - PAIR
    q_grad, k_grad, v_grad = [
        jnp.concatenate([most, rest], axis=1)
        for most, rest in zip(grads(self_sum, part, 3), grads(last_sum, PAIR, 3))
    ]
    o_grad = self_sum[:, 3 * part :].astype(F32)
    return (
        output,
        tokens_grad,
        memory_grad,
        first_gain,
        gain_sums[1],
        gain_sums[2],
        q_grad,
        k_grad,
        v_grad,
        o_grad,
        cross_q_grad,
        cross_k_grad,
        cross_v_grad,
        cross_o_grad,
        gate_grad,
        up_grad,
        down_grad,
    )


def solution(mesh):
    both = ("dp", "wide")
    weight = P("wide", "narrow")
    in_specs = (
        (P(both, None), P(both, None, None), P(both, None))
        + (P("wide"),) * 3
        + (weight,) * 11
        + (P(both, None),) * 3
    )
    out_specs = (
        (P(both, None), P(both, None), P(both, None, "narrow"))
        + (P("wide"),) * 3
        + (weight,) * 11
    )
    return jax.shard_map(local, mesh=mesh, in_specs=in_specs, out_specs=out_specs, check_vma=False)
```

```python
import functools
import math

import jax
import jax.numpy as jnp
from jax import lax
from jax.experimental import pallas as pl
from jax.experimental.pallas import tpu as pltpu
from jax.sharding import PartitionSpec as P

F32 = jnp.float32
BF16 = jnp.bfloat16
EPSILON = 1e-06
ROOT_TWO_OVER_PI = 0.7978845608028654
CUBIC = 0.044715
HEAD_DIM = 64
PAIR = 2 * HEAD_DIM
SCALE = HEAD_DIM ** (-0.5)
EXP2_SCALE = SCALE * math.log2(math.e)
HIDE = 1e30
TILE = 256
ROWS = 512
WEIGH = 4.0

NN = (((1,), (0,)), ((), ()))
NT = (((1,), (1,)), ((), ()))
TN = (((0,), (0,)), ((), ()))


def dot(left, right, dims):
    return lax.dot_general(left, right, dims, preferred_element_type=F32)


def params(mebibytes=24):
    return pltpu.CompilerParams(vmem_limit_bytes=mebibytes * 1024 * 1024)


def cost(flops, nbytes):
    return pl.CostEstimate(
        flops=int(flops * WEIGH), bytes_accessed=int(nbytes * WEIGH), transcendentals=0
    )


def pin(*arrays):
    return [pltpu.with_memory_space_constraint(array, pltpu.HBM) for array in arrays]


def shape_of(shape, dtype):
    return jax.ShapeDtypeStruct(shape, dtype)


def whole(shape):
    zeros = (0,) * len(shape)
    return pl.BlockSpec(shape, lambda *_: zeros)


def rows(width, height=None):
    height = ROWS if height is None else height
    return pl.BlockSpec((height, width), lambda t, *_: (t, 0))


def inverse_rms(values):
    return lax.rsqrt(jnp.mean(values * values, axis=1, keepdims=True) + EPSILON)


def norm_back(values, gain, upstream):
    factor = inverse_rms(values)
    scaled = upstream * gain
    mean = jnp.mean(values * scaled, axis=1, keepdims=True)
    grad = factor * scaled - values * (factor * factor * factor * mean)
    return grad, jnp.sum(upstream * values * factor, axis=0, keepdims=True)


def in_half(shape, half):
    return (lax.broadcasted_iota(jnp.int32, shape, 1) // HEAD_DIM) == half


def only_half(values, half):
    return jnp.where(in_half(values.shape, half), values, jnp.zeros_like(values))


def order_kernel(seg, blk, table, x, xp, row_ids, col_ids, pos_out, scalars, pos):
    step = pl.program_id(0)
    count = seg.shape[1]

    @pl.when(step == 0)
    def _():
        segments = seg[...]
        image = jnp.zeros_like(segments)
        for s in range(table.shape[1]):
            image = jnp.where(segments == s, table[0, s], image)
        first = (image == 0).astype(F32)
        before = lax.broadcasted_iota(jnp.int32, (count, count), 0) < lax.broadcasted_iota(
            jnp.int32, (count, count), 1
        )
        rank = dot(
            jnp.broadcast_to(first, (8, count)).astype(BF16),
            before.astype(F32).astype(BF16),
            NN,
        )[0:1]
        total = jnp.sum(first)
        index = lax.broadcasted_iota(jnp.int32, (1, count), 1).astype(F32)
        place = jnp.where(image == 0, rank, total + index - rank)
        pos[...] = place.astype(jnp.int32)
        pos_out[...] = jnp.broadcast_to(pos[...], (8, count))
        n0 = total.astype(jnp.int32)
        tiles = count // TILE
        visits0 = jnp.maximum(1, (n0 + TILE - 1) // TILE)
        start1 = jnp.minimum(tiles - 1, n0 // TILE)
        visits = visits0 + tiles - start1
        for v in range(tiles + 1):
            real = jnp.minimum(v, visits - 1)
            in_first = real < visits0
            scalars[v] = jnp.where(in_first, real, real - visits0 + start1)
            scalars[8 + v] = jnp.where(in_first, 0, 1)
        scalars[16] = visits
        scalars[17] = n0
        scalars[18] = visits0
        scalars[19] = start1
        scalars[20] = tiles - start1

    onehot = (
        lax.broadcasted_iota(jnp.int32, (TILE, count), 0) + step * TILE == pos[...]
    ).astype(F32).astype(BF16)
    xp[...] = dot(onehot, x[...], NN).astype(BF16)
    ids = jnp.concatenate(
        [
            seg[...].astype(F32),
            blk[...].astype(F32),
            jnp.zeros((126, count), F32),
        ],
        axis=0,
    ).astype(BF16)
    row_ids[...] = dot(ids[0:8], onehot, NT)
    col_ids[...] = dot(onehot, ids, NT)


def order_rows(seg, blk, table, x):
    count, width = x.shape
    return pl.pallas_call(
        order_kernel,
        grid=(count // TILE,),
        in_specs=[
            whole((1, count)),
            whole((1, count)),
            pl.BlockSpec(memory_space=pltpu.SMEM),
            whole((count, width)),
        ],
        out_specs=[
            rows(width, TILE),
            pl.BlockSpec((8, TILE), lambda t: (0, t)),
            rows(128, TILE),
            whole((8, count)),
            pl.BlockSpec(memory_space=pltpu.SMEM),
        ],
        out_shape=[
            pltpu.HBM((count, width), BF16),
            shape_of((8, count), F32),
            shape_of((count, 128), F32),
            shape_of((8, count), jnp.int32),
            shape_of((32,), jnp.int32),
        ],
        scratch_shapes=[pltpu.VMEM((1, count), jnp.int32)],
        compiler_params=params(),
        cost_estimate=cost(2 * count * count * width, 8 * count * width),
    )(seg, blk, table, *pin(x))


def order_more_kernel(pos, values, out):
    size, count = out.shape[0], values.shape[0]
    index = lax.broadcasted_iota(jnp.int32, (size, count), 0) + pl.program_id(0) * size
    onehot = (index == pos[0:1, :]).astype(F32).astype(BF16)
    out[...] = dot(onehot, values[...], NN).astype(BF16)


def order_more(pos, values):
    count, width = values.shape
    return pl.pallas_call(
        order_more_kernel,
        grid=(count // TILE,),
        in_specs=[whole((8, count)), whole((count, width))],
        out_specs=rows(width, TILE),
        out_shape=pltpu.HBM((count, width), BF16),
        compiler_params=params(),
        cost_estimate=cost(2 * count * count * width, 4 * count * width),
    )(pos, *pin(values))


def restore_kernel(pos, values, out):
    count = values.shape[0]
    onehot = (
        lax.broadcasted_iota(jnp.int32, (count, TILE), 0) == pos[0:1, :]
    ).astype(F32).astype(BF16)
    out[...] = dot(onehot, values[...], TN).astype(BF16)


def restore_rows(pos, values):
    count, width = values.shape
    return pl.pallas_call(
        restore_kernel,
        grid=(count // TILE,),
        in_specs=[pl.BlockSpec((8, TILE), lambda t: (0, t)), whole((count, width))],
        out_specs=rows(width, TILE),
        out_shape=shape_of((count, width), BF16),
        compiler_params=params(),
        cost_estimate=cost(2 * count * count * width, 4 * count * width),
    )(pos, *pin(values))


def fetch(pieces, places, columns, dest, sems, base=0):
    height = dest.shape[0] // 4
    copies = []
    for i, piece in enumerate(pieces):
        start = pl.multiple_of(places[i] * height, 16)
        copies.append(
            pltpu.make_async_copy(
                piece.at[pl.ds(0, height), columns],
                dest.at[pl.ds(start, height), :],
                sems.at[base + i],
            )
        )
    return copies


def fetch_half(gathered, half, columns, dest, sem):
    return pltpu.make_async_copy(gathered.at[half, :, columns], dest, sem)


def start_all(copies):
    for copy in copies:
        copy.start()


def wait_all(copies):
    for copy in copies:
        copy.wait()


ANY = pl.BlockSpec(memory_space=pl.ANY)
SCALARS = pl.BlockSpec(memory_space=pltpu.SMEM)


def project_kernel(places, x, gain, w0, w1, w2, w3, normed, out, weight, sems):
    @pl.when(pl.program_id(0) == 0)
    def _():
        copies = fetch((w0, w1, w2, w3), places, slice(0, weight.shape[1]), weight, sems)
        start_all(copies)
        wait_all(copies)

    values = x[...].astype(F32)
    n1 = (values * inverse_rms(values) * gain[...]).astype(BF16)
    normed[...] = n1
    out[...] = dot(n1, weight[...], NN).astype(BF16)


def norm_project(places, x, gain, pieces):
    count, width = x.shape
    outs = pieces[0].shape[1]
    return pl.pallas_call(
        project_kernel,
        grid=(count // ROWS,),
        in_specs=[SCALARS, rows(width), whole((1, width))] + [ANY] * 4,
        out_specs=[rows(width), rows(outs)],
        out_shape=[pltpu.HBM((count, width), BF16), shape_of((count, outs), BF16)],
        scratch_shapes=[pltpu.VMEM((width, outs), BF16), pltpu.SemaphoreType.DMA((4,))],
        compiler_params=params(),
        cost_estimate=cost(2 * count * width * outs, 4 * count * width + 2 * count * outs),
    )(places, *pin(x), gain, *pieces)


MEMORY_TILE = 1024
BACK_TILE = 512


def memory_kernel(places, columns, memory, w0, w1, w2, w3, out, weight, sems):
    @pl.when(pl.program_id(0) == 0)
    def _():
        copies = fetch((w0, w1, w2, w3), places, columns, weight, sems)
        start_all(copies)
        wait_all(copies)

    out[...] = dot(memory[...], weight[...], NN).astype(BF16)


def project_memory(places, memory, pieces, columns):
    count, width = memory.shape
    outs = columns.stop - columns.start

    def kernel(places, *refs):
        memory_kernel(places, columns, *refs)

    return pl.pallas_call(
        kernel,
        grid=(count // MEMORY_TILE,),
        in_specs=[SCALARS, rows(width, MEMORY_TILE)] + [ANY] * 4,
        out_specs=rows(outs, MEMORY_TILE),
        out_shape=pltpu.HBM((count, outs), BF16),
        scratch_shapes=[pltpu.VMEM((width, outs), BF16), pltpu.SemaphoreType.DMA((4,))],
        compiler_params=params(),
        cost_estimate=cost(2 * count * width * outs, 4 * count * width),
    )(places, *pin(memory), *pieces)


SELF_TILE = 128
SELF_WINDOW = 512
BACK_WINDOW = 640


def store_logs(ref, columns, logs, extra=None):
    spread = jnp.where(in_half((logs[0].shape[0], PAIR), 0), logs[0], logs[1]).T
    for half in range(2):
        line = spread[half * HEAD_DIM : half * HEAD_DIM + 1, :]
        if extra is not None:
            line = jnp.where(extra, line, ref[half : half + 1, columns])
        ref[half : half + 1, columns] = line


def self_forward_kernel(q, k, v, row_ids, col_ids, out, logs):
    count = q.shape[0]
    for tile in range(count // SELF_TILE):
        base = tile * SELF_TILE
        start = min(max(base - 256, 0), count - SELF_WINDOW)
        spot = slice(base, base + SELF_TILE)
        window = slice(start, start + SELF_WINDOW)
        seen = (col_ids[spot, 0:1] == row_ids[0:1, window]) & (
            row_ids[1:2, window] <= col_ids[spot, 1:2]
        )
        bias = jnp.where(seen, 0.0, -HIDE)
        keys = k[window, :]
        values = v[window, :]
        queries = q[spot, :]
        parts, totals = [], []
        for half in range(2):
            scores = dot(only_half(queries, half), keys, NT) * EXP2_SCALE + bias
            highest = jnp.max(scores, axis=1, keepdims=True)
            weights = jnp.exp2(scores - highest)
            total = jnp.sum(weights, axis=1, keepdims=True)
            parts.append(dot(weights.astype(BF16), values, NN) / total)
            totals.append(highest + jnp.log2(total))
        out[spot, :] = jnp.where(in_half(parts[0].shape, 0), parts[0], parts[1]).astype(BF16)
        store_logs(logs, spot, totals)


def self_forward(pair, qkv, row_ids, col_ids):
    count = qkv.shape[0]
    pairs = qkv.shape[1] // (3 * PAIR)

    def part(which):
        return pl.BlockSpec((count, PAIR), lambda p: (0, which * pairs + pair))

    return pl.pallas_call(
        self_forward_kernel,
        grid=(1,),
        in_specs=[part(0), part(1), part(2), whole((8, count)), whole((count, 128))],
        out_specs=[whole((count, PAIR)), whole((8, count))],
        out_shape=[pltpu.HBM((count, PAIR), BF16), pltpu.HBM((8, count), F32)],
        compiler_params=params(),
        cost_estimate=cost(16 * count * SELF_WINDOW * PAIR, 8 * count * PAIR),
    )(qkv, qkv, qkv, row_ids, col_ids)


def self_backward_kernel(q, k, v, grad, logs, deltas, row_ids, col_ids, dq, dk, dv, key_sum, value_sum):
    count = q.shape[0]
    key_sum[...] = jnp.zeros_like(key_sum)
    value_sum[...] = jnp.zeros_like(value_sum)
    for tile in range(count // TILE):
        base = tile * TILE
        start = min(max(base - 256, 0), count - BACK_WINDOW)
        spot = slice(base, base + TILE)
        window = slice(start, start + BACK_WINDOW)
        seen = (col_ids[window, 0:1] == row_ids[0:1, spot]) & (
            col_ids[window, 1:2] <= row_ids[1:2, spot]
        )
        bias = jnp.where(seen, 0.0, -HIDE)
        keys = k[window, :]
        values = v[window, :]
        queries = q[spot, :]
        grads = grad[spot, :]
        parts = []
        for half in range(2):
            one_query = only_half(queries, half)
            one_grad = only_half(grads, half)
            scores = dot(keys, one_query, NT) * EXP2_SCALE + bias
            weights = jnp.exp2(scores - logs[half : half + 1, spot])
            slopes = dot(values, one_grad, NT)
            pushed = (weights * (slopes - deltas[half : half + 1, spot])).astype(BF16)
            value_sum[window, :] += dot(weights.astype(BF16), one_grad, NN)
            key_sum[window, :] += dot(pushed, one_query, NN)
            parts.append(dot(pushed, keys, TN))
        dq[spot, :] = (
            jnp.where(in_half(parts[0].shape, 0), parts[0], parts[1]) * SCALE
        ).astype(BF16)
    dk[...] = (key_sum[...] * SCALE).astype(BF16)
    dv[...] = value_sum[...].astype(BF16)


def self_backward(pair, qkv, grad, logs, deltas, row_ids, col_ids):
    count = qkv.shape[0]
    pairs = qkv.shape[1] // (3 * PAIR)

    def part(which):
        return pl.BlockSpec((count, PAIR), lambda p: (0, which * pairs + pair))

    return pl.pallas_call(
        self_backward_kernel,
        grid=(1,),
        in_specs=[
            part(0),
            part(1),
            part(2),
            part(0),
            whole((8, count)),
            pl.BlockSpec((8, count), lambda p: (pair, 0)),
            whole((8, count)),
            whole((count, 128)),
        ],
        out_specs=[whole((count, PAIR))] * 3,
        out_shape=[pltpu.HBM((count, PAIR), BF16)] * 3,
        scratch_shapes=[pltpu.VMEM((count, PAIR), F32)] * 2,
        compiler_params=params(),
        cost_estimate=cost(40 * count * BACK_WINDOW * PAIR, 16 * count * PAIR),
    )(qkv, qkv, qkv, grad, logs, deltas, row_ids, col_ids)


KEYS = 1024


def visits_of(image, scalars):
    first = jnp.where(image == 0, 0, scalars[19])
    return first, jnp.where(image == 0, scalars[18], scalars[20])


def cross_forward_kernel(scalars, q, k, v, out, logs):
    image = pl.program_id(0)
    first, count = visits_of(image, scalars)

    def visit(i, carry):
        base = pl.multiple_of((first + i) * TILE, TILE)
        spot = pl.ds(base, TILE)
        queries = q[spot, :]
        parts, totals = [], []
        tops, sums = [None, None], [None, None]
        for start in range(0, k.shape[0], KEYS):
            keys = k[start : start + KEYS, :]
            values = v[start : start + KEYS, :]
            both = [dot(only_half(queries, half), keys, NT) for half in range(2)]
            for half, scores in enumerate(both):
                highest = jnp.max(scores, axis=1, keepdims=True) * EXP2_SCALE
                if start:
                    highest = jnp.maximum(highest, tops[half])
                weights = jnp.exp2(scores * EXP2_SCALE - highest).astype(BF16)
                mixed = dot(
                    weights,
                    jnp.where(in_half(values.shape, half), values, jnp.ones_like(values)),
                    NN,
                )
                if start:
                    mixed = mixed + sums[half] * jnp.exp2(tops[half] - highest)
                tops[half], sums[half] = highest, mixed
        for half in range(2):
            total = pltpu.roll(sums[half], HEAD_DIM, 1)
            parts.append(sums[half] / total)
            totals.append(tops[half] + jnp.log2(total))
        mixed = jnp.where(in_half(parts[0].shape, 0), parts[0], parts[1]).astype(BF16)
        limit = jnp.where(image == 0, 0, scalars[17]) - base
        row_mine = lax.broadcasted_iota(jnp.int32, mixed.shape, 0) >= limit
        lane_mine = lax.broadcasted_iota(jnp.int32, (1, TILE), 1) >= limit
        out[spot, :] = jnp.where(row_mine, mixed, out[spot, :])
        store_logs(logs, spot, totals, lane_mine)
        return carry

    lax.fori_loop(0, count, visit, 0)


def cross_forward(pair, scalars, q, keys_values, images):
    count, inner = q.shape
    pairs = inner // PAIR
    memory_rows = keys_values.shape[0] // images

    def part(which):
        return pl.BlockSpec((memory_rows, PAIR), lambda i, sc: (i, which * pairs + pair))

    return pl.pallas_call(
        cross_forward_kernel,
        grid_spec=pltpu.PrefetchScalarGridSpec(
            num_scalar_prefetch=1,
            grid=(images,),
            in_specs=[
                pl.BlockSpec((count, PAIR), lambda i, sc: (0, pair)),
                part(0),
                part(1),
            ],
            out_specs=[whole((count, PAIR)), whole((8, count))],
        ),
        out_shape=[pltpu.HBM((count, PAIR), BF16), pltpu.HBM((8, count), F32)],
        compiler_params=params(),
        cost_estimate=cost(20 * count * memory_rows * PAIR, 8 * memory_rows * PAIR),
    )(scalars, *pin(q, keys_values, keys_values))


def cross_backward_kernel(
    image, scalars, q, k, v, grad, logs, deltas, old, dq, dk, dv, key_sum, value_sum
):
    first, count = visits_of(jnp.int32(image), scalars)
    if image:
        dq[...] = old[...]

    def visit(i, fresh):
        base = pl.multiple_of((first + i) * TILE, TILE)
        spot = pl.ds(base, TILE)
        queries = q[spot, :]
        grads = grad[spot, :]
        keys = k[...]
        values = v[...]
        limit = scalars[17] - base
        lane_mine = (lax.broadcasted_iota(jnp.int32, (1, TILE), 1) >= limit) == (image == 1)
        parts = []
        for half in range(2):
            one_query = only_half(queries, half)
            one_grad = only_half(grads, half)
            log = jnp.where(lane_mine, logs[half : half + 1, spot], HIDE)
            scores = dot(keys, one_query, NT)
            weights = jnp.exp2(scores * EXP2_SCALE - log)
            slopes = dot(values, one_grad, NT)
            pushed = (weights * (slopes - deltas[half : half + 1, spot])).astype(BF16)
            value_part = dot(weights.astype(BF16), one_grad, NN)
            key_part = dot(pushed, one_query, NN)
            if fresh and half == 0:
                value_sum[...] = value_part
                key_sum[...] = key_part
            else:
                value_sum[...] += value_part
                key_sum[...] += key_part
            parts.append(dot(pushed, keys, TN))
        grad_query = (
            jnp.where(in_half(parts[0].shape, 0), parts[0], parts[1]) * SCALE
        ).astype(BF16)
        if image:
            row_mine = lax.broadcasted_iota(jnp.int32, grad_query.shape, 0) >= limit
            grad_query = jnp.where(row_mine, grad_query, dq[spot, :])
        dq[spot, :] = grad_query

    def later(i, carry):
        visit(i, False)
        return carry

    visit(0, True)
    lax.fori_loop(1, count, later, 0)
    dk[...] = (key_sum[...] * SCALE).astype(BF16)
    dv[...] = value_sum[...].astype(BF16)


def cross_backward(image, scalars, q, keys_values, grad, logs, deltas, images, old):
    count, inner = q.shape
    pairs = inner // PAIR
    memory_rows = keys_values.shape[0] // images
    token_spec = pl.BlockSpec((count, PAIR), lambda p, sc: (0, p))
    line = pl.BlockSpec((8, count), lambda p, sc: (p, 0))
    result = pl.BlockSpec((memory_rows, PAIR), lambda p, sc: (0, p))

    def part(which):
        return pl.BlockSpec((memory_rows, PAIR), lambda p, sc: (image, which * pairs + p))

    def first_kernel(scalars, q, k, v, grad, logs, deltas, *rest):
        cross_backward_kernel(image, scalars, q, k, v, grad, logs, deltas, None, *rest)

    def second_kernel(*refs):
        cross_backward_kernel(image, *refs)

    extra = [old] if image else []
    return pl.pallas_call(
        second_kernel if image else first_kernel,
        grid_spec=pltpu.PrefetchScalarGridSpec(
            num_scalar_prefetch=1,
            grid=(pairs,),
            in_specs=[token_spec, part(0), part(1), token_spec, line, line]
            + [token_spec] * len(extra),
            out_specs=[token_spec, result, result],
            scratch_shapes=[pltpu.VMEM((memory_rows, PAIR), F32)] * 2,
        ),
        out_shape=[
            pltpu.HBM((count, inner), BF16),
            pltpu.HBM((memory_rows, inner), BF16),
            pltpu.HBM((memory_rows, inner), BF16),
        ],
        compiler_params=params(32),
        cost_estimate=cost(25 * count * memory_rows * inner, 8 * memory_rows * inner),
    )(scalars, *pin(q, keys_values, keys_values, grad), logs, deltas, *pin(*extra))


def put_rows(places, product, keep, send, span=slice(None)):
    height = product.shape[0] // 4
    for i, ref in enumerate((keep, keep, send, send)):
        start = pl.multiple_of(places[i] * height, 16)
        ref[i % 2, 0:height, span] = product[pl.ds(start, height), :].astype(BF16)


def memory_back_kernel(
    columns, last, places, memory, dk, dv, w0, w1, w2, w3, *refs
):
    if last:
        before, keep_part, send_part, keep, send, weight, total, sems = refs
    else:
        keep_part, send_part, total_out, weight, total, sems = refs
    inner = dk.shape[1]

    @pl.when(pl.program_id(0) == 0)
    def _():
        copies = fetch((w0, w1, w2, w3), places, columns, weight, sems)
        start_all(copies)
        if last:
            total[...] = before[...]
        else:
            total[...] = jnp.zeros_like(total)
        wait_all(copies)

    both = jnp.concatenate([dk[...], dv[...]], axis=1)
    product = dot(both, weight[...], NT).astype(BF16)
    lower, upper = product[:, :inner], product[:, inner:]
    side = places[4]
    send_part[...] = jnp.where(side == 0, upper, lower)
    keep_part[...] = jnp.where(side == 0, lower, upper)
    total[...] += dot(memory[...], both, TN)

    @pl.when(pl.program_id(0) == pl.num_programs(0) - 1)
    def _():
        if last:
            put_rows(places, total, keep, send)
        else:
            total_out[...] = total[...]


def memory_back(places, memory, dk, dv, pieces, columns, image, before, spare):
    count, inner = dk.shape
    width = memory.shape[1]
    steps = count // BACK_TILE
    last = before is not None
    ranks = pltpu.HBM((2, width // 4, spare + 2 * inner), BF16)
    rank_spec = pl.BlockSpec((2, width // 4, 2 * inner), lambda t: (0, 0, 0))

    def kernel(*refs):
        memory_back_kernel(columns, last, *refs)

    return pl.pallas_call(
        kernel,
        grid=(steps,),
        in_specs=[
            SCALARS,
            pl.BlockSpec((BACK_TILE, width), lambda t: (image * steps + t, 0)),
            rows(inner, BACK_TILE),
            rows(inner, BACK_TILE),
        ]
        + [ANY] * 4
        + ([whole((width, 2 * inner))] if last else []),
        out_specs=[rows(inner, BACK_TILE), rows(inner, BACK_TILE)]
        + ([rank_spec, rank_spec] if last else [whole((width, 2 * inner))]),
        out_shape=[pltpu.HBM((count, inner), BF16)] * 2
        + ([ranks, ranks] if last else [shape_of((width, 2 * inner), F32)]),
        scratch_shapes=[
            pltpu.VMEM((width, 2 * inner), BF16),
            pltpu.VMEM((width, 2 * inner), F32),
            pltpu.SemaphoreType.DMA((4,)),
        ],
        compiler_params=params(),
        cost_estimate=cost(8 * count * width * inner, 8 * count * width),
    )(places, *pin(memory, dk, dv), *pieces, *([before] if last else []))


def weight_grads_kernel(plan, spans, places, left_refs, right_refs, keep, send, scratch):
    left_holds = scratch[: len(left_refs)]
    right_holds = scratch[len(left_refs) : -3]
    turned, product, sems = scratch[-3:]
    step = pl.program_id(0)
    lefts = [
        pltpu.make_async_copy(ref, hold, sems.at[i])
        for i, (ref, hold) in enumerate(zip(left_refs, left_holds))
    ]
    rights = [
        pltpu.make_async_copy(ref, hold, sems.at[len(left_refs) + i])
        for i, (ref, hold) in enumerate(zip(right_refs, right_holds))
    ]
    for at, (left, group) in enumerate(plan):
        fresh = at == 0 or plan[at - 1][0] != left

        @pl.when(step == at)
        def _():
            if at == 0:
                seen = set()
                for one, others in plan:
                    if one not in seen:
                        lefts[one].start()
                        seen.add(one)
                    for g in others:
                        rights[g].start()
            if fresh:
                lefts[left].wait()
                turned[...] = left_holds[left][...].T
            for g in group:
                rights[g].wait()
            right = join([right_holds[g] for g in group])
            columns = right.shape[1]
            product[:, 0:columns] = dot(turned[...], right, NN)
            put_rows(places, product.at[:, 0:columns], keep, send, spans[at])


def join(refs):
    values = [ref[...] for ref in refs]
    return values[0] if len(values) == 1 else jnp.concatenate(values, axis=1)


def flatten(groups):
    flat, sizes = [], []
    for group in groups:
        group = group if isinstance(group, (list, tuple)) else [group]
        flat += list(group)
        sizes.append(len(group))
    return flat, sizes


def weight_grads(places, lefts, rights, plan, into=(), first=0):
    count, width = lefts[0].shape
    flat, sizes = flatten(rights)
    groups, at = [], 0
    for size in sizes:
        groups.append(list(range(at, at + size)))
        at += size
    plan = [(left, [f for g in group for f in groups[g]]) for left, group in plan]
    columns = [sum(flat[f].shape[1] for f in group) for _, group in plan]
    step_columns = columns[0]
    share = width // 4
    total = sum(columns) + first * step_columns
    even = len(set(columns)) == 1
    spans = [
        slice(0, step_columns) if even else slice(sum(columns[:at]), sum(columns[: at + 1]))
        for at in range(len(plan))
    ]
    extra = list(into)
    def kernel(places, *refs):
        lefts_end = len(lefts)
        rights_end = lefts_end + len(flat)
        weight_grads_kernel(
            plan,
            spans,
            places,
            refs[:lefts_end],
            refs[lefts_end:rights_end],
            *refs[rights_end + len(extra) : rights_end + len(extra) + 2],
            refs[rights_end + len(extra) + 2 :],
        )

    start = 1 + len(lefts) + len(flat)
    return pl.pallas_call(
        kernel,
        grid=(len(plan),),
        in_specs=[SCALARS]
        + [ANY] * (len(lefts) + len(flat) + len(extra)),
        out_specs=[
            pl.BlockSpec((2, share, step_columns), lambda t: (0, 0, t + first))
            if even
            else whole((2, share, total))
        ]
        * 2,
        out_shape=[pltpu.HBM((2, share, total), BF16)] * 2,
        input_output_aliases={start: 0, start + 1: 1} if extra else {},
        scratch_shapes=[pltpu.VMEM(array.shape, array.dtype) for array in list(lefts) + flat]
        + [
            pltpu.VMEM((width, count), BF16),
            pltpu.VMEM((width, max(columns)), F32),
            pltpu.SemaphoreType.DMA((len(lefts) + len(flat),)),
        ],
        compiler_params=params(32),
        cost_estimate=cost(
            2 * count * width * sum(columns), 4 * count * width * len(plan)
        ),
    )(places, *pin(*lefts, *flat), *extra)


def middle_kernel(plan, parts, places, x, gain, *refs):
    mine, theirs, refs = refs[:parts], refs[parts : 2 * parts], refs[2 * parts :]
    pieces, (h1, n2, cq, out_mine, out_theirs, query, sems) = refs[:8], refs[8:]

    @pl.when(pl.program_id(0) == 0)
    def _():
        copies = (
            fetch(pieces[:4], places, plan[0], out_mine, sems, 0)
            + fetch(pieces[4:], places, plan[1], out_theirs, sems, 4)
            + fetch(pieces[:4], places, plan[2], query, sems, 8)
        )
        start_all(copies)
        wait_all(copies)

    values = (
        x[...].astype(F32)
        + dot(join(mine), out_mine[...], NT)
        + dot(join(theirs), out_theirs[...], NT)
    )
    h1[...] = values.astype(BF16)
    normed = (values * inverse_rms(values) * gain[...]).astype(BF16)
    n2[...] = normed
    cq[...] = dot(normed, query[...], NN).astype(BF16)


def middle_step(places, x, mine, theirs, gain, pieces, pieces_theirs, plan):
    count, width = x.shape
    half = sum(part.shape[1] for part in mine)

    def kernel(*refs):
        middle_kernel(plan, len(mine), *refs)

    return pl.pallas_call(
        kernel,
        grid=(count // ROWS,),
        in_specs=[SCALARS, rows(width), whole((1, width))]
        + [rows(PAIR)] * (2 * len(mine))
        + [ANY] * 8,
        out_specs=[rows(width), rows(width), rows(half)],
        out_shape=[
            pltpu.HBM((count, width), BF16),
            pltpu.HBM((count, width), BF16),
            pltpu.HBM((count, half), BF16),
        ],
        scratch_shapes=[pltpu.VMEM((width, half), BF16)] * 3 + [pltpu.SemaphoreType.DMA((12,))],
        compiler_params=params(),
        cost_estimate=cost(6 * count * width * half, 12 * count * width),
    )(places, *pin(x), gain, *pin(*mine), *theirs, *pieces, *pieces_theirs)


def head_sums(left, right):
    product = left.astype(F32) * right.astype(F32)
    width = product.shape[1]
    high = product.astype(BF16)
    low = (product - high.astype(F32)).astype(BF16)
    height = 8 * (width // PAIR)
    line = lax.broadcasted_iota(jnp.int32, (height, width), 0)
    head = lax.broadcasted_iota(jnp.int32, (height, width), 1) // HEAD_DIM
    choose = (
        ((line // 8) * 2 + line % 8 == head) & (line % 8 < 2)
    ).astype(F32).astype(BF16)
    return dot(choose, high, NT) + dot(choose, low, NT)


CHUNK = 512


def units_kernel(plan, parts, places, h1, gain, gy, *refs):
    mine, theirs, refs = refs[:parts], refs[parts : 2 * parts], refs[2 * parts :]
    late, refs = refs[0], refs[1:]
    (
        output,
        n3,
        hidden,
        grad_gate,
        grad_up,
        e2,
        dc,
        deltas,
        gain_grad,
        out_mine,
        out_theirs,
        units_mine,
        units_theirs,
        sems,
    ) = refs
    step = pl.program_id(0)

    side = places[4]
    out_copies = [
        fetch_half(late, side, plan[0], out_mine, sems.at[0]),
        fetch_half(late, 1 - side, plan[0], out_theirs, sems.at[1]),
    ]
    mine_copy = fetch_half(late, side, plan[1], units_mine, sems.at[2])
    theirs_copy = fetch_half(late, 1 - side, plan[1], units_theirs, sems.at[3])

    @pl.when(step == 0)
    def _():
        start_all(out_copies + [mine_copy, theirs_copy])
        gain_grad[...] = jnp.zeros_like(gain_grad)
        wait_all(out_copies)

    crossed_mine = join(mine)
    values = (
        h1[...].astype(F32)
        + dot(crossed_mine, out_mine[...], NT)
        + dot(join(theirs), out_theirs[...], NT)
    )
    normed = (values * inverse_rms(values) * gain[...]).astype(BF16)
    n3[...] = normed
    upstream = gy[...]
    mixed = jnp.zeros_like(values)
    back = jnp.zeros_like(values)
    unit = units_mine.shape[1] // 3
    for own in (True, False):
        weight = units_mine if own else units_theirs

        @pl.when(step == 0)
        def _():
            (mine_copy if own else theirs_copy).wait()

        for start in range(0, unit, CHUNK):
            gate_weight = weight[:, start : start + CHUNK]
            up_weight = weight[:, unit + start : unit + start + CHUNK]
            down_weight = weight[:, 2 * unit + start : 2 * unit + start + CHUNK]
            gate = dot(normed, gate_weight, NN)
            up = dot(normed, up_weight, NN)
            pushed = dot(upstream, down_weight, NN)
            square = gate * gate
            bend = jnp.tanh(ROOT_TWO_OVER_PI * gate * (1.0 + CUBIC * square))
            lift = 0.5 * (1.0 + bend)
            gelu = gate * lift
            slope = lift + (0.5 * ROOT_TWO_OVER_PI) * gate * (1.0 - bend * bend) * (
                1.0 + (3.0 * CUBIC) * square
            )
            units = (gelu * up).astype(BF16)
            push_gate = (pushed * up * slope).astype(BF16)
            push_up = (pushed * gelu).astype(BF16)
            mixed = mixed + dot(units, down_weight, NT)
            back = back + dot(push_gate, gate_weight, NT) + dot(push_up, up_weight, NT)
            if own:
                hidden[:, start : start + CHUNK] = units
                grad_gate[:, start : start + CHUNK] = push_gate
                grad_up[:, start : start + CHUNK] = push_up
    output[...] = (values + mixed).astype(BF16)
    grad, gain_part = norm_back(values, gain[...], back)
    low = (upstream.astype(F32) + grad).astype(BF16)
    e2[...] = low
    crossed = dot(low, out_mine[...], NN).astype(BF16)
    dc[...] = crossed
    deltas[...] = head_sums(crossed, crossed_mine)
    gain_grad[0:1, :] += gain_part


def units_step(places, h1, mine, theirs, gain, gy, late, plan):
    count, width = h1.shape
    half = sum(part.shape[1] for part in mine)
    unit = (plan[1].stop - plan[1].start) // 3
    lines = 8 * (half // PAIR)

    def kernel(*refs):
        units_kernel(plan, len(mine), *refs)

    return pl.pallas_call(
        kernel,
        grid=(count // ROWS,),
        in_specs=[
            SCALARS,
            rows(width),
            whole((1, width)),
            rows(width),
        ]
        + [rows(PAIR)] * (2 * len(mine))
        + [ANY],
        out_specs=[
            rows(width),
            rows(width),
            rows(unit),
            rows(unit),
            rows(unit),
            rows(width),
            rows(half),
            pl.BlockSpec((lines, ROWS), lambda t: (0, t)),
            whole((8, width)),
        ],
        out_shape=[
            pltpu.HBM((count, width), BF16),
            pltpu.HBM((count, width), BF16),
            pltpu.HBM((count, unit), BF16),
            pltpu.HBM((count, unit), BF16),
            pltpu.HBM((count, unit), BF16),
            pltpu.HBM((count, width), BF16),
            pltpu.HBM((count, half), BF16),
            pltpu.HBM((lines, count), F32),
            shape_of((8, width), F32),
        ],
        scratch_shapes=[pltpu.VMEM((width, half), BF16)] * 2
        + [pltpu.VMEM((width, 3 * unit), BF16)] * 2
        + [pltpu.SemaphoreType.DMA((4,))],
        compiler_params=params(58),
        cost_estimate=cost(30 * count * width * unit, 30 * count * width),
    )(places, *pin(h1), gain, *pin(gy, *mine), *theirs, *pin(late))


def turn_kernel(plan, parts, places, e2, h1, mine, theirs, gain, *refs):
    attended, refs = refs[:parts], refs[parts:]
    pieces, refs = refs[:4], refs[4:]
    late, e1, da, deltas, gain_grad, query_mine, query_theirs, out_mine, sems = refs

    @pl.when(pl.program_id(0) == 0)
    def _():
        copies = (
            fetch(pieces, places, plan[0], out_mine, sems, 0)
            + fetch(pieces, places, plan[1], query_mine, sems, 4)
            + [fetch_half(late, 1 - places[4], plan[2], query_theirs, sems.at[8])]
        )
        start_all(copies)
        gain_grad[...] = jnp.zeros_like(gain_grad)
        wait_all(copies)

    back = dot(mine[...], query_mine[...], NT) + dot(theirs[...], query_theirs[...], NT)
    grad, gain_part = norm_back(h1[...].astype(F32), gain[...], back)
    low = (e2[...].astype(F32) + grad).astype(BF16)
    e1[...] = low
    pushed = dot(low, out_mine[...], NN).astype(BF16)
    da[...] = pushed
    deltas[...] = head_sums(pushed, join(attended))
    gain_grad[0:1, :] += gain_part


def turn_step(places, e2, h1, mine, theirs, gain, attended, pieces, late, plan):
    count, width = h1.shape
    half = mine.shape[1]
    lines = 8 * (half // PAIR)

    def kernel(*refs):
        turn_kernel(plan, len(attended), *refs)

    return pl.pallas_call(
        kernel,
        grid=(count // ROWS,),
        in_specs=[
            SCALARS,
            rows(width),
            rows(width),
            rows(half),
            rows(half),
            whole((1, width)),
        ]
        + [rows(PAIR)] * len(attended)
        + [ANY] * 5,
        out_specs=[
            rows(width),
            rows(half),
            pl.BlockSpec((lines, ROWS), lambda t: (0, t)),
            whole((8, width)),
        ],
        out_shape=[
            pltpu.HBM((count, width), BF16),
            shape_of((count, half), BF16),
            shape_of((lines, count), F32),
            shape_of((8, width), F32),
        ],
        scratch_shapes=[pltpu.VMEM((width, half), BF16)] * 3 + [pltpu.SemaphoreType.DMA((9,))],
        compiler_params=params(),
        cost_estimate=cost(6 * count * width * half, 16 * count * width),
    )(places, *pin(e2, h1, mine), theirs, gain, *pin(*attended), *pieces, *pin(late))


def partial_kernel(parts, places, x, n1, second, third, *refs):
    part_refs, refs = refs[:parts], refs[parts:]
    w0, w1, w2, w3, out, keep, send, weight, total, gain_grad, sems = refs
    step = pl.program_id(0)

    @pl.when(step == 0)
    def _():
        copies = fetch((w0, w1, w2, w3), places, slice(0, weight.shape[1]), weight, sems)
        start_all(copies)
        gain_grad[...] = jnp.zeros_like(gain_grad)
        total[...] = jnp.zeros_like(total)
        wait_all(copies)

    back = dot(join(part_refs), weight[...], NT)
    out[...] = back.astype(BF16)
    values = x[...].astype(F32)
    gain_grad[0:1, :] += jnp.sum(back * values * inverse_rms(values), axis=0, keepdims=True)
    last = join([part_refs[i * (parts // 3) + parts // 3 - 1] for i in range(3)])
    total[...] += dot(n1[...], last, TN)

    @pl.when(step == pl.num_programs(0) - 1)
    def _():
        put_rows(places, total, keep, send)
        height = total.shape[0] // 4
        lines = jnp.concatenate(
            [
                gain_grad[0:1, :],
                second[0:1, :],
                third[0:1, :],
                jnp.zeros((13, gain_grad.shape[1]), F32),
            ],
            axis=0,
        )
        shares = [lines[:, w * height : (w + 1) * height] for w in range(4)]
        fill = jnp.zeros((16, total.shape[1] - height), F32)
        for i, ref in enumerate((keep, keep, send, send)):
            share = shares[0]
            for w in range(1, 4):
                share = jnp.where(places[i] == w, shares[w], share)
            ref[i % 2, height : height + 16, :] = jnp.concatenate([share, fill], axis=1).astype(
                BF16
            )


def partial_step(places, parts, x, n1, second, third, pieces):
    count, width = x.shape
    inner = sum(part.shape[1] for part in parts)
    ranks = (2, width // 4 + 16, 3 * PAIR)

    def kernel(*refs):
        partial_kernel(len(parts), *refs)

    return pl.pallas_call(
        kernel,
        grid=(count // ROWS,),
        in_specs=[SCALARS, rows(width), rows(width), whole((8, width)), whole((8, width))]
        + [rows(PAIR)] * len(parts)
        + [ANY] * 4,
        out_specs=[rows(width), whole(ranks), whole(ranks)],
        out_shape=[
            pltpu.HBM((count, width), BF16),
            shape_of(ranks, BF16),
            shape_of(ranks, BF16),
        ],
        scratch_shapes=[
            pltpu.VMEM((width, inner), BF16),
            pltpu.VMEM((width, 3 * PAIR), F32),
            pltpu.VMEM((8, width), F32),
            pltpu.SemaphoreType.DMA((4,)),
        ],
        compiler_params=params(),
        cost_estimate=cost(2 * count * width * (inner + 3 * PAIR), 8 * count * width),
    )(places, *pin(x, n1), second, third, *pin(*parts), *pieces)


def last_kernel(pos, e1, x, mine, theirs, gain, out, held):
    step = pl.program_id(0)
    half = pl.num_programs(0) // 2
    size = e1.shape[0]

    @pl.when(step < half)
    def _():
        back = mine[...].astype(F32) + theirs[...].astype(F32)
        grad, _ = norm_back(x[...].astype(F32), gain[...], back)
        held[pl.ds(pl.multiple_of(step * size, size), size), :] = (
            e1[...].astype(F32) + grad
        ).astype(BF16)

    @pl.when(step >= half)
    def _():
        onehot = (
            lax.broadcasted_iota(jnp.int32, (held.shape[0], size), 0) == pos[0:1, :]
        ).astype(F32).astype(BF16)
        out[...] = dot(onehot, held[...], TN).astype(BF16)


def last_step(pos, e1, x, mine, theirs, gain):
    count, width = x.shape
    steps = count // TILE

    def early(t):
        return (jnp.minimum(t, steps - 1), 0)

    def late(t):
        return jnp.maximum(t - steps, 0)

    tile = pl.BlockSpec((TILE, width), early)
    return pl.pallas_call(
        last_kernel,
        grid=(2 * steps,),
        in_specs=[pl.BlockSpec((8, TILE), lambda t: (0, late(t)))]
        + [tile] * 4
        + [whole((1, width))],
        out_specs=pl.BlockSpec((TILE, width), lambda t: (late(t), 0)),
        out_shape=shape_of((count, width), BF16),
        scratch_shapes=[pltpu.VMEM((count, width), BF16)],
        compiler_params=params(),
        cost_estimate=cost(2 * count * count * width, 12 * count * width),
    )(pos, *pin(e1, x, mine), theirs, gain)


def swap(values, axis, distance):
    size = lax.axis_size(axis)
    return lax.ppermute(values, axis, [(i, i ^ distance) for i in range(size)])


def after(values, *others):
    return lax.optimization_barrier((values,) + others)[0]


def gather_all(values):
    return lax.all_gather(values, ("narrow", "wide"), axis=0, tiled=True).reshape(
        lax.axis_size("narrow"), -1, values.shape[1]
    )


def sum_wide(values):
    return lax.psum_scatter(values, "wide", scatter_dimension=0, tiled=True)


def add(left, right):
    return (left.astype(F32) + right.astype(F32)).astype(BF16)


def add_pair(keep, got):
    return add(keep[0], got[0]), add(keep[1], got[1])


def line_inner():
    place = lax.axis_index("dp")
    return (place == 1) | (place == 2)


def line_first(values):
    if lax.axis_size("dp") != 4:
        return lax.psum(values, "dp")
    got = lax.ppermute(values, "dp", [(0, 1), (3, 2)])
    return jnp.where(line_inner(), add(values, got), values)


def line_second(values):
    if lax.axis_size("dp") != 4:
        return values
    return add(values, lax.ppermute(values, "dp", [(1, 2), (2, 1)]))


def line_third(values, *others):
    if lax.axis_size("dp") != 4:
        return values
    got = after(lax.ppermute(values, "dp", [(1, 0), (2, 3)]), *others)
    return jnp.where(line_inner(), values, got)


def local(
    tokens,
    memory,
    cotangent,
    norm1_gain,
    norm2_gain,
    norm3_gain,
    q_weight,
    k_weight,
    v_weight,
    o_weight,
    cross_q,
    cross_k,
    cross_v,
    cross_o,
    gate_weight,
    up_weight,
    down_weight,
    segment_ids,
    block_ids,
    image_table,
):
    width = tokens.shape[1]
    share = q_weight.shape[0]
    inner = q_weight.shape[1]
    unit = gate_weight.shape[1]
    images = memory.shape[0]
    flat_memory = memory.reshape(-1, width)
    place = lax.axis_index("wide")
    side = lax.axis_index("narrow")
    places = jnp.stack([place, place ^ 2, place ^ 1, place ^ 3, side]).astype(jnp.int32)

    gains = jnp.stack([norm1_gain, norm2_gain, norm3_gain])
    gains = jnp.pad(gains, ((0, 13), (0, 3 * inner - share)))
    early = jnp.concatenate(
        [jnp.concatenate([q_weight, k_weight, v_weight], axis=1), gains], axis=0
    )
    early_x = swap(early, "wide", 2)
    early_core = swap(early, "wide", 1)
    early_pieces = (early, early_x, early_core, swap(early_x, "wide", 1))
    lines = jnp.stack([piece[share : share + 3, :share] for piece in early_pieces])
    lines = lines.astype(F32)
    order = [
        jnp.sum(jnp.where((places[:4] == w)[:, None, None], lines, 0.0), axis=0)
        for w in range(4)
    ]
    all_gains = jnp.concatenate(order, axis=1)[:, None, :]

    mid = jnp.concatenate([cross_k, cross_v, cross_q, o_weight], axis=1)
    memory_columns = slice(0, 2 * inner)
    query_columns = slice(2 * inner, 3 * inner)
    out_columns = slice(3 * inner, 4 * inner)
    mid_x = swap(after(mid, early_x), "wide", 2)
    mid_core = swap(mid, "wide", 1)
    out_y = swap(o_weight, "narrow", 1)
    late = jnp.concatenate([cross_q, cross_o, gate_weight, up_weight, down_weight], axis=1)
    late_query_columns = slice(0, inner)
    late_columns = (slice(inner, 2 * inner), slice(2 * inner, 2 * inner + 3 * unit))

    x, row_ids, col_ids, pos, scalars = order_rows(
        segment_ids, block_ids, image_table, after(tokens, early_core, out_y)
    )
    late = gather_all(after(late, early_x, x))
    n1, qkv = norm_project(places, x, all_gains[0], early_pieces)
    pairs = inner // PAIR
    self_parts = [self_forward(0, after(qkv, mid_core), row_ids, col_ids)]
    out_yx = after(swap(out_y, "wide", 2), self_parts[0][0])
    out_pieces = (out_y, out_yx, swap(out_y, "wide", 1), swap(out_yx, "wide", 1))
    for pair in range(1, pairs):
        waits = out_pieces if pair == pairs - 1 else ()
        self_parts.append(
            self_forward(pair, after(qkv, self_parts[-1][0], *waits), row_ids, col_ids)
        )
    mid_x = after(mid_x, self_parts[-2][0])
    mid_pieces = (mid, mid_x, mid_core, swap(mid_x, "wide", 1))
    gy = order_more(pos, after(cotangent, self_parts[-1][0]))
    attended_theirs = [swap(part[0], "narrow", 1) for part in self_parts]
    attended = [part[0] for part in self_parts]
    keys_values = project_memory(
        places,
        after(flat_memory, gy, attended_theirs[0]),
        mid_pieces,
        memory_columns,
    )
    h1, n2, cq = middle_step(
        places,
        after(x, keys_values),
        attended,
        attended_theirs,
        all_gains[1],
        mid_pieces,
        out_pieces,
        (out_columns, slice(0, inner), query_columns),
    )
    cross_parts = [cross_forward(0, scalars, cq, keys_values, images)]
    crossed_theirs = []
    for pair in range(1, pairs):
        previous = [cross_parts[-1][0]] + crossed_theirs
        crossed_theirs.append(swap(cross_parts[-1][0], "narrow", 1))
        cross_parts.append(
            cross_forward(pair, scalars, after(cq, *previous), keys_values, images)
        )
    crossed = [part[0] for part in cross_parts]
    crossed_theirs.append(swap(crossed[-1], "narrow", 1))
    cross_logs = jnp.concatenate([part[1] for part in cross_parts], axis=0)
    (
        output,
        n3,
        hidden,
        grad_gate,
        grad_up,
        e2,
        dc,
        cross_deltas,
        third_gain,
    ) = units_step(
        places,
        h1,
        crossed,
        crossed_theirs,
        all_gains[2],
        gy,
        late,
        late_columns,
    )

    unit_keep, unit_send = weight_grads(
        places, (n3, gy), (grad_gate, grad_up, hidden), ((0, (0,)), (0, (1,)), (1, (2,)))
    )
    unit_stay, unit_leave = add_pair(unit_keep, swap(unit_send, "wide", 1))
    dcq, dck, dcv = cross_backward(
        0,
        scalars,
        cq,
        keys_values,
        after(dc, unit_leave),
        cross_logs,
        cross_deltas,
        images,
        None,
    )
    unit_part = add(unit_stay, swap(unit_leave, "wide", 2))
    keep0, send0, total = memory_back(
        places,
        flat_memory,
        after(dck, unit_part),
        dcv,
        mid_pieces,
        memory_columns,
        0,
        None,
        0,
    )
    unit_sum = lax.psum(unit_part, "dp")
    dcq, dck, dcv = cross_backward(
        1,
        scalars,
        cq,
        keys_values,
        after(dc, send0),
        cross_logs,
        cross_deltas,
        images,
        dcq,
    )
    dcq_theirs = swap(dcq, "narrow", 1)
    memory0 = add(keep0, swap(send0, "narrow", 1))
    keep1, send1, cross_keep, cross_send = memory_back(
        places,
        flat_memory,
        after(dck, memory0),
        dcv,
        mid_pieces,
        memory_columns,
        1,
        total,
        2 * inner,
    )
    cross_keep, cross_send = weight_grads(
        places,
        (after(n2, send1), e2),
        (dcq, crossed),
        ((0, (0,)), (1, (1,))),
        into=(cross_keep, cross_send),
        first=2,
    )
    e1, da, self_deltas, second_gain = turn_step(
        places,
        e2,
        h1,
        after(dcq, cross_send, unit_sum),
        dcq_theirs,
        all_gains[1],
        attended,
        mid_pieces,
        late,
        (out_columns, query_columns, late_query_columns),
    )
    got1 = swap(after(send1, dcq_theirs), "narrow", 1)
    cross_stay, cross_leave = add_pair(cross_keep, swap(cross_send, "wide", 1))
    da = after(da, cross_leave)
    back = []
    for pair in range(pairs):
        ready = after(da, *[part[0] for part in back])
        if pair == pairs - 1:
            early_back = list(back)
            self_keep, self_send = weight_grads(
                places,
                (after(n1, back[-1][0]), e1),
                [[part[i] for part in early_back] for i in range(3)] + [attended],
                ((0, (0, 1, 2)), (1, (3,))),
            )
            cross_part = add(cross_stay, swap(cross_leave, "wide", 2))
            ready = after(ready, cross_part, self_send)
            cross_part = line_first(cross_part)
        back.append(
            self_backward(
                pair, qkv, ready, self_parts[pair][1], self_deltas, row_ids, col_ids
            )
        )
    dq, dk, dv = [[part[i] for part in back] for i in range(3)]
    self_stay, self_leave = add_pair(self_keep, swap(self_send, "wide", 1))
    self_part = add(self_stay, swap(self_leave, "wide", 2))
    dn1, last_keep, last_send = partial_step(
        places,
        dq + dk + dv,
        after(x, self_leave),
        n1,
        second_gain,
        third_gain,
        early_pieces,
    )
    dn1_theirs = swap(dn1, "narrow", 1)
    memory1 = add(after(keep1, dn1), got1)
    last_stay, last_leave = add_pair(last_keep, swap(last_send, "wide", 1))
    last_part = add(last_stay, swap(last_leave, "wide", 2))
    output = restore_rows(pos, after(output, last_send, self_part))
    tokens_grad = last_step(pos, e1, x, dn1, dn1_theirs, all_gains[0])
    memory_grad = jnp.stack([after(memory0, self_part), memory1])
    cross_sum = line_third(line_second(cross_part), tokens_grad)
    self_second = line_second(line_first(self_part))
    self_sum = line_third(self_second, tokens_grad)
    last_sum = line_third(line_second(line_first(last_part)))
    gain_sums = last_sum[share:, :share].astype(F32)
    first_gain = gain_sums[0] + swap(after(gain_sums, self_second), "narrow", 1)[0]

    def grads(array, size, count):
        return [array[:share, i * size : (i + 1) * size].astype(F32) for i in range(count)]

    gate_grad, up_grad, down_grad = grads(after(unit_sum, self_part), unit, 3)
    cross_k_grad, cross_v_grad, cross_q_grad, cross_o_grad = grads(cross_sum, inner, 4)
    part = inner - PAIR
    q_grad, k_grad, v_grad = [
        jnp.concatenate([most, rest], axis=1)
        for most, rest in zip(grads(self_sum, part, 3), grads(last_sum, PAIR, 3))
    ]
    o_grad = self_sum[:, 3 * part :].astype(F32)
    return (
        output,
        tokens_grad,
        memory_grad,
        first_gain,
        gain_sums[1],
        gain_sums[2],
        q_grad,
        k_grad,
        v_grad,
        o_grad,
        cross_q_grad,
        cross_k_grad,
        cross_v_grad,
        cross_o_grad,
        gate_grad,
        up_grad,
        down_grad,
    )


def solution(mesh):
    both = ("dp", "wide")
    weight = P("wide", "narrow")
    in_specs = (
        (P(both, None), P(both, None, None), P(both, None))
        + (P("wide"),) * 3
        + (weight,) * 11
        + (P(both, None),) * 3
    )
    out_specs = (
        (P(both, None), P(both, None), P(both, None, "narrow"))
        + (P("wide"),) * 3
        + (weight,) * 11
    )
    return jax.shard_map(local, mesh=mesh, in_specs=in_specs, out_specs=out_specs, check_vma=False)
```

```python
import functools
import math

import jax
import jax.numpy as jnp
from jax import lax
from jax.experimental import pallas as pl
from jax.experimental.pallas import tpu as pltpu
from jax.sharding import PartitionSpec as P

F32 = jnp.float32
BF16 = jnp.bfloat16
EPSILON = 1e-06
ROOT_TWO_OVER_PI = 0.7978845608028654
CUBIC = 0.044715
HEAD_DIM = 64
PAIR = 2 * HEAD_DIM
SCALE = HEAD_DIM ** (-0.5)
EXP2_SCALE = SCALE * math.log2(math.e)
HIDE = 1e30
TILE = 256
ROWS = 512
WEIGH = 4.0

NN = (((1,), (0,)), ((), ()))
NT = (((1,), (1,)), ((), ()))
TN = (((0,), (0,)), ((), ()))


def dot(left, right, dims):
    return lax.dot_general(left, right, dims, preferred_element_type=F32)


def params(mebibytes=24):
    return pltpu.CompilerParams(vmem_limit_bytes=mebibytes * 1024 * 1024)


def cost(flops, nbytes):
    return pl.CostEstimate(
        flops=int(flops * WEIGH), bytes_accessed=int(nbytes * WEIGH), transcendentals=0
    )


def pin(*arrays):
    return [pltpu.with_memory_space_constraint(array, pltpu.HBM) for array in arrays]


def shape_of(shape, dtype):
    return jax.ShapeDtypeStruct(shape, dtype)


def whole(shape):
    zeros = (0,) * len(shape)
    return pl.BlockSpec(shape, lambda *_: zeros)


def rows(width, height=None):
    height = ROWS if height is None else height
    return pl.BlockSpec((height, width), lambda t, *_: (t, 0))


def inverse_rms(values):
    return lax.rsqrt(jnp.mean(values * values, axis=1, keepdims=True) + EPSILON)


def norm_back(values, gain, upstream):
    factor = inverse_rms(values)
    scaled = upstream * gain
    mean = jnp.mean(values * scaled, axis=1, keepdims=True)
    grad = factor * scaled - values * (factor * factor * factor * mean)
    return grad, jnp.sum(upstream * values * factor, axis=0, keepdims=True)


def in_half(shape, half):
    return (lax.broadcasted_iota(jnp.int32, shape, 1) // HEAD_DIM) == half


def only_half(values, half):
    return jnp.where(in_half(values.shape, half), values, jnp.zeros_like(values))


def order_kernel(seg, blk, table, x, xp, row_ids, col_ids, pos_out, scalars, pos):
    step = pl.program_id(0)
    count = seg.shape[1]

    @pl.when(step == 0)
    def _():
        segments = seg[...]
        image = jnp.zeros_like(segments)
        for s in range(table.shape[1]):
            image = jnp.where(segments == s, table[0, s], image)
        first = (image == 0).astype(F32)
        before = lax.broadcasted_iota(jnp.int32, (count, count), 0) < lax.broadcasted_iota(
            jnp.int32, (count, count), 1
        )
        rank = dot(
            jnp.broadcast_to(first, (8, count)).astype(BF16),
            before.astype(F32).astype(BF16),
            NN,
        )[0:1]
        total = jnp.sum(first)
        index = lax.broadcasted_iota(jnp.int32, (1, count), 1).astype(F32)
        place = jnp.where(image == 0, rank, total + index - rank)
        pos[...] = place.astype(jnp.int32)
        pos_out[...] = jnp.broadcast_to(pos[...], (8, count))
        n0 = total.astype(jnp.int32)
        tiles = count // TILE
        visits0 = jnp.maximum(1, (n0 + TILE - 1) // TILE)
        start1 = jnp.minimum(tiles - 1, n0 // TILE)
        visits = visits0 + tiles - start1
        for v in range(tiles + 1):
            real = jnp.minimum(v, visits - 1)
            in_first = real < visits0
            scalars[v] = jnp.where(in_first, real, real - visits0 + start1)
            scalars[8 + v] = jnp.where(in_first, 0, 1)
        scalars[16] = visits
        scalars[17] = n0
        scalars[18] = visits0
        scalars[19] = start1
        scalars[20] = tiles - start1

    onehot = (
        lax.broadcasted_iota(jnp.int32, (TILE, count), 0) + step * TILE == pos[...]
    ).astype(F32).astype(BF16)
    xp[...] = dot(onehot, x[...], NN).astype(BF16)
    ids = jnp.concatenate(
        [
            seg[...].astype(F32),
            blk[...].astype(F32),
            jnp.zeros((126, count), F32),
        ],
        axis=0,
    ).astype(BF16)
    row_ids[...] = dot(ids[0:8], onehot, NT)
    col_ids[...] = dot(onehot, ids, NT)


def order_rows(seg, blk, table, x):
    count, width = x.shape
    return pl.pallas_call(
        order_kernel,
        grid=(count // TILE,),
        in_specs=[
            whole((1, count)),
            whole((1, count)),
            pl.BlockSpec(memory_space=pltpu.SMEM),
            whole((count, width)),
        ],
        out_specs=[
            rows(width, TILE),
            pl.BlockSpec((8, TILE), lambda t: (0, t)),
            rows(128, TILE),
            whole((8, count)),
            pl.BlockSpec(memory_space=pltpu.SMEM),
        ],
        out_shape=[
            pltpu.HBM((count, width), BF16),
            shape_of((8, count), F32),
            shape_of((count, 128), F32),
            shape_of((8, count), jnp.int32),
            shape_of((32,), jnp.int32),
        ],
        scratch_shapes=[pltpu.VMEM((1, count), jnp.int32)],
        compiler_params=params(),
        cost_estimate=cost(2 * count * count * width, 8 * count * width),
    )(seg, blk, table, *pin(x))


def order_more_kernel(pos, values, out):
    size, count = out.shape[0], values.shape[0]
    index = lax.broadcasted_iota(jnp.int32, (size, count), 0) + pl.program_id(0) * size
    onehot = (index == pos[0:1, :]).astype(F32).astype(BF16)
    out[...] = dot(onehot, values[...], NN).astype(BF16)


def order_more(pos, values):
    count, width = values.shape
    return pl.pallas_call(
        order_more_kernel,
        grid=(count // TILE,),
        in_specs=[whole((8, count)), whole((count, width))],
        out_specs=rows(width, TILE),
        out_shape=pltpu.HBM((count, width), BF16),
        compiler_params=params(),
        cost_estimate=cost(2 * count * count * width, 4 * count * width),
    )(pos, *pin(values))


def restore_kernel(pos, values, out):
    count = values.shape[0]
    onehot = (
        lax.broadcasted_iota(jnp.int32, (count, TILE), 0) == pos[0:1, :]
    ).astype(F32).astype(BF16)
    out[...] = dot(onehot, values[...], TN).astype(BF16)


def restore_rows(pos, values):
    count, width = values.shape
    return pl.pallas_call(
        restore_kernel,
        grid=(count // TILE,),
        in_specs=[pl.BlockSpec((8, TILE), lambda t: (0, t)), whole((count, width))],
        out_specs=rows(width, TILE),
        out_shape=shape_of((count, width), BF16),
        compiler_params=params(),
        cost_estimate=cost(2 * count * count * width, 4 * count * width),
    )(pos, *pin(values))


def fetch(pieces, places, columns, dest, sems, base=0):
    height = dest.shape[0] // 4
    copies = []
    for i, piece in enumerate(pieces):
        start = pl.multiple_of(places[i] * height, 16)
        copies.append(
            pltpu.make_async_copy(
                piece.at[pl.ds(0, height), columns],
                dest.at[pl.ds(start, height), :],
                sems.at[base + i],
            )
        )
    return copies


def fetch_half(gathered, half, columns, dest, sem):
    return pltpu.make_async_copy(gathered.at[half, :, columns], dest, sem)


def start_all(copies):
    for copy in copies:
        copy.start()


def wait_all(copies):
    for copy in copies:
        copy.wait()


ANY = pl.BlockSpec(memory_space=pl.ANY)
SCALARS = pl.BlockSpec(memory_space=pltpu.SMEM)


def project_kernel(places, x, gain, w0, w1, w2, w3, normed, out, weight, sems):
    @pl.when(pl.program_id(0) == 0)
    def _():
        copies = fetch((w0, w1, w2, w3), places, slice(0, weight.shape[1]), weight, sems)
        start_all(copies)
        wait_all(copies)

    values = x[...].astype(F32)
    n1 = (values * inverse_rms(values) * gain[...]).astype(BF16)
    normed[...] = n1
    out[...] = dot(n1, weight[...], NN).astype(BF16)


def norm_project(places, x, gain, pieces):
    count, width = x.shape
    outs = pieces[0].shape[1]
    return pl.pallas_call(
        project_kernel,
        grid=(count // ROWS,),
        in_specs=[SCALARS, rows(width), whole((1, width))] + [ANY] * 4,
        out_specs=[rows(width), rows(outs)],
        out_shape=[pltpu.HBM((count, width), BF16), shape_of((count, outs), BF16)],
        scratch_shapes=[pltpu.VMEM((width, outs), BF16), pltpu.SemaphoreType.DMA((4,))],
        compiler_params=params(),
        cost_estimate=cost(2 * count * width * outs, 4 * count * width + 2 * count * outs),
    )(places, *pin(x), gain, *pieces)


MEMORY_TILE = 1024
BACK_TILE = 512


def memory_kernel(places, columns, memory, w0, w1, w2, w3, out, weight, sems):
    @pl.when(pl.program_id(0) == 0)
    def _():
        copies = fetch((w0, w1, w2, w3), places, columns, weight, sems)
        start_all(copies)
        wait_all(copies)

    out[...] = dot(memory[...], weight[...], NN).astype(BF16)


def project_memory(places, memory, pieces, columns):
    count, width = memory.shape
    outs = columns.stop - columns.start

    def kernel(places, *refs):
        memory_kernel(places, columns, *refs)

    return pl.pallas_call(
        kernel,
        grid=(count // MEMORY_TILE,),
        in_specs=[SCALARS, rows(width, MEMORY_TILE)] + [ANY] * 4,
        out_specs=rows(outs, MEMORY_TILE),
        out_shape=pltpu.HBM((count, outs), BF16),
        scratch_shapes=[pltpu.VMEM((width, outs), BF16), pltpu.SemaphoreType.DMA((4,))],
        compiler_params=params(),
        cost_estimate=cost(2 * count * width * outs, 4 * count * width),
    )(places, *pin(memory), *pieces)


SELF_TILE = 256
SELF_WINDOW = 640
BACK_WINDOW = 640


def store_logs(ref, columns, logs, extra=None):
    spread = jnp.where(in_half((logs[0].shape[0], PAIR), 0), logs[0], logs[1]).T
    for half in range(2):
        line = spread[half * HEAD_DIM : half * HEAD_DIM + 1, :]
        if extra is not None:
            line = jnp.where(extra, line, ref[half : half + 1, columns])
        ref[half : half + 1, columns] = line


def self_forward_kernel(q, k, v, row_ids, col_ids, out, logs):
    count = q.shape[0]
    for tile in range(count // SELF_TILE):
        base = tile * SELF_TILE
        start = min(max(base - 256, 0), count - SELF_WINDOW)
        spot = slice(base, base + SELF_TILE)
        window = slice(start, start + SELF_WINDOW)
        seen = (col_ids[spot, 0:1] == row_ids[0:1, window]) & (
            row_ids[1:2, window] <= col_ids[spot, 1:2]
        )
        bias = jnp.where(seen, 0.0, -HIDE)
        keys = k[window, :]
        values = v[window, :]
        queries = q[spot, :]
        parts, totals = [], []
        for half in range(2):
            scores = dot(only_half(queries, half), keys, NT) * EXP2_SCALE + bias
            highest = jnp.max(scores, axis=1, keepdims=True)
            weights = jnp.exp2(scores - highest)
            total = jnp.sum(weights, axis=1, keepdims=True)
            parts.append(dot(weights.astype(BF16), values, NN) / total)
            totals.append(highest + jnp.log2(total))
        out[spot, :] = jnp.where(in_half(parts[0].shape, 0), parts[0], parts[1]).astype(BF16)
        store_logs(logs, spot, totals)


def self_forward(pair, qkv, row_ids, col_ids):
    count = qkv.shape[0]
    pairs = qkv.shape[1] // (3 * PAIR)

    def part(which):
        return pl.BlockSpec((count, PAIR), lambda p: (0, which * pairs + pair))

    return pl.pallas_call(
        self_forward_kernel,
        grid=(1,),
        in_specs=[part(0), part(1), part(2), whole((8, count)), whole((count, 128))],
        out_specs=[whole((count, PAIR)), whole((8, count))],
        out_shape=[pltpu.HBM((count, PAIR), BF16), pltpu.HBM((8, count), F32)],
        compiler_params=params(),
        cost_estimate=cost(16 * count * SELF_WINDOW * PAIR, 8 * count * PAIR),
    )(qkv, qkv, qkv, row_ids, col_ids)


def self_backward_kernel(q, k, v, grad, logs, deltas, row_ids, col_ids, dq, dk, dv, key_sum, value_sum):
    count = q.shape[0]
    key_sum[...] = jnp.zeros_like(key_sum)
    value_sum[...] = jnp.zeros_like(value_sum)
    for tile in range(count // TILE):
        base = tile * TILE
        start = min(max(base - 256, 0), count - BACK_WINDOW)
        spot = slice(base, base + TILE)
        window = slice(start, start + BACK_WINDOW)
        seen = (col_ids[window, 0:1] == row_ids[0:1, spot]) & (
            col_ids[window, 1:2] <= row_ids[1:2, spot]
        )
        bias = jnp.where(seen, 0.0, -HIDE)
        keys = k[window, :]
        values = v[window, :]
        queries = q[spot, :]
        grads = grad[spot, :]
        parts = []
        for half in range(2):
            one_query = only_half(queries, half)
            one_grad = only_half(grads, half)
            scores = dot(keys, one_query, NT) * EXP2_SCALE + bias
            weights = jnp.exp2(scores - logs[half : half + 1, spot])
            slopes = dot(values, one_grad, NT)
            pushed = (weights * (slopes - deltas[half : half + 1, spot])).astype(BF16)
            value_sum[window, :] += dot(weights.astype(BF16), one_grad, NN)
            key_sum[window, :] += dot(pushed, one_query, NN)
            parts.append(dot(pushed, keys, TN))
        dq[spot, :] = (
            jnp.where(in_half(parts[0].shape, 0), parts[0], parts[1]) * SCALE
        ).astype(BF16)
    dk[...] = (key_sum[...] * SCALE).astype(BF16)
    dv[...] = value_sum[...].astype(BF16)


def self_backward(pair, qkv, grad, logs, deltas, row_ids, col_ids):
    count = qkv.shape[0]
    pairs = qkv.shape[1] // (3 * PAIR)

    def part(which):
        return pl.BlockSpec((count, PAIR), lambda p: (0, which * pairs + pair))

    return pl.pallas_call(
        self_backward_kernel,
        grid=(1,),
        in_specs=[
            part(0),
            part(1),
            part(2),
            part(0),
            whole((8, count)),
            pl.BlockSpec((8, count), lambda p: (pair, 0)),
            whole((8, count)),
            whole((count, 128)),
        ],
        out_specs=[whole((count, PAIR))] * 3,
        out_shape=[pltpu.HBM((count, PAIR), BF16)] * 3,
        scratch_shapes=[pltpu.VMEM((count, PAIR), F32)] * 2,
        compiler_params=params(),
        cost_estimate=cost(40 * count * BACK_WINDOW * PAIR, 16 * count * PAIR),
    )(qkv, qkv, qkv, grad, logs, deltas, row_ids, col_ids)


KEYS = 1024


def visits_of(image, scalars):
    first = jnp.where(image == 0, 0, scalars[19])
    return first, jnp.where(image == 0, scalars[18], scalars[20])


def cross_forward_kernel(scalars, q, k, v, out, logs):
    image = pl.program_id(0)
    first, count = visits_of(image, scalars)

    def visit(i, carry):
        base = pl.multiple_of((first + i) * TILE, TILE)
        spot = pl.ds(base, TILE)
        queries = q[spot, :]
        parts, totals = [], []
        tops, sums = [None, None], [None, None]
        for start in range(0, k.shape[0], KEYS):
            keys = k[start : start + KEYS, :]
            values = v[start : start + KEYS, :]
            both = [dot(only_half(queries, half), keys, NT) for half in range(2)]
            for half, scores in enumerate(both):
                highest = jnp.max(scores, axis=1, keepdims=True) * EXP2_SCALE
                if start:
                    highest = jnp.maximum(highest, tops[half])
                weights = jnp.exp2(scores * EXP2_SCALE - highest).astype(BF16)
                mixed = dot(
                    weights,
                    jnp.where(in_half(values.shape, half), values, jnp.ones_like(values)),
                    NN,
                )
                if start:
                    mixed = mixed + sums[half] * jnp.exp2(tops[half] - highest)
                tops[half], sums[half] = highest, mixed
        for half in range(2):
            total = pltpu.roll(sums[half], HEAD_DIM, 1)
            parts.append(sums[half] / total)
            totals.append(tops[half] + jnp.log2(total))
        mixed = jnp.where(in_half(parts[0].shape, 0), parts[0], parts[1]).astype(BF16)
        limit = jnp.where(image == 0, 0, scalars[17]) - base
        row_mine = lax.broadcasted_iota(jnp.int32, mixed.shape, 0) >= limit
        lane_mine = lax.broadcasted_iota(jnp.int32, (1, TILE), 1) >= limit
        out[spot, :] = jnp.where(row_mine, mixed, out[spot, :])
        store_logs(logs, spot, totals, lane_mine)
        return carry

    lax.fori_loop(0, count, visit, 0)


def cross_forward(pair, scalars, q, keys_values, images):
    count, inner = q.shape
    pairs = inner // PAIR
    memory_rows = keys_values.shape[0] // images

    def part(which):
        return pl.BlockSpec((memory_rows, PAIR), lambda i, sc: (i, which * pairs + pair))

    return pl.pallas_call(
        cross_forward_kernel,
        grid_spec=pltpu.PrefetchScalarGridSpec(
            num_scalar_prefetch=1,
            grid=(images,),
            in_specs=[
                pl.BlockSpec((count, PAIR), lambda i, sc: (0, pair)),
                part(0),
                part(1),
            ],
            out_specs=[whole((count, PAIR)), whole((8, count))],
        ),
        out_shape=[pltpu.HBM((count, PAIR), BF16), pltpu.HBM((8, count), F32)],
        compiler_params=params(),
        cost_estimate=cost(20 * count * memory_rows * PAIR, 8 * memory_rows * PAIR),
    )(scalars, *pin(q, keys_values, keys_values))


def cross_backward_kernel(
    image, scalars, q, k, v, grad, logs, deltas, old, dq, dk, dv, key_sum, value_sum
):
    first, count = visits_of(jnp.int32(image), scalars)
    if image:
        dq[...] = old[...]

    def visit(i, fresh):
        base = pl.multiple_of((first + i) * TILE, TILE)
        spot = pl.ds(base, TILE)
        queries = q[spot, :]
        grads = grad[spot, :]
        keys = k[...]
        values = v[...]
        limit = scalars[17] - base
        lane_mine = (lax.broadcasted_iota(jnp.int32, (1, TILE), 1) >= limit) == (image == 1)
        parts = []
        for half in range(2):
            one_query = only_half(queries, half)
            one_grad = only_half(grads, half)
            log = jnp.where(lane_mine, logs[half : half + 1, spot], HIDE)
            scores = dot(keys, one_query, NT)
            weights = jnp.exp2(scores * EXP2_SCALE - log)
            slopes = dot(values, one_grad, NT)
            pushed = (weights * (slopes - deltas[half : half + 1, spot])).astype(BF16)
            value_part = dot(weights.astype(BF16), one_grad, NN)
            key_part = dot(pushed, one_query, NN)
            if fresh and half == 0:
                value_sum[...] = value_part
                key_sum[...] = key_part
            else:
                value_sum[...] += value_part
                key_sum[...] += key_part
            parts.append(dot(pushed, keys, TN))
        grad_query = (
            jnp.where(in_half(parts[0].shape, 0), parts[0], parts[1]) * SCALE
        ).astype(BF16)
        if image:
            row_mine = lax.broadcasted_iota(jnp.int32, grad_query.shape, 0) >= limit
            grad_query = jnp.where(row_mine, grad_query, dq[spot, :])
        dq[spot, :] = grad_query

    def later(i, carry):
        visit(i, False)
        return carry

    visit(0, True)
    lax.fori_loop(1, count, later, 0)
    dk[...] = (key_sum[...] * SCALE).astype(BF16)
    dv[...] = value_sum[...].astype(BF16)


def cross_backward(image, scalars, q, keys_values, grad, logs, deltas, images, old):
    count, inner = q.shape
    pairs = inner // PAIR
    memory_rows = keys_values.shape[0] // images
    token_spec = pl.BlockSpec((count, PAIR), lambda p, sc: (0, p))
    line = pl.BlockSpec((8, count), lambda p, sc: (p, 0))
    result = pl.BlockSpec((memory_rows, PAIR), lambda p, sc: (0, p))

    def part(which):
        return pl.BlockSpec((memory_rows, PAIR), lambda p, sc: (image, which * pairs + p))

    def first_kernel(scalars, q, k, v, grad, logs, deltas, *rest):
        cross_backward_kernel(image, scalars, q, k, v, grad, logs, deltas, None, *rest)

    def second_kernel(*refs):
        cross_backward_kernel(image, *refs)

    extra = [old] if image else []
    return pl.pallas_call(
        second_kernel if image else first_kernel,
        grid_spec=pltpu.PrefetchScalarGridSpec(
            num_scalar_prefetch=1,
            grid=(pairs,),
            in_specs=[token_spec, part(0), part(1), token_spec, line, line]
            + [token_spec] * len(extra),
            out_specs=[token_spec, result, result],
            scratch_shapes=[pltpu.VMEM((memory_rows, PAIR), F32)] * 2,
        ),
        out_shape=[
            pltpu.HBM((count, inner), BF16),
            pltpu.HBM((memory_rows, inner), BF16),
            pltpu.HBM((memory_rows, inner), BF16),
        ],
        compiler_params=params(32),
        cost_estimate=cost(25 * count * memory_rows * inner, 8 * memory_rows * inner),
    )(scalars, *pin(q, keys_values, keys_values, grad), logs, deltas, *pin(*extra))


def put_rows(places, product, keep, send, span=slice(None)):
    height = product.shape[0] // 4
    for i, ref in enumerate((keep, keep, send, send)):
        start = pl.multiple_of(places[i] * height, 16)
        ref[i % 2, 0:height, span] = product[pl.ds(start, height), :].astype(BF16)


def memory_back_kernel(
    columns, last, places, memory, dk, dv, w0, w1, w2, w3, *refs
):
    if last:
        before, keep_part, send_part, keep, send, weight, total, sems = refs
    else:
        keep_part, send_part, send_more, total_out, weight, total, sems = refs
    inner = dk.shape[1]

    @pl.when(pl.program_id(0) == 0)
    def _():
        copies = fetch((w0, w1, w2, w3), places, columns, weight, sems)
        start_all(copies)
        if last:
            total[...] = before[...]
        else:
            total[...] = jnp.zeros_like(total)
        wait_all(copies)

    both = jnp.concatenate([dk[...], dv[...]], axis=1)
    product = dot(both, weight[...], NT).astype(BF16)
    lower, upper = product[:, :inner], product[:, inner:]
    side = places[4]
    leave = jnp.where(side == 0, upper, lower)
    if last:
        send_part[...] = leave
    else:

        @pl.when(pl.program_id(0) < pl.num_programs(0) // 2)
        def _():
            send_part[...] = leave

        @pl.when(pl.program_id(0) >= pl.num_programs(0) // 2)
        def _():
            send_more[...] = leave

    keep_part[...] = jnp.where(side == 0, lower, upper)
    total[...] += dot(memory[...], both, TN)

    @pl.when(pl.program_id(0) == pl.num_programs(0) - 1)
    def _():
        if last:
            put_rows(places, total, keep, send)
        else:
            total_out[...] = total[...]


def memory_back(places, memory, dk, dv, pieces, columns, image, before, spare):
    count, inner = dk.shape
    width = memory.shape[1]
    steps = count // BACK_TILE
    last = before is not None
    ranks = pltpu.HBM((2, width // 4, spare + 2 * inner), BF16)
    rank_spec = pl.BlockSpec((2, width // 4, 2 * inner), lambda t: (0, 0, 0))

    def kernel(*refs):
        memory_back_kernel(columns, last, *refs)

    return pl.pallas_call(
        kernel,
        grid=(steps,),
        in_specs=[
            SCALARS,
            pl.BlockSpec((BACK_TILE, width), lambda t: (image * steps + t, 0)),
            rows(inner, BACK_TILE),
            rows(inner, BACK_TILE),
        ]
        + [ANY] * 4
        + ([whole((width, 2 * inner))] if last else []),
        out_specs=[rows(inner, BACK_TILE)]
        + (
            [rows(inner, BACK_TILE), rank_spec, rank_spec]
            if last
            else [
                pl.BlockSpec((BACK_TILE, inner), lambda t: (jnp.minimum(t, steps // 2 - 1), 0)),
                pl.BlockSpec((BACK_TILE, inner), lambda t: (jnp.maximum(t - steps // 2, 0), 0)),
                whole((width, 2 * inner)),
            ]
        ),
        out_shape=[pltpu.HBM((count, inner), BF16)]
        + (
            [pltpu.HBM((count, inner), BF16), ranks, ranks]
            if last
            else [
                pltpu.HBM((count // 2, inner), BF16),
                pltpu.HBM((count // 2, inner), BF16),
                shape_of((width, 2 * inner), F32),
            ]
        ),
        scratch_shapes=[
            pltpu.VMEM((width, 2 * inner), BF16),
            pltpu.VMEM((width, 2 * inner), F32),
            pltpu.SemaphoreType.DMA((4,)),
        ],
        compiler_params=params(),
        cost_estimate=cost(8 * count * width * inner, 8 * count * width),
    )(places, *pin(memory, dk, dv), *pieces, *([before] if last else []))


def weight_grads_kernel(plan, spans, places, left_refs, right_refs, keep, send, scratch):
    left_holds = scratch[: len(left_refs)]
    right_holds = scratch[len(left_refs) : -3]
    turned, product, sems = scratch[-3:]
    step = pl.program_id(0)
    lefts = [
        pltpu.make_async_copy(ref, hold, sems.at[i])
        for i, (ref, hold) in enumerate(zip(left_refs, left_holds))
    ]
    rights = [
        pltpu.make_async_copy(ref, hold, sems.at[len(left_refs) + i])
        for i, (ref, hold) in enumerate(zip(right_refs, right_holds))
    ]
    for at, (left, group) in enumerate(plan):
        fresh = at == 0 or plan[at - 1][0] != left

        @pl.when(step == at)
        def _():
            if at == 0:
                lefts[left].start()
                for g in group:
                    rights[g].start()
            if fresh:
                lefts[left].wait()
            if at == 0:
                begun = {left}
                for one, others in plan[1:]:
                    if one not in begun:
                        lefts[one].start()
                        begun.add(one)
                    for g in others:
                        rights[g].start()
            if fresh:
                turned[...] = left_holds[left][...].T
            for g in group:
                rights[g].wait()
            right = join([right_holds[g] for g in group])
            columns = right.shape[1]
            product[:, 0:columns] = dot(turned[...], right, NN)
            put_rows(places, product.at[:, 0:columns], keep, send, spans[at])


def join(refs):
    values = [ref[...] for ref in refs]
    return values[0] if len(values) == 1 else jnp.concatenate(values, axis=1)


def flatten(groups):
    flat, sizes = [], []
    for group in groups:
        group = group if isinstance(group, (list, tuple)) else [group]
        flat += list(group)
        sizes.append(len(group))
    return flat, sizes


def weight_grads(places, lefts, rights, plan, into=(), first=0):
    count, width = lefts[0].shape
    flat, sizes = flatten(rights)
    groups, at = [], 0
    for size in sizes:
        groups.append(list(range(at, at + size)))
        at += size
    plan = [(left, [f for g in group for f in groups[g]]) for left, group in plan]
    columns = [sum(flat[f].shape[1] for f in group) for _, group in plan]
    step_columns = columns[0]
    share = width // 4
    total = sum(columns) + first * step_columns
    even = len(set(columns)) == 1
    spans = [
        slice(0, step_columns) if even else slice(sum(columns[:at]), sum(columns[: at + 1]))
        for at in range(len(plan))
    ]
    extra = list(into)
    def kernel(places, *refs):
        lefts_end = len(lefts)
        rights_end = lefts_end + len(flat)
        weight_grads_kernel(
            plan,
            spans,
            places,
            refs[:lefts_end],
            refs[lefts_end:rights_end],
            *refs[rights_end + len(extra) : rights_end + len(extra) + 2],
            refs[rights_end + len(extra) + 2 :],
        )

    start = 1 + len(lefts) + len(flat)
    return pl.pallas_call(
        kernel,
        grid=(len(plan),),
        in_specs=[SCALARS]
        + [ANY] * (len(lefts) + len(flat) + len(extra)),
        out_specs=[
            pl.BlockSpec((2, share, step_columns), lambda t: (0, 0, t + first))
            if even
            else whole((2, share, total))
        ]
        * 2,
        out_shape=[pltpu.HBM((2, share, total), BF16)] * 2,
        input_output_aliases={start: 0, start + 1: 1} if extra else {},
        scratch_shapes=[pltpu.VMEM(array.shape, array.dtype) for array in list(lefts) + flat]
        + [
            pltpu.VMEM((width, count), BF16),
            pltpu.VMEM((width, max(columns)), F32),
            pltpu.SemaphoreType.DMA((len(lefts) + len(flat),)),
        ],
        compiler_params=params(32),
        cost_estimate=cost(
            2 * count * width * sum(columns), 4 * count * width * len(plan)
        ),
    )(places, *pin(*lefts, *flat), *extra)


def middle_kernel(plan, parts, places, x, gain, *refs):
    mine, theirs, refs = refs[:parts], refs[parts : 2 * parts], refs[2 * parts :]
    pieces, (h1, n2, cq, out_mine, out_theirs, query, sems) = refs[:8], refs[8:]

    @pl.when(pl.program_id(0) == 0)
    def _():
        copies = (
            fetch(pieces[:4], places, plan[0], out_mine, sems, 0)
            + fetch(pieces[4:], places, plan[1], out_theirs, sems, 4)
            + fetch(pieces[:4], places, plan[2], query, sems, 8)
        )
        start_all(copies)
        wait_all(copies)

    values = (
        x[...].astype(F32)
        + dot(join(mine), out_mine[...], NT)
        + dot(join(theirs), out_theirs[...], NT)
    )
    h1[...] = values.astype(BF16)
    normed = (values * inverse_rms(values) * gain[...]).astype(BF16)
    n2[...] = normed
    cq[...] = dot(normed, query[...], NN).astype(BF16)


def middle_step(places, x, mine, theirs, gain, pieces, pieces_theirs, plan):
    count, width = x.shape
    half = sum(part.shape[1] for part in mine)

    def kernel(*refs):
        middle_kernel(plan, len(mine), *refs)

    return pl.pallas_call(
        kernel,
        grid=(count // ROWS,),
        in_specs=[SCALARS, rows(width), whole((1, width))]
        + [rows(PAIR)] * (2 * len(mine))
        + [ANY] * 8,
        out_specs=[rows(width), rows(width), rows(half)],
        out_shape=[
            pltpu.HBM((count, width), BF16),
            pltpu.HBM((count, width), BF16),
            pltpu.HBM((count, half), BF16),
        ],
        scratch_shapes=[pltpu.VMEM((width, half), BF16)] * 3 + [pltpu.SemaphoreType.DMA((12,))],
        compiler_params=params(),
        cost_estimate=cost(6 * count * width * half, 12 * count * width),
    )(places, *pin(x), gain, *pin(*mine), *theirs, *pieces, *pieces_theirs)


def head_sums(left, right):
    product = left.astype(F32) * right.astype(F32)
    width = product.shape[1]
    high = product.astype(BF16)
    low = (product - high.astype(F32)).astype(BF16)
    height = 8 * (width // PAIR)
    line = lax.broadcasted_iota(jnp.int32, (height, width), 0)
    head = lax.broadcasted_iota(jnp.int32, (height, width), 1) // HEAD_DIM
    choose = (
        ((line // 8) * 2 + line % 8 == head) & (line % 8 < 2)
    ).astype(F32).astype(BF16)
    return dot(choose, high, NT) + dot(choose, low, NT)


CHUNK = 512


def units_kernel(plan, parts, places, h1, gain, gy, *refs):
    mine, theirs, refs = refs[:parts], refs[parts : 2 * parts], refs[2 * parts :]
    late, refs = refs[0], refs[1:]
    (
        output,
        n3,
        hidden,
        grad_gate,
        grad_up,
        e2,
        dc,
        deltas,
        gain_grad,
        out_mine,
        out_theirs,
        units_mine,
        units_theirs,
        sems,
    ) = refs
    step = pl.program_id(0)

    side = places[4]
    out_copies = [
        fetch_half(late, side, plan[0], out_mine, sems.at[0]),
        fetch_half(late, 1 - side, plan[0], out_theirs, sems.at[1]),
    ]
    mine_copy = fetch_half(late, side, plan[1], units_mine, sems.at[2])
    theirs_copy = fetch_half(late, 1 - side, plan[1], units_theirs, sems.at[3])

    @pl.when(step == 0)
    def _():
        start_all(out_copies + [mine_copy, theirs_copy])
        gain_grad[...] = jnp.zeros_like(gain_grad)
        wait_all(out_copies)

    crossed_mine = join(mine)
    values = (
        h1[...].astype(F32)
        + dot(crossed_mine, out_mine[...], NT)
        + dot(join(theirs), out_theirs[...], NT)
    )
    normed = (values * inverse_rms(values) * gain[...]).astype(BF16)
    n3[...] = normed
    upstream = gy[...]
    mixed = jnp.zeros_like(values)
    back = jnp.zeros_like(values)
    unit = units_mine.shape[1] // 3
    for own in (True, False):
        weight = units_mine if own else units_theirs

        @pl.when(step == 0)
        def _():
            (mine_copy if own else theirs_copy).wait()

        for start in range(0, unit, CHUNK):
            gate_weight = weight[:, start : start + CHUNK]
            up_weight = weight[:, unit + start : unit + start + CHUNK]
            down_weight = weight[:, 2 * unit + start : 2 * unit + start + CHUNK]
            gate = dot(normed, gate_weight, NN)
            up = dot(normed, up_weight, NN)
            pushed = dot(upstream, down_weight, NN)
            square = gate * gate
            bend = jnp.tanh(ROOT_TWO_OVER_PI * gate * (1.0 + CUBIC * square))
            lift = 0.5 * (1.0 + bend)
            gelu = gate * lift
            slope = lift + (0.5 * ROOT_TWO_OVER_PI) * gate * (1.0 - bend * bend) * (
                1.0 + (3.0 * CUBIC) * square
            )
            units = (gelu * up).astype(BF16)
            push_gate = (pushed * up * slope).astype(BF16)
            push_up = (pushed * gelu).astype(BF16)
            mixed = mixed + dot(units, down_weight, NT)
            back = back + dot(push_gate, gate_weight, NT) + dot(push_up, up_weight, NT)
            if own:
                hidden[:, start : start + CHUNK] = units
                grad_gate[:, start : start + CHUNK] = push_gate
                grad_up[:, start : start + CHUNK] = push_up
    output[...] = (values + mixed).astype(BF16)
    grad, gain_part = norm_back(values, gain[...], back)
    low = (upstream.astype(F32) + grad).astype(BF16)
    e2[...] = low
    crossed = dot(low, out_mine[...], NN).astype(BF16)
    dc[...] = crossed
    deltas[...] = head_sums(crossed, crossed_mine)
    gain_grad[0:1, :] += gain_part


def units_step(places, h1, mine, theirs, gain, gy, late, plan):
    count, width = h1.shape
    half = sum(part.shape[1] for part in mine)
    unit = (plan[1].stop - plan[1].start) // 3
    lines = 8 * (half // PAIR)

    def kernel(*refs):
        units_kernel(plan, len(mine), *refs)

    return pl.pallas_call(
        kernel,
        grid=(count // ROWS,),
        in_specs=[
            SCALARS,
            rows(width),
            whole((1, width)),
            rows(width),
        ]
        + [rows(PAIR)] * (2 * len(mine))
        + [ANY],
        out_specs=[
            rows(width),
            rows(width),
            rows(unit),
            rows(unit),
            rows(unit),
            rows(width),
            rows(half),
            pl.BlockSpec((lines, ROWS), lambda t: (0, t)),
            whole((8, width)),
        ],
        out_shape=[
            pltpu.HBM((count, width), BF16),
            pltpu.HBM((count, width), BF16),
            pltpu.HBM((count, unit), BF16),
            pltpu.HBM((count, unit), BF16),
            pltpu.HBM((count, unit), BF16),
            pltpu.HBM((count, width), BF16),
            pltpu.HBM((count, half), BF16),
            pltpu.HBM((lines, count), F32),
            shape_of((8, width), F32),
        ],
        scratch_shapes=[pltpu.VMEM((width, half), BF16)] * 2
        + [pltpu.VMEM((width, 3 * unit), BF16)] * 2
        + [pltpu.SemaphoreType.DMA((4,))],
        compiler_params=params(58),
        cost_estimate=cost(30 * count * width * unit, 30 * count * width),
    )(places, *pin(h1), gain, *pin(gy, *mine), *theirs, *pin(late))


def turn_kernel(plan, parts, places, e2, h1, mine, theirs, gain, *refs):
    attended, refs = refs[:parts], refs[parts:]
    pieces, refs = refs[:4], refs[4:]
    late, e1, da, deltas, gain_grad, query_mine, query_theirs, out_mine, sems = refs

    @pl.when(pl.program_id(0) == 0)
    def _():
        copies = (
            fetch(pieces, places, plan[0], out_mine, sems, 0)
            + fetch(pieces, places, plan[1], query_mine, sems, 4)
            + [fetch_half(late, 1 - places[4], plan[2], query_theirs, sems.at[8])]
        )
        start_all(copies)
        gain_grad[...] = jnp.zeros_like(gain_grad)
        wait_all(copies)

    back = dot(mine[...], query_mine[...], NT) + dot(theirs[...], query_theirs[...], NT)
    grad, gain_part = norm_back(h1[...].astype(F32), gain[...], back)
    low = (e2[...].astype(F32) + grad).astype(BF16)
    e1[...] = low
    pushed = dot(low, out_mine[...], NN).astype(BF16)
    da[...] = pushed
    deltas[...] = head_sums(pushed, join(attended))
    gain_grad[0:1, :] += gain_part


def turn_step(places, e2, h1, mine, theirs, gain, attended, pieces, late, plan):
    count, width = h1.shape
    half = mine.shape[1]
    lines = 8 * (half // PAIR)

    def kernel(*refs):
        turn_kernel(plan, len(attended), *refs)

    return pl.pallas_call(
        kernel,
        grid=(count // ROWS,),
        in_specs=[
            SCALARS,
            rows(width),
            rows(width),
            rows(half),
            rows(half),
            whole((1, width)),
        ]
        + [rows(PAIR)] * len(attended)
        + [ANY] * 5,
        out_specs=[
            rows(width),
            rows(half),
            pl.BlockSpec((lines, ROWS), lambda t: (0, t)),
            whole((8, width)),
        ],
        out_shape=[
            pltpu.HBM((count, width), BF16),
            shape_of((count, half), BF16),
            shape_of((lines, count), F32),
            shape_of((8, width), F32),
        ],
        scratch_shapes=[pltpu.VMEM((width, half), BF16)] * 3 + [pltpu.SemaphoreType.DMA((9,))],
        compiler_params=params(),
        cost_estimate=cost(6 * count * width * half, 16 * count * width),
    )(places, *pin(e2, h1, mine), theirs, gain, *pin(*attended), *pieces, *pin(late))


def partial_kernel(parts, places, x, n1, second, third, *refs):
    part_refs, refs = refs[:parts], refs[parts:]
    w0, w1, w2, w3, out, keep, send, weight, total, gain_grad, sems = refs
    step = pl.program_id(0)

    @pl.when(step == 0)
    def _():
        copies = fetch((w0, w1, w2, w3), places, slice(0, weight.shape[1]), weight, sems)
        start_all(copies)
        gain_grad[...] = jnp.zeros_like(gain_grad)
        total[...] = jnp.zeros_like(total)
        wait_all(copies)

    back = dot(join(part_refs), weight[...], NT)
    out[...] = back.astype(BF16)
    values = x[...].astype(F32)
    gain_grad[0:1, :] += jnp.sum(back * values * inverse_rms(values), axis=0, keepdims=True)
    last = join([part_refs[i * (parts // 3) + parts // 3 - 1] for i in range(3)])
    total[...] += dot(n1[...], last, TN)

    @pl.when(step == pl.num_programs(0) - 1)
    def _():
        put_rows(places, total, keep, send)
        height = total.shape[0] // 4
        lines = jnp.concatenate(
            [
                gain_grad[0:1, :],
                second[0:1, :],
                third[0:1, :],
                jnp.zeros((13, gain_grad.shape[1]), F32),
            ],
            axis=0,
        )
        shares = [lines[:, w * height : (w + 1) * height] for w in range(4)]
        fill = jnp.zeros((16, total.shape[1] - height), F32)
        for i, ref in enumerate((keep, keep, send, send)):
            share = shares[0]
            for w in range(1, 4):
                share = jnp.where(places[i] == w, shares[w], share)
            ref[i % 2, height : height + 16, :] = jnp.concatenate([share, fill], axis=1).astype(
                BF16
            )


def partial_step(places, parts, x, n1, second, third, pieces):
    count, width = x.shape
    inner = sum(part.shape[1] for part in parts)
    ranks = (2, width // 4 + 16, 3 * PAIR)

    def kernel(*refs):
        partial_kernel(len(parts), *refs)

    return pl.pallas_call(
        kernel,
        grid=(count // ROWS,),
        in_specs=[SCALARS, rows(width), rows(width), whole((8, width)), whole((8, width))]
        + [rows(PAIR)] * len(parts)
        + [ANY] * 4,
        out_specs=[rows(width), whole(ranks), whole(ranks)],
        out_shape=[
            pltpu.HBM((count, width), BF16),
            shape_of(ranks, BF16),
            shape_of(ranks, BF16),
        ],
        scratch_shapes=[
            pltpu.VMEM((width, inner), BF16),
            pltpu.VMEM((width, 3 * PAIR), F32),
            pltpu.VMEM((8, width), F32),
            pltpu.SemaphoreType.DMA((4,)),
        ],
        compiler_params=params(),
        cost_estimate=cost(2 * count * width * (inner + 3 * PAIR), 8 * count * width),
    )(places, *pin(x, n1), second, third, *pin(*parts), *pieces)


def last_kernel(pos, e1, x, mine, theirs, gain, out, held):
    step = pl.program_id(0)
    half = pl.num_programs(0) // 2
    size = e1.shape[0]

    @pl.when(step < half)
    def _():
        back = mine[...].astype(F32) + theirs[...].astype(F32)
        grad, _ = norm_back(x[...].astype(F32), gain[...], back)
        held[pl.ds(pl.multiple_of(step * size, size), size), :] = (
            e1[...].astype(F32) + grad
        ).astype(BF16)

    @pl.when(step >= half)
    def _():
        onehot = (
            lax.broadcasted_iota(jnp.int32, (held.shape[0], size), 0) == pos[0:1, :]
        ).astype(F32).astype(BF16)
        out[...] = dot(onehot, held[...], TN).astype(BF16)


def last_step(pos, e1, x, mine, theirs, gain):
    count, width = x.shape
    steps = count // TILE

    def early(t):
        return (jnp.minimum(t, steps - 1), 0)

    def late(t):
        return jnp.maximum(t - steps, 0)

    tile = pl.BlockSpec((TILE, width), early)
    return pl.pallas_call(
        last_kernel,
        grid=(2 * steps,),
        in_specs=[pl.BlockSpec((8, TILE), lambda t: (0, late(t)))]
        + [tile] * 4
        + [whole((1, width))],
        out_specs=pl.BlockSpec((TILE, width), lambda t: (late(t), 0)),
        out_shape=shape_of((count, width), BF16),
        scratch_shapes=[pltpu.VMEM((count, width), BF16)],
        compiler_params=params(),
        cost_estimate=cost(2 * count * count * width, 12 * count * width),
    )(pos, *pin(e1, x, mine), theirs, gain)


def swap(values, axis, distance):
    size = lax.axis_size(axis)
    return lax.ppermute(values, axis, [(i, i ^ distance) for i in range(size)])


def after(values, *others):
    return lax.optimization_barrier((values,) + others)[0]


def gather_all(values):
    return lax.all_gather(values, ("narrow", "wide"), axis=0, tiled=True).reshape(
        lax.axis_size("narrow"), -1, values.shape[1]
    )


def sum_wide(values):
    return lax.psum_scatter(values, "wide", scatter_dimension=0, tiled=True)


def add(left, right):
    return (left.astype(F32) + right.astype(F32)).astype(BF16)


def add_pair(keep, got):
    return add(keep[0], got[0]), add(keep[1], got[1])


def line_inner():
    place = lax.axis_index("dp")
    return (place == 1) | (place == 2)


def line_first(values):
    if lax.axis_size("dp") != 4:
        return lax.psum(values, "dp")
    got = lax.ppermute(values, "dp", [(0, 1), (3, 2)])
    return jnp.where(line_inner(), add(values, got), values)


def line_second(values):
    if lax.axis_size("dp") != 4:
        return values
    return add(values, lax.ppermute(values, "dp", [(1, 2), (2, 1)]))


def line_third(values, *others):
    if lax.axis_size("dp") != 4:
        return values
    got = after(lax.ppermute(values, "dp", [(1, 0), (2, 3)]), *others)
    return jnp.where(line_inner(), values, got)


def local(
    tokens,
    memory,
    cotangent,
    norm1_gain,
    norm2_gain,
    norm3_gain,
    q_weight,
    k_weight,
    v_weight,
    o_weight,
    cross_q,
    cross_k,
    cross_v,
    cross_o,
    gate_weight,
    up_weight,
    down_weight,
    segment_ids,
    block_ids,
    image_table,
):
    width = tokens.shape[1]
    share = q_weight.shape[0]
    inner = q_weight.shape[1]
    unit = gate_weight.shape[1]
    images = memory.shape[0]
    flat_memory = memory.reshape(-1, width)
    place = lax.axis_index("wide")
    side = lax.axis_index("narrow")
    places = jnp.stack([place, place ^ 2, place ^ 1, place ^ 3, side]).astype(jnp.int32)

    gains = jnp.stack([norm1_gain, norm2_gain, norm3_gain])
    gains = jnp.pad(gains, ((0, 13), (0, 3 * inner - share)))
    early = jnp.concatenate(
        [jnp.concatenate([q_weight, k_weight, v_weight], axis=1), gains], axis=0
    )
    early_x = swap(early, "wide", 2)
    early_core = swap(early, "wide", 1)
    early_pieces = (early, early_x, early_core, swap(early_x, "wide", 1))
    lines = jnp.stack([piece[share : share + 3, :share] for piece in early_pieces])
    lines = lines.astype(F32)
    order = [
        jnp.sum(jnp.where((places[:4] == w)[:, None, None], lines, 0.0), axis=0)
        for w in range(4)
    ]
    all_gains = jnp.concatenate(order, axis=1)[:, None, :]

    mid = jnp.concatenate([cross_k, cross_v, cross_q, o_weight], axis=1)
    memory_columns = slice(0, 2 * inner)
    query_columns = slice(2 * inner, 3 * inner)
    out_columns = slice(3 * inner, 4 * inner)
    mid_x = swap(after(mid, early_x), "wide", 2)
    mid_core = swap(mid, "wide", 1)
    out_y = swap(o_weight, "narrow", 1)
    late = jnp.concatenate([cross_q, cross_o, gate_weight, up_weight, down_weight], axis=1)
    late_query_columns = slice(0, inner)
    late_columns = (slice(inner, 2 * inner), slice(2 * inner, 2 * inner + 3 * unit))

    x, row_ids, col_ids, pos, scalars = order_rows(
        segment_ids, block_ids, image_table, after(tokens, early_core, out_y)
    )
    late = gather_all(after(late, early_x, x))
    n1, qkv = norm_project(places, x, all_gains[0], early_pieces)
    pairs = inner // PAIR
    self_parts = [self_forward(0, after(qkv, mid_core), row_ids, col_ids)]
    out_yx = after(swap(out_y, "wide", 2), self_parts[0][0])
    out_pieces = (out_y, out_yx, swap(out_y, "wide", 1), swap(out_yx, "wide", 1))
    for pair in range(1, pairs):
        waits = out_pieces if pair == pairs - 1 else ()
        self_parts.append(
            self_forward(pair, after(qkv, self_parts[-1][0], *waits), row_ids, col_ids)
        )
    mid_x = after(mid_x, self_parts[-1][0])
    mid_pieces = (mid, mid_x, mid_core, swap(mid_x, "wide", 1))
    gy = order_more(pos, after(cotangent, self_parts[-1][0]))
    attended_theirs = [swap(part[0], "narrow", 1) for part in self_parts]
    attended = [part[0] for part in self_parts]
    keys_values = project_memory(
        places,
        after(flat_memory, gy, attended_theirs[0]),
        mid_pieces,
        memory_columns,
    )
    h1, n2, cq = middle_step(
        places,
        after(x, keys_values),
        attended,
        attended_theirs,
        all_gains[1],
        mid_pieces,
        out_pieces,
        (out_columns, slice(0, inner), query_columns),
    )
    cross_parts = [cross_forward(0, scalars, cq, keys_values, images)]
    crossed_theirs = []
    for pair in range(1, pairs):
        previous = [cross_parts[-1][0]] + crossed_theirs
        crossed_theirs.append(swap(cross_parts[-1][0], "narrow", 1))
        cross_parts.append(
            cross_forward(pair, scalars, after(cq, *previous), keys_values, images)
        )
    crossed = [part[0] for part in cross_parts]
    crossed_theirs.append(swap(crossed[-1], "narrow", 1))
    cross_logs = jnp.concatenate([part[1] for part in cross_parts], axis=0)
    (
        output,
        n3,
        hidden,
        grad_gate,
        grad_up,
        e2,
        dc,
        cross_deltas,
        third_gain,
    ) = units_step(
        places,
        h1,
        crossed,
        crossed_theirs,
        all_gains[2],
        gy,
        late,
        late_columns,
    )

    unit_keep, unit_send = weight_grads(
        places, (n3, gy), (grad_gate, grad_up, hidden), ((0, (0,)), (0, (1,)), (1, (2,)))
    )
    unit_stay, unit_leave = add_pair(unit_keep, swap(unit_send, "wide", 1))
    dcq, dck, dcv = cross_backward(
        0,
        scalars,
        cq,
        keys_values,
        after(dc, unit_leave),
        cross_logs,
        cross_deltas,
        images,
        None,
    )
    unit_part = add(unit_stay, swap(unit_leave, "wide", 2))
    keep0, send0, more0, total = memory_back(
        places,
        flat_memory,
        after(dck, unit_part),
        dcv,
        mid_pieces,
        memory_columns,
        0,
        None,
        0,
    )
    unit_sum = lax.psum(unit_part, "dp")
    dcq, dck, dcv = cross_backward(
        1,
        scalars,
        cq,
        keys_values,
        after(dc, send0),
        cross_logs,
        cross_deltas,
        images,
        dcq,
    )
    dcq_theirs = swap(dcq, "narrow", 1)
    got0 = swap(send0, "narrow", 1)
    got_more = swap(after(more0, dcq), "narrow", 1)
    keep1, send1, cross_keep, cross_send = memory_back(
        places,
        flat_memory,
        after(dck, got0),
        dcv,
        mid_pieces,
        memory_columns,
        1,
        total,
        2 * inner,
    )
    cross_keep, cross_send = weight_grads(
        places,
        (after(n2, send1), e2),
        (dcq, crossed),
        ((0, (0,)), (1, (1,))),
        into=(cross_keep, cross_send),
        first=2,
    )
    e1, da, self_deltas, second_gain = turn_step(
        places,
        e2,
        h1,
        after(dcq, cross_send, unit_sum),
        dcq_theirs,
        all_gains[1],
        attended,
        mid_pieces,
        late,
        (out_columns, query_columns, late_query_columns),
    )
    got1 = swap(after(send1, dcq_theirs, got0), "narrow", 1)
    cross_stay, cross_leave = add_pair(cross_keep, swap(cross_send, "wide", 1))
    da = after(da, cross_leave)
    back = []
    for pair in range(pairs):
        ready = after(da, *[part[0] for part in back])
        if pair == pairs - 1:
            early_back = list(back)
            self_keep, self_send = weight_grads(
                places,
                (after(n1, back[-1][0]), e1),
                [[part[i] for part in early_back] for i in range(3)] + [attended],
                ((0, (0, 1, 2)), (1, (3,))),
            )
            cross_part = add(cross_stay, swap(cross_leave, "wide", 2))
            ready = after(ready, cross_part, self_send)
            cross_part = line_first(cross_part)
        back.append(
            self_backward(
                pair, qkv, ready, self_parts[pair][1], self_deltas, row_ids, col_ids
            )
        )
    dq, dk, dv = [[part[i] for part in back] for i in range(3)]
    self_stay, self_leave = add_pair(self_keep, swap(self_send, "wide", 1))
    self_part = add(self_stay, swap(self_leave, "wide", 2))
    dn1, last_keep, last_send = partial_step(
        places,
        dq + dk + dv,
        after(x, self_leave),
        n1,
        second_gain,
        third_gain,
        early_pieces,
    )
    dn1_theirs = swap(dn1, "narrow", 1)
    memory0 = add(after(keep0, dn1), jnp.concatenate([got0, got_more]))
    memory1 = add(after(keep1, dn1), got1)
    last_stay, last_leave = add_pair(last_keep, swap(last_send, "wide", 1))
    last_part = add(last_stay, swap(last_leave, "wide", 2))
    output = restore_rows(pos, after(output, last_send, self_part))
    tokens_grad = last_step(pos, e1, x, dn1, dn1_theirs, all_gains[0])
    memory_grad = jnp.stack([after(memory0, self_part), memory1])
    cross_sum = line_third(line_second(cross_part), tokens_grad)
    self_second = line_second(line_first(self_part))
    self_sum = line_third(self_second, tokens_grad)
    last_sum = line_third(line_second(line_first(last_part)))
    gain_sums = last_sum[share:, :share].astype(F32)
    first_gain = gain_sums[0] + swap(after(gain_sums, self_second), "narrow", 1)[0]

    def grads(array, size, count):
        return [array[:share, i * size : (i + 1) * size].astype(F32) for i in range(count)]

    gate_grad, up_grad, down_grad = grads(after(unit_sum, self_part), unit, 3)
    cross_k_grad, cross_v_grad, cross_q_grad, cross_o_grad = grads(cross_sum, inner, 4)
    part = inner - PAIR
    q_grad, k_grad, v_grad = [
        jnp.concatenate([most, rest], axis=1)
        for most, rest in zip(grads(self_sum, part, 3), grads(last_sum, PAIR, 3))
    ]
    o_grad = self_sum[:, 3 * part :].astype(F32)
    return (
        output,
        tokens_grad,
        memory_grad,
        first_gain,
        gain_sums[1],
        gain_sums[2],
        q_grad,
        k_grad,
        v_grad,
        o_grad,
        cross_q_grad,
        cross_k_grad,
        cross_v_grad,
        cross_o_grad,
        gate_grad,
        up_grad,
        down_grad,
    )


def solution(mesh):
    both = ("dp", "wide")
    weight = P("wide", "narrow")
    in_specs = (
        (P(both, None), P(both, None, None), P(both, None))
        + (P("wide"),) * 3
        + (weight,) * 11
        + (P(both, None),) * 3
    )
    out_specs = (
        (P(both, None), P(both, None), P(both, None, "narrow"))
        + (P("wide"),) * 3
        + (weight,) * 11
    )
    return jax.shard_map(local, mesh=mesh, in_specs=in_specs, out_specs=out_specs, check_vma=False)
```

```python
import functools
import math

import jax
import jax.numpy as jnp
from jax import lax
from jax.experimental import pallas as pl
from jax.experimental.pallas import tpu as pltpu
from jax.sharding import PartitionSpec as P

F32 = jnp.float32
BF16 = jnp.bfloat16
EPSILON = 1e-06
ROOT_TWO_OVER_PI = 0.7978845608028654
CUBIC = 0.044715
HEAD_DIM = 64
PAIR = 2 * HEAD_DIM
SCALE = HEAD_DIM ** (-0.5)
EXP2_SCALE = SCALE * math.log2(math.e)
HIDE = 1e30
TILE = 256
ROWS = 512
WEIGH = 4.0

NN = (((1,), (0,)), ((), ()))
NT = (((1,), (1,)), ((), ()))
TN = (((0,), (0,)), ((), ()))


def dot(left, right, dims):
    return lax.dot_general(left, right, dims, preferred_element_type=F32)


def params(mebibytes=24):
    return pltpu.CompilerParams(vmem_limit_bytes=mebibytes * 1024 * 1024)


def cost(flops, nbytes):
    return pl.CostEstimate(
        flops=int(flops * WEIGH), bytes_accessed=int(nbytes * WEIGH), transcendentals=0
    )


def pin(*arrays):
    return [pltpu.with_memory_space_constraint(array, pltpu.HBM) for array in arrays]


def shape_of(shape, dtype):
    return jax.ShapeDtypeStruct(shape, dtype)


def whole(shape):
    zeros = (0,) * len(shape)
    return pl.BlockSpec(shape, lambda *_: zeros)


def rows(width, height=None):
    height = ROWS if height is None else height
    return pl.BlockSpec((height, width), lambda t, *_: (t, 0))


def inverse_rms(values):
    return lax.rsqrt(jnp.mean(values * values, axis=1, keepdims=True) + EPSILON)


def norm_back(values, gain, upstream):
    factor = inverse_rms(values)
    scaled = upstream * gain
    mean = jnp.mean(values * scaled, axis=1, keepdims=True)
    grad = factor * scaled - values * (factor * factor * factor * mean)
    return grad, jnp.sum(upstream * values * factor, axis=0, keepdims=True)


def in_half(shape, half):
    return (lax.broadcasted_iota(jnp.int32, shape, 1) // HEAD_DIM) == half


def only_half(values, half):
    return jnp.where(in_half(values.shape, half), values, jnp.zeros_like(values))


def order_kernel(seg, blk, table, x, xp, row_ids, col_ids, pos_out, scalars, pos):
    step = pl.program_id(0)
    count = seg.shape[1]

    @pl.when(step == 0)
    def _():
        segments = seg[...]
        image = jnp.zeros_like(segments)
        for s in range(table.shape[1]):
            image = jnp.where(segments == s, table[0, s], image)
        first = (image == 0).astype(F32)
        before = lax.broadcasted_iota(jnp.int32, (count, count), 0) < lax.broadcasted_iota(
            jnp.int32, (count, count), 1
        )
        rank = dot(
            jnp.broadcast_to(first, (8, count)).astype(BF16),
            before.astype(F32).astype(BF16),
            NN,
        )[0:1]
        total = jnp.sum(first)
        index = lax.broadcasted_iota(jnp.int32, (1, count), 1).astype(F32)
        place = jnp.where(image == 0, rank, total + index - rank)
        pos[...] = place.astype(jnp.int32)
        pos_out[...] = jnp.broadcast_to(pos[...], (8, count))
        n0 = total.astype(jnp.int32)
        tiles = count // TILE
        visits0 = jnp.maximum(1, (n0 + TILE - 1) // TILE)
        start1 = jnp.minimum(tiles - 1, n0 // TILE)
        visits = visits0 + tiles - start1
        for v in range(tiles + 1):
            real = jnp.minimum(v, visits - 1)
            in_first = real < visits0
            scalars[v] = jnp.where(in_first, real, real - visits0 + start1)
            scalars[8 + v] = jnp.where(in_first, 0, 1)
        scalars[16] = visits
        scalars[17] = n0
        scalars[18] = visits0
        scalars[19] = start1
        scalars[20] = tiles - start1

    onehot = (
        lax.broadcasted_iota(jnp.int32, (TILE, count), 0) + step * TILE == pos[...]
    ).astype(F32).astype(BF16)
    xp[...] = dot(onehot, x[...], NN).astype(BF16)
    ids = jnp.concatenate(
        [
            seg[...].astype(F32),
            blk[...].astype(F32),
            jnp.zeros((126, count), F32),
        ],
        axis=0,
    ).astype(BF16)
    row_ids[...] = dot(ids[0:8], onehot, NT)
    col_ids[...] = dot(onehot, ids, NT)


def order_rows(seg, blk, table, x):
    count, width = x.shape
    return pl.pallas_call(
        order_kernel,
        grid=(count // TILE,),
        in_specs=[
            whole((1, count)),
            whole((1, count)),
            pl.BlockSpec(memory_space=pltpu.SMEM),
            whole((count, width)),
        ],
        out_specs=[
            rows(width, TILE),
            pl.BlockSpec((8, TILE), lambda t: (0, t)),
            rows(128, TILE),
            whole((8, count)),
            pl.BlockSpec(memory_space=pltpu.SMEM),
        ],
        out_shape=[
            pltpu.HBM((count, width), BF16),
            shape_of((8, count), F32),
            shape_of((count, 128), F32),
            shape_of((8, count), jnp.int32),
            shape_of((32,), jnp.int32),
        ],
        scratch_shapes=[pltpu.VMEM((1, count), jnp.int32)],
        compiler_params=params(),
        cost_estimate=cost(2 * count * count * width, 8 * count * width),
    )(seg, blk, table, *pin(x))


def order_more_kernel(pos, values, out):
    size, count = out.shape[0], values.shape[0]
    index = lax.broadcasted_iota(jnp.int32, (size, count), 0) + pl.program_id(0) * size
    onehot = (index == pos[0:1, :]).astype(F32).astype(BF16)
    out[...] = dot(onehot, values[...], NN).astype(BF16)


def order_more(pos, values):
    count, width = values.shape
    return pl.pallas_call(
        order_more_kernel,
        grid=(count // TILE,),
        in_specs=[whole((8, count)), whole((count, width))],
        out_specs=rows(width, TILE),
        out_shape=pltpu.HBM((count, width), BF16),
        compiler_params=params(),
        cost_estimate=cost(2 * count * count * width, 4 * count * width),
    )(pos, *pin(values))


def restore_kernel(pos, values, out):
    count = values.shape[0]
    onehot = (
        lax.broadcasted_iota(jnp.int32, (count, TILE), 0) == pos[0:1, :]
    ).astype(F32).astype(BF16)
    out[...] = dot(onehot, values[...], TN).astype(BF16)


def restore_rows(pos, values):
    count, width = values.shape
    return pl.pallas_call(
        restore_kernel,
        grid=(count // TILE,),
        in_specs=[pl.BlockSpec((8, TILE), lambda t: (0, t)), whole((count, width))],
        out_specs=rows(width, TILE),
        out_shape=shape_of((count, width), BF16),
        compiler_params=params(),
        cost_estimate=cost(2 * count * count * width, 4 * count * width),
    )(pos, *pin(values))


def fetch(pieces, places, columns, dest, sems, base=0):
    height = dest.shape[0] // 4
    copies = []
    for i, piece in enumerate(pieces):
        start = pl.multiple_of(places[i] * height, 16)
        copies.append(
            pltpu.make_async_copy(
                piece.at[pl.ds(0, height), columns],
                dest.at[pl.ds(start, height), :],
                sems.at[base + i],
            )
        )
    return copies


def fetch_half(gathered, half, columns, dest, sem):
    return pltpu.make_async_copy(gathered.at[half, :, columns], dest, sem)


def start_all(copies):
    for copy in copies:
        copy.start()


def wait_all(copies):
    for copy in copies:
        copy.wait()


ANY = pl.BlockSpec(memory_space=pl.ANY)
SCALARS = pl.BlockSpec(memory_space=pltpu.SMEM)


def project_kernel(places, x, gain, w0, w1, w2, w3, normed, out, weight, sems):
    @pl.when(pl.program_id(0) == 0)
    def _():
        copies = fetch((w0, w1, w2, w3), places, slice(0, weight.shape[1]), weight, sems)
        start_all(copies)
        wait_all(copies)

    values = x[...].astype(F32)
    n1 = (values * inverse_rms(values) * gain[...]).astype(BF16)
    normed[...] = n1
    out[...] = dot(n1, weight[...], NN).astype(BF16)


def norm_project(places, x, gain, pieces):
    count, width = x.shape
    outs = pieces[0].shape[1]
    return pl.pallas_call(
        project_kernel,
        grid=(count // ROWS,),
        in_specs=[SCALARS, rows(width), whole((1, width))] + [ANY] * 4,
        out_specs=[rows(width), rows(outs)],
        out_shape=[pltpu.HBM((count, width), BF16), shape_of((count, outs), BF16)],
        scratch_shapes=[pltpu.VMEM((width, outs), BF16), pltpu.SemaphoreType.DMA((4,))],
        compiler_params=params(),
        cost_estimate=cost(2 * count * width * outs, 4 * count * width + 2 * count * outs),
    )(places, *pin(x), gain, *pieces)


MEMORY_TILE = 1024
BACK_TILE = 512


def memory_kernel(places, columns, memory, w0, w1, w2, w3, out, weight, sems):
    @pl.when(pl.program_id(0) == 0)
    def _():
        copies = fetch((w0, w1, w2, w3), places, columns, weight, sems)
        start_all(copies)
        wait_all(copies)

    out[...] = dot(memory[...], weight[...], NN).astype(BF16)


def project_memory(places, memory, pieces, columns):
    count, width = memory.shape
    outs = columns.stop - columns.start

    def kernel(places, *refs):
        memory_kernel(places, columns, *refs)

    return pl.pallas_call(
        kernel,
        grid=(count // MEMORY_TILE,),
        in_specs=[SCALARS, rows(width, MEMORY_TILE)] + [ANY] * 4,
        out_specs=rows(outs, MEMORY_TILE),
        out_shape=pltpu.HBM((count, outs), BF16),
        scratch_shapes=[pltpu.VMEM((width, outs), BF16), pltpu.SemaphoreType.DMA((4,))],
        compiler_params=params(),
        cost_estimate=cost(2 * count * width * outs, 4 * count * width),
    )(places, *pin(memory), *pieces)


SELF_TILE = 256
SELF_WINDOW = 640
BACK_WINDOW = 640


def store_logs(ref, columns, logs, extra=None):
    spread = jnp.where(in_half((logs[0].shape[0], PAIR), 0), logs[0], logs[1]).T
    for half in range(2):
        line = spread[half * HEAD_DIM : half * HEAD_DIM + 1, :]
        if extra is not None:
            line = jnp.where(extra, line, ref[half : half + 1, columns])
        ref[half : half + 1, columns] = line


def self_forward_kernel(q, k, v, row_ids, col_ids, out, logs):
    count = q.shape[0]
    for tile in range(count // SELF_TILE):
        base = tile * SELF_TILE
        start = min(max(base - 256, 0), count - SELF_WINDOW)
        spot = slice(base, base + SELF_TILE)
        window = slice(start, start + SELF_WINDOW)
        seen = (col_ids[spot, 0:1] == row_ids[0:1, window]) & (
            row_ids[1:2, window] <= col_ids[spot, 1:2]
        )
        bias = jnp.where(seen, 0.0, -HIDE)
        keys = k[window, :]
        values = v[window, :]
        queries = q[spot, :]
        parts, totals = [], []
        for half in range(2):
            scores = dot(only_half(queries, half), keys, NT) * EXP2_SCALE + bias
            highest = jnp.max(scores, axis=1, keepdims=True)
            weights = jnp.exp2(scores - highest)
            total = jnp.sum(weights, axis=1, keepdims=True)
            parts.append(dot(weights.astype(BF16), values, NN) / total)
            totals.append(highest + jnp.log2(total))
        out[spot, :] = jnp.where(in_half(parts[0].shape, 0), parts[0], parts[1]).astype(BF16)
        store_logs(logs, spot, totals)


def self_forward(pair, qkv, row_ids, col_ids):
    count = qkv.shape[0]
    pairs = qkv.shape[1] // (3 * PAIR)

    def part(which):
        return pl.BlockSpec((count, PAIR), lambda p: (0, which * pairs + pair))

    return pl.pallas_call(
        self_forward_kernel,
        grid=(1,),
        in_specs=[part(0), part(1), part(2), whole((8, count)), whole((count, 128))],
        out_specs=[whole((count, PAIR)), whole((8, count))],
        out_shape=[pltpu.HBM((count, PAIR), BF16), pltpu.HBM((8, count), F32)],
        compiler_params=params(),
        cost_estimate=cost(16 * count * SELF_WINDOW * PAIR, 8 * count * PAIR),
    )(qkv, qkv, qkv, row_ids, col_ids)


def self_backward_kernel(q, k, v, grad, logs, deltas, row_ids, col_ids, dq, dk, dv, key_sum, value_sum):
    count = q.shape[0]
    key_sum[...] = jnp.zeros_like(key_sum)
    value_sum[...] = jnp.zeros_like(value_sum)
    for tile in range(count // TILE):
        base = tile * TILE
        start = min(max(base - 256, 0), count - BACK_WINDOW)
        spot = slice(base, base + TILE)
        window = slice(start, start + BACK_WINDOW)
        seen = (col_ids[window, 0:1] == row_ids[0:1, spot]) & (
            col_ids[window, 1:2] <= row_ids[1:2, spot]
        )
        bias = jnp.where(seen, 0.0, -HIDE)
        keys = k[window, :]
        values = v[window, :]
        queries = q[spot, :]
        grads = grad[spot, :]
        parts = []
        for half in range(2):
            one_query = only_half(queries, half)
            one_grad = only_half(grads, half)
            scores = dot(keys, one_query, NT) * EXP2_SCALE + bias
            weights = jnp.exp2(scores - logs[half : half + 1, spot])
            slopes = dot(values, one_grad, NT)
            pushed = (weights * (slopes - deltas[half : half + 1, spot])).astype(BF16)
            value_sum[window, :] += dot(weights.astype(BF16), one_grad, NN)
            key_sum[window, :] += dot(pushed, one_query, NN)
            parts.append(dot(pushed, keys, TN))
        dq[spot, :] = (
            jnp.where(in_half(parts[0].shape, 0), parts[0], parts[1]) * SCALE
        ).astype(BF16)
    dk[...] = (key_sum[...] * SCALE).astype(BF16)
    dv[...] = value_sum[...].astype(BF16)


def self_backward(pair, qkv, grad, logs, deltas, row_ids, col_ids):
    count = qkv.shape[0]
    pairs = qkv.shape[1] // (3 * PAIR)

    def part(which):
        return pl.BlockSpec((count, PAIR), lambda p: (0, which * pairs + pair))

    return pl.pallas_call(
        self_backward_kernel,
        grid=(1,),
        in_specs=[
            part(0),
            part(1),
            part(2),
            part(0),
            whole((8, count)),
            pl.BlockSpec((8, count), lambda p: (pair, 0)),
            whole((8, count)),
            whole((count, 128)),
        ],
        out_specs=[whole((count, PAIR))] * 3,
        out_shape=[pltpu.HBM((count, PAIR), BF16)] * 3,
        scratch_shapes=[pltpu.VMEM((count, PAIR), F32)] * 2,
        compiler_params=params(),
        cost_estimate=cost(40 * count * BACK_WINDOW * PAIR, 16 * count * PAIR),
    )(qkv, qkv, qkv, grad, logs, deltas, row_ids, col_ids)


KEYS = 1024


def visits_of(image, scalars):
    first = jnp.where(image == 0, 0, scalars[19])
    return first, jnp.where(image == 0, scalars[18], scalars[20])


def cross_forward_kernel(scalars, q, k, v, out, logs):
    image = pl.program_id(0)
    first, count = visits_of(image, scalars)

    def visit(i, carry):
        base = pl.multiple_of((first + i) * TILE, TILE)
        spot = pl.ds(base, TILE)
        queries = q[spot, :]
        parts, totals = [], []
        tops, sums = [None, None], [None, None]
        for start in range(0, k.shape[0], KEYS):
            keys = k[start : start + KEYS, :]
            values = v[start : start + KEYS, :]
            both = [dot(only_half(queries, half), keys, NT) for half in range(2)]
            for half, scores in enumerate(both):
                highest = jnp.max(scores, axis=1, keepdims=True) * EXP2_SCALE
                if start:
                    highest = jnp.maximum(highest, tops[half])
                weights = jnp.exp2(scores * EXP2_SCALE - highest).astype(BF16)
                mixed = dot(
                    weights,
                    jnp.where(in_half(values.shape, half), values, jnp.ones_like(values)),
                    NN,
                )
                if start:
                    mixed = mixed + sums[half] * jnp.exp2(tops[half] - highest)
                tops[half], sums[half] = highest, mixed
        for half in range(2):
            total = pltpu.roll(sums[half], HEAD_DIM, 1)
            parts.append(sums[half] / total)
            totals.append(tops[half] + jnp.log2(total))
        mixed = jnp.where(in_half(parts[0].shape, 0), parts[0], parts[1]).astype(BF16)
        limit = jnp.where(image == 0, 0, scalars[17]) - base
        row_mine = lax.broadcasted_iota(jnp.int32, mixed.shape, 0) >= limit
        lane_mine = lax.broadcasted_iota(jnp.int32, (1, TILE), 1) >= limit
        out[spot, :] = jnp.where(row_mine, mixed, out[spot, :])
        store_logs(logs, spot, totals, lane_mine)
        return carry

    lax.fori_loop(0, count, visit, 0)


def cross_forward(pair, scalars, q, keys_values, images):
    count, inner = q.shape
    pairs = inner // PAIR
    memory_rows = keys_values.shape[0] // images

    def part(which):
        return pl.BlockSpec((memory_rows, PAIR), lambda i, sc: (i, which * pairs + pair))

    return pl.pallas_call(
        cross_forward_kernel,
        grid_spec=pltpu.PrefetchScalarGridSpec(
            num_scalar_prefetch=1,
            grid=(images,),
            in_specs=[
                pl.BlockSpec((count, PAIR), lambda i, sc: (0, pair)),
                part(0),
                part(1),
            ],
            out_specs=[whole((count, PAIR)), whole((8, count))],
        ),
        out_shape=[pltpu.HBM((count, PAIR), BF16), pltpu.HBM((8, count), F32)],
        compiler_params=params(),
        cost_estimate=cost(20 * count * memory_rows * PAIR, 8 * memory_rows * PAIR),
    )(scalars, *pin(q, keys_values, keys_values))


def cross_backward_kernel(
    image, scalars, q, k, v, grad, logs, deltas, old, dq, dk, dv, key_sum, value_sum
):
    first, count = visits_of(jnp.int32(image), scalars)
    if image:
        dq[...] = old[...]

    def visit(i, fresh):
        base = pl.multiple_of((first + i) * TILE, TILE)
        spot = pl.ds(base, TILE)
        queries = q[spot, :]
        grads = grad[spot, :]
        keys = k[...]
        values = v[...]
        limit = scalars[17] - base
        lane_mine = (lax.broadcasted_iota(jnp.int32, (1, TILE), 1) >= limit) == (image == 1)
        parts = []
        for half in range(2):
            one_query = only_half(queries, half)
            one_grad = only_half(grads, half)
            log = jnp.where(lane_mine, logs[half : half + 1, spot], HIDE)
            scores = dot(keys, one_query, NT)
            weights = jnp.exp2(scores * EXP2_SCALE - log)
            slopes = dot(values, one_grad, NT)
            pushed = (weights * (slopes - deltas[half : half + 1, spot])).astype(BF16)
            value_part = dot(weights.astype(BF16), one_grad, NN)
            key_part = dot(pushed, one_query, NN)
            if fresh and half == 0:
                value_sum[...] = value_part
                key_sum[...] = key_part
            else:
                value_sum[...] += value_part
                key_sum[...] += key_part
            parts.append(dot(pushed, keys, TN))
        grad_query = (
            jnp.where(in_half(parts[0].shape, 0), parts[0], parts[1]) * SCALE
        ).astype(BF16)
        if image:
            row_mine = lax.broadcasted_iota(jnp.int32, grad_query.shape, 0) >= limit
            grad_query = jnp.where(row_mine, grad_query, dq[spot, :])
        dq[spot, :] = grad_query

    def later(i, carry):
        visit(i, False)
        return carry

    visit(0, True)
    lax.fori_loop(1, count, later, 0)
    dk[...] = (key_sum[...] * SCALE).astype(BF16)
    dv[...] = value_sum[...].astype(BF16)


def cross_backward(image, scalars, q, keys_values, grad, logs, deltas, images, old):
    count, inner = q.shape
    pairs = inner // PAIR
    memory_rows = keys_values.shape[0] // images
    token_spec = pl.BlockSpec((count, PAIR), lambda p, sc: (0, p))
    line = pl.BlockSpec((8, count), lambda p, sc: (p, 0))
    result = pl.BlockSpec((memory_rows, PAIR), lambda p, sc: (0, p))

    def part(which):
        return pl.BlockSpec((memory_rows, PAIR), lambda p, sc: (image, which * pairs + p))

    def first_kernel(scalars, q, k, v, grad, logs, deltas, *rest):
        cross_backward_kernel(image, scalars, q, k, v, grad, logs, deltas, None, *rest)

    def second_kernel(*refs):
        cross_backward_kernel(image, *refs)

    extra = [old] if image else []
    return pl.pallas_call(
        second_kernel if image else first_kernel,
        grid_spec=pltpu.PrefetchScalarGridSpec(
            num_scalar_prefetch=1,
            grid=(pairs,),
            in_specs=[token_spec, part(0), part(1), token_spec, line, line]
            + [token_spec] * len(extra),
            out_specs=[token_spec, result, result],
            scratch_shapes=[pltpu.VMEM((memory_rows, PAIR), F32)] * 2,
        ),
        out_shape=[
            pltpu.HBM((count, inner), BF16),
            pltpu.HBM((memory_rows, inner), BF16),
            pltpu.HBM((memory_rows, inner), BF16),
        ],
        compiler_params=params(32),
        cost_estimate=cost(25 * count * memory_rows * inner, 8 * memory_rows * inner),
    )(scalars, *pin(q, keys_values, keys_values, grad), logs, deltas, *pin(*extra))


def put_rows(places, product, keep, send, span=slice(None)):
    height = product.shape[0] // 4
    for i, ref in enumerate((keep, keep, send, send)):
        start = pl.multiple_of(places[i] * height, 16)
        ref[i % 2, 0:height, span] = product[pl.ds(start, height), :].astype(BF16)


def memory_back_kernel(
    columns, last, places, memory, dk, dv, w0, w1, w2, w3, *refs
):
    if last:
        before, keep_part, send_part, keep, send, weight, total, sems = refs
    else:
        keep_part, send_part, send_more, total_out, weight, total, sems = refs
    inner = dk.shape[1]

    @pl.when(pl.program_id(0) == 0)
    def _():
        copies = fetch((w0, w1, w2, w3), places, columns, weight, sems)
        start_all(copies)
        if last:
            total[...] = before[...]
        else:
            total[...] = jnp.zeros_like(total)
        wait_all(copies)

    both = jnp.concatenate([dk[...], dv[...]], axis=1)
    product = dot(both, weight[...], NT).astype(BF16)
    lower, upper = product[:, :inner], product[:, inner:]
    side = places[4]
    leave = jnp.where(side == 0, upper, lower)
    if last:
        send_part[...] = leave
    else:

        early = pl.program_id(0) < pl.num_programs(0) // 2
        send_part[...] = jnp.where(early, leave, send_part[...])
        send_more[...] = leave

    keep_part[...] = jnp.where(side == 0, lower, upper)
    total[...] += dot(memory[...], both, TN)

    @pl.when(pl.program_id(0) == pl.num_programs(0) - 1)
    def _():
        if last:
            put_rows(places, total, keep, send)
        else:
            total_out[...] = total[...]


def memory_back(places, memory, dk, dv, pieces, columns, image, before, spare):
    count, inner = dk.shape
    width = memory.shape[1]
    steps = count // BACK_TILE
    last = before is not None
    ranks = pltpu.HBM((2, width // 4, spare + 2 * inner), BF16)
    rank_spec = pl.BlockSpec((2, width // 4, 2 * inner), lambda t: (0, 0, 0))

    def kernel(*refs):
        memory_back_kernel(columns, last, *refs)

    return pl.pallas_call(
        kernel,
        grid=(steps,),
        in_specs=[
            SCALARS,
            pl.BlockSpec((BACK_TILE, width), lambda t: (image * steps + t, 0)),
            rows(inner, BACK_TILE),
            rows(inner, BACK_TILE),
        ]
        + [ANY] * 4
        + ([whole((width, 2 * inner))] if last else []),
        out_specs=[rows(inner, BACK_TILE)]
        + (
            [rows(inner, BACK_TILE), rank_spec, rank_spec]
            if last
            else [
                pl.BlockSpec((BACK_TILE, inner), lambda t: (jnp.minimum(t, steps // 2 - 1), 0)),
                pl.BlockSpec((BACK_TILE, inner), lambda t: (jnp.maximum(t - steps // 2, 0), 0)),
                whole((width, 2 * inner)),
            ]
        ),
        out_shape=[pltpu.HBM((count, inner), BF16)]
        + (
            [pltpu.HBM((count, inner), BF16), ranks, ranks]
            if last
            else [
                pltpu.HBM((count // 2, inner), BF16),
                pltpu.HBM((count // 2, inner), BF16),
                shape_of((width, 2 * inner), F32),
            ]
        ),
        scratch_shapes=[
            pltpu.VMEM((width, 2 * inner), BF16),
            pltpu.VMEM((width, 2 * inner), F32),
            pltpu.SemaphoreType.DMA((4,)),
        ],
        compiler_params=params(),
        cost_estimate=cost(8 * count * width * inner, 8 * count * width),
    )(places, *pin(memory, dk, dv), *pieces, *([before] if last else []))


def weight_grads_kernel(plan, spans, places, left_refs, right_refs, keep, send, scratch):
    left_holds = scratch[: len(left_refs)]
    right_holds = scratch[len(left_refs) : -3]
    turned, product, sems = scratch[-3:]
    step = pl.program_id(0)
    lefts = [
        pltpu.make_async_copy(ref, hold, sems.at[i])
        for i, (ref, hold) in enumerate(zip(left_refs, left_holds))
    ]
    rights = [
        pltpu.make_async_copy(ref, hold, sems.at[len(left_refs) + i])
        for i, (ref, hold) in enumerate(zip(right_refs, right_holds))
    ]
    for at, (left, group) in enumerate(plan):
        fresh = at == 0 or plan[at - 1][0] != left

        @pl.when(step == at)
        def _():
            if at == 0:
                lefts[left].start()
                for g in group:
                    rights[g].start()
            if fresh:
                lefts[left].wait()
            if at == 0:
                begun = {left}
                for one, others in plan[1:]:
                    if one not in begun:
                        lefts[one].start()
                        begun.add(one)
                    for g in others:
                        rights[g].start()
            if fresh:
                turned[...] = left_holds[left][...].T
            for g in group:
                rights[g].wait()
            right = join([right_holds[g] for g in group])
            columns = right.shape[1]
            product[:, 0:columns] = dot(turned[...], right, NN)
            put_rows(places, product.at[:, 0:columns], keep, send, spans[at])


def join(refs):
    values = [ref[...] for ref in refs]
    return values[0] if len(values) == 1 else jnp.concatenate(values, axis=1)


def flatten(groups):
    flat, sizes = [], []
    for group in groups:
        group = group if isinstance(group, (list, tuple)) else [group]
        flat += list(group)
        sizes.append(len(group))
    return flat, sizes


def weight_grads(places, lefts, rights, plan, into=(), first=0):
    count, width = lefts[0].shape
    flat, sizes = flatten(rights)
    groups, at = [], 0
    for size in sizes:
        groups.append(list(range(at, at + size)))
        at += size
    plan = [(left, [f for g in group for f in groups[g]]) for left, group in plan]
    columns = [sum(flat[f].shape[1] for f in group) for _, group in plan]
    step_columns = columns[0]
    share = width // 4
    total = sum(columns) + first * step_columns
    even = len(set(columns)) == 1
    spans = [
        slice(0, step_columns) if even else slice(sum(columns[:at]), sum(columns[: at + 1]))
        for at in range(len(plan))
    ]
    extra = list(into)
    def kernel(places, *refs):
        lefts_end = len(lefts)
        rights_end = lefts_end + len(flat)
        weight_grads_kernel(
            plan,
            spans,
            places,
            refs[:lefts_end],
            refs[lefts_end:rights_end],
            *refs[rights_end + len(extra) : rights_end + len(extra) + 2],
            refs[rights_end + len(extra) + 2 :],
        )

    start = 1 + len(lefts) + len(flat)
    return pl.pallas_call(
        kernel,
        grid=(len(plan),),
        in_specs=[SCALARS]
        + [ANY] * (len(lefts) + len(flat) + len(extra)),
        out_specs=[
            pl.BlockSpec((2, share, step_columns), lambda t: (0, 0, t + first))
            if even
            else whole((2, share, total))
        ]
        * 2,
        out_shape=[pltpu.HBM((2, share, total), BF16)] * 2,
        input_output_aliases={start: 0, start + 1: 1} if extra else {},
        scratch_shapes=[pltpu.VMEM(array.shape, array.dtype) for array in list(lefts) + flat]
        + [
            pltpu.VMEM((width, count), BF16),
            pltpu.VMEM((width, max(columns)), F32),
            pltpu.SemaphoreType.DMA((len(lefts) + len(flat),)),
        ],
        compiler_params=params(32),
        cost_estimate=cost(
            2 * count * width * sum(columns), 4 * count * width * len(plan)
        ),
    )(places, *pin(*lefts, *flat), *extra)


def middle_kernel(plan, parts, places, x, gain, *refs):
    mine, theirs, refs = refs[:parts], refs[parts : 2 * parts], refs[2 * parts :]
    pieces, (h1, n2, cq, out_mine, out_theirs, query, sems) = refs[:8], refs[8:]

    @pl.when(pl.program_id(0) == 0)
    def _():
        copies = (
            fetch(pieces[:4], places, plan[0], out_mine, sems, 0)
            + fetch(pieces[4:], places, plan[1], out_theirs, sems, 4)
            + fetch(pieces[:4], places, plan[2], query, sems, 8)
        )
        start_all(copies)
        wait_all(copies)

    values = (
        x[...].astype(F32)
        + dot(join(mine), out_mine[...], NT)
        + dot(join(theirs), out_theirs[...], NT)
    )
    h1[...] = values.astype(BF16)
    normed = (values * inverse_rms(values) * gain[...]).astype(BF16)
    n2[...] = normed
    cq[...] = dot(normed, query[...], NN).astype(BF16)


def middle_step(places, x, mine, theirs, gain, pieces, pieces_theirs, plan):
    count, width = x.shape
    half = sum(part.shape[1] for part in mine)

    def kernel(*refs):
        middle_kernel(plan, len(mine), *refs)

    return pl.pallas_call(
        kernel,
        grid=(count // ROWS,),
        in_specs=[SCALARS, rows(width), whole((1, width))]
        + [rows(PAIR)] * (2 * len(mine))
        + [ANY] * 8,
        out_specs=[rows(width), rows(width), rows(half)],
        out_shape=[
            pltpu.HBM((count, width), BF16),
            pltpu.HBM((count, width), BF16),
            pltpu.HBM((count, half), BF16),
        ],
        scratch_shapes=[pltpu.VMEM((width, half), BF16)] * 3 + [pltpu.SemaphoreType.DMA((12,))],
        compiler_params=params(),
        cost_estimate=cost(6 * count * width * half, 12 * count * width),
    )(places, *pin(x), gain, *pin(*mine), *theirs, *pieces, *pieces_theirs)


def head_sums(left, right):
    product = left.astype(F32) * right.astype(F32)
    width = product.shape[1]
    high = product.astype(BF16)
    low = (product - high.astype(F32)).astype(BF16)
    height = 8 * (width // PAIR)
    line = lax.broadcasted_iota(jnp.int32, (height, width), 0)
    head = lax.broadcasted_iota(jnp.int32, (height, width), 1) // HEAD_DIM
    choose = (
        ((line // 8) * 2 + line % 8 == head) & (line % 8 < 2)
    ).astype(F32).astype(BF16)
    return dot(choose, high, NT) + dot(choose, low, NT)


CHUNK = 512


def units_kernel(plan, parts, places, h1, gain, gy, *refs):
    mine, theirs, refs = refs[:parts], refs[parts : 2 * parts], refs[2 * parts :]
    late, refs = refs[0], refs[1:]
    (
        output,
        n3,
        hidden,
        grad_gate,
        grad_up,
        e2,
        dc,
        deltas,
        gain_grad,
        out_mine,
        out_theirs,
        units_mine,
        units_theirs,
        sems,
    ) = refs
    step = pl.program_id(0)

    side = places[4]
    out_copies = [
        fetch_half(late, side, plan[0], out_mine, sems.at[0]),
        fetch_half(late, 1 - side, plan[0], out_theirs, sems.at[1]),
    ]
    mine_copy = fetch_half(late, side, plan[1], units_mine, sems.at[2])
    theirs_copy = fetch_half(late, 1 - side, plan[1], units_theirs, sems.at[3])

    @pl.when(step == 0)
    def _():
        start_all(out_copies + [mine_copy, theirs_copy])
        gain_grad[...] = jnp.zeros_like(gain_grad)
        wait_all(out_copies)

    crossed_mine = join(mine)
    values = (
        h1[...].astype(F32)
        + dot(crossed_mine, out_mine[...], NT)
        + dot(join(theirs), out_theirs[...], NT)
    )
    normed = (values * inverse_rms(values) * gain[...]).astype(BF16)
    n3[...] = normed
    upstream = gy[...]
    mixed = jnp.zeros_like(values)
    back = jnp.zeros_like(values)
    unit = units_mine.shape[1] // 3
    for own in (True, False):
        weight = units_mine if own else units_theirs

        @pl.when(step == 0)
        def _():
            (mine_copy if own else theirs_copy).wait()

        for start in range(0, unit, CHUNK):
            gate_weight = weight[:, start : start + CHUNK]
            up_weight = weight[:, unit + start : unit + start + CHUNK]
            down_weight = weight[:, 2 * unit + start : 2 * unit + start + CHUNK]
            gate = dot(normed, gate_weight, NN)
            up = dot(normed, up_weight, NN)
            pushed = dot(upstream, down_weight, NN)
            square = gate * gate
            bend = jnp.tanh(ROOT_TWO_OVER_PI * gate * (1.0 + CUBIC * square))
            lift = 0.5 * (1.0 + bend)
            gelu = gate * lift
            slope = lift + (0.5 * ROOT_TWO_OVER_PI) * gate * (1.0 - bend * bend) * (
                1.0 + (3.0 * CUBIC) * square
            )
            units = (gelu * up).astype(BF16)
            push_gate = (pushed * up * slope).astype(BF16)
            push_up = (pushed * gelu).astype(BF16)
            mixed = mixed + dot(units, down_weight, NT)
            back = back + dot(push_gate, gate_weight, NT) + dot(push_up, up_weight, NT)
            if own:
                hidden[:, start : start + CHUNK] = units
                grad_gate[:, start : start + CHUNK] = push_gate
                grad_up[:, start : start + CHUNK] = push_up
    output[...] = (values + mixed).astype(BF16)
    grad, gain_part = norm_back(values, gain[...], back)
    low = (upstream.astype(F32) + grad).astype(BF16)
    e2[...] = low
    crossed = dot(low, out_mine[...], NN).astype(BF16)
    dc[...] = crossed
    deltas[...] = head_sums(crossed, crossed_mine)
    gain_grad[0:1, :] += gain_part


def units_step(places, h1, mine, theirs, gain, gy, late, plan):
    count, width = h1.shape
    half = sum(part.shape[1] for part in mine)
    unit = (plan[1].stop - plan[1].start) // 3
    lines = 8 * (half // PAIR)

    def kernel(*refs):
        units_kernel(plan, len(mine), *refs)

    return pl.pallas_call(
        kernel,
        grid=(count // ROWS,),
        in_specs=[
            SCALARS,
            rows(width),
            whole((1, width)),
            rows(width),
        ]
        + [rows(PAIR)] * (2 * len(mine))
        + [ANY],
        out_specs=[
            rows(width),
            rows(width),
            rows(unit),
            rows(unit),
            rows(unit),
            rows(width),
            rows(half),
            pl.BlockSpec((lines, ROWS), lambda t: (0, t)),
            whole((8, width)),
        ],
        out_shape=[
            pltpu.HBM((count, width), BF16),
            pltpu.HBM((count, width), BF16),
            pltpu.HBM((count, unit), BF16),
            pltpu.HBM((count, unit), BF16),
            pltpu.HBM((count, unit), BF16),
            pltpu.HBM((count, width), BF16),
            pltpu.HBM((count, half), BF16),
            pltpu.HBM((lines, count), F32),
            shape_of((8, width), F32),
        ],
        scratch_shapes=[pltpu.VMEM((width, half), BF16)] * 2
        + [pltpu.VMEM((width, 3 * unit), BF16)] * 2
        + [pltpu.SemaphoreType.DMA((4,))],
        compiler_params=params(58),
        cost_estimate=cost(30 * count * width * unit, 30 * count * width),
    )(places, *pin(h1), gain, *pin(gy, *mine), *theirs, *pin(late))


def turn_kernel(plan, parts, places, e2, h1, mine, theirs, gain, *refs):
    attended, refs = refs[:parts], refs[parts:]
    pieces, refs = refs[:4], refs[4:]
    late, e1, da, deltas, gain_grad, query_mine, query_theirs, out_mine, sems = refs

    @pl.when(pl.program_id(0) == 0)
    def _():
        copies = (
            fetch(pieces, places, plan[0], out_mine, sems, 0)
            + fetch(pieces, places, plan[1], query_mine, sems, 4)
            + [fetch_half(late, 1 - places[4], plan[2], query_theirs, sems.at[8])]
        )
        start_all(copies)
        gain_grad[...] = jnp.zeros_like(gain_grad)
        wait_all(copies)

    back = dot(mine[...], query_mine[...], NT) + dot(theirs[...], query_theirs[...], NT)
    grad, gain_part = norm_back(h1[...].astype(F32), gain[...], back)
    low = (e2[...].astype(F32) + grad).astype(BF16)
    e1[...] = low
    pushed = dot(low, out_mine[...], NN).astype(BF16)
    da[...] = pushed
    deltas[...] = head_sums(pushed, join(attended))
    gain_grad[0:1, :] += gain_part


def turn_step(places, e2, h1, mine, theirs, gain, attended, pieces, late, plan):
    count, width = h1.shape
    half = mine.shape[1]
    lines = 8 * (half // PAIR)

    def kernel(*refs):
        turn_kernel(plan, len(attended), *refs)

    return pl.pallas_call(
        kernel,
        grid=(count // ROWS,),
        in_specs=[
            SCALARS,
            rows(width),
            rows(width),
            rows(half),
            rows(half),
            whole((1, width)),
        ]
        + [rows(PAIR)] * len(attended)
        + [ANY] * 5,
        out_specs=[
            rows(width),
            rows(half),
            pl.BlockSpec((lines, ROWS), lambda t: (0, t)),
            whole((8, width)),
        ],
        out_shape=[
            pltpu.HBM((count, width), BF16),
            shape_of((count, half), BF16),
            shape_of((lines, count), F32),
            shape_of((8, width), F32),
        ],
        scratch_shapes=[pltpu.VMEM((width, half), BF16)] * 3 + [pltpu.SemaphoreType.DMA((9,))],
        compiler_params=params(),
        cost_estimate=cost(6 * count * width * half, 16 * count * width),
    )(places, *pin(e2, h1, mine), theirs, gain, *pin(*attended), *pieces, *pin(late))


def partial_kernel(parts, places, x, n1, second, third, *refs):
    part_refs, refs = refs[:parts], refs[parts:]
    w0, w1, w2, w3, out, keep, send, weight, total, gain_grad, sems = refs
    step = pl.program_id(0)

    @pl.when(step == 0)
    def _():
        copies = fetch((w0, w1, w2, w3), places, slice(0, weight.shape[1]), weight, sems)
        start_all(copies)
        gain_grad[...] = jnp.zeros_like(gain_grad)
        total[...] = jnp.zeros_like(total)
        wait_all(copies)

    back = dot(join(part_refs), weight[...], NT)
    out[...] = back.astype(BF16)
    values = x[...].astype(F32)
    gain_grad[0:1, :] += jnp.sum(back * values * inverse_rms(values), axis=0, keepdims=True)
    last = join([part_refs[i * (parts // 3) + parts // 3 - 1] for i in range(3)])
    total[...] += dot(n1[...], last, TN)

    @pl.when(step == pl.num_programs(0) - 1)
    def _():
        put_rows(places, total, keep, send)
        height = total.shape[0] // 4
        lines = jnp.concatenate(
            [
                gain_grad[0:1, :],
                second[0:1, :],
                third[0:1, :],
                jnp.zeros((13, gain_grad.shape[1]), F32),
            ],
            axis=0,
        )
        shares = [lines[:, w * height : (w + 1) * height] for w in range(4)]
        fill = jnp.zeros((16, total.shape[1] - height), F32)
        for i, ref in enumerate((keep, keep, send, send)):
            share = shares[0]
            for w in range(1, 4):
                share = jnp.where(places[i] == w, shares[w], share)
            ref[i % 2, height : height + 16, :] = jnp.concatenate([share, fill], axis=1).astype(
                BF16
            )


def partial_step(places, parts, x, n1, second, third, pieces):
    count, width = x.shape
    inner = sum(part.shape[1] for part in parts)
    ranks = (2, width // 4 + 16, 3 * PAIR)

    def kernel(*refs):
        partial_kernel(len(parts), *refs)

    return pl.pallas_call(
        kernel,
        grid=(count // ROWS,),
        in_specs=[SCALARS, rows(width), rows(width), whole((8, width)), whole((8, width))]
        + [rows(PAIR)] * len(parts)
        + [ANY] * 4,
        out_specs=[rows(width), whole(ranks), whole(ranks)],
        out_shape=[
            pltpu.HBM((count, width), BF16),
            shape_of(ranks, BF16),
            shape_of(ranks, BF16),
        ],
        scratch_shapes=[
            pltpu.VMEM((width, inner), BF16),
            pltpu.VMEM((width, 3 * PAIR), F32),
            pltpu.VMEM((8, width), F32),
            pltpu.SemaphoreType.DMA((4,)),
        ],
        compiler_params=params(),
        cost_estimate=cost(2 * count * width * (inner + 3 * PAIR), 8 * count * width),
    )(places, *pin(x, n1), second, third, *pin(*parts), *pieces)


def last_kernel(pos, e1, x, mine, theirs, gain, out, held):
    step = pl.program_id(0)
    half = pl.num_programs(0) // 2
    size = e1.shape[0]

    @pl.when(step < half)
    def _():
        back = mine[...].astype(F32) + theirs[...].astype(F32)
        grad, _ = norm_back(x[...].astype(F32), gain[...], back)
        held[pl.ds(pl.multiple_of(step * size, size), size), :] = (
            e1[...].astype(F32) + grad
        ).astype(BF16)

    @pl.when(step >= half)
    def _():
        onehot = (
            lax.broadcasted_iota(jnp.int32, (held.shape[0], size), 0) == pos[0:1, :]
        ).astype(F32).astype(BF16)
        out[...] = dot(onehot, held[...], TN).astype(BF16)


def last_step(pos, e1, x, mine, theirs, gain):
    count, width = x.shape
    steps = count // TILE

    def early(t):
        return (jnp.minimum(t, steps - 1), 0)

    def late(t):
        return jnp.maximum(t - steps, 0)

    tile = pl.BlockSpec((TILE, width), early)
    return pl.pallas_call(
        last_kernel,
        grid=(2 * steps,),
        in_specs=[pl.BlockSpec((8, TILE), lambda t: (0, late(t)))]
        + [tile] * 4
        + [whole((1, width))],
        out_specs=pl.BlockSpec((TILE, width), lambda t: (late(t), 0)),
        out_shape=shape_of((count, width), BF16),
        scratch_shapes=[pltpu.VMEM((count, width), BF16)],
        compiler_params=params(),
        cost_estimate=cost(2 * count * count * width, 12 * count * width),
    )(pos, *pin(e1, x, mine), theirs, gain)


def swap(values, axis, distance):
    size = lax.axis_size(axis)
    return lax.ppermute(values, axis, [(i, i ^ distance) for i in range(size)])


def after(values, *others):
    return lax.optimization_barrier((values,) + others)[0]


def gather_all(values):
    return lax.all_gather(values, ("narrow", "wide"), axis=0, tiled=True).reshape(
        lax.axis_size("narrow"), -1, values.shape[1]
    )


def sum_wide(values):
    return lax.psum_scatter(values, "wide", scatter_dimension=0, tiled=True)


def add(left, right):
    return (left.astype(F32) + right.astype(F32)).astype(BF16)


def add_pair(keep, got):
    return add(keep[0], got[0]), add(keep[1], got[1])


def line_inner():
    place = lax.axis_index("dp")
    return (place == 1) | (place == 2)


def line_first(values):
    if lax.axis_size("dp") != 4:
        return lax.psum(values, "dp")
    got = lax.ppermute(values, "dp", [(0, 1), (3, 2)])
    return jnp.where(line_inner(), add(values, got), values)


def line_second(values):
    if lax.axis_size("dp") != 4:
        return values
    return add(values, lax.ppermute(values, "dp", [(1, 2), (2, 1)]))


def line_third(values, *others):
    if lax.axis_size("dp") != 4:
        return values
    got = after(lax.ppermute(values, "dp", [(1, 0), (2, 3)]), *others)
    return jnp.where(line_inner(), values, got)


def local(
    tokens,
    memory,
    cotangent,
    norm1_gain,
    norm2_gain,
    norm3_gain,
    q_weight,
    k_weight,
    v_weight,
    o_weight,
    cross_q,
    cross_k,
    cross_v,
    cross_o,
    gate_weight,
    up_weight,
    down_weight,
    segment_ids,
    block_ids,
    image_table,
):
    width = tokens.shape[1]
    share = q_weight.shape[0]
    inner = q_weight.shape[1]
    unit = gate_weight.shape[1]
    images = memory.shape[0]
    flat_memory = memory.reshape(-1, width)
    place = lax.axis_index("wide")
    side = lax.axis_index("narrow")
    places = jnp.stack([place, place ^ 2, place ^ 1, place ^ 3, side]).astype(jnp.int32)

    gains = jnp.stack([norm1_gain, norm2_gain, norm3_gain])
    gains = jnp.pad(gains, ((0, 13), (0, 3 * inner - share)))
    early = jnp.concatenate(
        [jnp.concatenate([q_weight, k_weight, v_weight], axis=1), gains], axis=0
    )
    early_x = swap(early, "wide", 2)
    early_core = swap(early, "wide", 1)
    early_pieces = (early, early_x, early_core, swap(early_x, "wide", 1))
    lines = jnp.stack([piece[share : share + 3, :share] for piece in early_pieces])
    lines = lines.astype(F32)
    order = [
        jnp.sum(jnp.where((places[:4] == w)[:, None, None], lines, 0.0), axis=0)
        for w in range(4)
    ]
    all_gains = jnp.concatenate(order, axis=1)[:, None, :]

    mid = jnp.concatenate([cross_k, cross_v, cross_q, o_weight], axis=1)
    memory_columns = slice(0, 2 * inner)
    query_columns = slice(2 * inner, 3 * inner)
    out_columns = slice(3 * inner, 4 * inner)
    mid_x = swap(after(mid, early_x), "wide", 2)
    mid_core = swap(mid, "wide", 1)
    out_y = swap(o_weight, "narrow", 1)
    late = jnp.concatenate([cross_q, cross_o, gate_weight, up_weight, down_weight], axis=1)
    late_query_columns = slice(0, inner)
    late_columns = (slice(inner, 2 * inner), slice(2 * inner, 2 * inner + 3 * unit))

    x, row_ids, col_ids, pos, scalars = order_rows(
        segment_ids, block_ids, image_table, after(tokens, early_core, out_y)
    )
    late = gather_all(after(late, early_x, x))
    n1, qkv = norm_project(places, x, all_gains[0], early_pieces)
    pairs = inner // PAIR
    self_parts = [self_forward(0, after(qkv, mid_core), row_ids, col_ids)]
    out_yx = after(swap(out_y, "wide", 2), self_parts[0][0])
    out_pieces = (out_y, out_yx, swap(out_y, "wide", 1), swap(out_yx, "wide", 1))
    for pair in range(1, pairs):
        waits = out_pieces if pair == pairs - 1 else ()
        self_parts.append(
            self_forward(pair, after(qkv, self_parts[-1][0], *waits), row_ids, col_ids)
        )
    mid_x = after(mid_x, self_parts[-1][0])
    mid_pieces = (mid, mid_x, mid_core, swap(mid_x, "wide", 1))
    gy = order_more(pos, after(cotangent, self_parts[-1][0]))
    attended_theirs = [swap(part[0], "narrow", 1) for part in self_parts]
    attended = [part[0] for part in self_parts]
    keys_values = project_memory(
        places,
        after(flat_memory, gy, attended_theirs[0]),
        mid_pieces,
        memory_columns,
    )
    h1, n2, cq = middle_step(
        places,
        after(x, keys_values),
        attended,
        attended_theirs,
        all_gains[1],
        mid_pieces,
        out_pieces,
        (out_columns, slice(0, inner), query_columns),
    )
    cross_parts = [cross_forward(0, scalars, cq, keys_values, images)]
    crossed_theirs = []
    for pair in range(1, pairs):
        previous = [cross_parts[-1][0]] + crossed_theirs
        crossed_theirs.append(swap(cross_parts[-1][0], "narrow", 1))
        cross_parts.append(
            cross_forward(pair, scalars, after(cq, *previous), keys_values, images)
        )
    crossed = [part[0] for part in cross_parts]
    crossed_theirs.append(swap(crossed[-1], "narrow", 1))
    cross_logs = jnp.concatenate([part[1] for part in cross_parts], axis=0)
    (
        output,
        n3,
        hidden,
        grad_gate,
        grad_up,
        e2,
        dc,
        cross_deltas,
        third_gain,
    ) = units_step(
        places,
        h1,
        crossed,
        crossed_theirs,
        all_gains[2],
        gy,
        late,
        late_columns,
    )

    unit_keep, unit_send = weight_grads(
        places, (n3, gy), (grad_gate, grad_up, hidden), ((0, (0,)), (0, (1,)), (1, (2,)))
    )
    unit_stay, unit_leave = add_pair(unit_keep, swap(unit_send, "wide", 1))
    dcq, dck, dcv = cross_backward(
        0,
        scalars,
        cq,
        keys_values,
        after(dc, unit_leave),
        cross_logs,
        cross_deltas,
        images,
        None,
    )
    unit_part = add(unit_stay, swap(unit_leave, "wide", 2))
    keep0, send0, more0, total = memory_back(
        places,
        flat_memory,
        after(dck, unit_part),
        dcv,
        mid_pieces,
        memory_columns,
        0,
        None,
        0,
    )
    unit_sum = lax.psum(unit_part, "dp")
    dcq, dck, dcv = cross_backward(
        1,
        scalars,
        cq,
        keys_values,
        after(dc, send0),
        cross_logs,
        cross_deltas,
        images,
        dcq,
    )
    dcq_theirs = swap(dcq, "narrow", 1)
    got0 = swap(send0, "narrow", 1)
    got_more = swap(after(more0, dcq), "narrow", 1)
    keep1, send1, cross_keep, cross_send = memory_back(
        places,
        flat_memory,
        after(dck, got0),
        dcv,
        mid_pieces,
        memory_columns,
        1,
        total,
        2 * inner,
    )
    cross_keep, cross_send = weight_grads(
        places,
        (after(n2, send1), e2),
        (dcq, crossed),
        ((0, (0,)), (1, (1,))),
        into=(cross_keep, cross_send),
        first=2,
    )
    e1, da, self_deltas, second_gain = turn_step(
        places,
        e2,
        h1,
        after(dcq, cross_send, unit_sum),
        dcq_theirs,
        all_gains[1],
        attended,
        mid_pieces,
        late,
        (out_columns, query_columns, late_query_columns),
    )
    got1 = swap(after(send1, dcq_theirs, got0), "narrow", 1)
    cross_stay, cross_leave = add_pair(cross_keep, swap(cross_send, "wide", 1))
    da = after(da, cross_leave)
    back = []
    for pair in range(pairs):
        ready = after(da, *[part[0] for part in back])
        if pair == pairs - 1:
            early_back = list(back)
            self_keep, self_send = weight_grads(
                places,
                (after(n1, back[-1][0]), e1),
                [[part[i] for part in early_back] for i in range(3)] + [attended],
                ((0, (0, 1, 2)), (1, (3,))),
            )
            cross_part = add(cross_stay, swap(cross_leave, "wide", 2))
            ready = after(ready, cross_part, self_send)
            cross_part = line_first(cross_part)
        back.append(
            self_backward(
                pair, qkv, ready, self_parts[pair][1], self_deltas, row_ids, col_ids
            )
        )
    dq, dk, dv = [[part[i] for part in back] for i in range(3)]
    self_stay, self_leave = add_pair(self_keep, swap(self_send, "wide", 1))
    self_part = add(self_stay, swap(self_leave, "wide", 2))
    dn1, last_keep, last_send = partial_step(
        places,
        dq + dk + dv,
        after(x, self_leave),
        n1,
        second_gain,
        third_gain,
        early_pieces,
    )
    dn1_theirs = swap(dn1, "narrow", 1)
    memory0 = add(after(keep0, dn1), jnp.concatenate([got0, got_more]))
    memory1 = add(after(keep1, dn1), got1)
    last_stay, last_leave = add_pair(last_keep, swap(last_send, "wide", 1))
    last_part = add(last_stay, swap(last_leave, "wide", 2))
    output = restore_rows(pos, after(output, last_send, self_part))
    tokens_grad = last_step(pos, e1, x, dn1, dn1_theirs, all_gains[0])
    memory_grad = jnp.stack([after(memory0, self_part), memory1])
    cross_sum = line_third(line_second(cross_part), tokens_grad)
    self_first = line_first(self_part)
    self_second = line_second(self_first)
    self_sum = line_third(self_second, tokens_grad)
    last_first = after(line_first(last_part), self_first)
    last_second = after(line_second(last_first), self_second)
    last_sum = line_third(last_second)
    gain_sums = last_sum[share:, :share].astype(F32)
    first_gain = gain_sums[0] + swap(after(gain_sums, self_second), "narrow", 1)[0]

    def grads(array, size, count):
        return [array[:share, i * size : (i + 1) * size].astype(F32) for i in range(count)]

    gate_grad, up_grad, down_grad = grads(after(unit_sum, self_part), unit, 3)
    cross_k_grad, cross_v_grad, cross_q_grad, cross_o_grad = grads(cross_sum, inner, 4)
    part = inner - PAIR
    q_grad, k_grad, v_grad = [
        jnp.concatenate([most, rest], axis=1)
        for most, rest in zip(grads(self_sum, part, 3), grads(last_sum, PAIR, 3))
    ]
    o_grad = self_sum[:, 3 * part :].astype(F32)
    return (
        output,
        tokens_grad,
        memory_grad,
        first_gain,
        gain_sums[1],
        gain_sums[2],
        q_grad,
        k_grad,
        v_grad,
        o_grad,
        cross_q_grad,
        cross_k_grad,
        cross_v_grad,
        cross_o_grad,
        gate_grad,
        up_grad,
        down_grad,
    )


def solution(mesh):
    both = ("dp", "wide")
    weight = P("wide", "narrow")
    in_specs = (
        (P(both, None), P(both, None, None), P(both, None))
        + (P("wide"),) * 3
        + (weight,) * 11
        + (P(both, None),) * 3
    )
    out_specs = (
        (P(both, None), P(both, None), P(both, None, "narrow"))
        + (P("wide"),) * 3
        + (weight,) * 11
    )
    return jax.shard_map(local, mesh=mesh, in_specs=in_specs, out_specs=out_specs, check_vma=False)
```

```python
import functools
import math

import jax
import jax.numpy as jnp
from jax import lax
from jax.experimental import pallas as pl
from jax.experimental.pallas import tpu as pltpu
from jax.sharding import PartitionSpec as P

F32 = jnp.float32
BF16 = jnp.bfloat16
EPSILON = 1e-06
ROOT_TWO_OVER_PI = 0.7978845608028654
CUBIC = 0.044715
HEAD_DIM = 64
PAIR = 2 * HEAD_DIM
SCALE = HEAD_DIM ** (-0.5)
EXP2_SCALE = SCALE * math.log2(math.e)
HIDE = 1e30
TILE = 256
ROWS = 512
WEIGH = 4.0

NN = (((1,), (0,)), ((), ()))
NT = (((1,), (1,)), ((), ()))
TN = (((0,), (0,)), ((), ()))


def dot(left, right, dims):
    return lax.dot_general(left, right, dims, preferred_element_type=F32)


def params(mebibytes=24):
    return pltpu.CompilerParams(vmem_limit_bytes=mebibytes * 1024 * 1024)


def cost(flops, nbytes):
    return pl.CostEstimate(
        flops=int(flops * WEIGH), bytes_accessed=int(nbytes * WEIGH), transcendentals=0
    )


def pin(*arrays):
    return [pltpu.with_memory_space_constraint(array, pltpu.HBM) for array in arrays]


def shape_of(shape, dtype):
    return jax.ShapeDtypeStruct(shape, dtype)


def whole(shape):
    zeros = (0,) * len(shape)
    return pl.BlockSpec(shape, lambda *_: zeros)


def rows(width, height=None):
    height = ROWS if height is None else height
    return pl.BlockSpec((height, width), lambda t, *_: (t, 0))


def inverse_rms(values):
    return lax.rsqrt(jnp.mean(values * values, axis=1, keepdims=True) + EPSILON)


def norm_back(values, gain, upstream):
    factor = inverse_rms(values)
    scaled = upstream * gain
    mean = jnp.mean(values * scaled, axis=1, keepdims=True)
    grad = factor * scaled - values * (factor * factor * factor * mean)
    return grad, jnp.sum(upstream * values * factor, axis=0, keepdims=True)


def in_half(shape, half):
    return (lax.broadcasted_iota(jnp.int32, shape, 1) // HEAD_DIM) == half


def only_half(values, half):
    return jnp.where(in_half(values.shape, half), values, jnp.zeros_like(values))


def order_kernel(seg, blk, table, x, xp, row_ids, col_ids, pos_out, scalars, pos):
    step = pl.program_id(0)
    count = seg.shape[1]

    @pl.when(step == 0)
    def _():
        segments = seg[...]
        image = jnp.zeros_like(segments)
        for s in range(table.shape[1]):
            image = jnp.where(segments == s, table[0, s], image)
        first = (image == 0).astype(F32)
        before = lax.broadcasted_iota(jnp.int32, (count, count), 0) < lax.broadcasted_iota(
            jnp.int32, (count, count), 1
        )
        rank = dot(
            jnp.broadcast_to(first, (8, count)).astype(BF16),
            before.astype(F32).astype(BF16),
            NN,
        )[0:1]
        total = jnp.sum(first)
        index = lax.broadcasted_iota(jnp.int32, (1, count), 1).astype(F32)
        place = jnp.where(image == 0, rank, total + index - rank)
        pos[...] = place.astype(jnp.int32)
        pos_out[...] = jnp.broadcast_to(pos[...], (8, count))
        n0 = total.astype(jnp.int32)
        tiles = count // TILE
        visits0 = jnp.maximum(1, (n0 + TILE - 1) // TILE)
        start1 = jnp.minimum(tiles - 1, n0 // TILE)
        visits = visits0 + tiles - start1
        for v in range(tiles + 1):
            real = jnp.minimum(v, visits - 1)
            in_first = real < visits0
            scalars[v] = jnp.where(in_first, real, real - visits0 + start1)
            scalars[8 + v] = jnp.where(in_first, 0, 1)
        scalars[16] = visits
        scalars[17] = n0
        scalars[18] = visits0
        scalars[19] = start1
        scalars[20] = tiles - start1

    onehot = (
        lax.broadcasted_iota(jnp.int32, (TILE, count), 0) + step * TILE == pos[...]
    ).astype(F32).astype(BF16)
    xp[...] = dot(onehot, x[...], NN).astype(BF16)
    ids = jnp.concatenate(
        [
            seg[...].astype(F32),
            blk[...].astype(F32),
            jnp.zeros((126, count), F32),
        ],
        axis=0,
    ).astype(BF16)
    row_ids[...] = dot(ids[0:8], onehot, NT)
    col_ids[...] = dot(onehot, ids, NT)


def order_rows(seg, blk, table, x):
    count, width = x.shape
    return pl.pallas_call(
        order_kernel,
        grid=(count // TILE,),
        in_specs=[
            whole((1, count)),
            whole((1, count)),
            pl.BlockSpec(memory_space=pltpu.SMEM),
            whole((count, width)),
        ],
        out_specs=[
            rows(width, TILE),
            pl.BlockSpec((8, TILE), lambda t: (0, t)),
            rows(128, TILE),
            whole((8, count)),
            pl.BlockSpec(memory_space=pltpu.SMEM),
        ],
        out_shape=[
            pltpu.HBM((count, width), BF16),
            shape_of((8, count), F32),
            shape_of((count, 128), F32),
            shape_of((8, count), jnp.int32),
            shape_of((32,), jnp.int32),
        ],
        scratch_shapes=[pltpu.VMEM((1, count), jnp.int32)],
        compiler_params=params(),
        cost_estimate=cost(2 * count * count * width, 8 * count * width),
    )(seg, blk, table, *pin(x))


def order_more_kernel(pos, values, out):
    size, count = out.shape[0], values.shape[0]
    index = lax.broadcasted_iota(jnp.int32, (size, count), 0) + pl.program_id(0) * size
    onehot = (index == pos[0:1, :]).astype(F32).astype(BF16)
    out[...] = dot(onehot, values[...], NN).astype(BF16)


def order_more(pos, values):
    count, width = values.shape
    return pl.pallas_call(
        order_more_kernel,
        grid=(count // TILE,),
        in_specs=[whole((8, count)), whole((count, width))],
        out_specs=rows(width, TILE),
        out_shape=pltpu.HBM((count, width), BF16),
        compiler_params=params(),
        cost_estimate=cost(2 * count * count * width, 4 * count * width),
    )(pos, *pin(values))


def restore_kernel(pos, values, out):
    count = values.shape[0]
    onehot = (
        lax.broadcasted_iota(jnp.int32, (count, ROWS), 0) == pos[0:1, :]
    ).astype(F32).astype(BF16)
    out[...] = dot(onehot, values[...], TN).astype(BF16)


def restore_rows(pos, values):
    count, width = values.shape
    return pl.pallas_call(
        restore_kernel,
        grid=(count // ROWS,),
        in_specs=[pl.BlockSpec((8, ROWS), lambda t: (0, t)), whole((count, width))],
        out_specs=rows(width, ROWS),
        out_shape=shape_of((count, width), BF16),
        compiler_params=params(),
        cost_estimate=cost(2 * count * count * width, 4 * count * width),
    )(pos, *pin(values))


def fetch(pieces, places, columns, dest, sems, base=0):
    height = dest.shape[0] // 4
    copies = []
    for i, piece in enumerate(pieces):
        start = pl.multiple_of(places[i] * height, 16)
        copies.append(
            pltpu.make_async_copy(
                piece.at[pl.ds(0, height), columns],
                dest.at[pl.ds(start, height), :],
                sems.at[base + i],
            )
        )
    return copies


def fetch_half(gathered, half, columns, dest, sem):
    return pltpu.make_async_copy(gathered.at[half, :, columns], dest, sem)


def start_all(copies):
    for copy in copies:
        copy.start()


def wait_all(copies):
    for copy in copies:
        copy.wait()


ANY = pl.BlockSpec(memory_space=pl.ANY)
SCALARS = pl.BlockSpec(memory_space=pltpu.SMEM)


def project_kernel(places, x, gain, w0, w1, w2, w3, normed, out, weight, sems):
    @pl.when(pl.program_id(0) == 0)
    def _():
        copies = fetch((w0, w1, w2, w3), places, slice(0, weight.shape[1]), weight, sems)
        start_all(copies)
        wait_all(copies)

    values = x[...].astype(F32)
    n1 = (values * inverse_rms(values) * gain[...]).astype(BF16)
    normed[...] = n1
    out[...] = dot(n1, weight[...], NN).astype(BF16)


def norm_project(places, x, gain, pieces):
    count, width = x.shape
    outs = pieces[0].shape[1]
    return pl.pallas_call(
        project_kernel,
        grid=(count // ROWS,),
        in_specs=[SCALARS, rows(width), whole((1, width))] + [ANY] * 4,
        out_specs=[rows(width), rows(outs)],
        out_shape=[pltpu.HBM((count, width), BF16), shape_of((count, outs), BF16)],
        scratch_shapes=[pltpu.VMEM((width, outs), BF16), pltpu.SemaphoreType.DMA((4,))],
        compiler_params=params(),
        cost_estimate=cost(2 * count * width * outs, 4 * count * width + 2 * count * outs),
    )(places, *pin(x), gain, *pieces)


MEMORY_TILE = 1024
BACK_TILE = 512


def memory_kernel(places, columns, memory, w0, w1, w2, w3, out, weight, sems):
    @pl.when(pl.program_id(0) == 0)
    def _():
        copies = fetch((w0, w1, w2, w3), places, columns, weight, sems)
        start_all(copies)
        wait_all(copies)

    out[...] = dot(memory[...], weight[...], NN).astype(BF16)


def project_memory(places, memory, pieces, columns):
    count, width = memory.shape
    outs = columns.stop - columns.start

    def kernel(places, *refs):
        memory_kernel(places, columns, *refs)

    return pl.pallas_call(
        kernel,
        grid=(count // MEMORY_TILE,),
        in_specs=[SCALARS, rows(width, MEMORY_TILE)] + [ANY] * 4,
        out_specs=rows(outs, MEMORY_TILE),
        out_shape=pltpu.HBM((count, outs), BF16),
        scratch_shapes=[pltpu.VMEM((width, outs), BF16), pltpu.SemaphoreType.DMA((4,))],
        compiler_params=params(),
        cost_estimate=cost(2 * count * width * outs, 4 * count * width),
    )(places, *pin(memory), *pieces)


SELF_TILE = 256
SELF_WINDOW = 640
BACK_WINDOW = 640


def store_logs(ref, columns, logs, extra=None):
    spread = jnp.where(in_half((logs[0].shape[0], PAIR), 0), logs[0], logs[1]).T
    for half in range(2):
        line = spread[half * HEAD_DIM : half * HEAD_DIM + 1, :]
        if extra is not None:
            line = jnp.where(extra, line, ref[half : half + 1, columns])
        ref[half : half + 1, columns] = line


def self_forward_kernel(q, k, v, row_ids, col_ids, out, logs):
    count = q.shape[0]
    for tile in range(count // SELF_TILE):
        base = tile * SELF_TILE
        start = min(max(base - 256, 0), count - SELF_WINDOW)
        spot = slice(base, base + SELF_TILE)
        window = slice(start, start + SELF_WINDOW)
        seen = (col_ids[spot, 0:1] == row_ids[0:1, window]) & (
            row_ids[1:2, window] <= col_ids[spot, 1:2]
        )
        bias = jnp.where(seen, 0.0, -HIDE)
        keys = k[window, :]
        values = v[window, :]
        queries = q[spot, :]
        parts, totals = [], []
        for half in range(2):
            scores = dot(only_half(queries, half), keys, NT) * EXP2_SCALE + bias
            highest = jnp.max(scores, axis=1, keepdims=True)
            weights = jnp.exp2(scores - highest)
            total = jnp.sum(weights, axis=1, keepdims=True)
            parts.append(dot(weights.astype(BF16), values, NN) / total)
            totals.append(highest + jnp.log2(total))
        out[spot, :] = jnp.where(in_half(parts[0].shape, 0), parts[0], parts[1]).astype(BF16)
        store_logs(logs, spot, totals)


def self_forward(pair, qkv, row_ids, col_ids):
    count = qkv.shape[0]
    pairs = qkv.shape[1] // (3 * PAIR)

    def part(which):
        return pl.BlockSpec((count, PAIR), lambda p: (0, which * pairs + pair))

    return pl.pallas_call(
        self_forward_kernel,
        grid=(1,),
        in_specs=[part(0), part(1), part(2), whole((8, count)), whole((count, 128))],
        out_specs=[whole((count, PAIR)), whole((8, count))],
        out_shape=[pltpu.HBM((count, PAIR), BF16), pltpu.HBM((8, count), F32)],
        compiler_params=params(),
        cost_estimate=cost(16 * count * SELF_WINDOW * PAIR, 8 * count * PAIR),
    )(qkv, qkv, qkv, row_ids, col_ids)


def self_backward_kernel(q, k, v, grad, logs, deltas, row_ids, col_ids, dq, dk, dv, key_sum, value_sum):
    count = q.shape[0]
    key_sum[...] = jnp.zeros_like(key_sum)
    value_sum[...] = jnp.zeros_like(value_sum)
    for tile in range(count // TILE):
        base = tile * TILE
        start = min(max(base - 256, 0), count - BACK_WINDOW)
        spot = slice(base, base + TILE)
        window = slice(start, start + BACK_WINDOW)
        seen = (col_ids[window, 0:1] == row_ids[0:1, spot]) & (
            col_ids[window, 1:2] <= row_ids[1:2, spot]
        )
        bias = jnp.where(seen, 0.0, -HIDE)
        keys = k[window, :]
        values = v[window, :]
        queries = q[spot, :]
        grads = grad[spot, :]
        parts = []
        for half in range(2):
            one_query = only_half(queries, half)
            one_grad = only_half(grads, half)
            scores = dot(keys, one_query, NT) * EXP2_SCALE + bias
            weights = jnp.exp2(scores - logs[half : half + 1, spot])
            slopes = dot(values, one_grad, NT)
            pushed = (weights * (slopes - deltas[half : half + 1, spot])).astype(BF16)
            value_sum[window, :] += dot(weights.astype(BF16), one_grad, NN)
            key_sum[window, :] += dot(pushed, one_query, NN)
            parts.append(dot(pushed, keys, TN))
        dq[spot, :] = (
            jnp.where(in_half(parts[0].shape, 0), parts[0], parts[1]) * SCALE
        ).astype(BF16)
    dk[...] = (key_sum[...] * SCALE).astype(BF16)
    dv[...] = value_sum[...].astype(BF16)


def self_backward(pair, qkv, grad, logs, deltas, row_ids, col_ids):
    count = qkv.shape[0]
    pairs = qkv.shape[1] // (3 * PAIR)

    def part(which):
        return pl.BlockSpec((count, PAIR), lambda p: (0, which * pairs + pair))

    return pl.pallas_call(
        self_backward_kernel,
        grid=(1,),
        in_specs=[
            part(0),
            part(1),
            part(2),
            part(0),
            whole((8, count)),
            pl.BlockSpec((8, count), lambda p: (pair, 0)),
            whole((8, count)),
            whole((count, 128)),
        ],
        out_specs=[whole((count, PAIR))] * 3,
        out_shape=[pltpu.HBM((count, PAIR), BF16)] * 3,
        scratch_shapes=[pltpu.VMEM((count, PAIR), F32)] * 2,
        compiler_params=params(),
        cost_estimate=cost(40 * count * BACK_WINDOW * PAIR, 16 * count * PAIR),
    )(qkv, qkv, qkv, grad, logs, deltas, row_ids, col_ids)


KEYS = 1024


def visits_of(image, scalars):
    first = jnp.where(image == 0, 0, scalars[19])
    return first, jnp.where(image == 0, scalars[18], scalars[20])


def cross_forward_kernel(scalars, q, k, v, out, logs):
    image = pl.program_id(0)
    first, count = visits_of(image, scalars)

    def visit(i, carry):
        base = pl.multiple_of((first + i) * TILE, TILE)
        spot = pl.ds(base, TILE)
        queries = q[spot, :]
        parts, totals = [], []
        tops, sums = [None, None], [None, None]
        for start in range(0, k.shape[0], KEYS):
            keys = k[start : start + KEYS, :]
            values = v[start : start + KEYS, :]
            both = [dot(only_half(queries, half), keys, NT) for half in range(2)]
            for half, scores in enumerate(both):
                highest = jnp.max(scores, axis=1, keepdims=True) * EXP2_SCALE
                if start:
                    highest = jnp.maximum(highest, tops[half])
                weights = jnp.exp2(scores * EXP2_SCALE - highest).astype(BF16)
                mixed = dot(
                    weights,
                    jnp.where(in_half(values.shape, half), values, jnp.ones_like(values)),
                    NN,
                )
                if start:
                    mixed = mixed + sums[half] * jnp.exp2(tops[half] - highest)
                tops[half], sums[half] = highest, mixed
        for half in range(2):
            total = pltpu.roll(sums[half], HEAD_DIM, 1)
            parts.append(sums[half] / total)
            totals.append(tops[half] + jnp.log2(total))
        mixed = jnp.where(in_half(parts[0].shape, 0), parts[0], parts[1]).astype(BF16)
        limit = jnp.where(image == 0, 0, scalars[17]) - base
        row_mine = lax.broadcasted_iota(jnp.int32, mixed.shape, 0) >= limit
        lane_mine = lax.broadcasted_iota(jnp.int32, (1, TILE), 1) >= limit
        out[spot, :] = jnp.where(row_mine, mixed, out[spot, :])
        store_logs(logs, spot, totals, lane_mine)
        return carry

    lax.fori_loop(0, count, visit, 0)


def cross_forward(pair, scalars, q, keys_values, images):
    count, inner = q.shape
    pairs = inner // PAIR
    memory_rows = keys_values.shape[0] // images

    def part(which):
        return pl.BlockSpec((memory_rows, PAIR), lambda i, sc: (i, which * pairs + pair))

    return pl.pallas_call(
        cross_forward_kernel,
        grid_spec=pltpu.PrefetchScalarGridSpec(
            num_scalar_prefetch=1,
            grid=(images,),
            in_specs=[
                pl.BlockSpec((count, PAIR), lambda i, sc: (0, pair)),
                part(0),
                part(1),
            ],
            out_specs=[whole((count, PAIR)), whole((8, count))],
        ),
        out_shape=[pltpu.HBM((count, PAIR), BF16), pltpu.HBM((8, count), F32)],
        compiler_params=params(),
        cost_estimate=cost(20 * count * memory_rows * PAIR, 8 * memory_rows * PAIR),
    )(scalars, *pin(q, keys_values, keys_values))


def cross_backward_kernel(
    image, scalars, q, k, v, grad, logs, deltas, old, dq, dk, dv, key_sum, value_sum
):
    first, count = visits_of(jnp.int32(image), scalars)
    if image:
        dq[...] = old[...]

    def visit(i, fresh):
        base = pl.multiple_of((first + i) * TILE, TILE)
        spot = pl.ds(base, TILE)
        queries = q[spot, :]
        grads = grad[spot, :]
        keys = k[...]
        values = v[...]
        limit = scalars[17] - base
        lane_mine = (lax.broadcasted_iota(jnp.int32, (1, TILE), 1) >= limit) == (image == 1)
        parts = []
        for half in range(2):
            one_query = only_half(queries, half)
            one_grad = only_half(grads, half)
            log = jnp.where(lane_mine, logs[half : half + 1, spot], HIDE)
            scores = dot(keys, one_query, NT)
            weights = jnp.exp2(scores * EXP2_SCALE - log)
            slopes = dot(values, one_grad, NT)
            pushed = (weights * (slopes - deltas[half : half + 1, spot])).astype(BF16)
            value_part = dot(weights.astype(BF16), one_grad, NN)
            key_part = dot(pushed, one_query, NN)
            if fresh and half == 0:
                value_sum[...] = value_part
                key_sum[...] = key_part
            else:
                value_sum[...] += value_part
                key_sum[...] += key_part
            parts.append(dot(pushed, keys, TN))
        grad_query = (
            jnp.where(in_half(parts[0].shape, 0), parts[0], parts[1]) * SCALE
        ).astype(BF16)
        if image:
            row_mine = lax.broadcasted_iota(jnp.int32, grad_query.shape, 0) >= limit
            grad_query = jnp.where(row_mine, grad_query, dq[spot, :])
        dq[spot, :] = grad_query

    def later(i, carry):
        visit(i, False)
        return carry

    visit(0, True)
    lax.fori_loop(1, count, later, 0)
    dk[...] = (key_sum[...] * SCALE).astype(BF16)
    dv[...] = value_sum[...].astype(BF16)


def cross_backward(image, scalars, q, keys_values, grad, logs, deltas, images, old):
    count, inner = q.shape
    pairs = inner // PAIR
    memory_rows = keys_values.shape[0] // images
    token_spec = pl.BlockSpec((count, PAIR), lambda p, sc: (0, p))
    line = pl.BlockSpec((8, count), lambda p, sc: (p, 0))
    result = pl.BlockSpec((memory_rows, PAIR), lambda p, sc: (0, p))

    def part(which):
        return pl.BlockSpec((memory_rows, PAIR), lambda p, sc: (image, which * pairs + p))

    def first_kernel(scalars, q, k, v, grad, logs, deltas, *rest):
        cross_backward_kernel(image, scalars, q, k, v, grad, logs, deltas, None, *rest)

    def second_kernel(*refs):
        cross_backward_kernel(image, *refs)

    extra = [old] if image else []
    return pl.pallas_call(
        second_kernel if image else first_kernel,
        grid_spec=pltpu.PrefetchScalarGridSpec(
            num_scalar_prefetch=1,
            grid=(pairs,),
            in_specs=[token_spec, part(0), part(1), token_spec, line, line]
            + [token_spec] * len(extra),
            out_specs=[token_spec, result, result],
            scratch_shapes=[pltpu.VMEM((memory_rows, PAIR), F32)] * 2,
        ),
        out_shape=[
            pltpu.HBM((count, inner), BF16),
            pltpu.HBM((memory_rows, inner), BF16),
            pltpu.HBM((memory_rows, inner), BF16),
        ],
        compiler_params=params(32),
        cost_estimate=cost(25 * count * memory_rows * inner, 8 * memory_rows * inner),
    )(scalars, *pin(q, keys_values, keys_values, grad), logs, deltas, *pin(*extra))


def put_rows(places, product, keep, send, span=slice(None)):
    height = product.shape[0] // 4
    for i, ref in enumerate((keep, keep, send, send)):
        start = pl.multiple_of(places[i] * height, 16)
        ref[i % 2, 0:height, span] = product[pl.ds(start, height), :].astype(BF16)


def memory_back_kernel(
    columns, last, places, memory, dk, dv, w0, w1, w2, w3, *refs
):
    if last:
        before, keep_part, send_part, keep, send, weight, total, sems = refs
    else:
        keep_part, send_part, send_more, total_out, weight, total, sems = refs
    inner = dk.shape[1]

    @pl.when(pl.program_id(0) == 0)
    def _():
        copies = fetch((w0, w1, w2, w3), places, columns, weight, sems)
        start_all(copies)
        if last:
            total[...] = before[...]
        else:
            total[...] = jnp.zeros_like(total)
        wait_all(copies)

    both = jnp.concatenate([dk[...], dv[...]], axis=1)
    product = dot(both, weight[...], NT).astype(BF16)
    lower, upper = product[:, :inner], product[:, inner:]
    side = places[4]
    leave = jnp.where(side == 0, upper, lower)
    if last:
        send_part[...] = leave
    else:

        early = pl.program_id(0) < pl.num_programs(0) // 2
        send_part[...] = jnp.where(early, leave, send_part[...])
        send_more[...] = leave

    keep_part[...] = jnp.where(side == 0, lower, upper)
    total[...] += dot(memory[...], both, TN)

    @pl.when(pl.program_id(0) == pl.num_programs(0) - 1)
    def _():
        if last:
            put_rows(places, total, keep, send)
        else:
            total_out[...] = total[...]


def memory_back(places, memory, dk, dv, pieces, columns, image, before, spare):
    count, inner = dk.shape
    width = memory.shape[1]
    steps = count // BACK_TILE
    last = before is not None
    ranks = pltpu.HBM((2, width // 4, spare + 2 * inner), BF16)
    rank_spec = pl.BlockSpec((2, width // 4, 2 * inner), lambda t: (0, 0, 0))

    def kernel(*refs):
        memory_back_kernel(columns, last, *refs)

    return pl.pallas_call(
        kernel,
        grid=(steps,),
        in_specs=[
            SCALARS,
            pl.BlockSpec((BACK_TILE, width), lambda t: (image * steps + t, 0)),
            rows(inner, BACK_TILE),
            rows(inner, BACK_TILE),
        ]
        + [ANY] * 4
        + ([whole((width, 2 * inner))] if last else []),
        out_specs=[rows(inner, BACK_TILE)]
        + (
            [rows(inner, BACK_TILE), rank_spec, rank_spec]
            if last
            else [
                pl.BlockSpec((BACK_TILE, inner), lambda t: (jnp.minimum(t, steps // 2 - 1), 0)),
                pl.BlockSpec((BACK_TILE, inner), lambda t: (jnp.maximum(t - steps // 2, 0), 0)),
                whole((width, 2 * inner)),
            ]
        ),
        out_shape=[pltpu.HBM((count, inner), BF16)]
        + (
            [pltpu.HBM((count, inner), BF16), ranks, ranks]
            if last
            else [
                pltpu.HBM((count // 2, inner), BF16),
                pltpu.HBM((count // 2, inner), BF16),
                shape_of((width, 2 * inner), F32),
            ]
        ),
        scratch_shapes=[
            pltpu.VMEM((width, 2 * inner), BF16),
            pltpu.VMEM((width, 2 * inner), F32),
            pltpu.SemaphoreType.DMA((4,)),
        ],
        compiler_params=params(),
        cost_estimate=cost(8 * count * width * inner, 8 * count * width),
    )(places, *pin(memory, dk, dv), *pieces, *([before] if last else []))


def weight_grads_kernel(plan, spans, places, left_refs, right_refs, keep, send, scratch):
    left_holds = scratch[: len(left_refs)]
    right_holds = scratch[len(left_refs) : -3]
    turned, product, sems = scratch[-3:]
    step = pl.program_id(0)
    lefts = [
        pltpu.make_async_copy(ref, hold, sems.at[i])
        for i, (ref, hold) in enumerate(zip(left_refs, left_holds))
    ]
    rights = [
        pltpu.make_async_copy(ref, hold, sems.at[len(left_refs) + i])
        for i, (ref, hold) in enumerate(zip(right_refs, right_holds))
    ]
    for at, (left, group) in enumerate(plan):
        fresh = at == 0 or plan[at - 1][0] != left

        @pl.when(step == at)
        def _():
            if at == 0:
                lefts[left].start()
                for g in group:
                    rights[g].start()
            if fresh:
                lefts[left].wait()
            if at == 0:
                begun = {left}
                for one, others in plan[1:]:
                    if one not in begun:
                        lefts[one].start()
                        begun.add(one)
                    for g in others:
                        rights[g].start()
            if fresh:
                turned[...] = left_holds[left][...].T
            for g in group:
                rights[g].wait()
            right = join([right_holds[g] for g in group])
            columns = right.shape[1]
            product[:, 0:columns] = dot(turned[...], right, NN)
            put_rows(places, product.at[:, 0:columns], keep, send, spans[at])


def join(refs):
    values = [ref[...] for ref in refs]
    return values[0] if len(values) == 1 else jnp.concatenate(values, axis=1)


def flatten(groups):
    flat, sizes = [], []
    for group in groups:
        group = group if isinstance(group, (list, tuple)) else [group]
        flat += list(group)
        sizes.append(len(group))
    return flat, sizes


def weight_grads(places, lefts, rights, plan, into=(), first=0):
    count, width = lefts[0].shape
    flat, sizes = flatten(rights)
    groups, at = [], 0
    for size in sizes:
        groups.append(list(range(at, at + size)))
        at += size
    plan = [(left, [f for g in group for f in groups[g]]) for left, group in plan]
    columns = [sum(flat[f].shape[1] for f in group) for _, group in plan]
    step_columns = columns[0]
    share = width // 4
    total = sum(columns) + first * step_columns
    even = len(set(columns)) == 1
    spans = [
        slice(0, step_columns) if even else slice(sum(columns[:at]), sum(columns[: at + 1]))
        for at in range(len(plan))
    ]
    extra = list(into)
    def kernel(places, *refs):
        lefts_end = len(lefts)
        rights_end = lefts_end + len(flat)
        weight_grads_kernel(
            plan,
            spans,
            places,
            refs[:lefts_end],
            refs[lefts_end:rights_end],
            *refs[rights_end + len(extra) : rights_end + len(extra) + 2],
            refs[rights_end + len(extra) + 2 :],
        )

    start = 1 + len(lefts) + len(flat)
    return pl.pallas_call(
        kernel,
        grid=(len(plan),),
        in_specs=[SCALARS]
        + [ANY] * (len(lefts) + len(flat) + len(extra)),
        out_specs=[
            pl.BlockSpec((2, share, step_columns), lambda t: (0, 0, t + first))
            if even
            else whole((2, share, total))
        ]
        * 2,
        out_shape=[pltpu.HBM((2, share, total), BF16)] * 2,
        input_output_aliases={start: 0, start + 1: 1} if extra else {},
        scratch_shapes=[pltpu.VMEM(array.shape, array.dtype) for array in list(lefts) + flat]
        + [
            pltpu.VMEM((width, count), BF16),
            pltpu.VMEM((width, max(columns)), F32),
            pltpu.SemaphoreType.DMA((len(lefts) + len(flat),)),
        ],
        compiler_params=params(32),
        cost_estimate=cost(
            2 * count * width * sum(columns), 4 * count * width * len(plan)
        ),
    )(places, *pin(*lefts, *flat), *extra)


def middle_kernel(plan, parts, places, x, gain, *refs):
    mine, theirs, refs = refs[:parts], refs[parts : 2 * parts], refs[2 * parts :]
    pieces, (h1, n2, cq, out_mine, out_theirs, query, sems) = refs[:8], refs[8:]

    @pl.when(pl.program_id(0) == 0)
    def _():
        copies = (
            fetch(pieces[:4], places, plan[0], out_mine, sems, 0)
            + fetch(pieces[4:], places, plan[1], out_theirs, sems, 4)
            + fetch(pieces[:4], places, plan[2], query, sems, 8)
        )
        start_all(copies)
        wait_all(copies)

    values = (
        x[...].astype(F32)
        + dot(join(mine), out_mine[...], NT)
        + dot(join(theirs), out_theirs[...], NT)
    )
    h1[...] = values.astype(BF16)
    normed = (values * inverse_rms(values) * gain[...]).astype(BF16)
    n2[...] = normed
    cq[...] = dot(normed, query[...], NN).astype(BF16)


def middle_step(places, x, mine, theirs, gain, pieces, pieces_theirs, plan):
    count, width = x.shape
    half = sum(part.shape[1] for part in mine)

    def kernel(*refs):
        middle_kernel(plan, len(mine), *refs)

    return pl.pallas_call(
        kernel,
        grid=(count // ROWS,),
        in_specs=[SCALARS, rows(width), whole((1, width))]
        + [rows(PAIR)] * (2 * len(mine))
        + [ANY] * 8,
        out_specs=[rows(width), rows(width), rows(half)],
        out_shape=[
            pltpu.HBM((count, width), BF16),
            pltpu.HBM((count, width), BF16),
            pltpu.HBM((count, half), BF16),
        ],
        scratch_shapes=[pltpu.VMEM((width, half), BF16)] * 3 + [pltpu.SemaphoreType.DMA((12,))],
        compiler_params=params(),
        cost_estimate=cost(6 * count * width * half, 12 * count * width),
    )(places, *pin(x), gain, *pin(*mine), *theirs, *pieces, *pieces_theirs)


def head_sums(left, right):
    product = left.astype(F32) * right.astype(F32)
    width = product.shape[1]
    high = product.astype(BF16)
    low = (product - high.astype(F32)).astype(BF16)
    height = 8 * (width // PAIR)
    line = lax.broadcasted_iota(jnp.int32, (height, width), 0)
    head = lax.broadcasted_iota(jnp.int32, (height, width), 1) // HEAD_DIM
    choose = (
        ((line // 8) * 2 + line % 8 == head) & (line % 8 < 2)
    ).astype(F32).astype(BF16)
    return dot(choose, high, NT) + dot(choose, low, NT)


CHUNK = 512


def units_kernel(plan, parts, places, h1, gain, gy, *refs):
    mine, theirs, refs = refs[:parts], refs[parts : 2 * parts], refs[2 * parts :]
    late, refs = refs[0], refs[1:]
    (
        output,
        n3,
        hidden,
        grad_gate,
        grad_up,
        e2,
        dc,
        deltas,
        gain_grad,
        out_mine,
        out_theirs,
        units_mine,
        units_theirs,
        sems,
    ) = refs
    step = pl.program_id(0)

    side = places[4]
    out_copies = [
        fetch_half(late, side, plan[0], out_mine, sems.at[0]),
        fetch_half(late, 1 - side, plan[0], out_theirs, sems.at[1]),
    ]
    mine_copy = fetch_half(late, side, plan[1], units_mine, sems.at[2])
    theirs_copy = fetch_half(late, 1 - side, plan[1], units_theirs, sems.at[3])

    @pl.when(step == 0)
    def _():
        start_all(out_copies + [mine_copy, theirs_copy])
        gain_grad[...] = jnp.zeros_like(gain_grad)
        wait_all(out_copies)

    crossed_mine = join(mine)
    values = (
        h1[...].astype(F32)
        + dot(crossed_mine, out_mine[...], NT)
        + dot(join(theirs), out_theirs[...], NT)
    )
    normed = (values * inverse_rms(values) * gain[...]).astype(BF16)
    n3[...] = normed
    upstream = gy[...]
    mixed = jnp.zeros_like(values)
    back = jnp.zeros_like(values)
    unit = units_mine.shape[1] // 3
    for own in (True, False):
        weight = units_mine if own else units_theirs

        @pl.when(step == 0)
        def _():
            (mine_copy if own else theirs_copy).wait()

        for start in range(0, unit, CHUNK):
            gate_weight = weight[:, start : start + CHUNK]
            up_weight = weight[:, unit + start : unit + start + CHUNK]
            down_weight = weight[:, 2 * unit + start : 2 * unit + start + CHUNK]
            gate = dot(normed, gate_weight, NN)
            up = dot(normed, up_weight, NN)
            pushed = dot(upstream, down_weight, NN)
            square = gate * gate
            bend = jnp.tanh(ROOT_TWO_OVER_PI * gate * (1.0 + CUBIC * square))
            lift = 0.5 * (1.0 + bend)
            gelu = gate * lift
            slope = lift + (0.5 * ROOT_TWO_OVER_PI) * gate * (1.0 - bend * bend) * (
                1.0 + (3.0 * CUBIC) * square
            )
            units = (gelu * up).astype(BF16)
            push_gate = (pushed * up * slope).astype(BF16)
            push_up = (pushed * gelu).astype(BF16)
            mixed = mixed + dot(units, down_weight, NT)
            back = back + dot(push_gate, gate_weight, NT) + dot(push_up, up_weight, NT)
            if own:
                hidden[:, start : start + CHUNK] = units
                grad_gate[:, start : start + CHUNK] = push_gate
                grad_up[:, start : start + CHUNK] = push_up
    output[...] = (values + mixed).astype(BF16)
    grad, gain_part = norm_back(values, gain[...], back)
    low = (upstream.astype(F32) + grad).astype(BF16)
    e2[...] = low
    crossed = dot(low, out_mine[...], NN).astype(BF16)
    dc[...] = crossed
    deltas[...] = head_sums(crossed, crossed_mine)
    gain_grad[0:1, :] += gain_part


def units_step(places, h1, mine, theirs, gain, gy, late, plan):
    count, width = h1.shape
    half = sum(part.shape[1] for part in mine)
    unit = (plan[1].stop - plan[1].start) // 3
    lines = 8 * (half // PAIR)

    def kernel(*refs):
        units_kernel(plan, len(mine), *refs)

    return pl.pallas_call(
        kernel,
        grid=(count // ROWS,),
        in_specs=[
            SCALARS,
            rows(width),
            whole((1, width)),
            rows(width),
        ]
        + [rows(PAIR)] * (2 * len(mine))
        + [ANY],
        out_specs=[
            rows(width),
            rows(width),
            rows(unit),
            rows(unit),
            rows(unit),
            rows(width),
            rows(half),
            pl.BlockSpec((lines, ROWS), lambda t: (0, t)),
            whole((8, width)),
        ],
        out_shape=[
            pltpu.HBM((count, width), BF16),
            pltpu.HBM((count, width), BF16),
            pltpu.HBM((count, unit), BF16),
            pltpu.HBM((count, unit), BF16),
            pltpu.HBM((count, unit), BF16),
            pltpu.HBM((count, width), BF16),
            pltpu.HBM((count, half), BF16),
            pltpu.HBM((lines, count), F32),
            shape_of((8, width), F32),
        ],
        scratch_shapes=[pltpu.VMEM((width, half), BF16)] * 2
        + [pltpu.VMEM((width, 3 * unit), BF16)] * 2
        + [pltpu.SemaphoreType.DMA((4,))],
        compiler_params=params(58),
        cost_estimate=cost(30 * count * width * unit, 30 * count * width),
    )(places, *pin(h1), gain, *pin(gy, *mine), *theirs, *pin(late))


def turn_kernel(plan, parts, places, e2, h1, mine, theirs, gain, *refs):
    attended, refs = refs[:parts], refs[parts:]
    pieces, refs = refs[:4], refs[4:]
    late, e1, da, deltas, gain_grad, query_mine, query_theirs, out_mine, sems = refs

    @pl.when(pl.program_id(0) == 0)
    def _():
        copies = (
            fetch(pieces, places, plan[0], out_mine, sems, 0)
            + fetch(pieces, places, plan[1], query_mine, sems, 4)
            + [fetch_half(late, 1 - places[4], plan[2], query_theirs, sems.at[8])]
        )
        start_all(copies)
        gain_grad[...] = jnp.zeros_like(gain_grad)
        wait_all(copies)

    back = dot(mine[...], query_mine[...], NT) + dot(theirs[...], query_theirs[...], NT)
    grad, gain_part = norm_back(h1[...].astype(F32), gain[...], back)
    low = (e2[...].astype(F32) + grad).astype(BF16)
    e1[...] = low
    pushed = dot(low, out_mine[...], NN).astype(BF16)
    da[...] = pushed
    deltas[...] = head_sums(pushed, join(attended))
    gain_grad[0:1, :] += gain_part


def turn_step(places, e2, h1, mine, theirs, gain, attended, pieces, late, plan):
    count, width = h1.shape
    half = mine.shape[1]
    lines = 8 * (half // PAIR)

    def kernel(*refs):
        turn_kernel(plan, len(attended), *refs)

    return pl.pallas_call(
        kernel,
        grid=(count // ROWS,),
        in_specs=[
            SCALARS,
            rows(width),
            rows(width),
            rows(half),
            rows(half),
            whole((1, width)),
        ]
        + [rows(PAIR)] * len(attended)
        + [ANY] * 5,
        out_specs=[
            rows(width),
            rows(half),
            pl.BlockSpec((lines, ROWS), lambda t: (0, t)),
            whole((8, width)),
        ],
        out_shape=[
            pltpu.HBM((count, width), BF16),
            shape_of((count, half), BF16),
            shape_of((lines, count), F32),
            shape_of((8, width), F32),
        ],
        scratch_shapes=[pltpu.VMEM((width, half), BF16)] * 3 + [pltpu.SemaphoreType.DMA((9,))],
        compiler_params=params(),
        cost_estimate=cost(6 * count * width * half, 16 * count * width),
    )(places, *pin(e2, h1, mine), theirs, gain, *pin(*attended), *pieces, *pin(late))


def partial_kernel(parts, places, x, n1, second, third, *refs):
    part_refs, refs = refs[:parts], refs[parts:]
    w0, w1, w2, w3, out, keep, send, weight, total, gain_grad, sems = refs
    step = pl.program_id(0)

    @pl.when(step == 0)
    def _():
        copies = fetch((w0, w1, w2, w3), places, slice(0, weight.shape[1]), weight, sems)
        start_all(copies)
        gain_grad[...] = jnp.zeros_like(gain_grad)
        total[...] = jnp.zeros_like(total)
        wait_all(copies)

    back = dot(join(part_refs), weight[...], NT)
    out[...] = back.astype(BF16)
    values = x[...].astype(F32)
    gain_grad[0:1, :] += jnp.sum(back * values * inverse_rms(values), axis=0, keepdims=True)
    last = join([part_refs[i * (parts // 3) + parts // 3 - 1] for i in range(3)])
    total[...] += dot(n1[...], last, TN)

    @pl.when(step == pl.num_programs(0) - 1)
    def _():
        put_rows(places, total, keep, send)
        height = total.shape[0] // 4
        lines = jnp.concatenate(
            [
                gain_grad[0:1, :],
                second[0:1, :],
                third[0:1, :],
                jnp.zeros((13, gain_grad.shape[1]), F32),
            ],
            axis=0,
        )
        shares = [lines[:, w * height : (w + 1) * height] for w in range(4)]
        fill = jnp.zeros((16, total.shape[1] - height), F32)
        for i, ref in enumerate((keep, keep, send, send)):
            share = shares[0]
            for w in range(1, 4):
                share = jnp.where(places[i] == w, shares[w], share)
            ref[i % 2, height : height + 16, :] = jnp.concatenate([share, fill], axis=1).astype(
                BF16
            )


def partial_step(places, parts, x, n1, second, third, pieces):
    count, width = x.shape
    inner = sum(part.shape[1] for part in parts)
    ranks = (2, width // 4 + 16, 3 * PAIR)

    def kernel(*refs):
        partial_kernel(len(parts), *refs)

    return pl.pallas_call(
        kernel,
        grid=(count // ROWS,),
        in_specs=[SCALARS, rows(width), rows(width), whole((8, width)), whole((8, width))]
        + [rows(PAIR)] * len(parts)
        + [ANY] * 4,
        out_specs=[rows(width), whole(ranks), whole(ranks)],
        out_shape=[
            pltpu.HBM((count, width), BF16),
            shape_of(ranks, BF16),
            shape_of(ranks, BF16),
        ],
        scratch_shapes=[
            pltpu.VMEM((width, inner), BF16),
            pltpu.VMEM((width, 3 * PAIR), F32),
            pltpu.VMEM((8, width), F32),
            pltpu.SemaphoreType.DMA((4,)),
        ],
        compiler_params=params(),
        cost_estimate=cost(2 * count * width * (inner + 3 * PAIR), 8 * count * width),
    )(places, *pin(x, n1), second, third, *pin(*parts), *pieces)


def last_kernel(pos, e1, x, mine, theirs, gain, out, held):
    step = pl.program_id(0)
    half = pl.num_programs(0) // 2
    size = e1.shape[0]

    @pl.when(step < half)
    def _():
        back = mine[...].astype(F32) + theirs[...].astype(F32)
        grad, _ = norm_back(x[...].astype(F32), gain[...], back)
        held[pl.ds(pl.multiple_of(step * size, size), size), :] = (
            e1[...].astype(F32) + grad
        ).astype(BF16)

    @pl.when(step >= half)
    def _():
        onehot = (
            lax.broadcasted_iota(jnp.int32, (held.shape[0], size), 0) == pos[0:1, :]
        ).astype(F32).astype(BF16)
        out[...] = dot(onehot, held[...], TN).astype(BF16)


def last_step(pos, e1, x, mine, theirs, gain):
    count, width = x.shape
    steps = count // ROWS

    def early(t):
        return (jnp.minimum(t, steps - 1), 0)

    def late(t):
        return jnp.maximum(t - steps, 0)

    tile = pl.BlockSpec((ROWS, width), early)
    return pl.pallas_call(
        last_kernel,
        grid=(2 * steps,),
        in_specs=[pl.BlockSpec((8, ROWS), lambda t: (0, late(t)))]
        + [tile] * 4
        + [whole((1, width))],
        out_specs=pl.BlockSpec((ROWS, width), lambda t: (late(t), 0)),
        out_shape=shape_of((count, width), BF16),
        scratch_shapes=[pltpu.VMEM((count, width), BF16)],
        compiler_params=params(),
        cost_estimate=cost(2 * count * count * width, 12 * count * width),
    )(pos, *pin(e1, x, mine), theirs, gain)


def swap(values, axis, distance):
    size = lax.axis_size(axis)
    return lax.ppermute(values, axis, [(i, i ^ distance) for i in range(size)])


def after(values, *others):
    return lax.optimization_barrier((values,) + others)[0]


def gather_all(values):
    return lax.all_gather(values, ("narrow", "wide"), axis=0, tiled=True).reshape(
        lax.axis_size("narrow"), -1, values.shape[1]
    )


def sum_wide(values):
    return lax.psum_scatter(values, "wide", scatter_dimension=0, tiled=True)


def add(left, right):
    return (left.astype(F32) + right.astype(F32)).astype(BF16)


def add_pair(keep, got):
    return add(keep[0], got[0]), add(keep[1], got[1])


def line_inner():
    place = lax.axis_index("dp")
    return (place == 1) | (place == 2)


def line_first(values):
    if lax.axis_size("dp") != 4:
        return lax.psum(values, "dp")
    got = lax.ppermute(values, "dp", [(0, 1), (3, 2)])
    return jnp.where(line_inner(), add(values, got), values)


def line_second(values):
    if lax.axis_size("dp") != 4:
        return values
    return add(values, lax.ppermute(values, "dp", [(1, 2), (2, 1)]))


def line_third(values, *others):
    if lax.axis_size("dp") != 4:
        return values
    got = after(lax.ppermute(values, "dp", [(1, 0), (2, 3)]), *others)
    return jnp.where(line_inner(), values, got)


def local(
    tokens,
    memory,
    cotangent,
    norm1_gain,
    norm2_gain,
    norm3_gain,
    q_weight,
    k_weight,
    v_weight,
    o_weight,
    cross_q,
    cross_k,
    cross_v,
    cross_o,
    gate_weight,
    up_weight,
    down_weight,
    segment_ids,
    block_ids,
    image_table,
):
    width = tokens.shape[1]
    share = q_weight.shape[0]
    inner = q_weight.shape[1]
    unit = gate_weight.shape[1]
    images = memory.shape[0]
    flat_memory = memory.reshape(-1, width)
    place = lax.axis_index("wide")
    side = lax.axis_index("narrow")
    places = jnp.stack([place, place ^ 2, place ^ 1, place ^ 3, side]).astype(jnp.int32)

    gains = jnp.stack([norm1_gain, norm2_gain, norm3_gain])
    gains = jnp.pad(gains, ((0, 13), (0, 3 * inner - share)))
    early = jnp.concatenate(
        [jnp.concatenate([q_weight, k_weight, v_weight], axis=1), gains], axis=0
    )
    early_x = swap(early, "wide", 2)
    early_core = swap(early, "wide", 1)
    early_pieces = (early, early_x, early_core, swap(early_x, "wide", 1))
    lines = jnp.stack([piece[share : share + 3, :share] for piece in early_pieces])
    lines = lines.astype(F32)
    order = [
        jnp.sum(jnp.where((places[:4] == w)[:, None, None], lines, 0.0), axis=0)
        for w in range(4)
    ]
    all_gains = jnp.concatenate(order, axis=1)[:, None, :]

    mid = jnp.concatenate([cross_k, cross_v, cross_q, o_weight], axis=1)
    memory_columns = slice(0, 2 * inner)
    query_columns = slice(2 * inner, 3 * inner)
    out_columns = slice(3 * inner, 4 * inner)
    mid_x = swap(after(mid, early_x), "wide", 2)
    mid_core = swap(mid, "wide", 1)
    out_y = swap(o_weight, "narrow", 1)
    late = jnp.concatenate([cross_q, cross_o, gate_weight, up_weight, down_weight], axis=1)
    late_query_columns = slice(0, inner)
    late_columns = (slice(inner, 2 * inner), slice(2 * inner, 2 * inner + 3 * unit))

    x, row_ids, col_ids, pos, scalars = order_rows(
        segment_ids, block_ids, image_table, after(tokens, early_core, out_y)
    )
    late = gather_all(after(late, early_x, x))
    n1, qkv = norm_project(places, x, all_gains[0], early_pieces)
    pairs = inner // PAIR
    self_parts = [self_forward(0, after(qkv, mid_core), row_ids, col_ids)]
    out_yx = after(swap(out_y, "wide", 2), self_parts[0][0])
    out_pieces = (out_y, out_yx, swap(out_y, "wide", 1), swap(out_yx, "wide", 1))
    for pair in range(1, pairs):
        waits = out_pieces if pair == pairs - 1 else ()
        self_parts.append(
            self_forward(pair, after(qkv, self_parts[-1][0], *waits), row_ids, col_ids)
        )
    mid_x = after(mid_x, self_parts[-1][0])
    mid_pieces = (mid, mid_x, mid_core, swap(mid_x, "wide", 1))
    gy = order_more(pos, after(cotangent, self_parts[-1][0]))
    attended_theirs = [swap(part[0], "narrow", 1) for part in self_parts]
    attended = [part[0] for part in self_parts]
    keys_values = project_memory(
        places,
        after(flat_memory, gy, attended_theirs[0]),
        mid_pieces,
        memory_columns,
    )
    h1, n2, cq = middle_step(
        places,
        after(x, keys_values),
        attended,
        attended_theirs,
        all_gains[1],
        mid_pieces,
        out_pieces,
        (out_columns, slice(0, inner), query_columns),
    )
    cross_parts = [cross_forward(0, scalars, cq, keys_values, images)]
    crossed_theirs = []
    for pair in range(1, pairs):
        previous = [cross_parts[-1][0]] + crossed_theirs
        crossed_theirs.append(swap(cross_parts[-1][0], "narrow", 1))
        cross_parts.append(
            cross_forward(pair, scalars, after(cq, *previous), keys_values, images)
        )
    crossed = [part[0] for part in cross_parts]
    crossed_theirs.append(swap(crossed[-1], "narrow", 1))
    cross_logs = jnp.concatenate([part[1] for part in cross_parts], axis=0)
    (
        output,
        n3,
        hidden,
        grad_gate,
        grad_up,
        e2,
        dc,
        cross_deltas,
        third_gain,
    ) = units_step(
        places,
        h1,
        crossed,
        crossed_theirs,
        all_gains[2],
        gy,
        late,
        late_columns,
    )

    unit_keep, unit_send = weight_grads(
        places, (n3, gy), (grad_gate, grad_up, hidden), ((0, (0,)), (0, (1,)), (1, (2,)))
    )
    unit_stay, unit_leave = add_pair(unit_keep, swap(unit_send, "wide", 1))
    dcq, dck, dcv = cross_backward(
        0,
        scalars,
        cq,
        keys_values,
        after(dc, unit_leave),
        cross_logs,
        cross_deltas,
        images,
        None,
    )
    unit_part = add(unit_stay, swap(unit_leave, "wide", 2))
    keep0, send0, more0, total = memory_back(
        places,
        flat_memory,
        after(dck, unit_part),
        dcv,
        mid_pieces,
        memory_columns,
        0,
        None,
        0,
    )
    unit_sum = lax.psum(unit_part, "dp")
    dcq, dck, dcv = cross_backward(
        1,
        scalars,
        cq,
        keys_values,
        after(dc, send0),
        cross_logs,
        cross_deltas,
        images,
        dcq,
    )
    dcq_theirs = swap(dcq, "narrow", 1)
    got0 = swap(send0, "narrow", 1)
    got_more = swap(after(more0, dcq), "narrow", 1)
    keep1, send1, cross_keep, cross_send = memory_back(
        places,
        flat_memory,
        after(dck, got0),
        dcv,
        mid_pieces,
        memory_columns,
        1,
        total,
        2 * inner,
    )
    cross_keep, cross_send = weight_grads(
        places,
        (after(n2, send1), e2),
        (dcq, crossed),
        ((0, (0,)), (1, (1,))),
        into=(cross_keep, cross_send),
        first=2,
    )
    e1, da, self_deltas, second_gain = turn_step(
        places,
        e2,
        h1,
        after(dcq, cross_send, unit_sum),
        dcq_theirs,
        all_gains[1],
        attended,
        mid_pieces,
        late,
        (out_columns, query_columns, late_query_columns),
    )
    got1 = swap(after(send1, dcq_theirs, got0), "narrow", 1)
    cross_stay, cross_leave = add_pair(cross_keep, swap(cross_send, "wide", 1))
    da = after(da, cross_leave)
    back = []
    for pair in range(pairs):
        ready = after(da, *[part[0] for part in back])
        if pair == pairs - 1:
            early_back = list(back)
            self_keep, self_send = weight_grads(
                places,
                (after(n1, back[-1][0]), e1),
                [[part[i] for part in early_back] for i in range(3)] + [attended],
                ((0, (0, 1, 2)), (1, (3,))),
            )
            cross_part = add(cross_stay, swap(cross_leave, "wide", 2))
            ready = after(ready, cross_part, self_send)
            cross_part = line_first(cross_part)
        back.append(
            self_backward(
                pair, qkv, ready, self_parts[pair][1], self_deltas, row_ids, col_ids
            )
        )
    dq, dk, dv = [[part[i] for part in back] for i in range(3)]
    self_stay, self_leave = add_pair(self_keep, swap(self_send, "wide", 1))
    self_part = add(self_stay, swap(self_leave, "wide", 2))
    dn1, last_keep, last_send = partial_step(
        places,
        dq + dk + dv,
        after(x, self_leave),
        n1,
        second_gain,
        third_gain,
        early_pieces,
    )
    dn1_theirs = swap(dn1, "narrow", 1)
    memory0 = add(after(keep0, dn1), jnp.concatenate([got0, got_more]))
    memory1 = add(after(keep1, dn1), got1)
    last_stay, last_leave = add_pair(last_keep, swap(last_send, "wide", 1))
    last_part = add(last_stay, swap(last_leave, "wide", 2))
    output = restore_rows(pos, after(output, last_send, self_part))
    tokens_grad = last_step(pos, e1, x, dn1, dn1_theirs, all_gains[0])
    memory_grad = jnp.stack([after(memory0, self_part), memory1])
    cross_sum = line_third(line_second(cross_part), tokens_grad)
    self_second = line_second(line_first(self_part))
    self_sum = line_third(self_second, tokens_grad)
    last_sum = line_third(line_second(line_first(last_part)))
    gain_sums = last_sum[share:, :share].astype(F32)
    first_gain = gain_sums[0] + swap(after(gain_sums, self_second), "narrow", 1)[0]

    def grads(array, size, count):
        return [array[:share, i * size : (i + 1) * size].astype(F32) for i in range(count)]

    gate_grad, up_grad, down_grad = grads(after(unit_sum, self_part), unit, 3)
    cross_k_grad, cross_v_grad, cross_q_grad, cross_o_grad = grads(cross_sum, inner, 4)
    part = inner - PAIR
    q_grad, k_grad, v_grad = [
        jnp.concatenate([most, rest], axis=1)
        for most, rest in zip(grads(self_sum, part, 3), grads(last_sum, PAIR, 3))
    ]
    o_grad = self_sum[:, 3 * part :].astype(F32)
    return (
        output,
        tokens_grad,
        memory_grad,
        first_gain,
        gain_sums[1],
        gain_sums[2],
        q_grad,
        k_grad,
        v_grad,
        o_grad,
        cross_q_grad,
        cross_k_grad,
        cross_v_grad,
        cross_o_grad,
        gate_grad,
        up_grad,
        down_grad,
    )


def solution(mesh):
    both = ("dp", "wide")
    weight = P("wide", "narrow")
    in_specs = (
        (P(both, None), P(both, None, None), P(both, None))
        + (P("wide"),) * 3
        + (weight,) * 11
        + (P(both, None),) * 3
    )
    out_specs = (
        (P(both, None), P(both, None), P(both, None, "narrow"))
        + (P("wide"),) * 3
        + (weight,) * 11
    )
    return jax.shard_map(local, mesh=mesh, in_specs=in_specs, out_specs=out_specs, check_vma=False)
```
